32 devices in a mesh: dp: 8 (over z, x), mp: 4 (over y, core).
Axes of the slice: x: 2, y: 2, z: 4, core: 2. Of those that a mesh axis runs over, the one named last changes fastest.
Arguments:
- big_copy: bfloat16 [4, 62208, 128], P('mp', 'dp')
- big_master: float32 [4, 62208, 128], P('mp', 'dp'), may hold values from -0.18 to 0.18
- big_first: float32 [4, 62208, 128], P('mp', 'dp'), may hold values from -9e-07 to 9e-07
- big_second: float32 [4, 62208, 128], P('mp', 'dp'), may hold values from 9.4e-16 to 1.5e-14
- ada_copy: bfloat16 [18579456], P(('dp', 'mp')), may hold values from -0.1875 to 0.1875
- ada_master: float32 [18579456], P(('dp', 'mp')), may hold values from -0.18 to 0.18
- ada_first: float32 [18579456], P(('dp', 'mp')), may hold values from -9e-07 to 9e-07
- ada_second: float32 [18579456], P(('dp', 'mp')), may hold values from 9.4e-16 to 1.5e-14
- rest_copy: bfloat16 [2813184], P(('dp', 'mp'))
- rest_master: float32 [2813184], P(('dp', 'mp')), may hold values from -0.18 to 0.18
- rest_first: float32 [2813184], P(('dp', 'mp')), may hold values from -9e-07 to 9e-07
- rest_second: float32 [2813184], P(('dp', 'mp')), may hold values from 9.4e-16 to 1.5e-14
- owner_tiles: int32 [62208], replicated, may hold values from 0 to 62207, as said below
- kept_patches: float32 [2, 32, 128, 16], P(None, ('dp', 'mp')), may hold values from -6 to 6
- kept_pos: int32 [2, 32, 128], P(None, ('dp', 'mp')), may hold values from 0 to 255, as said below
- timestep: int32 [2, 32], P(None, ('dp', 'mp')), may hold values from 0 to 999
- label: int32 [2, 32], P(None, ('dp', 'mp')), may hold values from 0 to 1000
- owner: int32 [2, 32], P(None, ('dp', 'mp')), may hold values from 0 to 7, as said below
- target: float32 [2, 32, 256, 16], P(None, ('dp', 'mp')), may hold values from -6 to 6
- step: int32 [1], replicated, may hold values from 1 to 20
Outputs:
- loss: float32 [1], replicated
- grad_norm: float32 [1], replicated
- big_master_new: float32 [4, 62208, 128], P('mp', 'dp')
- big_first_new: float32 [4, 62208, 128], P('mp', 'dp')
- big_second_new: float32 [4, 62208, 128], P('mp', 'dp')
- big_copy_new: bfloat16 [4, 62208, 128], P('mp', 'dp')
- ada_master_new: float32 [18579456], P(('dp', 'mp'))
- ada_first_new: float32 [18579456], P(('dp', 'mp'))
- ada_second_new: float32 [18579456], P(('dp', 'mp'))
- ada_copy_new: bfloat16 [18579456], P(('dp', 'mp'))
- rest_master_new: float32 [2813184], P(('dp', 'mp'))
- rest_first_new: float32 [2813184], P(('dp', 'mp'))
- rest_second_new: float32 [2813184], P(('dp', 'mp'))
- rest_copy_new: bfloat16 [2813184], P(('dp', 'mp'))
The draws below stay inside these ranges and needn't reach their ends.
Inputs may be any that keep to these rules, and one draw needn't show every extreme that they name: `owner_tiles`: a permutation of 0 .. 62207. `kept_pos`: the 128 positions of one image are distinct. For each micro-batch b and each m there is one r in 0 .. 8 - 1 with owner[b, d * 4 + m] = d XOR r for every d.
All inputs are finite; a program needn't handle non-finite values.
Results may differ from the reference program's by a relative error of at most 0.007.
Values may be sent and summed in bfloat16 or wider, within the bound.
A program may use at most 512 MiB of HBM per device.

```python
import math
import jax
import jax.numpy as jnp
from jax import lax

D = 1152
HEADS = 16
HD = 72
FF = 4608
PD = 16
FREQ = 256
CLASSES = 1001
GRID = 16
MICRO = 2
SEQ = 256
KEEP = 128
IMGS = 32
TILES = 62208
ADA = 18579456
REST = 2813184
N_DP = 8
N_MP = 4


def tile_order(key):
    return jax.random.permutation(jax.random.fold_in(key, 11), TILES).astype(jnp.int32)


def draw_owner_tiles(key, part):
    return tile_order(key)


def draw_big_copy(key, part):
    layer_length = TILES * 128 // 2
    head_width = HEADS * HD // N_MP
    hidden_width = FF // N_MP
    starts = jnp.arange(TILES, dtype=jnp.int32) * 128 % layer_length
    edge_one = D * 3 * head_width
    edge_two = edge_one + head_width * D
    edge_three = edge_two + D * hidden_width
    scales = jnp.where(starts < edge_one, D ** (-0.5), jnp.where(starts < edge_two, 3.0 * (HEADS * HD) ** (-0.5), jnp.where(starts < edge_three, D ** (-0.5), 1.5 * FF ** (-0.5))))
    scales = scales.astype(jnp.float32)[tile_order(key)]
    noise = jax.random.normal(jax.random.fold_in(key, 5), (N_MP, TILES, 128), jnp.float32)
    return (noise * scales[None, :, None]).astype(jnp.bfloat16)


def draw_rest_copy(key, part):
    total_rows = 2 * PD + FREQ + D + CLASSES + 1
    rows = jnp.arange(REST, dtype=jnp.int32) % total_rows
    edge_one = PD
    edge_two = edge_one + FREQ
    edge_three = edge_two + D
    edge_four = edge_three + CLASSES + 1
    scales = jnp.where(rows < edge_one, PD ** (-0.5), jnp.where(rows < edge_two, 1.4 * FREQ ** (-0.5), jnp.where(rows < edge_three, 1.6 * D ** (-0.5), jnp.where(rows < edge_four, 1.0, D ** (-0.5)))))
    noise = jax.random.normal(jax.random.fold_in(key, 6), (REST,), jnp.float32)
    return (noise * scales.astype(jnp.float32)).astype(jnp.bfloat16)


def draw_kept_pos(key, part):
    subkeys = jax.random.split(jax.random.fold_in(key, 3), MICRO * IMGS)
    picks = jax.vmap(lambda subkey: jax.random.permutation(subkey, SEQ)[:KEEP])(subkeys)
    return picks.reshape(MICRO, IMGS, KEEP).astype(jnp.int32)


def draw_owner(key, part):
    masks = jax.random.randint(jax.random.fold_in(key, 4), (MICRO, 1, N_MP), 0, N_DP).astype(jnp.int32)
    ranks = jnp.arange(N_DP, dtype=jnp.int32)[None, :, None]
    return jnp.bitwise_xor(ranks, masks).reshape(MICRO, IMGS).astype(jnp.int32)


def set_ends(array, own_key, least, largest):
    longest = array.shape.index(max(array.shape))
    spots = []
    for shift in (0, 1):
        where = [jax.random.randint(jax.random.fold_in(own_key, axis), (), 0, length) for axis, length in enumerate(array.shape)]
        where[longest] = (where[longest] + shift) % array.shape[longest]
        spots.append(tuple(where))
    return array.at[spots[0]].set(least).at[spots[1]].set(largest)


def shard_levels(stream_key, extent, cuts, smallest, high):
    factor_of = 1.0
    for position, parts in cuts:
        steps = jax.random.uniform(jax.random.fold_in(jax.random.fold_in(stream_key, 6), position), (parts,), jnp.float32, smallest / len(cuts), high / len(cuts))
        factor_of = factor_of * jnp.repeat(jnp.exp(steps), extent[position] // parts).reshape((-1,) + (1,) * (len(extent) - 1 - position))
    return factor_of


def normal_values(own_key, dims, deviation, most, cuts=(), kind=jnp.bfloat16):
    loudness = shard_levels(own_key, dims, cuts, -0.22, 0.18) if cuts else 1.0
    result = jax.random.normal(own_key, dims, jnp.float32) * deviation * loudness
    return jnp.minimum(jnp.maximum(result, -most), most).astype(kind)


def setup_inputs(seed: int = 0) -> dict:
    streams_of = jax.random.split(jax.random.key(seed), 21)
    return {
        "big_copy": draw_big_copy(jax.random.fold_in(streams_of[20], 71), 0),
        "big_master": normal_values(streams_of[1], (N_MP, TILES, 128), 0.03, 0.18, ((0, 4), (1, 8)), jnp.float32),
        "big_first": normal_values(streams_of[2], (N_MP, TILES, 128), 0.00000015, 8.999999749903509e-07, ((0, 4), (1, 8)), jnp.float32),
        "big_second": jnp.clip(jnp.exp(math.log(1.499999973677505e-14) - 2.7699256 * jax.random.uniform(streams_of[3], (N_MP, TILES, 128), jnp.float32) ** shard_levels(streams_of[3], (N_MP, TILES, 128), ((0, 4), (1, 8)), -0.2, 0.2)), 9.400000012922617e-16, 1.499999973677505e-14),
        "ada_copy": normal_values(streams_of[4], (ADA,), D ** -0.5, 0.1875, ((0, 32),)),
        "ada_master": normal_values(streams_of[5], (ADA,), 0.03, 0.18, ((0, 32),), jnp.float32),
        "ada_first": normal_values(streams_of[6], (ADA,), 0.00000015, 8.999999749903509e-07, ((0, 32),), jnp.float32),
        "ada_second": jnp.clip(jnp.exp(math.log(1.499999973677505e-14) - 2.7699256 * jax.random.uniform(streams_of[7], (ADA,), jnp.float32) ** shard_levels(streams_of[7], (ADA,), ((0, 32),), -0.2, 0.2)), 9.400000012922617e-16, 1.499999973677505e-14),
        "rest_copy": draw_rest_copy(jax.random.fold_in(streams_of[20], 71), 0),
        "rest_master": normal_values(streams_of[9], (REST,), 0.03, 0.18, ((0, 32),), jnp.float32),
        "rest_first": normal_values(streams_of[10], (REST,), 0.00000015, 8.999999749903509e-07, ((0, 32),), jnp.float32),
        "rest_second": jnp.clip(jnp.exp(math.log(1.499999973677505e-14) - 2.7699256 * jax.random.uniform(streams_of[11], (REST,), jnp.float32) ** shard_levels(streams_of[11], (REST,), ((0, 32),), -0.2, 0.2)), 9.400000012922617e-16, 1.499999973677505e-14),
        "owner_tiles": draw_owner_tiles(jax.random.fold_in(streams_of[20], 71), 0),
        "kept_patches": normal_values(streams_of[13], (MICRO, IMGS, KEEP, PD), 1.0, 6.0, ((1, 32),), jnp.float32),
        "kept_pos": draw_kept_pos(jax.random.fold_in(streams_of[20], 71), 0),
        "timestep": set_ends(jax.random.randint(streams_of[15], (MICRO, IMGS), 0, 1000), jax.random.fold_in(streams_of[15], 1), 0, 999).astype(jnp.int32),
        "label": set_ends(jax.random.randint(streams_of[16], (MICRO, IMGS), 0, CLASSES), jax.random.fold_in(streams_of[16], 1), 0, CLASSES - 1).astype(jnp.int32),
        "owner": draw_owner(jax.random.fold_in(streams_of[20], 71), 0),
        "target": normal_values(streams_of[18], (MICRO, IMGS, SEQ, PD), 1.0, 6.0, ((1, 32),), jnp.float32),
        "step": jax.random.randint(streams_of[19], (1,), 1, 21).astype(jnp.int32),
    }


@jax.custom_vjp
def low(v):
    return lax.optimization_barrier(v.astype(jnp.bfloat16)).astype(jnp.float32)

@jax.custom_vjp
def low_back(v):
    return v

def low_keep(v):
    return (low(v), None)

def low_pass(kept, grad):
    return (grad,)

def back_keep(v):
    return (v, None)

def back_low(kept, grad):
    return (low(grad),)
low.defvjp(low_keep, low_pass)
low_back.defvjp(back_keep, back_low)
EPS_NORM = 1e-06
MAX_NORM = 0.01
RATE = 0.02
DECAY = 0.1
BETA_ONE = 0.9
BETA_TWO = 0.999
ADAM_EPS = 1e-08
MASKED_WEIGHT = 0.1
highest = lax.Precision.HIGHEST

def matmul(left, right):
    return jnp.dot(left, right, precision=highest, preferred_element_type=jnp.float32)

def normalize(values):
    center = values - lax.optimization_barrier(jnp.mean(values, axis=-1, keepdims=True))
    return center * lax.rsqrt(lax.optimization_barrier(jnp.mean(center * center, axis=-1, keepdims=True)) + EPS_NORM)

def position_table(columns):
    quarter = columns // 4
    omegas = 1.0 / 10000.0 ** (jnp.arange(quarter, dtype=jnp.float32) / quarter)
    places = jnp.arange(GRID * GRID, dtype=jnp.int32)

    def half_table(coords):
        angles = coords.astype(jnp.float32)[:, None] * omegas[None, :]
        return jnp.concatenate([jnp.sin(angles), jnp.cos(angles)], axis=1)
    return jnp.concatenate([half_table(places % GRID), half_table(places // GRID)], axis=1)

def time_features(stamp):
    halves = FREQ // 2
    frequency = jnp.exp(-math.log(10000.0) * jnp.arange(halves, dtype=jnp.float32) / halves)
    angles = stamp.astype(jnp.float32) * frequency
    return jnp.concatenate([jnp.cos(angles), jnp.sin(angles)])

def layer_weights(big, level):
    head_width = HEADS * HD // N_MP
    hidden_width = FF // N_MP
    lengths = [D * 3 * head_width, head_width * D, D * hidden_width, hidden_width * D]
    offset = level * sum(lengths)
    pieces = []
    for length in lengths:
        pieces.append(big[:, offset:offset + length])
        offset += length
    packed = pieces[0].reshape(N_MP, D, 3, HEADS // N_MP, HD)
    project = [jnp.transpose(packed[:, :, index], (1, 0, 2, 3)).reshape(D, HEADS * HD) for index in range(3)]
    proj_weight = pieces[1].reshape(HEADS * HD, D)
    up_weight = jnp.transpose(pieces[2].reshape(N_MP, D, hidden_width), (1, 0, 2)).reshape(D, FF)
    down_weight = pieces[3].reshape(FF, D)
    return (project[0], project[1], project[2], proj_weight, up_weight, down_weight)

def split_rest(rest):
    matrix = rest.reshape(D, -1).T
    counts = [PD, FREQ, D, CLASSES, 1, PD]
    pieces = []
    offset = 0
    for count in counts:
        pieces.append(matrix[offset:offset + count])
        offset += count
    return (pieces[0], pieces[1], pieces[2], pieces[3], pieces[4][0], pieces[5].T)

def block(state, weights, modulate):
    query_weight, key_weight, value_weight, proj_weight, up_weight, down_weight = weights
    shift_one, scale_one, gate_one, shift_two, scale_two, gate_two = jnp.split(modulate, 6)
    rows = state.shape[0]
    hidden_one = low(normalize(state) * (1.0 + scale_one) + shift_one)

    def heads_of(weight):
        return low(low_back(matmul(hidden_one, weight))).reshape(rows, HEADS, HD)
    queries, key_rows, value_rows = (heads_of(query_weight), heads_of(key_weight), heads_of(value_weight))
    scores = low_back(jnp.einsum('qhe,khe->hqk', queries, key_rows, precision=highest))
    probs = low(jax.nn.softmax(scores * HD ** (-0.5), axis=-1))
    mixed = jnp.einsum('hqk,khe->qhe', probs, value_rows, precision=highest)
    attended = low(low_back(mixed)).reshape(rows, HEADS * HD)
    middle = state + gate_one * low_back(matmul(attended, proj_weight))
    hidden_two = low(normalize(middle) * (1.0 + scale_two) + shift_two)
    activated = low(jax.nn.gelu(low_back(matmul(hidden_two, up_weight)), approximate=True))
    return middle + gate_two * low_back(matmul(activated, down_weight))

def image_loss(big, ada, rest, item):
    patches, place, stamp, tag, goal = item
    embed_weight, time_one, time_two, table, mask_token, head_weight = split_rest(rest)
    features = low(time_features(stamp))[None, :]
    hidden_time = low(jax.nn.silu(matmul(features, time_one)))
    condition = matmul(hidden_time, time_two)[0] + table[tag]
    signal = low(jax.nn.silu(condition))[None, :]
    modulate = low_back(matmul(signal, ada))[0]
    positions = position_table(D)
    state = matmul(low(patches), embed_weight) + positions[place]
    state = block(state, layer_weights(big, 0), modulate[:6 * D])
    sent = low(low_back(state))
    hits = (jnp.arange(SEQ, dtype=jnp.int32)[:, None] == place[None, :]).astype(jnp.float32)
    kept = lax.optimization_barrier(jnp.sum(hits, axis=1, keepdims=True))
    state = matmul(hits, sent) + (1.0 - kept) * mask_token[None, :] + positions
    state = block(state, layer_weights(big, 1), modulate[6 * D:12 * D])
    head_in = low(normalize(state) * (1.0 + modulate[13 * D:]) + modulate[12 * D:13 * D])
    output = low_back(matmul(head_in, head_weight))
    error = output - goal
    weight = kept + MASKED_WEIGHT * (1.0 - kept)
    return jnp.sum(weight * error * error)

def adam_update(grad, master, first, second, clip, count):
    scaled = grad * clip
    first = BETA_ONE * first + (1.0 - BETA_ONE) * scaled
    second = BETA_TWO * second + (1.0 - BETA_TWO) * scaled * scaled
    fix_one = 1.0 - BETA_ONE ** count
    fix_two = 1.0 - BETA_TWO ** count
    master = master - RATE * (first / fix_one / (jnp.sqrt(second / fix_two) + ADAM_EPS) + DECAY * master)
    return (master, first, second, master.astype(jnp.bfloat16))

def reference(big_copy, big_master, big_first, big_second, ada_copy, ada_master, ada_first, ada_second, rest_copy, rest_master, rest_first, rest_second, owner_tiles, kept_patches, kept_pos, timestep, label, owner, target, step):
    inverse = jnp.zeros((TILES,), jnp.int32).at[owner_tiles].set(jnp.arange(TILES, dtype=jnp.int32))
    big = jnp.take(big_copy.astype(jnp.float32), inverse, axis=1).reshape(N_MP, TILES * 128)
    ada = ada_copy.astype(jnp.float32).reshape(D, 14 * D)
    rest = rest_copy.astype(jnp.float32)
    slots = owner * N_MP + jnp.arange(IMGS, dtype=jnp.int32)[None, :] % N_MP
    goals = jax.vmap(lambda whole, picks: whole[picks])(target, slots)
    data = (kept_patches.reshape(-1, KEEP, PD), kept_pos.reshape(-1, KEEP), timestep.reshape(-1), label.reshape(-1), goals.reshape(-1, SEQ, PD))

    def objective(big_value, ada_value, rest_value):
        per_image = lax.map(jax.checkpoint(lambda item: image_loss(big_value, ada_value, rest_value, item)), data)
        return jnp.sum(per_image) / (PD * MICRO * IMGS * KEEP)
    loss, pull = jax.vjp(objective, big, ada, rest)
    grad_big, grad_ada, grad_rest = pull(jnp.ones_like(loss))
    grad_tiles = grad_big.reshape(N_MP, TILES, 128)[:, owner_tiles]
    grad_ada = grad_ada.reshape(-1)
    squares = jnp.sum(grad_tiles * grad_tiles) + jnp.sum(grad_ada * grad_ada) + jnp.sum(grad_rest * grad_rest)
    grad_norm = jnp.sqrt(squares)
    clip = jnp.minimum(1.0, MAX_NORM / (grad_norm + 1e-06))
    count = step[0].astype(jnp.float32)
    big_out = adam_update(grad_tiles, big_master, big_first, big_second, clip, count)
    ada_out = adam_update(grad_ada, ada_master, ada_first, ada_second, clip, count)
    rest_out = adam_update(grad_rest, rest_master, rest_first, rest_second, clip, count)
    return (loss.reshape(1), grad_norm.reshape(1), big_out[0], big_out[1], big_out[2], big_out[3], ada_out[0], ada_out[1], ada_out[2], ada_out[3], rest_out[0], rest_out[1], rest_out[2], rest_out[3])
```

```python
import functools
import math

import jax
import jax.numpy as jnp
from jax import lax
from jax.experimental import pallas as pl
from jax.experimental.pallas import tpu as pltpu
from jax.sharding import PartitionSpec as P

D = 1152
HEADS = 16
HD = 72
FF = 4608
PD = 16
FREQ = 256
CLASSES = 1001
GRID = 16
SEQ = 256
KEEP = 128


EPS_NORM = 1e-06
MAX_NORM = 0.01
RATE = 0.02
DECAY = 0.1
BETA_ONE = 0.9
BETA_TWO = 0.999
ADAM_EPS = 1e-08
MASKED_WEIGHT = 0.1
highest = lax.Precision.HIGHEST


def partner_2(value, axis, stride):
    mask = 2**stride
    pairs = [(source, source ^ mask) for source in range(lax.axis_size(axis))]
    return lax.ppermute(value, axis, pairs)


def product(left, right):
    return jnp.dot(left, right, preferred_element_type=jnp.float32)


def normalize(values):
    center = values - jnp.mean(values, axis=-1, keepdims=True)
    spread = lax.rsqrt(jnp.mean(center * center, axis=-1, keepdims=True) + EPS_NORM)
    return (center * spread, spread)


def normalize_back(grad_normed, normed, spread):
    adjusted = grad_normed - jnp.mean(grad_normed, axis=-1, keepdims=True)
    adjusted = adjusted - normed * jnp.mean(grad_normed * normed, axis=-1, keepdims=True)
    return spread * adjusted


def position_table(columns):
    quarter = columns // 4
    omegas = 1.0 / 10000.0 ** (jnp.arange(quarter, dtype=jnp.float32) / quarter)
    places = jnp.arange(GRID * GRID, dtype=jnp.int32)

    def half_table(coords):
        angles = coords.astype(jnp.float32)[:, None] * omegas[None, :]
        return jnp.concatenate([jnp.sin(angles), jnp.cos(angles)], axis=1)

    return jnp.concatenate([half_table(places % GRID), half_table(places // GRID)], axis=1)


def time_features(stamp):
    halves = FREQ // 2
    frequency = jnp.exp(-math.log(10000.0) * jnp.arange(halves, dtype=jnp.float32) / halves)
    angles = stamp.astype(jnp.float32) * frequency
    return jnp.concatenate([jnp.cos(angles), jnp.sin(angles)])


def row_gather(values):
    return lax.all_gather(values, "mp", axis=0, tiled=True)


def row_sum(values):
    return lax.psum_scatter(values, "mp", scatter_dimension=0, tiled=True)


def route_bit(route, bit):
    return jnp.bitwise_and(jnp.right_shift(route, bit), 1) == 1


def route_ids(values, route, levels):
    for bit in range(levels):
        partner = partner_2(values, "dp", bit)
        values = jnp.where(route_bit(route, bit), partner, values)
    return values


def route_rows(values, route, levels):
    for bit in range(levels):
        partner = partner_2(values, "dp", bit)
        values = jnp.where(route_bit(route, bit), partner, values)
    return values


def route_back(values, route, levels):
    for bit in range(levels):
        partner = partner_2(values, "dp", bit)
        values = jnp.where(route_bit(route, bit), partner, values)
    return values


def unpack_big(flat, columns, groups):
    head_width = HEADS * HD // groups
    hidden_width = FF // groups
    shapes = [
        (columns, 3 * head_width),
        (head_width, columns),
        (columns, hidden_width),
        (hidden_width, columns),
    ]
    levels = []
    offset = 0
    for level_index in range(2):
        pieces = []
        for dims in shapes:
            length = dims[0] * dims[1]
            pieces.append(flat[offset : offset + length].reshape(dims))
            offset += length
        levels.append(tuple(pieces))
    return levels


def unpack_rest(flat, columns):
    matrix = flat.reshape(columns, -1).T
    counts = [PD, FREQ, columns, CLASSES, 1, PD]
    pieces = []
    offset = 0
    for count in counts:
        pieces.append(matrix[offset : offset + count])
        offset += count
    return (pieces[0], pieces[1], pieces[2], pieces[3], pieces[4][0], pieces[5].T)


def split_heads(packed, groups, rows):
    third = packed.shape[1] // 3
    return [
        packed[:, index * third : (index + 1) * third].reshape(groups, rows, third // HD, HD)
        for index in range(3)
    ]


def attention_probs(queries, key_rows):
    scores = jnp.einsum("gqhe,gkhe->ghqk", queries, key_rows, preferred_element_type=jnp.float32)
    return jax.nn.softmax(scores * HD ** (-0.5), axis=-1)


def block_forward(state, weights, modulate):
    qkv_weight, proj_weight, up_weight, down_weight = weights
    shift_one, scale_one, gate_one, shift_two, scale_two, gate_two = jnp.split(modulate, 6)
    rows = state.shape[0]
    normed_one, spread_one = normalize(state)
    full_one = row_gather((normed_one * (1.0 + scale_one) + shift_one).astype(jnp.bfloat16))
    groups = full_one.shape[0] // rows
    packed = product(full_one, qkv_weight).astype(jnp.bfloat16)
    queries, key_rows, value_rows = split_heads(packed, groups, rows)
    probs = attention_probs(queries, key_rows)
    mixed = jnp.einsum(
        "ghqk,gkhe->gqhe",
        probs.astype(jnp.bfloat16),
        value_rows,
        preferred_element_type=jnp.float32,
    )
    attended = mixed.astype(jnp.bfloat16).reshape(groups * rows, -1)
    branch_one = row_sum(product(attended, proj_weight))
    middle = state + gate_one * branch_one
    normed_two, spread_two = normalize(middle)
    full_two = row_gather((normed_two * (1.0 + scale_two) + shift_two).astype(jnp.bfloat16))
    hidden_pre = product(full_two, up_weight)
    activated = jax.nn.gelu(hidden_pre, approximate=True).astype(jnp.bfloat16)
    branch_two = row_sum(product(activated, down_weight))
    result = middle + gate_two * branch_two
    saved = (
        normed_one,
        spread_one,
        full_one,
        packed,
        attended,
        branch_one,
        normed_two,
        spread_two,
        full_two,
        hidden_pre,
        activated,
        branch_two,
    )
    return (result, saved)


def block_backward(grad_out, saved, weights, modulate):
    (
        normed_one,
        spread_one,
        full_one,
        packed,
        attended,
        branch_one,
        normed_two,
        spread_two,
        full_two,
        hidden_pre,
        activated,
        branch_two,
    ) = saved
    qkv_weight, proj_weight, up_weight, down_weight = weights
    shift_one, scale_one, gate_one, shift_two, scale_two, gate_two = jnp.split(modulate, 6)
    rows = grad_out.shape[0]
    groups = full_one.shape[0] // rows
    grad_gate_two = jnp.sum(grad_out * branch_two, axis=0)
    back_two = row_gather((gate_two * grad_out).astype(jnp.bfloat16))
    grad_down = product(activated.T, back_two)
    grad_act = product(back_two, down_weight.T)
    unused, gelu_back = jax.vjp(lambda pre: jax.nn.gelu(pre, approximate=True), hidden_pre)
    grad_pre = gelu_back(grad_act)[0].astype(jnp.bfloat16)
    grad_up = product(full_two.T, grad_pre)
    grad_hidden_two = row_sum(product(grad_pre, up_weight.T))
    grad_shift_two = jnp.sum(grad_hidden_two, axis=0)
    grad_scale_two = jnp.sum(grad_hidden_two * normed_two, axis=0)
    grad_middle = grad_out + normalize_back(
        grad_hidden_two * (1.0 + scale_two), normed_two, spread_two
    )
    grad_gate_one = jnp.sum(grad_middle * branch_one, axis=0)
    back_one = row_gather((gate_one * grad_middle).astype(jnp.bfloat16))
    grad_proj = product(attended.T, back_one)
    grad_attended = product(back_one, proj_weight.T).astype(jnp.bfloat16)
    queries, key_rows, value_rows = split_heads(packed, groups, rows)
    probs = attention_probs(queries, key_rows)
    grad_mixed = grad_attended.reshape(queries.shape)
    grad_probs = jnp.einsum(
        "gqhe,gkhe->ghqk", grad_mixed, value_rows, preferred_element_type=jnp.float32
    )
    grad_values = jnp.einsum(
        "ghqk,gqhe->gkhe",
        probs.astype(jnp.bfloat16),
        grad_mixed,
        preferred_element_type=jnp.float32,
    )
    grad_scores = (
        probs * (grad_probs - jnp.sum(grad_probs * probs, axis=-1, keepdims=True)) * HD ** (-0.5)
    )
    grad_scores = grad_scores.astype(jnp.bfloat16)
    grad_queries = jnp.einsum(
        "ghqk,gkhe->gqhe", grad_scores, key_rows, preferred_element_type=jnp.float32
    )
    grad_keys = jnp.einsum(
        "ghqk,gqhe->gkhe", grad_scores, queries, preferred_element_type=jnp.float32
    )
    grad_packed = jnp.concatenate(
        [
            grad_part.reshape(groups * rows, -1)
            for grad_part in (grad_queries, grad_keys, grad_values)
        ],
        axis=1,
    ).astype(jnp.bfloat16)
    grad_qkv = product(full_one.T, grad_packed)
    grad_hidden_one = row_sum(product(grad_packed, qkv_weight.T))
    grad_shift_one = jnp.sum(grad_hidden_one, axis=0)
    grad_scale_one = jnp.sum(grad_hidden_one * normed_one, axis=0)
    grad_state = grad_middle + normalize_back(
        grad_hidden_one * (1.0 + scale_one), normed_one, spread_one
    )
    grad_mod = jnp.concatenate(
        [
            grad_shift_one,
            grad_scale_one,
            grad_gate_one,
            grad_shift_two,
            grad_scale_two,
            grad_gate_two,
        ]
    )
    return (grad_state, grad_mod, (grad_qkv, grad_proj, grad_up, grad_down))


def condition(stamp, tag, time_one, time_two, table):
    features = time_features(stamp).astype(jnp.bfloat16)[None, :]
    pre_time = product(features, time_one)
    hidden_time = jax.nn.silu(pre_time).astype(jnp.bfloat16)
    cond_value = product(hidden_time, time_two)[0] + table[tag].astype(jnp.float32)
    signal = jax.nn.silu(cond_value).astype(jnp.bfloat16)
    return (signal, (features, pre_time, hidden_time, cond_value))


def condition_back(grad_signal, saved, time_two, tag, table_rows):
    features, pre_time, hidden_time, cond_value = saved
    unused, silu_back = jax.vjp(jax.nn.silu, cond_value)
    grad_cond = silu_back(grad_signal)[0]
    grad_time_two = hidden_time.astype(jnp.float32).T * grad_cond[None, :]
    grad_hidden = jnp.dot(time_two.astype(jnp.float32), grad_cond, precision=highest)
    unused_pre, pre_back = jax.vjp(jax.nn.silu, pre_time)
    grad_pre = pre_back(grad_hidden[None, :])[0]
    grad_time_one = features.astype(jnp.float32).T * grad_pre
    grad_table = (jnp.arange(table_rows, dtype=jnp.int32)[:, None] == tag) * grad_cond[None, :]
    return (grad_time_one, grad_time_two, grad_table)


def adam_update(grad, master, first, second, clip, count):
    scaled = grad * clip
    first = BETA_ONE * first + (1.0 - BETA_ONE) * scaled
    second = BETA_TWO * second + (1.0 - BETA_TWO) * scaled * scaled
    fix_one = 1.0 - BETA_ONE**count
    fix_two = 1.0 - BETA_TWO**count
    master = master - RATE * (
        first / fix_one / (jnp.sqrt(second / fix_two) + ADAM_EPS) + DECAY * master
    )
    return (master, first, second, master.astype(jnp.bfloat16))


def local_general(
    big_copy,
    big_master,
    big_first,
    big_second,
    ada_copy,
    ada_master,
    ada_first,
    ada_second,
    rest_copy,
    rest_master,
    rest_first,
    rest_second,
    owner_tiles,
    kept_patches,
    kept_pos,
    timestep,
    label,
    owner,
    target,
    step,
):
    groups = lax.axis_size("mp")
    ranks = lax.axis_size("dp")
    levels_dp = ranks.bit_length() - 1
    my_rank = lax.axis_index("dp")
    tiles = owner_tiles.shape[0]
    columns = D
    gathered = lax.all_gather(big_copy, "dp", axis=1, tiled=True)[0]
    inverse = jnp.zeros((tiles,), jnp.int32).at[owner_tiles].set(jnp.arange(tiles, dtype=jnp.int32))
    big_flat = jnp.take(gathered, inverse, axis=0).reshape(-1)
    ada_flat, rest_flat = (
        lax.all_gather(ada_copy, ("dp", "mp"), axis=0, tiled=True),
        lax.all_gather(rest_copy, ("dp", "mp"), axis=0, tiled=True),
    )
    levels = unpack_big(big_flat, columns, groups)
    ada_matrix = ada_flat.reshape(columns, 14 * columns)
    embed_weight, time_one, time_two, table, mask_token, head_weight = unpack_rest(
        rest_flat, columns
    )
    positions = position_table(columns)
    images = ranks * groups
    inv_count = 1.0 / (PD * kept_patches.shape[0] * images * KEEP)
    zeros_six = jnp.zeros((6 * columns,), jnp.bfloat16)
    zeros_eight = jnp.zeros((8 * columns,), jnp.bfloat16)

    def micro_step(carry, inputs):
        grads_big, grads_rest, loss_sum = carry
        patches, place, stamp, tag, dest, goal = inputs
        route = jnp.bitwise_xor(dest, my_rank)
        signal_enc, saved_enc = condition(stamp, tag, time_one, time_two, table)
        mod_enc = product(signal_enc[None, :], ada_matrix[:, : 6 * columns])[0]
        embedded = product(patches.astype(jnp.bfloat16), embed_weight) + jnp.take(
            positions, place, axis=0
        )
        enc_out, enc_saved = block_forward(embedded, levels[0], mod_enc)
        sent = enc_out.astype(jnp.bfloat16)
        meta = jnp.concatenate([place, stamp[None], tag[None]])
        got_meta = route_ids(meta, route, levels_dp)
        arrived = route_rows(sent, route, levels_dp)
        keep_rows = place.shape[0]
        dec_place = got_meta[:keep_rows]
        dec_tag = got_meta[keep_rows + 1]
        signal_dec, saved_dec = condition(got_meta[keep_rows], dec_tag, time_one, time_two, table)
        mod_dec = product(signal_dec[None, :], ada_matrix[:, 6 * columns :])[0]
        hits = jnp.arange(SEQ, dtype=jnp.int32)[:, None] == dec_place[None, :]
        kept = jnp.sum(hits.astype(jnp.float32), axis=1, keepdims=True)
        dec_in = (
            product(hits.astype(jnp.bfloat16), arrived)
            + (1.0 - kept) * mask_token.astype(jnp.float32)[None, :]
            + positions
        )
        dec_out, dec_saved = block_forward(dec_in, levels[1], mod_dec[: 6 * columns])
        final_shift = mod_dec[6 * columns : 7 * columns]
        final_scale = mod_dec[7 * columns :]
        normed_final, spread_final = normalize(dec_out)
        head_in = (normed_final * (1.0 + final_scale) + final_shift).astype(jnp.bfloat16)
        output = product(head_in, head_weight)
        error = output - goal
        weight = kept + MASKED_WEIGHT * (1.0 - kept)
        loss_part = jnp.sum(weight * error * error) * inv_count
        grad_output = (2.0 * inv_count * weight * error).astype(jnp.bfloat16)
        grad_head = product(head_in.T, grad_output)
        grad_head_in = product(grad_output, head_weight.T)
        grad_final = jnp.concatenate(
            [jnp.sum(grad_head_in, axis=0), jnp.sum(grad_head_in * normed_final, axis=0)]
        )
        grad_dec_out = normalize_back(
            grad_head_in * (1.0 + final_scale), normed_final, spread_final
        )
        grad_dec_in, grad_mod_dec, dec_grads = block_backward(
            grad_dec_out, dec_saved, levels[1], mod_dec[: 6 * columns]
        )
        grad_mask = jnp.sum((1.0 - kept) * grad_dec_in, axis=0)
        grad_arrived = jnp.take(grad_dec_in, dec_place, axis=0).astype(jnp.bfloat16)
        grad_sent = route_back(grad_arrived, route, levels_dp)
        grad_embedded, grad_mod_enc, enc_grads = block_backward(
            grad_sent.astype(jnp.float32), enc_saved, levels[0], mod_enc
        )
        grad_embed = jnp.dot(
            patches.astype(jnp.bfloat16).astype(jnp.float32).T, grad_embedded, precision=highest
        )
        vector_enc = grad_mod_enc.astype(jnp.bfloat16)
        vector_dec = jnp.concatenate([grad_mod_dec, grad_final]).astype(jnp.bfloat16)
        grad_signal_enc = product(ada_matrix[:, : 6 * columns], vector_enc)
        grad_signal_dec = product(ada_matrix[:, 6 * columns :], vector_dec)
        time_enc = condition_back(grad_signal_enc, saved_enc, time_two, tag, table.shape[0])
        time_dec = condition_back(grad_signal_dec, saved_dec, time_two, dec_tag, table.shape[0])
        rest_terms = [
            grad_embed,
            time_enc[0] + time_dec[0],
            time_enc[1] + time_dec[1],
            time_enc[2] + time_dec[2],
            grad_mask[None, :],
            grad_head.T,
        ]
        grads_rest = grads_rest + jnp.concatenate(rest_terms, axis=0)
        big_terms = [
            term.reshape(-1) for level_grads in (enc_grads, dec_grads) for term in level_grads
        ]
        grads_big = grads_big + jnp.concatenate(big_terms)
        signal_pair = jnp.stack([signal_enc, signal_dec])
        vector_pair = jnp.stack(
            [jnp.concatenate([vector_enc, zeros_eight]), jnp.concatenate([zeros_six, vector_dec])]
        )
        return ((grads_big, grads_rest, loss_sum + loss_part), (signal_pair, vector_pair))

    inputs = (
        kept_patches[:, 0],
        kept_pos[:, 0],
        timestep[:, 0],
        label[:, 0],
        owner[:, 0],
        target[:, 0],
    )
    start_carry = (
        jnp.zeros(big_flat.shape, jnp.float32),
        jnp.zeros((rest_flat.shape[0] // columns, columns), jnp.float32),
        jnp.zeros((), jnp.float32),
    )
    finals, factors = lax.scan(micro_step, start_carry, inputs)
    grads_big, grads_matrix, loss_sum = finals
    grads_rest = grads_matrix.T.reshape(-1)
    signal_rows = factors[0].reshape(-1, columns)
    vector_rows = factors[1].reshape(-1, 14 * columns)
    tile_part = jnp.take(grads_big.reshape(tiles, 128), owner_tiles, axis=0)
    owned_big = lax.psum_scatter(tile_part, "dp", scatter_dimension=0, tiled=True)
    local_ada = product(signal_rows.T, vector_rows).reshape(-1)
    owned_ada, owned_rest = (
        lax.psum_scatter(local_ada, ("dp", "mp"), scatter_dimension=0, tiled=True),
        lax.psum_scatter(grads_rest, ("dp", "mp"), scatter_dimension=0, tiled=True),
    )
    squares = (
        jnp.sum(owned_big * owned_big)
        + jnp.sum(owned_ada * owned_ada)
        + jnp.sum(owned_rest * owned_rest)
    )
    loss_total, square_total = lax.psum((loss_sum, squares), ("dp", "mp"))
    grad_norm = jnp.sqrt(square_total)
    clip = jnp.minimum(1.0, MAX_NORM / (grad_norm + 1e-06))
    count = step[0].astype(jnp.float32)
    big_out = adam_update(
        owned_big.reshape(big_master.shape), big_master, big_first, big_second, clip, count
    )
    ada_out = adam_update(owned_ada, ada_master, ada_first, ada_second, clip, count)
    rest_out = adam_update(owned_rest, rest_master, rest_first, rest_second, clip, count)
    return (
        loss_total.reshape(1),
        grad_norm.reshape(1),
        big_out[0],
        big_out[1],
        big_out[2],
        big_out[3],
        ada_out[0],
        ada_out[1],
        ada_out[2],
        ada_out[3],
        rest_out[0],
        rest_out[1],
        rest_out[2],
        rest_out[3],
    )


WORLD_AXES = ("dp", "mp")
CHUNK_ROWS = 1136
REST_ROWS = 2 * PD + FREQ + D + CLASSES + 1


def tile_place(tiles, ranks):
    counts = [count // ranks for count in matrix_tiles()]
    layer_tiles = sum(matrix_tiles())
    level = tiles // layer_tiles
    inside = tiles % layer_tiles
    dest = jnp.zeros_like(tiles)
    slot = jnp.zeros_like(tiles)
    start = 0
    base = 0
    for count, total in zip(counts, matrix_tiles()):
        local_tile = inside - start
        here = (local_tile >= 0) & (local_tile < total)
        dest = jnp.where(here, local_tile // count, dest)
        slot = jnp.where(here, base + level * count + local_tile % count, slot)
        start += total
        base += 2 * count
    return dest, slot


def matrix_tiles():
    groups = 4
    head_width = HEADS * HD // groups
    hidden_width = FF // groups
    sizes = [D * 3 * head_width, head_width * D, D * hidden_width, hidden_width * D]
    return [size // 128 for size in sizes]


def rank_within(dest, ranks):
    n = dest.shape[0]
    inner = 96
    outer = n // inner
    hot = (dest.reshape(outer, inner)[None] == jnp.arange(ranks)[:, None, None]).astype(jnp.bfloat16)
    upto = (jnp.arange(inner)[:, None] < jnp.arange(inner)[None, :]).astype(jnp.bfloat16)
    before = jnp.einsum("roi,ij->roj", hot, upto, preferred_element_type=jnp.float32)
    totals = jnp.sum(hot.astype(jnp.float32), axis=2)
    over = (jnp.arange(outer)[:, None] < jnp.arange(outer)[None, :]).astype(jnp.float32)
    prior = jnp.dot(totals, over, precision=highest)
    rank = jnp.sum(hot.astype(jnp.float32) * (before + prior[:, :, None]), axis=0)
    return rank.astype(jnp.int32).reshape(n), jnp.sum(totals, axis=1).astype(jnp.int32)


def widen(source, dest, rows):
    step = 16
    whole = rows // step

    def body(i, unused):
        at = pl.ds(pl.multiple_of(i * step, step), step)
        dest[at, :] = source[at, :].astype(dest.dtype)
        return unused

    lax.fori_loop(0, whole, body, 0)


def pack_kernel(n, capacity, pos_ref, slot_ref, fill_ref, x_ref, buf_ref, tag_ref, wide, sorted_rows):
    ranks = fill_ref.shape[0]
    total = ranks * capacity
    widen(x_ref, wide, n)

    def fill(r, unused):
        def one(i, carry):
            tag_ref[r * capacity + i] = n
            return carry

        return lax.fori_loop(fill_ref[r], capacity, one, unused)

    lax.fori_loop(0, ranks, fill, 0)

    def move(i, unused):
        for j in range(16):
            k = i * 16 + j
            p = pos_ref[k]
            sorted_rows[pl.ds(p, 1), :] = wide[pl.ds(k, 1), :]
            tag_ref[p] = slot_ref[k]
        return unused

    lax.fori_loop(0, n // 16, move, 0)
    widen(sorted_rows, buf_ref, total)


def scatter_kernel(n, total, tag_ref, buf_ref, out_ref, wide):
    widen(buf_ref, wide, total)

    def move(i, unused):
        for j in range(16):
            k = i * 16 + j
            out_ref[pl.ds(tag_ref[k], 1), :] = wide[pl.ds(k, 1), :]
        return unused

    lax.fori_loop(0, total // 16, move, 0)


def gather_kernel(total, index_ref, x_ref, out_ref, wide_out):
    def move(i, unused):
        for j in range(16):
            k = i * 16 + j
            wide_out[pl.ds(k, 1), :] = x_ref[pl.ds(index_ref[k], 1), :]
        return unused

    lax.fori_loop(0, total // 16, move, 0)
    widen(wide_out, out_ref, total)


SMEM = pl.BlockSpec(memory_space=pltpu.SMEM)
VMEM = pl.BlockSpec(memory_space=pltpu.VMEM)
PARAMS = pltpu.CompilerParams(vmem_limit_bytes=48 * 1024 * 1024)


def pack_rows(rows, pos, slot, fill, capacity):
    n = rows.shape[0]
    ranks = fill.shape[0]
    total = ranks * capacity
    return pl.pallas_call(
        functools.partial(pack_kernel, n, capacity),
        out_shape=(
            jax.ShapeDtypeStruct((total, 128), jnp.bfloat16),
            jax.ShapeDtypeStruct((total + 16,), jnp.int32),
        ),
        in_specs=[SMEM, SMEM, SMEM, VMEM],
        out_specs=(VMEM, SMEM),
        scratch_shapes=[
            pltpu.VMEM((n, 128), jnp.float32),
            pltpu.VMEM((total + 16, 128), jnp.float32),
        ],
        compiler_params=PARAMS,
        name="pack_rows",
    )(pos, slot, fill, rows)


def scatter_rows(rows, tags, n):
    total = rows.shape[0]
    return pl.pallas_call(
        functools.partial(scatter_kernel, n, total),
        out_shape=jax.ShapeDtypeStruct((n + 16, 128), jnp.float32),
        in_specs=[SMEM, VMEM],
        out_specs=VMEM,
        scratch_shapes=[pltpu.VMEM((total, 128), jnp.float32)],
        compiler_params=PARAMS,
        name="scatter_rows",
    )(tags, rows)


def gather_rows(rows, index, dtype):
    total = index.shape[0]
    return pl.pallas_call(
        functools.partial(gather_kernel, total),
        out_shape=jax.ShapeDtypeStruct((total, 128), dtype),
        in_specs=[SMEM, VMEM],
        out_specs=VMEM,
        scratch_shapes=[pltpu.VMEM((total, 128), jnp.float32)],
        compiler_params=PARAMS,
        name="gather_rows",
    )(index, rows)


def swap_ranks(buf, ranks):
    rest = buf.shape[1:]
    split = buf.reshape((ranks, buf.shape[0] // ranks) + rest)
    return lax.all_to_all(split, "dp", 0, 0).reshape(buf.shape)


def round_positions(dest, rank, counts, capacity, turn):
    ranks = counts.shape[0]
    low = turn * capacity
    inside = (rank >= low) & (rank < low + capacity)
    pos = jnp.where(inside, dest * capacity + rank - low, ranks * capacity)
    fill = jnp.clip(counts - low, 0, capacity)
    return pos, fill, inside


def tiles_to_slots(rows, dest, slot, rank, counts, rounds):
    n = rows.shape[0]
    ranks = counts.shape[0]

    def turn_of(turn):
        pos, fill, unused = round_positions(dest, rank, counts, CHUNK_ROWS, turn)
        buf, tags = pack_rows(rows, pos, slot, fill, CHUNK_ROWS)
        got = swap_ranks(buf, ranks)
        got_tags = swap_ranks(tags[: ranks * CHUNK_ROWS], ranks)
        return scatter_rows(got, got_tags, n), got_tags

    first, tags = turn_of(0)

    def more(carry):
        turn, slots = carry
        added, more_tags = turn_of(turn)
        fresh = jnp.zeros((n + 16,), jnp.bool_).at[more_tags].set(True)
        return turn + 1, jnp.where(fresh[:, None], added, slots)

    unused, slots = lax.while_loop(lambda carry: carry[0] < rounds, more, (1, first))
    return slots[:n], tags


def slots_to_tiles(slots, tags, dest, slot, rank, counts, rounds):
    n = dest.shape[0]
    ranks = counts.shape[0]
    padded = jnp.concatenate([slots, jnp.zeros((16, 128), slots.dtype)])

    def turn_of(turn, turn_tags):
        pos, unused, inside = round_positions(dest, rank, counts, CHUNK_ROWS, turn)
        buf = gather_rows(padded, turn_tags, jnp.bfloat16)
        got = swap_ranks(buf, ranks).astype(jnp.float32)
        return gather_rows(got, jnp.minimum(pos, ranks * CHUNK_ROWS - 1), jnp.float32), inside

    first, unused = turn_of(0, tags)

    def more(carry):
        turn, rows = carry
        pos, fill, unused = round_positions(dest, rank, counts, CHUNK_ROWS, turn)
        empty = jnp.full((ranks * CHUNK_ROWS + 1,), n, jnp.int32)
        turn_tags = swap_ranks(empty.at[pos].set(slot)[:-1].at[:].get(), ranks)
        added, inside = turn_of(turn, turn_tags)
        return turn + 1, jnp.where(inside[:, None], added, rows)

    unused, rows = lax.while_loop(lambda carry: carry[0] < rounds, more, (1, first))
    return rows


def slot_matrices(slots, ranks):
    widths = [3 * HEADS * HD // 4, D, FF // 4, D]
    levels = [[], []]
    base = 0
    for total, width in zip(matrix_tiles(), widths):
        count = total // ranks
        for level in range(2):
            part = slots[base : base + count]
            levels[level].append(part.reshape(count * 128 // width, width))
            base += count
    return levels


def matrices_slots(levels):
    parts = []
    for index in range(4):
        for level in range(2):
            parts.append(levels[level][index].reshape(-1, 128))
    return jnp.concatenate(parts)


def gather_matrix(part):
    whole = lax.all_gather(part, ("mp", "dp"), axis=0, tiled=False)
    groups = lax.axis_size("mp")
    return whole.reshape(groups, -1, part.shape[1])


def scatter_matrix(parts):
    ranks = lax.axis_size("dp")
    stacked = jnp.stack([part.reshape(ranks, -1, part.shape[1]) for part in parts])
    merged = stacked.reshape((-1,) + stacked.shape[2:])
    return lax.psum_scatter(merged, ("mp", "dp"), scatter_dimension=0, tiled=False)


def heads_of(packed, images):
    third = packed[0].shape[1] // 3
    pieces = []
    for index in range(3):
        cols = [
            part[:, index * third : (index + 1) * third].reshape(images, -1, third // HD, HD)
            for part in packed
        ]
        pieces.append(jnp.concatenate(cols, axis=2).transpose(0, 2, 1, 3))
    return pieces


def own_forward(state, weights, modulate):
    qkv_weight, proj_weight, up_weight, down_weight = weights
    groups = qkv_weight.shape[0]
    images, rows, columns = state.shape
    shift_one, scale_one, gate_one, shift_two, scale_two, gate_two = [
        modulate[:, index, None, :] for index in range(6)
    ]
    normed_one, spread_one = normalize(state)
    full_one = (normed_one * (1.0 + scale_one) + shift_one).astype(jnp.bfloat16)
    flat_one = full_one.reshape(-1, columns)
    packed = [product(flat_one, qkv_weight[m]).astype(jnp.bfloat16) for m in range(groups)]
    queries, key_rows, value_rows = heads_of(packed, images)
    scores = jnp.einsum(
        "ghqe,ghke->ghqk", queries, key_rows, preferred_element_type=jnp.float32
    )
    probs = jax.nn.softmax(scores * HD ** (-0.5), axis=-1)
    mixed = jnp.einsum(
        "ghqk,ghke->ghqe",
        probs.astype(jnp.bfloat16),
        value_rows,
        preferred_element_type=jnp.float32,
    ).astype(jnp.bfloat16)
    attended = mixed.transpose(0, 2, 1, 3).reshape(-1, columns)
    branch_one = product(attended, proj_weight.reshape(-1, columns)).reshape(state.shape)
    middle = state + gate_one * branch_one
    normed_two, spread_two = normalize(middle)
    full_two = (normed_two * (1.0 + scale_two) + shift_two).astype(jnp.bfloat16)
    flat_two = full_two.reshape(-1, columns)
    hidden_pre = [product(flat_two, up_weight[m]) for m in range(groups)]
    activated = [jax.nn.gelu(pre, approximate=True).astype(jnp.bfloat16) for pre in hidden_pre]
    branch_two = sum(product(activated[m], down_weight[m]) for m in range(groups))
    branch_two = branch_two.reshape(state.shape)
    result = middle + gate_two * branch_two
    saved = (
        normed_one,
        spread_one,
        flat_one,
        queries,
        key_rows,
        value_rows,
        attended,
        branch_one,
        normed_two,
        spread_two,
        flat_two,
        hidden_pre,
        activated,
        branch_two,
    )
    return (result, saved)


def own_backward(grad_out, saved, weights, modulate):
    (
        normed_one,
        spread_one,
        flat_one,
        queries,
        key_rows,
        value_rows,
        attended,
        branch_one,
        normed_two,
        spread_two,
        flat_two,
        hidden_pre,
        activated,
        branch_two,
    ) = saved
    qkv_weight, proj_weight, up_weight, down_weight = weights
    groups = qkv_weight.shape[0]
    images, rows, columns = grad_out.shape
    shift_one, scale_one, gate_one, shift_two, scale_two, gate_two = [
        modulate[:, index, None, :] for index in range(6)
    ]
    grad_gate_two = jnp.sum(grad_out * branch_two, axis=1)
    back_two = (gate_two * grad_out).astype(jnp.bfloat16).reshape(-1, columns)
    grad_down = []
    grad_up = []
    grad_pres = []
    for m in range(groups):
        grad_down.append(product(activated[m].T, back_two).astype(jnp.bfloat16))
        grad_act = product(back_two, down_weight[m].T)
        unused, gelu_back = jax.vjp(lambda pre: jax.nn.gelu(pre, approximate=True), hidden_pre[m])
        grad_pre = gelu_back(grad_act)[0].astype(jnp.bfloat16)
        grad_up.append(product(flat_two.T, grad_pre).astype(jnp.bfloat16))
        grad_pres.append(grad_pre)
    grad_hidden_two = sum(product(grad_pres[m], up_weight[m].T) for m in range(groups))
    grad_hidden_two = grad_hidden_two.reshape(grad_out.shape)
    grad_shift_two = jnp.sum(grad_hidden_two, axis=1)
    grad_scale_two = jnp.sum(grad_hidden_two * normed_two, axis=1)
    grad_middle = grad_out + normalize_back(
        grad_hidden_two * (1.0 + scale_two), normed_two, spread_two
    )
    grad_gate_one = jnp.sum(grad_middle * branch_one, axis=1)
    back_one = (gate_one * grad_middle).astype(jnp.bfloat16).reshape(-1, columns)
    grad_proj = product(attended.T, back_one).astype(jnp.bfloat16).reshape(groups, -1, columns)
    grad_attended = product(back_one, proj_weight.reshape(-1, columns).T).astype(jnp.bfloat16)
    grad_mixed = grad_attended.reshape(images, rows, HEADS, HD).transpose(0, 2, 1, 3)
    scores = jnp.einsum(
        "ghqe,ghke->ghqk", queries, key_rows, preferred_element_type=jnp.float32
    )
    probs = jax.nn.softmax(scores * HD ** (-0.5), axis=-1)
    grad_probs = jnp.einsum(
        "ghqe,ghke->ghqk", grad_mixed, value_rows, preferred_element_type=jnp.float32
    )
    grad_values = jnp.einsum(
        "ghqk,ghqe->ghke",
        probs.astype(jnp.bfloat16),
        grad_mixed,
        preferred_element_type=jnp.float32,
    )
    grad_scores = (
        probs * (grad_probs - jnp.sum(grad_probs * probs, axis=-1, keepdims=True)) * HD ** (-0.5)
    ).astype(jnp.bfloat16)
    grad_queries = jnp.einsum(
        "ghqk,ghke->ghqe", grad_scores, key_rows, preferred_element_type=jnp.float32
    )
    grad_keys = jnp.einsum(
        "ghqk,ghqe->ghke", grad_scores, queries, preferred_element_type=jnp.float32
    )
    parts = [
        part.astype(jnp.bfloat16).transpose(0, 2, 1, 3).reshape(images * rows, groups, -1)
        for part in (grad_queries, grad_keys, grad_values)
    ]
    grad_qkv = []
    grad_hidden_one = 0.0
    for m in range(groups):
        grad_packed = jnp.concatenate([part[:, m] for part in parts], axis=1)
        grad_qkv.append(product(flat_one.T, grad_packed).astype(jnp.bfloat16))
        grad_hidden_one = grad_hidden_one + product(grad_packed, qkv_weight[m].T)
    grad_hidden_one = grad_hidden_one.reshape(grad_out.shape)
    grad_shift_one = jnp.sum(grad_hidden_one, axis=1)
    grad_scale_one = jnp.sum(grad_hidden_one * normed_one, axis=1)
    grad_state = grad_middle + normalize_back(
        grad_hidden_one * (1.0 + scale_one), normed_one, spread_one
    )
    grad_mod = jnp.concatenate(
        [
            grad_shift_one,
            grad_scale_one,
            grad_gate_one,
            grad_shift_two,
            grad_scale_two,
            grad_gate_two,
        ],
        axis=1,
    )
    return (grad_state, grad_mod, (grad_qkv, [grad_proj[m] for m in range(groups)], grad_up, grad_down))


def contract(left, right, left_axis, right_axis):
    return lax.dot_general(
        left,
        right,
        (((left_axis,), (right_axis,)), ((), ())),
        preferred_element_type=jnp.float32,
    )


def contract_wide(left, right, left_axis, right_axis):
    return lax.dot_general(
        left.astype(jnp.float32),
        right.astype(jnp.float32),
        (((left_axis,), (right_axis,)), ((), ())),
        precision=highest,
        preferred_element_type=jnp.float32,
    )


def silu_back(values, grads):
    unused, pull = jax.vjp(jax.nn.silu, values)
    return pull(grads)[0]


def local(
    big_copy,
    big_master,
    big_first,
    big_second,
    ada_copy,
    ada_master,
    ada_first,
    ada_second,
    rest_copy,
    rest_master,
    rest_first,
    rest_second,
    owner_tiles,
    kept_patches,
    kept_pos,
    timestep,
    label,
    owner,
    target,
    step,
):
    groups = lax.axis_size("mp")
    ranks = lax.axis_size("dp")
    world = groups * ranks
    my_rank = lax.axis_index("dp")
    micro = kept_patches.shape[0]
    own_columns = D // world
    columns = D

    owned = big_copy.shape[1]
    all_dest, unused_slot = tile_place(owner_tiles, ranks)
    all_hot = all_dest.reshape(ranks, owned, 1) == jnp.arange(ranks)
    rounds = (jnp.max(jnp.sum(all_hot.astype(jnp.int32), axis=1)) + CHUNK_ROWS - 1) // CHUNK_ROWS
    own_tiles = lax.dynamic_slice(owner_tiles, (my_rank * owned,), (owned,))
    dest, slot = tile_place(own_tiles, ranks)
    rank, counts = rank_within(dest, ranks)
    slots, tags = tiles_to_slots(big_copy[0], dest, slot, rank, counts, rounds)
    slices = slot_matrices(slots.astype(jnp.bfloat16), ranks)
    weights = [[gather_matrix(part) for part in level] for level in slices]

    facts = jnp.concatenate([timestep[:, 0], label[:, 0]])
    facts = lax.all_gather(facts, WORLD_AXES, axis=0, tiled=False)
    stamps = facts[:, :micro].reshape(-1)
    tags_all = facts[:, micro:].reshape(-1)
    rest_own = rest_copy.reshape(own_columns, REST_ROWS)
    edges = [0, PD, PD + FREQ, PD + FREQ + D, PD + FREQ + D + CLASSES, REST_ROWS]
    win_t, one_t, two_t, table_t, tail_t = [
        rest_own[:, edges[i] : edges[i + 1]] for i in range(5)
    ]
    ends = lax.all_gather(
        jnp.concatenate([win_t, tail_t], axis=1), WORLD_AXES, axis=0, tiled=True
    )
    embed_weight = ends[:, :PD].T
    mask_token = ends[:, PD].astype(jnp.float32)
    head_weight = ends[:, PD + 1 :]
    features = jax.vmap(time_features)(stamps).astype(jnp.bfloat16)
    pre_time = contract(features, one_t, 1, 1)
    hidden_own = jax.nn.silu(pre_time).astype(jnp.bfloat16)
    hidden_all = lax.all_gather(hidden_own.T, WORLD_AXES, axis=0, tiled=True)
    picks = (tags_all[:, None] == jnp.arange(CLASSES, dtype=jnp.int32)[None, :]).astype(
        jnp.bfloat16
    )
    cond_own = contract(hidden_all, two_t, 0, 1) + contract(picks, table_t, 1, 1)
    signal_own = jax.nn.silu(cond_own).astype(jnp.bfloat16)
    ada_own = ada_copy.reshape(own_columns, 14 * columns)
    mods = lax.psum_scatter(
        product(signal_own, ada_own), WORLD_AXES, scatter_dimension=0, tiled=True
    )
    mod_enc = mods[:, : 6 * columns].reshape(micro, 6, columns)
    mod_dec = mods[:, 6 * columns : 12 * columns].reshape(micro, 6, columns)
    final_shift = mods[:, None, 12 * columns : 13 * columns]
    final_scale = mods[:, None, 13 * columns :]

    goals = lax.all_gather(target[:, 0], "dp", axis=0, tiled=False)
    goal = jnp.stack([goals[owner[b, 0], b] for b in range(micro)])
    positions = position_table(columns)
    images = ranks * groups
    inv_count = 1.0 / (PD * micro * images * KEEP)
    place = kept_pos[:, 0]
    patches = kept_patches[:, 0].astype(jnp.bfloat16)
    hits = (
        jnp.arange(SEQ, dtype=jnp.int32)[None, :, None] == place[:, None, :]
    ).astype(jnp.float32)
    hits_low = hits.astype(jnp.bfloat16)
    kept = jnp.sum(hits, axis=2)[:, :, None]
    embedded = product(patches.reshape(-1, PD), embed_weight).reshape(micro, KEEP, columns)
    embedded = embedded + jnp.take(positions, place, axis=0)
    enc_out, enc_saved = own_forward(embedded, weights[0], mod_enc)
    sent = enc_out.astype(jnp.bfloat16)
    dec_in = (
        jnp.einsum("bpr,brd->bpd", hits_low, sent, preferred_element_type=jnp.float32)
        + (1.0 - kept) * mask_token[None, None, :]
        + positions[None]
    )
    dec_out, dec_saved = own_forward(dec_in, weights[1], mod_dec)
    normed_final, spread_final = normalize(dec_out)
    head_in = (normed_final * (1.0 + final_scale) + final_shift).astype(jnp.bfloat16)
    flat_head = head_in.reshape(-1, columns)
    output = product(flat_head, head_weight).reshape(micro, SEQ, PD)
    error = output - goal
    weight = kept + MASKED_WEIGHT * (1.0 - kept)
    loss_sum = jnp.sum(weight * error * error) * inv_count

    grad_output = (2.0 * inv_count * weight * error).astype(jnp.bfloat16).reshape(-1, PD)
    grad_head = contract(grad_output, flat_head, 0, 0)
    grad_head_in = product(grad_output, head_weight.T).reshape(dec_out.shape)
    grad_final = jnp.concatenate(
        [jnp.sum(grad_head_in, axis=1), jnp.sum(grad_head_in * normed_final, axis=1)], axis=1
    )
    grad_dec_out = normalize_back(grad_head_in * (1.0 + final_scale), normed_final, spread_final)
    grad_dec_in, grad_mod_dec, dec_grads = own_backward(
        grad_dec_out, dec_saved, weights[1], mod_dec
    )
    dec_sums = [scatter_matrix(parts) for parts in dec_grads]
    grad_mask = jnp.sum((1.0 - kept) * grad_dec_in, axis=(0, 1))[None, :]
    grad_sent = jnp.einsum(
        "bpr,bpd->brd",
        hits_low,
        grad_dec_in.astype(jnp.bfloat16),
        preferred_element_type=jnp.float32,
    )
    grad_embedded, grad_mod_enc, enc_grads = own_backward(
        grad_sent, enc_saved, weights[0], mod_enc
    )
    enc_sums = [scatter_matrix(parts) for parts in enc_grads]
    grad_embed = contract_wide(
        patches.reshape(-1, PD), grad_embedded.reshape(-1, columns), 0, 0
    )

    vectors = jnp.concatenate([grad_mod_enc, grad_mod_dec, grad_final], axis=1)
    vectors = lax.all_gather(vectors.astype(jnp.bfloat16), WORLD_AXES, axis=0, tiled=True)
    owned_ada = contract(signal_own, vectors, 0, 0).reshape(-1)
    grad_signal = contract(vectors, ada_own, 1, 1)
    grad_cond = silu_back(cond_own, grad_signal)
    grad_two_t = contract_wide(grad_cond, hidden_all, 0, 1)
    grad_table_t = contract_wide(grad_cond, picks, 0, 0)
    shared = jnp.concatenate(
        [contract_wide(grad_cond, two_t, 1, 0), grad_embed, grad_mask, grad_head], axis=0
    )
    shared = shared.reshape(-1, world, own_columns).transpose(1, 0, 2)
    shared = lax.psum_scatter(shared, WORLD_AXES, scatter_dimension=0, tiled=False)
    count_all = micro * world
    grad_pre = silu_back(pre_time, shared[:count_all])
    grad_one_t = contract_wide(grad_pre, features, 0, 0)
    ends_t = shared[count_all:].T
    owned_rest = jnp.concatenate(
        [ends_t[:, :PD], grad_one_t, grad_two_t, grad_table_t, ends_t[:, PD:]], axis=1
    ).reshape(-1)

    sums = matrices_slots(
        [[part.astype(jnp.float32) for part in level] for level in (enc_sums, dec_sums)]
    )
    squares = jnp.sum(sums * sums) + jnp.sum(owned_ada * owned_ada) + jnp.sum(owned_rest * owned_rest)
    totals = lax.psum(jnp.stack([loss_sum, squares]), WORLD_AXES)
    owned_big = slots_to_tiles(sums, tags, dest, slot, rank, counts, rounds)
    grad_norm = jnp.sqrt(totals[1])
    clip = jnp.minimum(1.0, MAX_NORM / (grad_norm + 1e-06))
    count = step[0].astype(jnp.float32)
    big_out = adam_update(
        owned_big.reshape(big_master.shape), big_master, big_first, big_second, clip, count
    )
    ada_out = adam_update(owned_ada, ada_master, ada_first, ada_second, clip, count)
    rest_out = adam_update(owned_rest, rest_master, rest_first, rest_second, clip, count)
    return (
        totals[:1],
        grad_norm.reshape(1),
        big_out[0],
        big_out[1],
        big_out[2],
        big_out[3],
        ada_out[0],
        ada_out[1],
        ada_out[2],
        ada_out[3],
        rest_out[0],
        rest_out[1],
        rest_out[2],
        rest_out[3],
    )


def whole_columns(mesh):
    ranks, groups = mesh.shape["dp"], mesh.shape["mp"]
    return groups == 4 and D % (ranks * groups) == 0 and ranks == 8


def solution(mesh):
    body = local if whole_columns(mesh) else local_general
    in_specs = (
        P("mp", "dp", None),
        P("mp", "dp", None),
        P("mp", "dp", None),
        P("mp", "dp", None),
        P(("dp", "mp")),
        P(("dp", "mp")),
        P(("dp", "mp")),
        P(("dp", "mp")),
        P(("dp", "mp")),
        P(("dp", "mp")),
        P(("dp", "mp")),
        P(("dp", "mp")),
        P(),
        P(None, ("dp", "mp"), None, None),
        P(None, ("dp", "mp"), None),
        P(None, ("dp", "mp")),
        P(None, ("dp", "mp")),
        P(None, ("dp", "mp")),
        P(None, ("dp", "mp"), None, None),
        P(),
    )
    out_specs = (
        P(),
        P(),
        P("mp", "dp", None),
        P("mp", "dp", None),
        P("mp", "dp", None),
        P("mp", "dp", None),
        P(("dp", "mp")),
        P(("dp", "mp")),
        P(("dp", "mp")),
        P(("dp", "mp")),
        P(("dp", "mp")),
        P(("dp", "mp")),
        P(("dp", "mp")),
        P(("dp", "mp")),
    )
    return jax.shard_map(body, mesh=mesh, in_specs=in_specs, out_specs=out_specs, check_vma=False)
```

```python
import functools
import math

import jax
import jax.numpy as jnp
from jax import lax
from jax.experimental import pallas as pl
from jax.experimental.pallas import tpu as pltpu
from jax.sharding import PartitionSpec as P

D = 1152
HEADS = 16
HD = 72
FF = 4608
PD = 16
FREQ = 256
CLASSES = 1001
GRID = 16
SEQ = 256
KEEP = 128


EPS_NORM = 1e-06
MAX_NORM = 0.01
RATE = 0.02
DECAY = 0.1
BETA_ONE = 0.9
BETA_TWO = 0.999
ADAM_EPS = 1e-08
MASKED_WEIGHT = 0.1
highest = lax.Precision.HIGHEST


def partner_2(value, axis, stride):
    mask = 2**stride
    pairs = [(source, source ^ mask) for source in range(lax.axis_size(axis))]
    return lax.ppermute(value, axis, pairs)


def product(left, right):
    return jnp.dot(left, right, preferred_element_type=jnp.float32)


def normalize(values):
    center = values - jnp.mean(values, axis=-1, keepdims=True)
    spread = lax.rsqrt(jnp.mean(center * center, axis=-1, keepdims=True) + EPS_NORM)
    return (center * spread, spread)


def normalize_back(grad_normed, normed, spread):
    adjusted = grad_normed - jnp.mean(grad_normed, axis=-1, keepdims=True)
    adjusted = adjusted - normed * jnp.mean(grad_normed * normed, axis=-1, keepdims=True)
    return spread * adjusted


def position_table(columns):
    quarter = columns // 4
    omegas = 1.0 / 10000.0 ** (jnp.arange(quarter, dtype=jnp.float32) / quarter)
    places = jnp.arange(GRID * GRID, dtype=jnp.int32)

    def half_table(coords):
        angles = coords.astype(jnp.float32)[:, None] * omegas[None, :]
        return jnp.concatenate([jnp.sin(angles), jnp.cos(angles)], axis=1)

    return jnp.concatenate([half_table(places % GRID), half_table(places // GRID)], axis=1)


def time_features(stamp):
    halves = FREQ // 2
    frequency = jnp.exp(-math.log(10000.0) * jnp.arange(halves, dtype=jnp.float32) / halves)
    angles = stamp.astype(jnp.float32) * frequency
    return jnp.concatenate([jnp.cos(angles), jnp.sin(angles)])


def row_gather(values):
    return lax.all_gather(values, "mp", axis=0, tiled=True)


def row_sum(values):
    return lax.psum_scatter(values, "mp", scatter_dimension=0, tiled=True)


def route_bit(route, bit):
    return jnp.bitwise_and(jnp.right_shift(route, bit), 1) == 1


def route_ids(values, route, levels):
    for bit in range(levels):
        partner = partner_2(values, "dp", bit)
        values = jnp.where(route_bit(route, bit), partner, values)
    return values


def route_rows(values, route, levels):
    for bit in range(levels):
        partner = partner_2(values, "dp", bit)
        values = jnp.where(route_bit(route, bit), partner, values)
    return values


def route_back(values, route, levels):
    for bit in range(levels):
        partner = partner_2(values, "dp", bit)
        values = jnp.where(route_bit(route, bit), partner, values)
    return values


def unpack_big(flat, columns, groups):
    head_width = HEADS * HD // groups
    hidden_width = FF // groups
    shapes = [
        (columns, 3 * head_width),
        (head_width, columns),
        (columns, hidden_width),
        (hidden_width, columns),
    ]
    levels = []
    offset = 0
    for level_index in range(2):
        pieces = []
        for dims in shapes:
            length = dims[0] * dims[1]
            pieces.append(flat[offset : offset + length].reshape(dims))
            offset += length
        levels.append(tuple(pieces))
    return levels


def unpack_rest(flat, columns):
    matrix = flat.reshape(columns, -1).T
    counts = [PD, FREQ, columns, CLASSES, 1, PD]
    pieces = []
    offset = 0
    for count in counts:
        pieces.append(matrix[offset : offset + count])
        offset += count
    return (pieces[0], pieces[1], pieces[2], pieces[3], pieces[4][0], pieces[5].T)


def split_heads(packed, groups, rows):
    third = packed.shape[1] // 3
    return [
        packed[:, index * third : (index + 1) * third].reshape(groups, rows, third // HD, HD)
        for index in range(3)
    ]


def attention_probs(queries, key_rows):
    scores = jnp.einsum("gqhe,gkhe->ghqk", queries, key_rows, preferred_element_type=jnp.float32)
    return jax.nn.softmax(scores * HD ** (-0.5), axis=-1)


def block_forward(state, weights, modulate):
    qkv_weight, proj_weight, up_weight, down_weight = weights
    shift_one, scale_one, gate_one, shift_two, scale_two, gate_two = jnp.split(modulate, 6)
    rows = state.shape[0]
    normed_one, spread_one = normalize(state)
    full_one = row_gather((normed_one * (1.0 + scale_one) + shift_one).astype(jnp.bfloat16))
    groups = full_one.shape[0] // rows
    packed = product(full_one, qkv_weight).astype(jnp.bfloat16)
    queries, key_rows, value_rows = split_heads(packed, groups, rows)
    probs = attention_probs(queries, key_rows)
    mixed = jnp.einsum(
        "ghqk,gkhe->gqhe",
        probs.astype(jnp.bfloat16),
        value_rows,
        preferred_element_type=jnp.float32,
    )
    attended = mixed.astype(jnp.bfloat16).reshape(groups * rows, -1)
    branch_one = row_sum(product(attended, proj_weight))
    middle = state + gate_one * branch_one
    normed_two, spread_two = normalize(middle)
    full_two = row_gather((normed_two * (1.0 + scale_two) + shift_two).astype(jnp.bfloat16))
    hidden_pre = product(full_two, up_weight)
    activated = jax.nn.gelu(hidden_pre, approximate=True).astype(jnp.bfloat16)
    branch_two = row_sum(product(activated, down_weight))
    result = middle + gate_two * branch_two
    saved = (
        normed_one,
        spread_one,
        full_one,
        packed,
        attended,
        branch_one,
        normed_two,
        spread_two,
        full_two,
        hidden_pre,
        activated,
        branch_two,
    )
    return (result, saved)


def block_backward(grad_out, saved, weights, modulate):
    (
        normed_one,
        spread_one,
        full_one,
        packed,
        attended,
        branch_one,
        normed_two,
        spread_two,
        full_two,
        hidden_pre,
        activated,
        branch_two,
    ) = saved
    qkv_weight, proj_weight, up_weight, down_weight = weights
    shift_one, scale_one, gate_one, shift_two, scale_two, gate_two = jnp.split(modulate, 6)
    rows = grad_out.shape[0]
    groups = full_one.shape[0] // rows
    grad_gate_two = jnp.sum(grad_out * branch_two, axis=0)
    back_two = row_gather((gate_two * grad_out).astype(jnp.bfloat16))
    grad_down = product(activated.T, back_two)
    grad_act = product(back_two, down_weight.T)
    unused, gelu_back = jax.vjp(lambda pre: jax.nn.gelu(pre, approximate=True), hidden_pre)
    grad_pre = gelu_back(grad_act)[0].astype(jnp.bfloat16)
    grad_up = product(full_two.T, grad_pre)
    grad_hidden_two = row_sum(product(grad_pre, up_weight.T))
    grad_shift_two = jnp.sum(grad_hidden_two, axis=0)
    grad_scale_two = jnp.sum(grad_hidden_two * normed_two, axis=0)
    grad_middle = grad_out + normalize_back(
        grad_hidden_two * (1.0 + scale_two), normed_two, spread_two
    )
    grad_gate_one = jnp.sum(grad_middle * branch_one, axis=0)
    back_one = row_gather((gate_one * grad_middle).astype(jnp.bfloat16))
    grad_proj = product(attended.T, back_one)
    grad_attended = product(back_one, proj_weight.T).astype(jnp.bfloat16)
    queries, key_rows, value_rows = split_heads(packed, groups, rows)
    probs = attention_probs(queries, key_rows)
    grad_mixed = grad_attended.reshape(queries.shape)
    grad_probs = jnp.einsum(
        "gqhe,gkhe->ghqk", grad_mixed, value_rows, preferred_element_type=jnp.float32
    )
    grad_values = jnp.einsum(
        "ghqk,gqhe->gkhe",
        probs.astype(jnp.bfloat16),
        grad_mixed,
        preferred_element_type=jnp.float32,
    )
    grad_scores = (
        probs * (grad_probs - jnp.sum(grad_probs * probs, axis=-1, keepdims=True)) * HD ** (-0.5)
    )
    grad_scores = grad_scores.astype(jnp.bfloat16)
    grad_queries = jnp.einsum(
        "ghqk,gkhe->gqhe", grad_scores, key_rows, preferred_element_type=jnp.float32
    )
    grad_keys = jnp.einsum(
        "ghqk,gqhe->gkhe", grad_scores, queries, preferred_element_type=jnp.float32
    )
    grad_packed = jnp.concatenate(
        [
            grad_part.reshape(groups * rows, -1)
            for grad_part in (grad_queries, grad_keys, grad_values)
        ],
        axis=1,
    ).astype(jnp.bfloat16)
    grad_qkv = product(full_one.T, grad_packed)
    grad_hidden_one = row_sum(product(grad_packed, qkv_weight.T))
    grad_shift_one = jnp.sum(grad_hidden_one, axis=0)
    grad_scale_one = jnp.sum(grad_hidden_one * normed_one, axis=0)
    grad_state = grad_middle + normalize_back(
        grad_hidden_one * (1.0 + scale_one), normed_one, spread_one
    )
    grad_mod = jnp.concatenate(
        [
            grad_shift_one,
            grad_scale_one,
            grad_gate_one,
            grad_shift_two,
            grad_scale_two,
            grad_gate_two,
        ]
    )
    return (grad_state, grad_mod, (grad_qkv, grad_proj, grad_up, grad_down))


def condition(stamp, tag, time_one, time_two, table):
    features = time_features(stamp).astype(jnp.bfloat16)[None, :]
    pre_time = product(features, time_one)
    hidden_time = jax.nn.silu(pre_time).astype(jnp.bfloat16)
    cond_value = product(hidden_time, time_two)[0] + table[tag].astype(jnp.float32)
    signal = jax.nn.silu(cond_value).astype(jnp.bfloat16)
    return (signal, (features, pre_time, hidden_time, cond_value))


def condition_back(grad_signal, saved, time_two, tag, table_rows):
    features, pre_time, hidden_time, cond_value = saved
    unused, silu_back = jax.vjp(jax.nn.silu, cond_value)
    grad_cond = silu_back(grad_signal)[0]
    grad_time_two = hidden_time.astype(jnp.float32).T * grad_cond[None, :]
    grad_hidden = jnp.dot(time_two.astype(jnp.float32), grad_cond, precision=highest)
    unused_pre, pre_back = jax.vjp(jax.nn.silu, pre_time)
    grad_pre = pre_back(grad_hidden[None, :])[0]
    grad_time_one = features.astype(jnp.float32).T * grad_pre
    grad_table = (jnp.arange(table_rows, dtype=jnp.int32)[:, None] == tag) * grad_cond[None, :]
    return (grad_time_one, grad_time_two, grad_table)


def adam_update(grad, master, first, second, clip, count):
    scaled = grad * clip
    first = BETA_ONE * first + (1.0 - BETA_ONE) * scaled
    second = BETA_TWO * second + (1.0 - BETA_TWO) * scaled * scaled
    fix_one = 1.0 - BETA_ONE**count
    fix_two = 1.0 - BETA_TWO**count
    master = master - RATE * (
        first / fix_one / (jnp.sqrt(second / fix_two) + ADAM_EPS) + DECAY * master
    )
    return (master, first, second, master.astype(jnp.bfloat16))


def local_general(
    big_copy,
    big_master,
    big_first,
    big_second,
    ada_copy,
    ada_master,
    ada_first,
    ada_second,
    rest_copy,
    rest_master,
    rest_first,
    rest_second,
    owner_tiles,
    kept_patches,
    kept_pos,
    timestep,
    label,
    owner,
    target,
    step,
):
    groups = lax.axis_size("mp")
    ranks = lax.axis_size("dp")
    levels_dp = ranks.bit_length() - 1
    my_rank = lax.axis_index("dp")
    tiles = owner_tiles.shape[0]
    columns = D
    gathered = lax.all_gather(big_copy, "dp", axis=1, tiled=True)[0]
    inverse = jnp.zeros((tiles,), jnp.int32).at[owner_tiles].set(jnp.arange(tiles, dtype=jnp.int32))
    big_flat = jnp.take(gathered, inverse, axis=0).reshape(-1)
    ada_flat, rest_flat = (
        lax.all_gather(ada_copy, ("dp", "mp"), axis=0, tiled=True),
        lax.all_gather(rest_copy, ("dp", "mp"), axis=0, tiled=True),
    )
    levels = unpack_big(big_flat, columns, groups)
    ada_matrix = ada_flat.reshape(columns, 14 * columns)
    embed_weight, time_one, time_two, table, mask_token, head_weight = unpack_rest(
        rest_flat, columns
    )
    positions = position_table(columns)
    images = ranks * groups
    inv_count = 1.0 / (PD * kept_patches.shape[0] * images * KEEP)
    zeros_six = jnp.zeros((6 * columns,), jnp.bfloat16)
    zeros_eight = jnp.zeros((8 * columns,), jnp.bfloat16)

    def micro_step(carry, inputs):
        grads_big, grads_rest, loss_sum = carry
        patches, place, stamp, tag, dest, goal = inputs
        route = jnp.bitwise_xor(dest, my_rank)
        signal_enc, saved_enc = condition(stamp, tag, time_one, time_two, table)
        mod_enc = product(signal_enc[None, :], ada_matrix[:, : 6 * columns])[0]
        embedded = product(patches.astype(jnp.bfloat16), embed_weight) + jnp.take(
            positions, place, axis=0
        )
        enc_out, enc_saved = block_forward(embedded, levels[0], mod_enc)
        sent = enc_out.astype(jnp.bfloat16)
        meta = jnp.concatenate([place, stamp[None], tag[None]])
        got_meta = route_ids(meta, route, levels_dp)
        arrived = route_rows(sent, route, levels_dp)
        keep_rows = place.shape[0]
        dec_place = got_meta[:keep_rows]
        dec_tag = got_meta[keep_rows + 1]
        signal_dec, saved_dec = condition(got_meta[keep_rows], dec_tag, time_one, time_two, table)
        mod_dec = product(signal_dec[None, :], ada_matrix[:, 6 * columns :])[0]
        hits = jnp.arange(SEQ, dtype=jnp.int32)[:, None] == dec_place[None, :]
        kept = jnp.sum(hits.astype(jnp.float32), axis=1, keepdims=True)
        dec_in = (
            product(hits.astype(jnp.bfloat16), arrived)
            + (1.0 - kept) * mask_token.astype(jnp.float32)[None, :]
            + positions
        )
        dec_out, dec_saved = block_forward(dec_in, levels[1], mod_dec[: 6 * columns])
        final_shift = mod_dec[6 * columns : 7 * columns]
        final_scale = mod_dec[7 * columns :]
        normed_final, spread_final = normalize(dec_out)
        head_in = (normed_final * (1.0 + final_scale) + final_shift).astype(jnp.bfloat16)
        output = product(head_in, head_weight)
        error = output - goal
        weight = kept + MASKED_WEIGHT * (1.0 - kept)
        loss_part = jnp.sum(weight * error * error) * inv_count
        grad_output = (2.0 * inv_count * weight * error).astype(jnp.bfloat16)
        grad_head = product(head_in.T, grad_output)
        grad_head_in = product(grad_output, head_weight.T)
        grad_final = jnp.concatenate(
            [jnp.sum(grad_head_in, axis=0), jnp.sum(grad_head_in * normed_final, axis=0)]
        )
        grad_dec_out = normalize_back(
            grad_head_in * (1.0 + final_scale), normed_final, spread_final
        )
        grad_dec_in, grad_mod_dec, dec_grads = block_backward(
            grad_dec_out, dec_saved, levels[1], mod_dec[: 6 * columns]
        )
        grad_mask = jnp.sum((1.0 - kept) * grad_dec_in, axis=0)
        grad_arrived = jnp.take(grad_dec_in, dec_place, axis=0).astype(jnp.bfloat16)
        grad_sent = route_back(grad_arrived, route, levels_dp)
        grad_embedded, grad_mod_enc, enc_grads = block_backward(
            grad_sent.astype(jnp.float32), enc_saved, levels[0], mod_enc
        )
        grad_embed = jnp.dot(
            patches.astype(jnp.bfloat16).astype(jnp.float32).T, grad_embedded, precision=highest
        )
        vector_enc = grad_mod_enc.astype(jnp.bfloat16)
        vector_dec = jnp.concatenate([grad_mod_dec, grad_final]).astype(jnp.bfloat16)
        grad_signal_enc = product(ada_matrix[:, : 6 * columns], vector_enc)
        grad_signal_dec = product(ada_matrix[:, 6 * columns :], vector_dec)
        time_enc = condition_back(grad_signal_enc, saved_enc, time_two, tag, table.shape[0])
        time_dec = condition_back(grad_signal_dec, saved_dec, time_two, dec_tag, table.shape[0])
        rest_terms = [
            grad_embed,
            time_enc[0] + time_dec[0],
            time_enc[1] + time_dec[1],
            time_enc[2] + time_dec[2],
            grad_mask[None, :],
            grad_head.T,
        ]
        grads_rest = grads_rest + jnp.concatenate(rest_terms, axis=0)
        big_terms = [
            term.reshape(-1) for level_grads in (enc_grads, dec_grads) for term in level_grads
        ]
        grads_big = grads_big + jnp.concatenate(big_terms)
        signal_pair = jnp.stack([signal_enc, signal_dec])
        vector_pair = jnp.stack(
            [jnp.concatenate([vector_enc, zeros_eight]), jnp.concatenate([zeros_six, vector_dec])]
        )
        return ((grads_big, grads_rest, loss_sum + loss_part), (signal_pair, vector_pair))

    inputs = (
        kept_patches[:, 0],
        kept_pos[:, 0],
        timestep[:, 0],
        label[:, 0],
        owner[:, 0],
        target[:, 0],
    )
    start_carry = (
        jnp.zeros(big_flat.shape, jnp.float32),
        jnp.zeros((rest_flat.shape[0] // columns, columns), jnp.float32),
        jnp.zeros((), jnp.float32),
    )
    finals, factors = lax.scan(micro_step, start_carry, inputs)
    grads_big, grads_matrix, loss_sum = finals
    grads_rest = grads_matrix.T.reshape(-1)
    signal_rows = factors[0].reshape(-1, columns)
    vector_rows = factors[1].reshape(-1, 14 * columns)
    tile_part = jnp.take(grads_big.reshape(tiles, 128), owner_tiles, axis=0)
    owned_big = lax.psum_scatter(tile_part, "dp", scatter_dimension=0, tiled=True)
    local_ada = product(signal_rows.T, vector_rows).reshape(-1)
    owned_ada, owned_rest = (
        lax.psum_scatter(local_ada, ("dp", "mp"), scatter_dimension=0, tiled=True),
        lax.psum_scatter(grads_rest, ("dp", "mp"), scatter_dimension=0, tiled=True),
    )
    squares = (
        jnp.sum(owned_big * owned_big)
        + jnp.sum(owned_ada * owned_ada)
        + jnp.sum(owned_rest * owned_rest)
    )
    loss_total, square_total = lax.psum((loss_sum, squares), ("dp", "mp"))
    grad_norm = jnp.sqrt(square_total)
    clip = jnp.minimum(1.0, MAX_NORM / (grad_norm + 1e-06))
    count = step[0].astype(jnp.float32)
    big_out = adam_update(
        owned_big.reshape(big_master.shape), big_master, big_first, big_second, clip, count
    )
    ada_out = adam_update(owned_ada, ada_master, ada_first, ada_second, clip, count)
    rest_out = adam_update(owned_rest, rest_master, rest_first, rest_second, clip, count)
    return (
        loss_total.reshape(1),
        grad_norm.reshape(1),
        big_out[0],
        big_out[1],
        big_out[2],
        big_out[3],
        ada_out[0],
        ada_out[1],
        ada_out[2],
        ada_out[3],
        rest_out[0],
        rest_out[1],
        rest_out[2],
        rest_out[3],
    )


CHUNK_ROWS = 1136
REST_ROWS = 2 * PD + FREQ + D + CLASSES + 1


def tile_place(tiles, ranks):
    counts = [count // ranks for count in matrix_tiles()]
    layer_tiles = sum(matrix_tiles())
    level = tiles // layer_tiles
    inside = tiles % layer_tiles
    dest = jnp.zeros_like(tiles)
    slot = jnp.zeros_like(tiles)
    start = 0
    base = 0
    for count, total in zip(counts, matrix_tiles()):
        local_tile = inside - start
        here = (local_tile >= 0) & (local_tile < total)
        dest = jnp.where(here, local_tile // count, dest)
        slot = jnp.where(here, base + level * count + local_tile % count, slot)
        start += total
        base += 2 * count
    return dest, slot


def matrix_tiles():
    groups = 4
    head_width = HEADS * HD // groups
    hidden_width = FF // groups
    sizes = [D * 3 * head_width, head_width * D, D * hidden_width, hidden_width * D]
    return [size // 128 for size in sizes]


def rank_within(dest, ranks):
    n = dest.shape[0]
    inner = 96
    outer = n // inner
    hot = (dest.reshape(outer, inner)[None] == jnp.arange(ranks)[:, None, None]).astype(jnp.bfloat16)
    upto = (jnp.arange(inner)[:, None] < jnp.arange(inner)[None, :]).astype(jnp.bfloat16)
    before = jnp.einsum("roi,ij->roj", hot, upto, preferred_element_type=jnp.float32)
    totals = jnp.sum(hot.astype(jnp.float32), axis=2)
    over = (jnp.arange(outer)[:, None] < jnp.arange(outer)[None, :]).astype(jnp.float32)
    prior = jnp.dot(totals, over, precision=highest)
    rank = jnp.sum(hot.astype(jnp.float32) * (before + prior[:, :, None]), axis=0)
    return rank.astype(jnp.int32).reshape(n), jnp.sum(totals, axis=1).astype(jnp.int32)


def widen(source, dest, rows):
    step = 16
    whole = rows // step

    def body(i, unused):
        at = pl.ds(pl.multiple_of(i * step, step), step)
        dest[at, :] = source[at, :].astype(dest.dtype)
        return unused

    lax.fori_loop(0, whole, body, 0)


def pack_kernel(n, capacity, pos_ref, slot_ref, fill_ref, x_ref, buf_ref, tag_ref, wide, sorted_rows):
    ranks = fill_ref.shape[0]
    total = ranks * capacity
    widen(x_ref, wide, n)

    def fill(r, unused):
        def one(i, carry):
            tag_ref[r * capacity + i] = n
            return carry

        return lax.fori_loop(fill_ref[r], capacity, one, unused)

    lax.fori_loop(0, ranks, fill, 0)

    def move(i, unused):
        for j in range(16):
            k = i * 16 + j
            p = pos_ref[k]
            sorted_rows[pl.ds(p, 1), :] = wide[pl.ds(k, 1), :]
            tag_ref[p] = slot_ref[k]
        return unused

    lax.fori_loop(0, n // 16, move, 0)
    widen(sorted_rows, buf_ref, total)


def scatter_kernel(n, total, tag_ref, buf_ref, out_ref, wide):
    widen(buf_ref, wide, total)

    def move(i, unused):
        for j in range(16):
            k = i * 16 + j
            out_ref[pl.ds(tag_ref[k], 1), :] = wide[pl.ds(k, 1), :]
        return unused

    lax.fori_loop(0, total // 16, move, 0)


def gather_kernel(total, index_ref, x_ref, out_ref, wide_out):
    def move(i, unused):
        for j in range(16):
            k = i * 16 + j
            wide_out[pl.ds(k, 1), :] = x_ref[pl.ds(index_ref[k], 1), :]
        return unused

    lax.fori_loop(0, total // 16, move, 0)
    widen(wide_out, out_ref, total)


SMEM = pl.BlockSpec(memory_space=pltpu.SMEM)
VMEM = pl.BlockSpec(memory_space=pltpu.VMEM)
PARAMS = pltpu.CompilerParams(vmem_limit_bytes=48 * 1024 * 1024)


def pack_rows(rows, pos, slot, fill, capacity):
    n = rows.shape[0]
    ranks = fill.shape[0]
    total = ranks * capacity
    return pl.pallas_call(
        functools.partial(pack_kernel, n, capacity),
        out_shape=(
            jax.ShapeDtypeStruct((total, 128), jnp.bfloat16),
            jax.ShapeDtypeStruct((total + 16,), jnp.int32),
        ),
        in_specs=[SMEM, SMEM, SMEM, VMEM],
        out_specs=(VMEM, SMEM),
        scratch_shapes=[
            pltpu.VMEM((n, 128), jnp.float32),
            pltpu.VMEM((total + 16, 128), jnp.float32),
        ],
        compiler_params=PARAMS,
        name="pack_rows",
    )(pos, slot, fill, rows)


def scatter_rows(rows, tags, n):
    total = rows.shape[0]
    return pl.pallas_call(
        functools.partial(scatter_kernel, n, total),
        out_shape=jax.ShapeDtypeStruct((n + 16, 128), jnp.float32),
        in_specs=[SMEM, VMEM],
        out_specs=VMEM,
        scratch_shapes=[pltpu.VMEM((total, 128), jnp.float32)],
        compiler_params=PARAMS,
        name="scatter_rows",
    )(tags, rows)


def gather_rows(rows, index, dtype):
    total = index.shape[0]
    return pl.pallas_call(
        functools.partial(gather_kernel, total),
        out_shape=jax.ShapeDtypeStruct((total, 128), dtype),
        in_specs=[SMEM, VMEM],
        out_specs=VMEM,
        scratch_shapes=[pltpu.VMEM((total, 128), jnp.float32)],
        compiler_params=PARAMS,
        name="gather_rows",
    )(index, rows)


MESH = pl.DeviceIdType.MESH
LAG = 2
SLOTS = 4
GATHER_SLOTS = 12


def coordinates():
    rank = lax.axis_index("dp")
    group = lax.axis_index("mp")
    return lax.div(rank, 2), lax.rem(rank, 2), lax.div(group, 2), lax.rem(group, 2)


def device_at(z, x, y, core):
    return (z * 2 + x, y * 2 + core)


def neighbours():
    z, x, y, core = coordinates()
    along_x = device_at(z, 1 - x, y, core)
    along_y = device_at(z, x, 1 - y, core)
    first = tuple(jnp.where(core == 0, b, a) for a, b in zip(along_x, along_y))
    second = tuple(jnp.where(core == 0, a, b) for a, b in zip(along_x, along_y))
    others = [device_at(lax.rem(z + step, 4), x, y, core) for step in (1, 2, 3)]
    return device_at(z, x, y, 1 - core), first, second, others


def greet(peers):
    barrier = pltpu.get_barrier_semaphore()
    for peer in peers:
        pl.semaphore_signal(barrier, inc=1, device_id=peer, device_id_type=MESH)
    pl.semaphore_wait(barrier, len(peers))


def block_of(ref, entry, group, at, side=None):
    stacked, rows, width = entry
    sides = slice(None) if side is None else side
    if stacked:
        return ref.at[group, :, sides, at, :]
    return ref.at[:, sides, at, pl.ds(pl.multiple_of(group * width, 128), width)]


def slice_of(ref, entry, group, z, x, at):
    stacked, rows, width = entry
    if stacked:
        return ref.at[group, z, x, at, :]
    return ref.at[z, x, at, pl.ds(pl.multiple_of(group * width, 128), width)]


def chunk_ranges(plan, chunk):
    ranges = []
    start = 0
    for stacked, rows, width in plan:
        ranges.append((start, start + rows // chunk))
        start += rows // chunk
    return ranges, start


def in_range(unit, low, high):
    return (unit >= low) & (unit < high)


def remote(source, target, send, receive, peer):
    return pltpu.make_async_remote_copy(
        src_ref=source,
        dst_ref=target,
        send_sem=send,
        recv_sem=receive,
        device_id=peer,
        device_id_type=MESH,
    )


def gather_whole_kernel(plan, chunk, *refs):
    count = len(plan)
    slices, wholes = refs[:count], refs[count : 2 * count]
    held, other_held, own_sem, out_sem, z_send, z_recv, a_send, a_recv, b_send, b_recv, c_send, c_recv = refs[2 * count :]
    z, x, y, core = coordinates()
    other, first, second, others = neighbours()
    mine_first = jnp.where(core == 0, y, x)
    mine_second = jnp.where(core == 0, x, y)
    ranges, total = chunk_ranges(plan, chunk)
    greet([other, first, second] + others)

    def copies(stage, k, unit):
        entry = plan[k]
        slot = lax.rem(unit, GATHER_SLOTS)
        at = pl.ds(pl.multiple_of((unit - ranges[k][0]) * chunk, chunk), chunk)
        cols = pl.ds(0, entry[2])
        own = held.at[slot, mine_first, mine_second, z, :, cols]
        if stage == 0:
            source = slices[k].at[at, :]
            return [pltpu.make_async_copy(source, own, own_sem.at[slot])] + [
                remote(source, own, z_send.at[i, slot], z_recv.at[i, slot], others[i])
                for i in range(3)
            ]
        if stage == 1:
            part = held.at[slot, mine_first, mine_second, :, :, cols]
            return [remote(part, part, a_send.at[slot], a_recv.at[slot], second)]
        if stage == 2:
            part = held.at[slot, mine_first, :, :, :, cols]
            return [remote(part, part, b_send.at[slot], b_recv.at[slot], first)]
        if stage == 3:
            source = held.at[slot, :, :, :, :, cols]
            target = other_held.at[slot, :, :, :, :, cols]
            return [remote(source, target, c_send.at[slot], c_recv.at[slot], other)]
        made = []
        from_other = stage == 5
        ref, owner = (other_held, 1 - core) if from_other else (held, core)
        for i in range(2):
            for j in range(2):
                side = jnp.where(owner == 0, j, i)
                group = 2 * jnp.where(owner == 0, i, j) + owner
                made.append(
                    pltpu.make_async_copy(
                        ref.at[slot, i, j, :, :, cols],
                        block_of(wholes[k], entry, group, at, side),
                        out_sem.at[int(from_other), 2 * i + j, slot],
                    )
                )
        return made

    def go(unit, waits, starts):
        for k in range(count):

            @pl.when(in_range(unit, *ranges[k]))
            def _(k=k):
                for stage in waits:
                    for copy in copies(stage, k, unit):
                        copy.wait()
                for stage in starts:
                    for copy in copies(stage, k, unit):
                        copy.start()

    def step(t, unused):
        go(t - 1 - 4 * LAG, (4, 5), ())
        go(t - 4 * LAG, (3,), (5,))
        go(t - 3 * LAG, (2,), (3, 4))
        go(t - 2 * LAG, (1,), (2,))
        go(t - LAG, (0,), (1,))
        go(t, (), (0,))
        return unused

    lax.fori_loop(0, total + 1 + 4 * LAG, step, 0)


def whole_shape(entry):
    stacked, rows, width = entry
    return (4, 4, 2, rows, width) if stacked else (4, 2, rows, 4 * width)


def gather_whole(plan, slices, chunk, number, name):
    ANY = pl.BlockSpec(memory_space=pl.ANY)
    count = len(plan)
    dma = pltpu.SemaphoreType.DMA
    kind = slices[0].dtype
    size = sum(math.prod(whole_shape(entry)) for entry in plan) * kind.itemsize
    held = pltpu.VMEM((GATHER_SLOTS, 2, 2, 4, chunk, max(entry[2] for entry in plan)), kind)
    each = dma((GATHER_SLOTS,))
    three = dma((3, GATHER_SLOTS))
    return pl.pallas_call(
        functools.partial(gather_whole_kernel, plan, chunk),
        out_shape=[jax.ShapeDtypeStruct(whole_shape(entry), kind) for entry in plan],
        in_specs=[ANY] * count,
        out_specs=[ANY] * count,
        scratch_shapes=[held, held, each, dma((2, 4, GATHER_SLOTS)), three, three] + [each] * 6,
        compiler_params=pltpu.CompilerParams(
            collective_id=number, has_side_effects=True, vmem_limit_bytes=48 * 1024 * 1024
        ),
        cost_estimate=pl.CostEstimate(flops=0, bytes_accessed=2 * size, transcendentals=0),
        name=name,
    )(*slices)


def sum_slices_kernel(plan, chunk, *refs):
    count = len(plan)
    parts, outs = refs[:count], refs[count : 2 * count]
    (own, from_core, from_first, from_second, from_z, half, quarter, eighth) = refs[
        2 * count : 2 * count + 8
    ]
    own_sem, core_send, core_recv, a_send, a_recv, b_send, b_recv, z_send, z_recv = refs[
        2 * count + 8 :
    ]
    z, x, y, core = coordinates()
    other, first, second, others = neighbours()
    mine_first = jnp.where(core == 0, y, x)
    mine_second = jnp.where(core == 0, x, y)
    ranges, total = chunk_ranges(plan, chunk)
    greet([other, first, second] + others)

    def copies(stage, width, unit, k=None):
        slot = lax.rem(unit, SLOTS)
        pair = lax.rem(unit, 2)
        cols = pl.ds(0, width)
        if stage == 0:
            made = []
            for j in range(2):
                mine = own.at[pair, j, :, :, :, cols]
                theirs = from_core.at[pair, j, :, :, :, cols]
                if k is None:
                    made.append(pltpu.make_async_copy(mine, mine, own_sem.at[j, pair]))
                    made.append(remote(mine, theirs, core_send.at[j, pair], core_recv.at[j, pair], other))
                else:
                    at = pl.ds(pl.multiple_of((unit - ranges[k][0]) * chunk, chunk), chunk)
                    kept = block_of(parts[k], plan[k], 2 * j + core, at)
                    sent = block_of(parts[k], plan[k], 2 * j + 1 - core, at)
                    made.append(pltpu.make_async_copy(kept, mine, own_sem.at[j, pair]))
                    made.append(remote(sent, theirs, core_send.at[j, pair], core_recv.at[j, pair], other))
            return made
        if stage == 1:
            source = half.at[slot, 1 - mine_first, :, :, :, cols]
            target = from_first.at[slot, :, :, :, cols]
            return [remote(source, target, a_send.at[slot], a_recv.at[slot], first)]
        if stage == 2:
            source = quarter.at[slot, 1 - mine_second, :, :, cols]
            target = from_second.at[slot, :, :, cols]
            return [remote(source, target, b_send.at[slot], b_recv.at[slot], second)]
        made = []
        for i in range(3):
            source = eighth.at[slot, lax.rem(z + i + 1, 4), :, cols]
            target = from_z.at[slot, i, :, cols]
            made.append(remote(source, target, z_send.at[i, slot], z_recv.at[i, slot], others[i]))
        return made

    def wide(ref, index, cols):
        return ref[(*index, slice(None), cols)].astype(jnp.float32)

    def add(stage, width, unit):
        slot = lax.rem(unit, SLOTS)
        pair = lax.rem(unit, 2)
        cols = slice(0, width)
        if stage == 0:
            for i in range(2):
                for j in range(2):
                    lead = jnp.where(core == 0, i, j)
                    last = jnp.where(core == 0, j, i)
                    for k in range(4):
                        value = wide(own, (pair, i, k, j), cols) + wide(from_core, (pair, i, k, j), cols)
                        half[slot, lead, last, k, :, cols] = value.astype(half.dtype)
        elif stage == 1:
            for j in range(2):
                for k in range(4):
                    value = wide(half, (slot, mine_first, j, k), cols) + wide(
                        from_first, (slot, j, k), cols
                    )
                    quarter[slot, j, k, :, cols] = value.astype(quarter.dtype)
        else:
            for k in range(4):
                value = wide(quarter, (slot, mine_second, k), cols) + wide(
                    from_second, (slot, k), cols
                )
                eighth[slot, k, :, cols] = value.astype(eighth.dtype)

    widths = sorted({entry[2] for entry in plan})

    def go(unit, stage):
        for width in widths:
            inside = functools.reduce(
                jnp.logical_or,
                [in_range(unit, *ranges[k]) for k in range(count) if plan[k][2] == width],
            )

            @pl.when(inside)
            def _(width=width):
                for copy in copies(stage, width, unit):
                    copy.wait()
                add(stage, width, unit)
                for copy in copies(stage + 1, width, unit):
                    copy.start()

    def finish(unit):
        for k in range(count):

            @pl.when(in_range(unit, *ranges[k]))
            def _(k=k):
                width = plan[k][2]
                slot = lax.rem(unit, SLOTS)
                cols = slice(0, width)
                for copy in copies(3, width, unit):
                    copy.wait()
                at = pl.ds(pl.multiple_of((unit - ranges[k][0]) * chunk, chunk), chunk)
                value = wide(eighth, (slot, z), cols)
                for i in range(3):
                    value = value + wide(from_z, (slot, i), cols)
                outs[k][at, :] = value

    def begin(unit):
        for k in range(count):

            @pl.when(in_range(unit, *ranges[k]))
            def _(k=k):
                for copy in copies(0, plan[k][2], unit, k):
                    copy.start()

    def step(t, unused):
        finish(t - 1 - 3 * LAG)
        go(t - 1 - 2 * LAG, 2)
        go(t - 1 - LAG, 1)
        go(t - 1, 0)
        begin(t)
        return unused

    lax.fori_loop(0, total + 1 + 3 * LAG, step, 0)


def sum_slices(plan, parts, chunk, number, name):
    count = len(plan)
    dma = pltpu.SemaphoreType.DMA
    kind = parts[0].dtype
    width = max(entry[2] for entry in plan)
    size = sum(math.prod(whole_shape(entry)) for entry in plan) * kind.itemsize
    buffers = [
        (2, 2, 4, 2, chunk, width),
        (2, 2, 4, 2, chunk, width),
        (SLOTS, 2, 4, chunk, width),
        (SLOTS, 4, chunk, width),
        (SLOTS, 3, chunk, width),
        (SLOTS, 2, 2, 4, chunk, width),
        (SLOTS, 2, 4, chunk, width),
        (SLOTS, 4, chunk, width),
    ]
    return pl.pallas_call(
        functools.partial(sum_slices_kernel, plan, chunk),
        out_shape=[jax.ShapeDtypeStruct((entry[1], entry[2]), jnp.float32) for entry in plan],
        in_specs=[pl.BlockSpec(memory_space=pl.ANY)] * count,
        out_specs=[VMEM] * count,
        scratch_shapes=[pltpu.VMEM(shape, kind) for shape in buffers]
        + [dma((2, 2))] * 3
        + [dma((SLOTS,))] * 4
        + [dma((3, SLOTS))] * 2,
        compiler_params=pltpu.CompilerParams(
            collective_id=number, has_side_effects=True, vmem_limit_bytes=48 * 1024 * 1024
        ),
        cost_estimate=pl.CostEstimate(flops=0, bytes_accessed=2 * size, transcendentals=0),
        name=name,
    )(*parts)


def push_kernel(world, x_ref, out_ref, send_sem, recv_sem):
    groups = lax.axis_size("mp")
    me = lax.axis_index("dp") * groups + lax.axis_index("mp")

    def peer(i):
        to = lax.rem(me + i, world)
        return (lax.div(to, groups), lax.rem(to, groups))

    barrier = pltpu.get_barrier_semaphore()

    def hail(i, unused):
        pl.semaphore_signal(barrier, inc=1, device_id=peer(i), device_id_type=MESH)
        return unused

    lax.fori_loop(1, world, hail, 0)
    out_ref[me] = x_ref[...]
    pl.semaphore_wait(barrier, world - 1)

    def copy(i):
        return remote(x_ref, out_ref.at[me], send_sem.at[i], recv_sem.at[i], peer(i))

    def start(i, unused):
        copy(i).start()
        return unused

    def finish(i, unused):
        copy(i).wait()
        return unused

    lax.fori_loop(1, world, start, 0)
    lax.fori_loop(1, world, finish, 0)


def push_all(value, world, number, name):
    dma = pltpu.SemaphoreType.DMA
    return pl.pallas_call(
        functools.partial(push_kernel, world),
        out_shape=jax.ShapeDtypeStruct((world,) + value.shape, value.dtype),
        in_specs=[VMEM],
        out_specs=VMEM,
        scratch_shapes=[dma((world,)), dma((world,))],
        compiler_params=pltpu.CompilerParams(collective_id=number, has_side_effects=True),
        name=name,
    )(value)


def swap_ranks(buf, ranks):
    rest = buf.shape[1:]
    split = buf.reshape((ranks, buf.shape[0] // ranks) + rest)
    return lax.all_to_all(split, "dp", 0, 0).reshape(buf.shape)


def round_positions(dest, rank, counts, capacity, turn):
    ranks = counts.shape[0]
    low = turn * capacity
    inside = (rank >= low) & (rank < low + capacity)
    pos = jnp.where(inside, dest * capacity + rank - low, ranks * capacity)
    fill = jnp.clip(counts - low, 0, capacity)
    return pos, fill, inside


def tiles_to_slots(rows, dest, slot, rank, counts, rounds):
    n = rows.shape[0]
    ranks = counts.shape[0]

    def turn_of(turn):
        pos, fill, unused = round_positions(dest, rank, counts, CHUNK_ROWS, turn)
        buf, tags = pack_rows(rows, pos, slot, fill, CHUNK_ROWS)
        got = swap_ranks(buf, ranks)
        got_tags = swap_ranks(tags[: ranks * CHUNK_ROWS], ranks)
        return scatter_rows(got, got_tags, n), got_tags

    first, tags = turn_of(0)

    def more(carry):
        turn, slots = carry
        added, more_tags = turn_of(turn)
        fresh = jnp.zeros((n + 16,), jnp.bool_).at[more_tags].set(True)
        return turn + 1, jnp.where(fresh[:, None], added, slots)

    unused, slots = lax.while_loop(lambda carry: carry[0] < rounds, more, (1, first))
    return slots[:n], tags


def slots_to_tiles(slots, tags, dest, slot, rank, counts, rounds):
    n = dest.shape[0]
    ranks = counts.shape[0]
    padded = jnp.concatenate([slots, jnp.zeros((16, 128), slots.dtype)])

    def turn_of(turn, turn_tags):
        pos, unused, inside = round_positions(dest, rank, counts, CHUNK_ROWS, turn)
        buf = gather_rows(padded, turn_tags, jnp.bfloat16)
        got = swap_ranks(buf, ranks).astype(jnp.float32)
        return gather_rows(got, jnp.minimum(pos, ranks * CHUNK_ROWS - 1), jnp.float32), inside

    first, unused = turn_of(0, tags)

    def more(carry):
        turn, rows = carry
        pos, fill, unused = round_positions(dest, rank, counts, CHUNK_ROWS, turn)
        empty = jnp.full((ranks * CHUNK_ROWS + 1,), n, jnp.int32)
        turn_tags = swap_ranks(empty.at[pos].set(slot)[:-1].at[:].get(), ranks)
        added, inside = turn_of(turn, turn_tags)
        return turn + 1, jnp.where(inside[:, None], added, rows)

    unused, rows = lax.while_loop(lambda carry: carry[0] < rounds, more, (1, first))
    return rows


def slot_matrices(slots, ranks):
    widths = [3 * HEADS * HD // 4, D, FF // 4, D]
    levels = [[], []]
    base = 0
    for total, width in zip(matrix_tiles(), widths):
        count = total // ranks
        for level in range(2):
            part = slots[base : base + count]
            levels[level].append(part.reshape(count * 128 // width, width))
            base += count
    return levels


def matrices_slots(levels):
    parts = []
    for index in range(4):
        for level in range(2):
            parts.append(levels[level][index].reshape(-1, 128))
    return jnp.concatenate(parts)


QKV_WIDTH = 896
PROJ_ROWS = 48


def layer_plan(ranks):
    return (
        (False, D // ranks, QKV_WIDTH),
        (True, PROJ_ROWS, D),
        (False, D // ranks, FF // 4),
        (True, FF // 4 // ranks, D),
    )


def pad_to(values, axis, size):
    widths = [(0, 0)] * values.ndim
    widths[axis] = (0, size - values.shape[axis])
    return jnp.pad(values, widths)


def pad_slices(level):
    return [pad_to(level[0], 1, QKV_WIDTH), pad_to(level[1], 0, PROJ_ROWS), level[2], level[3]]


def trim_slices(level, ranks):
    return [level[0][:, : 3 * HEADS * HD // 4], level[1][: HEADS * HD // 4 // ranks], level[2], level[3]]


def whole_weights(wholes, ranks):
    qkv, proj, up, down = wholes
    own_rows = HEADS * HD // 4 // ranks
    proj = proj.reshape(4, ranks, PROJ_ROWS, D)[:, :, :own_rows].reshape(-1, D)
    return (qkv.reshape(D, -1), proj, up.reshape(D, -1), down.reshape(-1, D))


def whole_parts(grads, ranks):
    qkv, proj, up, down = grads
    shapes = [whole_shape(entry) for entry in layer_plan(ranks)]
    proj = pad_to(proj.reshape(4, ranks, -1, D), 2, PROJ_ROWS)
    return [part.reshape(shape) for part, shape in zip((qkv, proj, up, down), shapes)]


def heads_of(packed, images):
    split = packed.reshape(images, -1, 4, QKV_WIDTH)[..., : 3 * HEADS * HD // 4]
    split = split.reshape(images, -1, 4, 3, HEADS // 4, HD).transpose(3, 0, 2, 4, 1, 5)
    split = split.reshape(3, images, HEADS, -1, HD)
    return split[0], split[1], split[2]


def columns_of(parts, images):
    stacked = jnp.stack(parts).reshape(3, images, 4, HEADS // 4, -1, HD)
    flat = stacked.transpose(1, 4, 2, 0, 3, 5).reshape(-1, 4, 3 * HEADS * HD // 4)
    return pad_to(flat, 2, QKV_WIDTH).reshape(-1, 4 * QKV_WIDTH)


def own_forward(state, weights, modulate):
    qkv_weight, proj_weight, up_weight, down_weight = weights
    images, rows, columns = state.shape
    shift_one, scale_one, gate_one, shift_two, scale_two, gate_two = [
        modulate[:, index, None, :] for index in range(6)
    ]
    normed_one, spread_one = normalize(state)
    full_one = (normed_one * (1.0 + scale_one) + shift_one).astype(jnp.bfloat16)
    flat_one = full_one.reshape(-1, columns)
    packed = product(flat_one, qkv_weight).astype(jnp.bfloat16)
    queries, key_rows, value_rows = heads_of(packed, images)
    scores = jnp.einsum(
        "ghqe,ghke->ghqk", queries, key_rows, preferred_element_type=jnp.float32
    )
    probs = jax.nn.softmax(scores * HD ** (-0.5), axis=-1)
    mixed = jnp.einsum(
        "ghqk,ghke->ghqe",
        probs.astype(jnp.bfloat16),
        value_rows,
        preferred_element_type=jnp.float32,
    ).astype(jnp.bfloat16)
    attended = mixed.transpose(0, 2, 1, 3).reshape(-1, columns)
    branch_one = product(attended, proj_weight).reshape(state.shape)
    middle = state + gate_one * branch_one
    normed_two, spread_two = normalize(middle)
    full_two = (normed_two * (1.0 + scale_two) + shift_two).astype(jnp.bfloat16)
    flat_two = full_two.reshape(-1, columns)
    hidden_pre = product(flat_two, up_weight)
    activated = jax.nn.gelu(hidden_pre, approximate=True).astype(jnp.bfloat16)
    branch_two = product(activated, down_weight).reshape(state.shape)
    result = middle + gate_two * branch_two
    saved = (
        normed_one,
        spread_one,
        flat_one,
        queries,
        key_rows,
        value_rows,
        attended,
        branch_one,
        normed_two,
        spread_two,
        flat_two,
        hidden_pre,
        activated,
        branch_two,
    )
    return (result, saved)


def own_backward(grad_out, saved, weights, modulate):
    (
        normed_one,
        spread_one,
        flat_one,
        queries,
        key_rows,
        value_rows,
        attended,
        branch_one,
        normed_two,
        spread_two,
        flat_two,
        hidden_pre,
        activated,
        branch_two,
    ) = saved
    qkv_weight, proj_weight, up_weight, down_weight = weights
    images, rows, columns = grad_out.shape
    shift_one, scale_one, gate_one, shift_two, scale_two, gate_two = [
        modulate[:, index, None, :] for index in range(6)
    ]
    grad_gate_two = jnp.sum(grad_out * branch_two, axis=1)
    back_two = (gate_two * grad_out).astype(jnp.bfloat16).reshape(-1, columns)
    grad_down = product(activated.T, back_two).astype(jnp.bfloat16)
    grad_act = product(back_two, down_weight.T)
    unused, gelu_back = jax.vjp(lambda pre: jax.nn.gelu(pre, approximate=True), hidden_pre)
    grad_pre = gelu_back(grad_act)[0].astype(jnp.bfloat16)
    grad_up = product(flat_two.T, grad_pre).astype(jnp.bfloat16)
    grad_hidden_two = product(grad_pre, up_weight.T)
    grad_hidden_two = grad_hidden_two.reshape(grad_out.shape)
    grad_shift_two = jnp.sum(grad_hidden_two, axis=1)
    grad_scale_two = jnp.sum(grad_hidden_two * normed_two, axis=1)
    grad_middle = grad_out + normalize_back(
        grad_hidden_two * (1.0 + scale_two), normed_two, spread_two
    )
    grad_gate_one = jnp.sum(grad_middle * branch_one, axis=1)
    back_one = (gate_one * grad_middle).astype(jnp.bfloat16).reshape(-1, columns)
    grad_proj = product(attended.T, back_one).astype(jnp.bfloat16)
    grad_attended = product(back_one, proj_weight.T).astype(jnp.bfloat16)
    grad_mixed = grad_attended.reshape(images, rows, HEADS, HD).transpose(0, 2, 1, 3)
    scores = jnp.einsum(
        "ghqe,ghke->ghqk", queries, key_rows, preferred_element_type=jnp.float32
    )
    probs = jax.nn.softmax(scores * HD ** (-0.5), axis=-1)
    grad_probs = jnp.einsum(
        "ghqe,ghke->ghqk", grad_mixed, value_rows, preferred_element_type=jnp.float32
    )
    grad_values = jnp.einsum(
        "ghqk,ghqe->ghke",
        probs.astype(jnp.bfloat16),
        grad_mixed,
        preferred_element_type=jnp.float32,
    )
    grad_scores = (
        probs * (grad_probs - jnp.sum(grad_probs * probs, axis=-1, keepdims=True)) * HD ** (-0.5)
    ).astype(jnp.bfloat16)
    grad_queries = jnp.einsum(
        "ghqk,ghke->ghqe", grad_scores, key_rows, preferred_element_type=jnp.float32
    )
    grad_keys = jnp.einsum(
        "ghqk,ghqe->ghke", grad_scores, queries, preferred_element_type=jnp.float32
    )
    parts = [part.astype(jnp.bfloat16) for part in (grad_queries, grad_keys, grad_values)]
    grad_packed = columns_of(parts, images)
    grad_qkv = product(flat_one.T, grad_packed).astype(jnp.bfloat16)
    grad_hidden_one = product(grad_packed, qkv_weight.T)
    grad_hidden_one = grad_hidden_one.reshape(grad_out.shape)
    grad_shift_one = jnp.sum(grad_hidden_one, axis=1)
    grad_scale_one = jnp.sum(grad_hidden_one * normed_one, axis=1)
    grad_state = grad_middle + normalize_back(
        grad_hidden_one * (1.0 + scale_one), normed_one, spread_one
    )
    grad_mod = jnp.concatenate(
        [
            grad_shift_one,
            grad_scale_one,
            grad_gate_one,
            grad_shift_two,
            grad_scale_two,
            grad_gate_two,
        ],
        axis=1,
    )
    return (grad_state, grad_mod, (grad_qkv, grad_proj, grad_up, grad_down))


def contract(left, right, left_axis, right_axis):
    return lax.dot_general(
        left,
        right,
        (((left_axis,), (right_axis,)), ((), ())),
        preferred_element_type=jnp.float32,
    )


def contract_wide(left, right, left_axis, right_axis):
    return lax.dot_general(
        left.astype(jnp.float32),
        right.astype(jnp.float32),
        (((left_axis,), (right_axis,)), ((), ())),
        precision=highest,
        preferred_element_type=jnp.float32,
    )


def silu_back(values, grads):
    unused, pull = jax.vjp(jax.nn.silu, values)
    return pull(grads)[0]


def local(
    big_copy,
    big_master,
    big_first,
    big_second,
    ada_copy,
    ada_master,
    ada_first,
    ada_second,
    rest_copy,
    rest_master,
    rest_first,
    rest_second,
    owner_tiles,
    kept_patches,
    kept_pos,
    timestep,
    label,
    owner,
    target,
    step,
):
    groups = lax.axis_size("mp")
    ranks = lax.axis_size("dp")
    world = groups * ranks
    my_rank = lax.axis_index("dp")
    micro = kept_patches.shape[0]
    own_columns = D // world
    columns = D

    owned = big_copy.shape[1]
    all_dest, unused_slot = tile_place(owner_tiles, ranks)
    all_hot = all_dest.reshape(ranks, owned, 1) == jnp.arange(ranks)
    rounds = (jnp.max(jnp.sum(all_hot.astype(jnp.int32), axis=1)) + CHUNK_ROWS - 1) // CHUNK_ROWS
    own_tiles = lax.dynamic_slice(owner_tiles, (my_rank * owned,), (owned,))
    dest, slot = tile_place(own_tiles, ranks)
    rank, counts = rank_within(dest, ranks)
    slots, tags = tiles_to_slots(big_copy[0], dest, slot, rank, counts, rounds)
    slices = slot_matrices(slots.astype(jnp.bfloat16), ranks)
    plan = layer_plan(ranks) * 2
    wholes = gather_whole(
        plan, pad_slices(slices[0]) + pad_slices(slices[1]), 16, 1, "gather_weights"
    )
    weights = [whole_weights(wholes[:4], ranks), whole_weights(wholes[4:], ranks)]

    rest_own = rest_copy.reshape(own_columns, REST_ROWS)
    edges = [0, PD, PD + FREQ, PD + FREQ + D, PD + FREQ + D + CLASSES, REST_ROWS]
    win_t, one_t, two_t, table_t, tail_t = [
        rest_own[:, edges[i] : edges[i + 1]] for i in range(5)
    ]
    ends_size = own_columns * (2 * PD + 1)
    told = jnp.concatenate(
        [
            jnp.concatenate([win_t, tail_t], axis=1).astype(jnp.float32).reshape(-1),
            timestep[:, 0].astype(jnp.float32),
            label[:, 0].astype(jnp.float32),
        ]
    )
    told = pad_to(told, 0, 1280).reshape(-1, 128)
    told = push_all(told, world, 6, "push_inputs").reshape(world, -1)
    facts = told[:, ends_size : ends_size + 2 * micro].astype(jnp.int32)
    facts = facts.reshape(ranks, groups, 2 * micro).transpose(1, 0, 2).reshape(world, -1)
    stamps = facts[:, :micro].reshape(-1)
    tags_all = facts[:, micro:].reshape(-1)
    ends = told[:, :ends_size].reshape(columns, -1).astype(jnp.bfloat16)
    embed_weight = ends[:, :PD].T
    mask_token = ends[:, PD].astype(jnp.float32)
    head_weight = ends[:, PD + 1 :]
    count_all = micro * world
    features = jax.vmap(time_features)(stamps).astype(jnp.bfloat16)
    pre_time = contract(features, one_t, 1, 1)
    hidden_own = jax.nn.silu(pre_time).astype(jnp.bfloat16)
    hidden_size = count_all * own_columns
    hidden_all = pad_to(hidden_own.reshape(-1), 0, 4096).reshape(-1, 128)
    hidden_all = push_all(hidden_all, world, 7, "push_hidden").reshape(world, -1)
    hidden_all = hidden_all[:, :hidden_size].reshape(world, count_all, own_columns)
    hidden_all = hidden_all.transpose(1, 0, 2).reshape(count_all, columns)
    picks = (tags_all[:, None] == jnp.arange(CLASSES, dtype=jnp.int32)[None, :]).astype(
        jnp.bfloat16
    )
    cond_own = contract(hidden_all, two_t, 1, 1) + contract(picks, table_t, 1, 1)
    signal_own = jax.nn.silu(cond_own).astype(jnp.bfloat16)
    ada_own = ada_copy.reshape(own_columns, 14 * columns)
    mod_rows = micro * 14
    mod_entry = (True, 32, columns)
    mods = product(signal_own, ada_own).reshape(world, mod_rows, columns)
    mods = pad_to(mods, 1, mod_entry[1]).reshape(whole_shape(mod_entry))
    mods = sum_slices((mod_entry,), [mods], 16, 3, "sum_mods")[0]
    mods = mods[:mod_rows].reshape(micro, 14, columns)
    mod_enc = mods[:, :6]
    mod_dec = mods[:, 6:12]
    final_shift = mods[:, 12:13]
    final_scale = mods[:, 13:]

    goals = lax.all_gather(target[:, 0], "dp", axis=0, tiled=False)
    goal = jnp.stack([goals[owner[b, 0], b] for b in range(micro)])
    positions = position_table(columns)
    images = ranks * groups
    inv_count = 1.0 / (PD * micro * images * KEEP)
    place = kept_pos[:, 0]
    patches = kept_patches[:, 0].astype(jnp.bfloat16)
    hits = (
        jnp.arange(SEQ, dtype=jnp.int32)[None, :, None] == place[:, None, :]
    ).astype(jnp.float32)
    hits_low = hits.astype(jnp.bfloat16)
    kept = jnp.sum(hits, axis=2)[:, :, None]
    embedded = product(patches.reshape(-1, PD), embed_weight).reshape(micro, KEEP, columns)
    embedded = embedded + jnp.take(positions, place, axis=0)
    enc_out, enc_saved = own_forward(embedded, weights[0], mod_enc)
    sent = enc_out.astype(jnp.bfloat16)
    dec_in = (
        jnp.einsum("bpr,brd->bpd", hits_low, sent, preferred_element_type=jnp.float32)
        + (1.0 - kept) * mask_token[None, None, :]
        + positions[None]
    )
    dec_out, dec_saved = own_forward(dec_in, weights[1], mod_dec)
    normed_final, spread_final = normalize(dec_out)
    head_in = (normed_final * (1.0 + final_scale) + final_shift).astype(jnp.bfloat16)
    flat_head = head_in.reshape(-1, columns)
    output = product(flat_head, head_weight).reshape(micro, SEQ, PD)
    error = output - goal
    weight = kept + MASKED_WEIGHT * (1.0 - kept)
    loss_sum = jnp.sum(weight * error * error) * inv_count

    grad_output = (2.0 * inv_count * weight * error).astype(jnp.bfloat16).reshape(-1, PD)
    grad_head = contract(grad_output, flat_head, 0, 0)
    grad_head_in = product(grad_output, head_weight.T).reshape(dec_out.shape)
    grad_final = jnp.concatenate(
        [jnp.sum(grad_head_in, axis=1), jnp.sum(grad_head_in * normed_final, axis=1)], axis=1
    )
    grad_dec_out = normalize_back(grad_head_in * (1.0 + final_scale), normed_final, spread_final)
    grad_dec_in, grad_mod_dec, dec_grads = own_backward(
        grad_dec_out, dec_saved, weights[1], mod_dec
    )
    grad_mask = jnp.sum((1.0 - kept) * grad_dec_in, axis=(0, 1))[None, :]
    grad_sent = jnp.einsum(
        "bpr,bpd->brd",
        hits_low,
        grad_dec_in.astype(jnp.bfloat16),
        preferred_element_type=jnp.float32,
    )
    grad_embedded, grad_mod_enc, enc_grads = own_backward(
        grad_sent, enc_saved, weights[0], mod_enc
    )
    sums = sum_slices(
        plan, whole_parts(enc_grads, ranks) + whole_parts(dec_grads, ranks), 16, 2, "sum_gradients"
    )
    sums = matrices_slots([trim_slices(sums[:4], ranks), trim_slices(sums[4:], ranks)])
    grad_embed = contract_wide(
        patches.reshape(-1, PD), grad_embedded.reshape(-1, columns), 0, 0
    )

    vectors = jnp.concatenate([grad_mod_enc, grad_mod_dec, grad_final], axis=1)
    vectors = vectors.astype(jnp.bfloat16).reshape(mod_rows, columns)
    vectors = pad_to(vectors, 0, mod_entry[1])
    vectors = gather_whole((mod_entry,), [vectors], 16, 4, "gather_vectors")[0]
    vectors = vectors.reshape(world, mod_entry[1], columns)[:, :mod_rows].reshape(count_all, -1)
    owned_ada = contract(signal_own, vectors, 0, 0).reshape(-1)
    grad_signal = contract(vectors, ada_own, 1, 1)
    grad_cond = silu_back(cond_own, grad_signal)
    grad_two_t = contract_wide(grad_cond, hidden_all, 0, 0)
    grad_table_t = contract_wide(grad_cond, picks, 0, 0)
    shared = jnp.concatenate(
        [contract_wide(grad_cond, two_t, 1, 0), grad_embed, grad_mask, grad_head], axis=0
    )
    shared_rows = shared.shape[0]
    shared = shared.reshape(shared_rows, ranks, groups, own_columns).transpose(2, 1, 0, 3)
    shared = pad_to(shared.reshape(world, -1), 1, 4096)
    shared_entry = (True, 32, 128)
    shared = sum_slices(
        (shared_entry,), [shared.reshape(whole_shape(shared_entry))], 32, 5, "sum_shared"
    )[0]
    shared = shared.reshape(-1)[: shared_rows * own_columns].reshape(shared_rows, own_columns)
    grad_pre = silu_back(pre_time, shared[:count_all])
    grad_one_t = contract_wide(grad_pre, features, 0, 0)
    ends_t = shared[count_all:].T
    owned_rest = jnp.concatenate(
        [ends_t[:, :PD], grad_one_t, grad_two_t, grad_table_t, ends_t[:, PD:]], axis=1
    ).reshape(-1)

    squares = jnp.sum(sums * sums) + jnp.sum(owned_ada * owned_ada) + jnp.sum(owned_rest * owned_rest)
    totals = jnp.broadcast_to(pad_to(jnp.stack([loss_sum, squares]), 0, 128), (8, 128))
    totals = jnp.sum(push_all(totals, world, 8, "push_totals")[:, 0, :2], axis=0)
    owned_big = slots_to_tiles(sums, tags, dest, slot, rank, counts, rounds)
    grad_norm = jnp.sqrt(totals[1])
    clip = jnp.minimum(1.0, MAX_NORM / (grad_norm + 1e-06))
    count = step[0].astype(jnp.float32)
    big_out = adam_update(
        owned_big.reshape(big_master.shape), big_master, big_first, big_second, clip, count
    )
    ada_out = adam_update(owned_ada, ada_master, ada_first, ada_second, clip, count)
    rest_out = adam_update(owned_rest, rest_master, rest_first, rest_second, clip, count)
    return (
        totals[:1],
        grad_norm.reshape(1),
        big_out[0],
        big_out[1],
        big_out[2],
        big_out[3],
        ada_out[0],
        ada_out[1],
        ada_out[2],
        ada_out[3],
        rest_out[0],
        rest_out[1],
        rest_out[2],
        rest_out[3],
    )


def whole_columns(mesh):
    ranks, groups = mesh.shape["dp"], mesh.shape["mp"]
    return groups == 4 and D % (ranks * groups) == 0 and ranks == 8


def solution(mesh):
    body = local if whole_columns(mesh) else local_general
    in_specs = (
        P("mp", "dp", None),
        P("mp", "dp", None),
        P("mp", "dp", None),
        P("mp", "dp", None),
        P(("dp", "mp")),
        P(("dp", "mp")),
        P(("dp", "mp")),
        P(("dp", "mp")),
        P(("dp", "mp")),
        P(("dp", "mp")),
        P(("dp", "mp")),
        P(("dp", "mp")),
        P(),
        P(None, ("dp", "mp"), None, None),
        P(None, ("dp", "mp"), None),
        P(None, ("dp", "mp")),
        P(None, ("dp", "mp")),
        P(None, ("dp", "mp")),
        P(None, ("dp", "mp"), None, None),
        P(),
    )
    out_specs = (
        P(),
        P(),
        P("mp", "dp", None),
        P("mp", "dp", None),
        P("mp", "dp", None),
        P("mp", "dp", None),
        P(("dp", "mp")),
        P(("dp", "mp")),
        P(("dp", "mp")),
        P(("dp", "mp")),
        P(("dp", "mp")),
        P(("dp", "mp")),
        P(("dp", "mp")),
        P(("dp", "mp")),
    )
    return jax.shard_map(body, mesh=mesh, in_specs=in_specs, out_specs=out_specs, check_vma=False)
```

```python
import functools
import math

import jax
import jax.numpy as jnp
from jax import lax
from jax.experimental import pallas as pl
from jax.experimental.pallas import tpu as pltpu
from jax.sharding import PartitionSpec as P

D = 1152
HEADS = 16
HD = 72
FF = 4608
PD = 16
FREQ = 256
CLASSES = 1001
GRID = 16
SEQ = 256
KEEP = 128


EPS_NORM = 1e-06
MAX_NORM = 0.01
RATE = 0.02
DECAY = 0.1
BETA_ONE = 0.9
BETA_TWO = 0.999
ADAM_EPS = 1e-08
MASKED_WEIGHT = 0.1
highest = lax.Precision.HIGHEST


def partner_2(value, axis, stride):
    mask = 2**stride
    pairs = [(source, source ^ mask) for source in range(lax.axis_size(axis))]
    return lax.ppermute(value, axis, pairs)


def product(left, right):
    return jnp.dot(left, right, preferred_element_type=jnp.float32)


def normalize(values):
    center = values - jnp.mean(values, axis=-1, keepdims=True)
    spread = lax.rsqrt(jnp.mean(center * center, axis=-1, keepdims=True) + EPS_NORM)
    return (center * spread, spread)


def normalize_back(grad_normed, normed, spread):
    adjusted = grad_normed - jnp.mean(grad_normed, axis=-1, keepdims=True)
    adjusted = adjusted - normed * jnp.mean(grad_normed * normed, axis=-1, keepdims=True)
    return spread * adjusted


def position_table(columns):
    quarter = columns // 4
    omegas = 1.0 / 10000.0 ** (jnp.arange(quarter, dtype=jnp.float32) / quarter)
    places = jnp.arange(GRID * GRID, dtype=jnp.int32)

    def half_table(coords):
        angles = coords.astype(jnp.float32)[:, None] * omegas[None, :]
        return jnp.concatenate([jnp.sin(angles), jnp.cos(angles)], axis=1)

    return jnp.concatenate([half_table(places % GRID), half_table(places // GRID)], axis=1)


def time_features(stamp):
    halves = FREQ // 2
    frequency = jnp.exp(-math.log(10000.0) * jnp.arange(halves, dtype=jnp.float32) / halves)
    angles = stamp.astype(jnp.float32) * frequency
    return jnp.concatenate([jnp.cos(angles), jnp.sin(angles)])


def row_gather(values):
    return lax.all_gather(values, "mp", axis=0, tiled=True)


def row_sum(values):
    return lax.psum_scatter(values, "mp", scatter_dimension=0, tiled=True)


def route_bit(route, bit):
    return jnp.bitwise_and(jnp.right_shift(route, bit), 1) == 1


def route_ids(values, route, levels):
    for bit in range(levels):
        partner = partner_2(values, "dp", bit)
        values = jnp.where(route_bit(route, bit), partner, values)
    return values


def route_rows(values, route, levels):
    for bit in range(levels):
        partner = partner_2(values, "dp", bit)
        values = jnp.where(route_bit(route, bit), partner, values)
    return values


def route_back(values, route, levels):
    for bit in range(levels):
        partner = partner_2(values, "dp", bit)
        values = jnp.where(route_bit(route, bit), partner, values)
    return values


def unpack_big(flat, columns, groups):
    head_width = HEADS * HD // groups
    hidden_width = FF // groups
    shapes = [
        (columns, 3 * head_width),
        (head_width, columns),
        (columns, hidden_width),
        (hidden_width, columns),
    ]
    levels = []
    offset = 0
    for level_index in range(2):
        pieces = []
        for dims in shapes:
            length = dims[0] * dims[1]
            pieces.append(flat[offset : offset + length].reshape(dims))
            offset += length
        levels.append(tuple(pieces))
    return levels


def unpack_rest(flat, columns):
    matrix = flat.reshape(columns, -1).T
    counts = [PD, FREQ, columns, CLASSES, 1, PD]
    pieces = []
    offset = 0
    for count in counts:
        pieces.append(matrix[offset : offset + count])
        offset += count
    return (pieces[0], pieces[1], pieces[2], pieces[3], pieces[4][0], pieces[5].T)


def split_heads(packed, groups, rows):
    third = packed.shape[1] // 3
    return [
        packed[:, index * third : (index + 1) * third].reshape(groups, rows, third // HD, HD)
        for index in range(3)
    ]


def attention_probs(queries, key_rows):
    scores = jnp.einsum("gqhe,gkhe->ghqk", queries, key_rows, preferred_element_type=jnp.float32)
    return jax.nn.softmax(scores * HD ** (-0.5), axis=-1)


def block_forward(state, weights, modulate):
    qkv_weight, proj_weight, up_weight, down_weight = weights
    shift_one, scale_one, gate_one, shift_two, scale_two, gate_two = jnp.split(modulate, 6)
    rows = state.shape[0]
    normed_one, spread_one = normalize(state)
    full_one = row_gather((normed_one * (1.0 + scale_one) + shift_one).astype(jnp.bfloat16))
    groups = full_one.shape[0] // rows
    packed = product(full_one, qkv_weight).astype(jnp.bfloat16)
    queries, key_rows, value_rows = split_heads(packed, groups, rows)
    probs = attention_probs(queries, key_rows)
    mixed = jnp.einsum(
        "ghqk,gkhe->gqhe",
        probs.astype(jnp.bfloat16),
        value_rows,
        preferred_element_type=jnp.float32,
    )
    attended = mixed.astype(jnp.bfloat16).reshape(groups * rows, -1)
    branch_one = row_sum(product(attended, proj_weight))
    middle = state + gate_one * branch_one
    normed_two, spread_two = normalize(middle)
    full_two = row_gather((normed_two * (1.0 + scale_two) + shift_two).astype(jnp.bfloat16))
    hidden_pre = product(full_two, up_weight)
    activated = jax.nn.gelu(hidden_pre, approximate=True).astype(jnp.bfloat16)
    branch_two = row_sum(product(activated, down_weight))
    result = middle + gate_two * branch_two
    saved = (
        normed_one,
        spread_one,
        full_one,
        packed,
        attended,
        branch_one,
        normed_two,
        spread_two,
        full_two,
        hidden_pre,
        activated,
        branch_two,
    )
    return (result, saved)


def block_backward(grad_out, saved, weights, modulate):
    (
        normed_one,
        spread_one,
        full_one,
        packed,
        attended,
        branch_one,
        normed_two,
        spread_two,
        full_two,
        hidden_pre,
        activated,
        branch_two,
    ) = saved
    qkv_weight, proj_weight, up_weight, down_weight = weights
    shift_one, scale_one, gate_one, shift_two, scale_two, gate_two = jnp.split(modulate, 6)
    rows = grad_out.shape[0]
    groups = full_one.shape[0] // rows
    grad_gate_two = jnp.sum(grad_out * branch_two, axis=0)
    back_two = row_gather((gate_two * grad_out).astype(jnp.bfloat16))
    grad_down = product(activated.T, back_two)
    grad_act = product(back_two, down_weight.T)
    unused, gelu_back = jax.vjp(lambda pre: jax.nn.gelu(pre, approximate=True), hidden_pre)
    grad_pre = gelu_back(grad_act)[0].astype(jnp.bfloat16)
    grad_up = product(full_two.T, grad_pre)
    grad_hidden_two = row_sum(product(grad_pre, up_weight.T))
    grad_shift_two = jnp.sum(grad_hidden_two, axis=0)
    grad_scale_two = jnp.sum(grad_hidden_two * normed_two, axis=0)
    grad_middle = grad_out + normalize_back(
        grad_hidden_two * (1.0 + scale_two), normed_two, spread_two
    )
    grad_gate_one = jnp.sum(grad_middle * branch_one, axis=0)
    back_one = row_gather((gate_one * grad_middle).astype(jnp.bfloat16))
    grad_proj = product(attended.T, back_one)
    grad_attended = product(back_one, proj_weight.T).astype(jnp.bfloat16)
    queries, key_rows, value_rows = split_heads(packed, groups, rows)
    probs = attention_probs(queries, key_rows)
    grad_mixed = grad_attended.reshape(queries.shape)
    grad_probs = jnp.einsum(
        "gqhe,gkhe->ghqk", grad_mixed, value_rows, preferred_element_type=jnp.float32
    )
    grad_values = jnp.einsum(
        "ghqk,gqhe->gkhe",
        probs.astype(jnp.bfloat16),
        grad_mixed,
        preferred_element_type=jnp.float32,
    )
    grad_scores = (
        probs * (grad_probs - jnp.sum(grad_probs * probs, axis=-1, keepdims=True)) * HD ** (-0.5)
    )
    grad_scores = grad_scores.astype(jnp.bfloat16)
    grad_queries = jnp.einsum(
        "ghqk,gkhe->gqhe", grad_scores, key_rows, preferred_element_type=jnp.float32
    )
    grad_keys = jnp.einsum(
        "ghqk,gqhe->gkhe", grad_scores, queries, preferred_element_type=jnp.float32
    )
    grad_packed = jnp.concatenate(
        [
            grad_part.reshape(groups * rows, -1)
            for grad_part in (grad_queries, grad_keys, grad_values)
        ],
        axis=1,
    ).astype(jnp.bfloat16)
    grad_qkv = product(full_one.T, grad_packed)
    grad_hidden_one = row_sum(product(grad_packed, qkv_weight.T))
    grad_shift_one = jnp.sum(grad_hidden_one, axis=0)
    grad_scale_one = jnp.sum(grad_hidden_one * normed_one, axis=0)
    grad_state = grad_middle + normalize_back(
        grad_hidden_one * (1.0 + scale_one), normed_one, spread_one
    )
    grad_mod = jnp.concatenate(
        [
            grad_shift_one,
            grad_scale_one,
            grad_gate_one,
            grad_shift_two,
            grad_scale_two,
            grad_gate_two,
        ]
    )
    return (grad_state, grad_mod, (grad_qkv, grad_proj, grad_up, grad_down))


def condition(stamp, tag, time_one, time_two, table):
    features = time_features(stamp).astype(jnp.bfloat16)[None, :]
    pre_time = product(features, time_one)
    hidden_time = jax.nn.silu(pre_time).astype(jnp.bfloat16)
    cond_value = product(hidden_time, time_two)[0] + table[tag].astype(jnp.float32)
    signal = jax.nn.silu(cond_value).astype(jnp.bfloat16)
    return (signal, (features, pre_time, hidden_time, cond_value))


def condition_back(grad_signal, saved, time_two, tag, table_rows):
    features, pre_time, hidden_time, cond_value = saved
    unused, silu_back = jax.vjp(jax.nn.silu, cond_value)
    grad_cond = silu_back(grad_signal)[0]
    grad_time_two = hidden_time.astype(jnp.float32).T * grad_cond[None, :]
    grad_hidden = jnp.dot(time_two.astype(jnp.float32), grad_cond, precision=highest)
    unused_pre, pre_back = jax.vjp(jax.nn.silu, pre_time)
    grad_pre = pre_back(grad_hidden[None, :])[0]
    grad_time_one = features.astype(jnp.float32).T * grad_pre
    grad_table = (jnp.arange(table_rows, dtype=jnp.int32)[:, None] == tag) * grad_cond[None, :]
    return (grad_time_one, grad_time_two, grad_table)


def adam_update(grad, master, first, second, clip, count):
    scaled = grad * clip
    first = BETA_ONE * first + (1.0 - BETA_ONE) * scaled
    second = BETA_TWO * second + (1.0 - BETA_TWO) * scaled * scaled
    fix_one = 1.0 - BETA_ONE**count
    fix_two = 1.0 - BETA_TWO**count
    master = master - RATE * (
        first / fix_one / (jnp.sqrt(second / fix_two) + ADAM_EPS) + DECAY * master
    )
    return (master, first, second, master.astype(jnp.bfloat16))


def local_general(
    big_copy,
    big_master,
    big_first,
    big_second,
    ada_copy,
    ada_master,
    ada_first,
    ada_second,
    rest_copy,
    rest_master,
    rest_first,
    rest_second,
    owner_tiles,
    kept_patches,
    kept_pos,
    timestep,
    label,
    owner,
    target,
    step,
):
    groups = lax.axis_size("mp")
    ranks = lax.axis_size("dp")
    levels_dp = ranks.bit_length() - 1
    my_rank = lax.axis_index("dp")
    tiles = owner_tiles.shape[0]
    columns = D
    gathered = lax.all_gather(big_copy, "dp", axis=1, tiled=True)[0]
    inverse = jnp.zeros((tiles,), jnp.int32).at[owner_tiles].set(jnp.arange(tiles, dtype=jnp.int32))
    big_flat = jnp.take(gathered, inverse, axis=0).reshape(-1)
    ada_flat, rest_flat = (
        lax.all_gather(ada_copy, ("dp", "mp"), axis=0, tiled=True),
        lax.all_gather(rest_copy, ("dp", "mp"), axis=0, tiled=True),
    )
    levels = unpack_big(big_flat, columns, groups)
    ada_matrix = ada_flat.reshape(columns, 14 * columns)
    embed_weight, time_one, time_two, table, mask_token, head_weight = unpack_rest(
        rest_flat, columns
    )
    positions = position_table(columns)
    images = ranks * groups
    inv_count = 1.0 / (PD * kept_patches.shape[0] * images * KEEP)
    zeros_six = jnp.zeros((6 * columns,), jnp.bfloat16)
    zeros_eight = jnp.zeros((8 * columns,), jnp.bfloat16)

    def micro_step(carry, inputs):
        grads_big, grads_rest, loss_sum = carry
        patches, place, stamp, tag, dest, goal = inputs
        route = jnp.bitwise_xor(dest, my_rank)
        signal_enc, saved_enc = condition(stamp, tag, time_one, time_two, table)
        mod_enc = product(signal_enc[None, :], ada_matrix[:, : 6 * columns])[0]
        embedded = product(patches.astype(jnp.bfloat16), embed_weight) + jnp.take(
            positions, place, axis=0
        )
        enc_out, enc_saved = block_forward(embedded, levels[0], mod_enc)
        sent = enc_out.astype(jnp.bfloat16)
        meta = jnp.concatenate([place, stamp[None], tag[None]])
        got_meta = route_ids(meta, route, levels_dp)
        arrived = route_rows(sent, route, levels_dp)
        keep_rows = place.shape[0]
        dec_place = got_meta[:keep_rows]
        dec_tag = got_meta[keep_rows + 1]
        signal_dec, saved_dec = condition(got_meta[keep_rows], dec_tag, time_one, time_two, table)
        mod_dec = product(signal_dec[None, :], ada_matrix[:, 6 * columns :])[0]
        hits = jnp.arange(SEQ, dtype=jnp.int32)[:, None] == dec_place[None, :]
        kept = jnp.sum(hits.astype(jnp.float32), axis=1, keepdims=True)
        dec_in = (
            product(hits.astype(jnp.bfloat16), arrived)
            + (1.0 - kept) * mask_token.astype(jnp.float32)[None, :]
            + positions
        )
        dec_out, dec_saved = block_forward(dec_in, levels[1], mod_dec[: 6 * columns])
        final_shift = mod_dec[6 * columns : 7 * columns]
        final_scale = mod_dec[7 * columns :]
        normed_final, spread_final = normalize(dec_out)
        head_in = (normed_final * (1.0 + final_scale) + final_shift).astype(jnp.bfloat16)
        output = product(head_in, head_weight)
        error = output - goal
        weight = kept + MASKED_WEIGHT * (1.0 - kept)
        loss_part = jnp.sum(weight * error * error) * inv_count
        grad_output = (2.0 * inv_count * weight * error).astype(jnp.bfloat16)
        grad_head = product(head_in.T, grad_output)
        grad_head_in = product(grad_output, head_weight.T)
        grad_final = jnp.concatenate(
            [jnp.sum(grad_head_in, axis=0), jnp.sum(grad_head_in * normed_final, axis=0)]
        )
        grad_dec_out = normalize_back(
            grad_head_in * (1.0 + final_scale), normed_final, spread_final
        )
        grad_dec_in, grad_mod_dec, dec_grads = block_backward(
            grad_dec_out, dec_saved, levels[1], mod_dec[: 6 * columns]
        )
        grad_mask = jnp.sum((1.0 - kept) * grad_dec_in, axis=0)
        grad_arrived = jnp.take(grad_dec_in, dec_place, axis=0).astype(jnp.bfloat16)
        grad_sent = route_back(grad_arrived, route, levels_dp)
        grad_embedded, grad_mod_enc, enc_grads = block_backward(
            grad_sent.astype(jnp.float32), enc_saved, levels[0], mod_enc
        )
        grad_embed = jnp.dot(
            patches.astype(jnp.bfloat16).astype(jnp.float32).T, grad_embedded, precision=highest
        )
        vector_enc = grad_mod_enc.astype(jnp.bfloat16)
        vector_dec = jnp.concatenate([grad_mod_dec, grad_final]).astype(jnp.bfloat16)
        grad_signal_enc = product(ada_matrix[:, : 6 * columns], vector_enc)
        grad_signal_dec = product(ada_matrix[:, 6 * columns :], vector_dec)
        time_enc = condition_back(grad_signal_enc, saved_enc, time_two, tag, table.shape[0])
        time_dec = condition_back(grad_signal_dec, saved_dec, time_two, dec_tag, table.shape[0])
        rest_terms = [
            grad_embed,
            time_enc[0] + time_dec[0],
            time_enc[1] + time_dec[1],
            time_enc[2] + time_dec[2],
            grad_mask[None, :],
            grad_head.T,
        ]
        grads_rest = grads_rest + jnp.concatenate(rest_terms, axis=0)
        big_terms = [
            term.reshape(-1) for level_grads in (enc_grads, dec_grads) for term in level_grads
        ]
        grads_big = grads_big + jnp.concatenate(big_terms)
        signal_pair = jnp.stack([signal_enc, signal_dec])
        vector_pair = jnp.stack(
            [jnp.concatenate([vector_enc, zeros_eight]), jnp.concatenate([zeros_six, vector_dec])]
        )
        return ((grads_big, grads_rest, loss_sum + loss_part), (signal_pair, vector_pair))

    inputs = (
        kept_patches[:, 0],
        kept_pos[:, 0],
        timestep[:, 0],
        label[:, 0],
        owner[:, 0],
        target[:, 0],
    )
    start_carry = (
        jnp.zeros(big_flat.shape, jnp.float32),
        jnp.zeros((rest_flat.shape[0] // columns, columns), jnp.float32),
        jnp.zeros((), jnp.float32),
    )
    finals, factors = lax.scan(micro_step, start_carry, inputs)
    grads_big, grads_matrix, loss_sum = finals
    grads_rest = grads_matrix.T.reshape(-1)
    signal_rows = factors[0].reshape(-1, columns)
    vector_rows = factors[1].reshape(-1, 14 * columns)
    tile_part = jnp.take(grads_big.reshape(tiles, 128), owner_tiles, axis=0)
    owned_big = lax.psum_scatter(tile_part, "dp", scatter_dimension=0, tiled=True)
    local_ada = product(signal_rows.T, vector_rows).reshape(-1)
    owned_ada, owned_rest = (
        lax.psum_scatter(local_ada, ("dp", "mp"), scatter_dimension=0, tiled=True),
        lax.psum_scatter(grads_rest, ("dp", "mp"), scatter_dimension=0, tiled=True),
    )
    squares = (
        jnp.sum(owned_big * owned_big)
        + jnp.sum(owned_ada * owned_ada)
        + jnp.sum(owned_rest * owned_rest)
    )
    loss_total, square_total = lax.psum((loss_sum, squares), ("dp", "mp"))
    grad_norm = jnp.sqrt(square_total)
    clip = jnp.minimum(1.0, MAX_NORM / (grad_norm + 1e-06))
    count = step[0].astype(jnp.float32)
    big_out = adam_update(
        owned_big.reshape(big_master.shape), big_master, big_first, big_second, clip, count
    )
    ada_out = adam_update(owned_ada, ada_master, ada_first, ada_second, clip, count)
    rest_out = adam_update(owned_rest, rest_master, rest_first, rest_second, clip, count)
    return (
        loss_total.reshape(1),
        grad_norm.reshape(1),
        big_out[0],
        big_out[1],
        big_out[2],
        big_out[3],
        ada_out[0],
        ada_out[1],
        ada_out[2],
        ada_out[3],
        rest_out[0],
        rest_out[1],
        rest_out[2],
        rest_out[3],
    )


CHUNK_ROWS = 1152
REST_ROWS = 2 * PD + FREQ + D + CLASSES + 1


def tile_place(tiles, ranks):
    counts = [count // ranks for count in matrix_tiles()]
    layer_tiles = sum(matrix_tiles())
    level = tiles // layer_tiles
    inside = tiles % layer_tiles
    dest = jnp.zeros_like(tiles)
    slot = jnp.zeros_like(tiles)
    start = 0
    base = 0
    for count, total in zip(counts, matrix_tiles()):
        local_tile = inside - start
        here = (local_tile >= 0) & (local_tile < total)
        dest = jnp.where(here, local_tile // count, dest)
        slot = jnp.where(here, base + level * count + local_tile % count, slot)
        start += total
        base += 2 * count
    return dest, slot


def matrix_tiles():
    groups = 4
    head_width = HEADS * HD // groups
    hidden_width = FF // groups
    sizes = [D * 3 * head_width, head_width * D, D * hidden_width, hidden_width * D]
    return [size // 128 for size in sizes]


def rank_within(dest, ranks):
    n = dest.shape[0]
    inner = 96
    outer = n // inner
    hot = (dest.reshape(outer, inner)[None] == jnp.arange(ranks)[:, None, None]).astype(jnp.bfloat16)
    upto = (jnp.arange(inner)[:, None] < jnp.arange(inner)[None, :]).astype(jnp.bfloat16)
    before = jnp.einsum("roi,ij->roj", hot, upto, preferred_element_type=jnp.float32)
    totals = jnp.sum(hot.astype(jnp.float32), axis=2)
    over = (jnp.arange(outer)[:, None] < jnp.arange(outer)[None, :]).astype(jnp.float32)
    prior = jnp.dot(totals, over, precision=highest)
    rank = jnp.sum(hot.astype(jnp.float32) * (before + prior[:, :, None]), axis=0)
    return rank.astype(jnp.int32).reshape(n), jnp.sum(totals, axis=1).astype(jnp.int32)


def widen(source, dest, rows):
    step = 128 if rows % 128 == 0 else 16
    whole = rows // step

    def body(i, unused):
        at = pl.ds(pl.multiple_of(i * step, step), step)
        dest[at, :] = source[at, :].astype(dest.dtype)
        return unused

    lax.fori_loop(0, whole, body, 0)


def pack_kernel(n, pos_ref, x_ref, buf_ref, wide, sorted_rows):
    widen(x_ref, wide, n)

    def move(i, unused):
        places = [pos_ref[i * 16 + j] for j in range(16)]
        rows = [wide[pl.ds(i * 16 + j, 1), :] for j in range(16)]
        for place, row in zip(places, rows):
            sorted_rows[pl.ds(place, 1), :] = row
        return unused

    lax.fori_loop(0, n // 16, move, 0)
    widen(sorted_rows, buf_ref, buf_ref.shape[0])


def scatter_kernel(total, tag_ref, buf_ref, out_ref, wide, slots):
    widen(buf_ref, wide, total)

    def move(i, unused):
        tags = [tag_ref[i * 16 + j] for j in range(16)]
        rows = [wide[pl.ds(i * 16 + j, 1), :] for j in range(16)]
        for tag, row in zip(tags, rows):
            slots[pl.ds(tag, 1), :] = row
        return unused

    lax.fori_loop(0, total // 16, move, 0)
    widen(slots, out_ref, out_ref.shape[0])


def gather_kernel(total, index_ref, x_ref, out_ref, wide_out):
    def move(i, unused):
        index = [index_ref[i * 16 + j] for j in range(16)]
        rows = [x_ref[pl.ds(place, 1), :] for place in index]
        for j in range(16):
            wide_out[pl.ds(i * 16 + j, 1), :] = rows[j]
        return unused

    lax.fori_loop(0, total // 16, move, 0)
    widen(wide_out, out_ref, total)


SMEM = pl.BlockSpec(memory_space=pltpu.SMEM)
VMEM = pl.BlockSpec(memory_space=pltpu.VMEM)
PARAMS = pltpu.CompilerParams(vmem_limit_bytes=48 * 1024 * 1024)


def pack_rows(rows, pos, total):
    n = rows.shape[0]
    return pl.pallas_call(
        functools.partial(pack_kernel, n),
        out_shape=jax.ShapeDtypeStruct((total, 128), jnp.bfloat16),
        in_specs=[SMEM, VMEM],
        out_specs=VMEM,
        scratch_shapes=[
            pltpu.VMEM((n, 128), jnp.float32),
            pltpu.VMEM((total + 16, 128), jnp.float32),
        ],
        compiler_params=PARAMS,
        name="pack_rows",
    )(pos, rows)


def pack_tags(pos, slot, fill, capacity):
    n = pos.shape[0]
    total = fill.shape[0] * capacity
    lines = total // 128
    here = (pos // 128)[:, None] == jnp.arange(lines)[None, :]
    high = jnp.where(here, (slot // 128)[:, None], 0)
    low = jnp.where(here, (slot % 128)[:, None], 0)
    lanes = ((pos % 128)[:, None] == jnp.arange(128)[None, :]).astype(jnp.bfloat16)
    parts = jnp.concatenate([high, low], axis=1).astype(jnp.bfloat16)
    found = contract(parts, lanes, 0, 0).astype(jnp.int32)
    tags = (found[:lines] * 128 + found[lines:]).reshape(fill.shape[0], capacity)
    return jnp.where(jnp.arange(capacity)[None, :] < fill[:, None], tags, n).reshape(-1)


def scatter_rows(rows, tags, n):
    total = rows.shape[0]
    return pl.pallas_call(
        functools.partial(scatter_kernel, total),
        out_shape=jax.ShapeDtypeStruct((n + 16, 128), jnp.bfloat16),
        in_specs=[SMEM, VMEM],
        out_specs=VMEM,
        scratch_shapes=[
            pltpu.VMEM((total, 128), jnp.float32),
            pltpu.VMEM((n + 16, 128), jnp.float32),
        ],
        compiler_params=PARAMS,
        name="scatter_rows",
    )(tags, rows)


def gather_rows(rows, index, dtype):
    total = index.shape[0]
    return pl.pallas_call(
        functools.partial(gather_kernel, total),
        out_shape=jax.ShapeDtypeStruct((total, 128), dtype),
        in_specs=[SMEM, VMEM],
        out_specs=VMEM,
        scratch_shapes=[pltpu.VMEM((total, 128), jnp.float32)],
        compiler_params=PARAMS,
        name="gather_rows",
    )(index, rows)


MESH = pl.DeviceIdType.MESH
LAG = 2
SLOTS = 4
GATHER_SLOTS = 12


def coordinates():
    rank = lax.axis_index("dp")
    group = lax.axis_index("mp")
    return lax.div(rank, 2), lax.rem(rank, 2), lax.div(group, 2), lax.rem(group, 2)


def device_at(z, x, y, core):
    return (z * 2 + x, y * 2 + core)


def neighbours():
    z, x, y, core = coordinates()
    along_x = device_at(z, 1 - x, y, core)
    along_y = device_at(z, x, 1 - y, core)
    first = tuple(jnp.where(core == 0, b, a) for a, b in zip(along_x, along_y))
    second = tuple(jnp.where(core == 0, a, b) for a, b in zip(along_x, along_y))
    others = [device_at(lax.rem(z + step, 4), x, y, core) for step in (1, 2, 3)]
    return device_at(z, x, y, 1 - core), first, second, others


def greet(peers):
    barrier = pltpu.get_barrier_semaphore()
    for peer in peers:
        pl.semaphore_signal(barrier, inc=1, device_id=peer, device_id_type=MESH)
    pl.semaphore_wait(barrier, len(peers))


def block_of(ref, entry, group, at, side=None):
    stacked, rows, width = entry
    sides = slice(None) if side is None else side
    if stacked:
        return ref.at[group, :, sides, at, :]
    return ref.at[:, sides, at, pl.ds(pl.multiple_of(group * width, 128), width)]


def slice_of(ref, entry, group, z, x, at):
    stacked, rows, width = entry
    if stacked:
        return ref.at[group, z, x, at, :]
    return ref.at[z, x, at, pl.ds(pl.multiple_of(group * width, 128), width)]


def chunk_ranges(plan, chunk):
    ranges = []
    start = 0
    for stacked, rows, width in plan:
        ranges.append((start, start + rows // chunk))
        start += rows // chunk
    return ranges, start


def in_range(unit, low, high):
    return (unit >= low) & (unit < high)


def remote(source, target, send, receive, peer):
    return pltpu.make_async_remote_copy(
        src_ref=source,
        dst_ref=target,
        send_sem=send,
        recv_sem=receive,
        device_id=peer,
        device_id_type=MESH,
    )


def gather_job(plan, chunk, slices, wholes, scratch):
    count = len(plan)
    held, other_held, own_sem, out_sem, z_send, z_recv, a_send, a_recv, b_send, b_recv, c_send, c_recv = scratch
    z, x, y, core = coordinates()
    other, first, second, others = neighbours()
    mine_first = jnp.where(core == 0, y, x)
    mine_second = jnp.where(core == 0, x, y)
    ranges, total = chunk_ranges(plan, chunk)

    def copies(stage, k, unit):
        entry = plan[k]
        slot = lax.rem(unit, GATHER_SLOTS)
        at = pl.ds(pl.multiple_of((unit - ranges[k][0]) * chunk, chunk), chunk)
        cols = pl.ds(0, entry[2])
        own = held.at[slot, mine_first, mine_second, z, :, cols]
        if stage == 0:
            source = slices[k].at[at, :]
            return [pltpu.make_async_copy(source, own, own_sem.at[slot])] + [
                remote(source, own, z_send.at[i, slot], z_recv.at[i, slot], others[i])
                for i in range(3)
            ]
        if stage == 1:
            part = held.at[slot, mine_first, mine_second, :, :, cols]
            return [remote(part, part, a_send.at[slot], a_recv.at[slot], second)]
        if stage == 2:
            part = held.at[slot, mine_first, :, :, :, cols]
            return [remote(part, part, b_send.at[slot], b_recv.at[slot], first)]
        if stage == 3:
            source = held.at[slot, :, :, :, :, cols]
            target = other_held.at[slot, :, :, :, :, cols]
            return [remote(source, target, c_send.at[slot], c_recv.at[slot], other)]
        made = []
        from_other = stage == 5
        ref, owner = (other_held, 1 - core) if from_other else (held, core)
        for i in range(2):
            for j in range(2):
                side = jnp.where(owner == 0, j, i)
                group = 2 * jnp.where(owner == 0, i, j) + owner
                made.append(
                    pltpu.make_async_copy(
                        ref.at[slot, i, j, :, :, cols],
                        block_of(wholes[k], entry, group, at, side),
                        out_sem.at[int(from_other), 2 * i + j, slot],
                    )
                )
        return made

    def go(unit, waits, starts):
        for k in range(count):

            @pl.when(in_range(unit, *ranges[k]))
            def _(k=k):
                for stage in waits:
                    for copy in copies(stage, k, unit):
                        copy.wait()
                for stage in starts:
                    for copy in copies(stage, k, unit):
                        copy.start()

    def step(t):
        go(t - 1 - 4 * LAG, (4, 5), ())
        go(t - 4 * LAG, (3,), (5,))
        go(t - 3 * LAG, (2,), (3, 4))
        go(t - 2 * LAG, (1,), (2,))
        go(t - LAG, (0,), (1,))
        go(t, (), (0,))

    return step, total + 1 + 4 * LAG


def whole_shape(entry):
    stacked, rows, width = entry
    return (4, 4, 2, rows, width) if stacked else (4, 2, rows, 4 * width)


def gather_scratch(plan, chunk, kind):
    dma = pltpu.SemaphoreType.DMA
    held = pltpu.VMEM((GATHER_SLOTS, 2, 2, 4, chunk, max(entry[2] for entry in plan)), kind)
    each = dma((GATHER_SLOTS,))
    three = dma((3, GATHER_SLOTS))
    return [held, held, each, dma((2, 4, GATHER_SLOTS)), three, three] + [each] * 6


def sum_job(plan, chunk, parts, outs, scratch):
    count = len(plan)
    own, from_core, from_first, from_second, from_z, half, quarter, eighth = scratch[:8]
    own_sem, core_send, core_recv, a_send, a_recv, b_send, b_recv, z_send, z_recv = scratch[8:]
    z, x, y, core = coordinates()
    other, first, second, others = neighbours()
    mine_first = jnp.where(core == 0, y, x)
    mine_second = jnp.where(core == 0, x, y)
    ranges, total = chunk_ranges(plan, chunk)

    def copies(stage, width, unit, k=None):
        slot = lax.rem(unit, SLOTS)
        pair = lax.rem(unit, 2)
        cols = pl.ds(0, width)
        if stage == 0:
            made = []
            for j in range(2):
                mine = own.at[pair, j, :, :, :, cols]
                theirs = from_core.at[pair, j, :, :, :, cols]
                if k is None:
                    made.append(pltpu.make_async_copy(mine, mine, own_sem.at[j, pair]))
                    made.append(remote(mine, theirs, core_send.at[j, pair], core_recv.at[j, pair], other))
                else:
                    at = pl.ds(pl.multiple_of((unit - ranges[k][0]) * chunk, chunk), chunk)
                    kept = block_of(parts[k], plan[k], 2 * j + core, at)
                    sent = block_of(parts[k], plan[k], 2 * j + 1 - core, at)
                    made.append(pltpu.make_async_copy(kept, mine, own_sem.at[j, pair]))
                    made.append(remote(sent, theirs, core_send.at[j, pair], core_recv.at[j, pair], other))
            return made
        if stage == 1:
            source = half.at[slot, 1 - mine_first, :, :, :, cols]
            target = from_first.at[slot, :, :, :, cols]
            return [remote(source, target, a_send.at[slot], a_recv.at[slot], first)]
        if stage == 2:
            source = quarter.at[slot, 1 - mine_second, :, :, cols]
            target = from_second.at[slot, :, :, cols]
            return [remote(source, target, b_send.at[slot], b_recv.at[slot], second)]
        made = []
        for i in range(3):
            source = eighth.at[slot, lax.rem(z + i + 1, 4), :, cols]
            target = from_z.at[slot, i, :, cols]
            made.append(remote(source, target, z_send.at[i, slot], z_recv.at[i, slot], others[i]))
        return made

    def wide(ref, index, cols):
        return ref[(*index, slice(None), cols)].astype(jnp.float32)

    def add(stage, width, unit):
        slot = lax.rem(unit, SLOTS)
        pair = lax.rem(unit, 2)
        cols = slice(0, width)
        if stage == 0:
            for i in range(2):
                for j in range(2):
                    lead = jnp.where(core == 0, i, j)
                    last = jnp.where(core == 0, j, i)
                    for k in range(4):
                        value = wide(own, (pair, i, k, j), cols) + wide(from_core, (pair, i, k, j), cols)
                        half[slot, lead, last, k, :, cols] = value.astype(half.dtype)
        elif stage == 1:
            for j in range(2):
                for k in range(4):
                    value = wide(half, (slot, mine_first, j, k), cols) + wide(
                        from_first, (slot, j, k), cols
                    )
                    quarter[slot, j, k, :, cols] = value.astype(quarter.dtype)
        else:
            for k in range(4):
                value = wide(quarter, (slot, mine_second, k), cols) + wide(
                    from_second, (slot, k), cols
                )
                eighth[slot, k, :, cols] = value.astype(eighth.dtype)

    widths = sorted({entry[2] for entry in plan})

    def go(unit, stage):
        for width in widths:
            inside = functools.reduce(
                jnp.logical_or,
                [in_range(unit, *ranges[k]) for k in range(count) if plan[k][2] == width],
            )

            @pl.when(inside)
            def _(width=width):
                for copy in copies(stage, width, unit):
                    copy.wait()
                add(stage, width, unit)
                for copy in copies(stage + 1, width, unit):
                    copy.start()

    def finish(unit):
        for k in range(count):

            @pl.when(in_range(unit, *ranges[k]))
            def _(k=k):
                width = plan[k][2]
                slot = lax.rem(unit, SLOTS)
                cols = slice(0, width)
                for copy in copies(3, width, unit):
                    copy.wait()
                at = pl.ds(pl.multiple_of((unit - ranges[k][0]) * chunk, chunk), chunk)
                value = wide(eighth, (slot, z), cols)
                for i in range(3):
                    value = value + wide(from_z, (slot, i), cols)
                outs[k][at, :] = value

    def begin(unit):
        for k in range(count):

            @pl.when(in_range(unit, *ranges[k]))
            def _(k=k):
                for copy in copies(0, plan[k][2], unit, k):
                    copy.start()

    def step(t):
        finish(t - 1 - 3 * LAG)
        go(t - 1 - 2 * LAG, 2)
        go(t - 1 - LAG, 1)
        go(t - 1, 0)
        begin(t)

    return step, total + 1 + 3 * LAG


def sum_scratch(plan, chunk, kind):
    dma = pltpu.SemaphoreType.DMA
    width = max(entry[2] for entry in plan)
    buffers = [
        (2, 2, 4, 2, chunk, width),
        (2, 2, 4, 2, chunk, width),
        (SLOTS, 2, 4, chunk, width),
        (SLOTS, 4, chunk, width),
        (SLOTS, 3, chunk, width),
        (SLOTS, 2, 2, 4, chunk, width),
        (SLOTS, 2, 4, chunk, width),
        (SLOTS, 4, chunk, width),
    ]
    return (
        [pltpu.VMEM(shape, kind) for shape in buffers]
        + [dma((2, 2))] * 3
        + [dma((SLOTS,))] * 4
        + [dma((3, SLOTS))] * 2
    )


def direct_job(kind, sources, targets, scratch):
    source, target = sources[0], targets[0]
    own_sem, send_sem, recv_sem = scratch
    ranks, groups = lax.axis_size("dp"), lax.axis_size("mp")
    rank, group = lax.axis_index("dp"), lax.axis_index("mp")
    me, count = (rank * groups + group, ranks * groups) if kind == "push" else (rank, ranks)

    def part(index):
        return source.at[index] if kind == "swap" else source

    own = pltpu.make_async_copy(part(me), target.at[me], own_sem)

    def copy(i):
        to = lax.rem(me + i, count)
        peer = (lax.div(to, groups), lax.rem(to, groups)) if kind == "push" else (to, group)
        return remote(part(to), target.at[me], send_sem.at[i], recv_sem.at[i], peer)

    def start(i, unused):
        copy(i).start()
        return unused

    def finish(i, unused):
        copy(i).wait()
        return unused

    def begin():
        own.start()
        lax.fori_loop(1, count, start, 0)

    def end():
        own.wait()
        lax.fori_loop(1, count, finish, 0)

    return begin, end


def travel_kernel(jobs, scratch_counts, *refs):
    refs = list(refs)

    def take(number):
        taken = refs[:number]
        del refs[:number]
        return taken

    sources = [take(len(job[1])) for job in jobs]
    targets = [take(len(job[1])) for job in jobs]
    scratch = [take(number) for number in scratch_counts]
    steps = []
    direct = []
    for (kind, plan, chunk), source, target, mine in zip(jobs, sources, targets, scratch):
        if kind == "gather":
            steps.append(gather_job(plan, chunk, source, target, mine))
        elif kind == "sum":
            steps.append(sum_job(plan, chunk, source, target, mine))
        else:
            direct.append(direct_job(kind, source, target, mine))
    if direct:
        greet_all()
    else:
        other, first, second, others = neighbours()
        greet([other, first, second] + others)
    for begin, unused_end in direct:
        begin()

    def step(t, unused):
        for one, unused_count in steps:
            one(t)
        return unused

    if steps:
        lax.fori_loop(0, max(count for unused_step, count in steps), step, 0)
    for unused_begin, end in direct:
        end()


def greet_all():
    groups = lax.axis_size("mp")
    world = lax.axis_size("dp") * groups
    me = lax.axis_index("dp") * groups + lax.axis_index("mp")
    barrier = pltpu.get_barrier_semaphore()

    def hail(i, unused):
        to = lax.rem(me + i, world)
        peer = (lax.div(to, groups), lax.rem(to, groups))
        pl.semaphore_signal(barrier, inc=1, device_id=peer, device_id_type=MESH)
        return unused

    lax.fori_loop(1, world, hail, 0)
    pl.semaphore_wait(barrier, world - 1)


def travel(jobs, arrays, number, name):
    ANY = pl.BlockSpec(memory_space=pl.ANY)
    dma = pltpu.SemaphoreType.DMA
    ranks, groups = lax.axis_size("dp"), lax.axis_size("mp")
    scratch = []
    shapes = []
    specs = []
    for (kind, plan, chunk), mine in zip(jobs, arrays):
        dtype = mine[0].dtype
        if kind == "gather":
            scratch.append(gather_scratch(plan, chunk, dtype))
            shapes += [jax.ShapeDtypeStruct(whole_shape(entry), dtype) for entry in plan]
            specs += [ANY] * len(plan)
        elif kind == "sum":
            scratch.append(sum_scratch(plan, chunk, dtype))
            shapes += [jax.ShapeDtypeStruct(entry[1:], jnp.float32) for entry in plan]
            specs += [VMEM] * len(plan)
        else:
            count = ranks * groups if kind == "push" else ranks
            scratch.append([dma, dma((count,)), dma((count,))])
            shape = mine[0].shape if kind == "swap" else (count,) + mine[0].shape
            shapes.append(jax.ShapeDtypeStruct(shape, dtype))
            specs.append(ANY)
    flat = [array for mine in arrays for array in mine]
    outs = pl.pallas_call(
        functools.partial(travel_kernel, jobs, [len(mine) for mine in scratch]),
        out_shape=shapes,
        in_specs=[ANY] * len(flat),
        out_specs=specs,
        scratch_shapes=[one for mine in scratch for one in mine],
        compiler_params=pltpu.CompilerParams(
            collective_id=number, has_side_effects=True, vmem_limit_bytes=48 * 1024 * 1024
        ),
        name=name,
    )(*flat)
    results = []
    for unused_kind, plan, unused_chunk in jobs:
        results.append(outs[: len(plan)])
        outs = outs[len(plan) :]
    return results


def push_kernel(world, x_ref, out_ref, send_sem, recv_sem):
    groups = lax.axis_size("mp")
    me = lax.axis_index("dp") * groups + lax.axis_index("mp")

    def peer(i):
        to = lax.rem(me + i, world)
        return (lax.div(to, groups), lax.rem(to, groups))

    barrier = pltpu.get_barrier_semaphore()

    def hail(i, unused):
        pl.semaphore_signal(barrier, inc=1, device_id=peer(i), device_id_type=MESH)
        return unused

    lax.fori_loop(1, world, hail, 0)
    out_ref[me] = x_ref[...]
    pl.semaphore_wait(barrier, world - 1)

    def copy(i):
        return remote(x_ref, out_ref.at[me], send_sem.at[i], recv_sem.at[i], peer(i))

    def start(i, unused):
        copy(i).start()
        return unused

    def finish(i, unused):
        copy(i).wait()
        return unused

    lax.fori_loop(1, world, start, 0)
    lax.fori_loop(1, world, finish, 0)


def push_all(value, world, number, name):
    dma = pltpu.SemaphoreType.DMA
    return pl.pallas_call(
        functools.partial(push_kernel, world),
        out_shape=jax.ShapeDtypeStruct((world,) + value.shape, value.dtype),
        in_specs=[VMEM],
        out_specs=VMEM,
        scratch_shapes=[dma((world,)), dma((world,))],
        compiler_params=pltpu.CompilerParams(collective_id=number, has_side_effects=True),
        name=name,
    )(value)


def swap_ranks(buf, ranks):
    rest = buf.shape[1:]
    split = buf.reshape((ranks, buf.shape[0] // ranks) + rest)
    return lax.all_to_all(split, "dp", 0, 0).reshape(buf.shape)


def round_positions(dest, rank, counts, capacity, turn):
    ranks = counts.shape[0]
    low = turn * capacity
    inside = (rank >= low) & (rank < low + capacity)
    pos = jnp.where(inside, dest * capacity + rank - low, ranks * capacity)
    fill = jnp.clip(counts - low, 0, capacity)
    return pos, fill, inside


def tiles_to_slots(rows, dest, slot, rank, counts, rounds, carry_first):
    n = rows.shape[0]
    ranks = counts.shape[0]
    total = ranks * CHUNK_ROWS

    def packed(turn):
        pos, fill, unused = round_positions(dest, rank, counts, CHUNK_ROWS, turn)
        return pack_rows(rows, pos, total), pack_tags(pos, slot, fill, CHUNK_ROWS)

    got, tags = carry_first(*packed(0))
    first = scatter_rows(got, tags, n)

    def more(carry):
        turn, slots = carry
        more_rows, more_tags = [swap_ranks(part, ranks) for part in packed(turn)]
        added = scatter_rows(more_rows, more_tags, n)
        fresh = jnp.zeros((n + 16,), jnp.bool_).at[more_tags].set(True)
        return turn + 1, jnp.where(fresh[:, None], added, slots)

    unused, slots = lax.while_loop(lambda carry: carry[0] < rounds, more, (1, first))
    return slots, tags


def slots_to_tiles(slots, first, dest, slot, rank, counts, rounds):
    ranks = counts.shape[0]
    total = ranks * CHUNK_ROWS

    def landed(got, turn):
        pos, unused, inside = round_positions(dest, rank, counts, CHUNK_ROWS, turn)
        return gather_rows(got, jnp.minimum(pos, total - 1), jnp.float32), inside

    def more(carry):
        turn, rows = carry
        pos, fill, unused = round_positions(dest, rank, counts, CHUNK_ROWS, turn)
        turn_tags = swap_ranks(pack_tags(pos, slot, fill, CHUNK_ROWS), ranks)
        got = swap_ranks(gather_rows(slots, turn_tags, jnp.bfloat16), ranks)
        added, inside = landed(got.astype(jnp.float32), turn)
        return turn + 1, jnp.where(inside[:, None], added, rows)

    start = (1, landed(first.astype(jnp.float32), 0)[0])
    unused, rows = lax.while_loop(lambda carry: carry[0] < rounds, more, start)
    return rows


QKV_WIDTH = 896
PROJ_ROWS = 48


def layer_plan(ranks):
    return (
        (False, D // ranks, QKV_WIDTH),
        (True, PROJ_ROWS, D),
        (False, D // ranks, FF // 4),
        (True, FF // 4 // ranks, D),
    )


def pad_to(values, axis, size):
    widths = [(0, 0)] * values.ndim
    widths[axis] = (0, size - values.shape[axis])
    return jnp.pad(values, widths)


def slice_places(ranks):
    widths = [3 * HEADS * HD // 4, D, FF // 4, D]
    places = []
    base = 0
    for total, width in zip(matrix_tiles(), widths):
        count = total // ranks
        places.append((count * 128 // width, width, (base, base + count)))
        base += 2 * count
    return places


def row_group(width):
    rows = 128 // math.gcd(width, 128)
    return rows, rows * width // 128


def lane_pieces(start, size, source_width):
    pieces = []
    done = 0
    while done < size:
        row, column = divmod(start + done, source_width)
        block, lane = divmod(column, 128)
        length = min(128 - lane, source_width - column, size - done)
        pieces.append((row, block, lane, done, length))
        done += length
    return pieces


def join_pieces(pieces, load, rows):
    lanes = lax.broadcasted_iota(jnp.int32, (rows, 128), 1)
    value = None
    for row, block, lane, here, length in pieces:
        part = load(row, block)
        if lane != here:
            part = pltpu.roll(part, (here - lane) % 128, 1)
        if value is None:
            inside = lanes < here + length
            value = part if here + length == 128 else jnp.where(inside, part, 0.0)
        else:
            value = jnp.where((lanes >= here) & (lanes < here + length), part, value)
    return value


def spread_kernel(ranks, low_ref, *refs):
    outs, wide, slots_ref = refs[:8], refs[8], refs[9]
    widen(low_ref, slots_ref, low_ref.shape[0])
    for index, (rows, width, bases) in enumerate(slice_places(ranks)):
        group, tiles = row_group(width)
        count = rows // group
        blocks = -(-width // 128)
        for level in range(2):
            out = outs[level * 4 + index]
            for row in range(group):
                for block in range(blocks):
                    start = row * width + block * 128
                    pieces = lane_pieces(start, min(128, width - block * 128), 128)

                    def load(tile, unused, base=bases[level]):
                        return slots_ref[pl.ds(base + tile, count, stride=tiles), :]

                    value = join_pieces(pieces, load, count)
                    at = pl.ds(row, count, stride=group) if group > 1 else pl.ds(0, count)
                    wide[block, at, :] = value
            padded = out.shape[0]
            for block in range(blocks):
                if padded > rows:
                    wide[block, rows:padded, :] = jnp.zeros((padded - rows, 128), jnp.float32)
                out[:, block * 128 : (block + 1) * 128] = wide[block, :padded, :].astype(out.dtype)


def collect_kernel(ranks, *refs):
    parts, slots_ref, square_ref, wide = refs[:8], refs[8], refs[9], refs[10]
    square_ref[...] = jnp.zeros_like(square_ref)
    end = slots_ref.shape[0]
    total = 0
    for index, (rows, width, bases) in enumerate(slice_places(ranks)):
        group, tiles = row_group(width)
        count = rows // group
        total += 2 * count * tiles
        for level in range(2):
            part = parts[level * 4 + index]
            for block in range(-(-width // 128)):
                wide[block, :rows, :] = part[:rows, block * 128 : (block + 1) * 128]
            for tile in range(tiles):
                pieces = lane_pieces(tile * 128, 128, width)

                def load(row, block):
                    at = pl.ds(row, count, stride=group) if group > 1 else pl.ds(0, count)
                    return wide[block, at, :]

                value = join_pieces(pieces, load, count)
                slots_ref[pl.ds(bases[level] + tile, count, stride=tiles), :] = value
                square_ref[:1, :] += jnp.sum(value * value, axis=0, keepdims=True)
    slots_ref[total:end, :] = jnp.zeros((end - total, 128), jnp.float32)


def spread_slots(slots, ranks):
    plan = layer_plan(ranks) * 2
    tall = max(entry[1] for entry in plan)
    broad = max(entry[2] for entry in plan)
    return pl.pallas_call(
        functools.partial(spread_kernel, ranks),
        out_shape=[jax.ShapeDtypeStruct(entry[1:], jnp.bfloat16) for entry in plan],
        in_specs=[VMEM],
        out_specs=[VMEM] * len(plan),
        scratch_shapes=[
            pltpu.VMEM((broad // 128, tall, 128), jnp.float32),
            pltpu.VMEM(slots.shape, jnp.float32),
        ],
        compiler_params=PARAMS,
        name="spread_slots",
    )(slots)


def collect_slots(parts, rows, ranks):
    tall = max(part.shape[0] for part in parts)
    broad = max(part.shape[1] for part in parts)
    return pl.pallas_call(
        functools.partial(collect_kernel, ranks),
        out_shape=(
            jax.ShapeDtypeStruct((rows, 128), jnp.float32),
            jax.ShapeDtypeStruct((8, 128), jnp.float32),
        ),
        in_specs=[VMEM] * len(parts),
        out_specs=(VMEM, VMEM),
        scratch_shapes=[pltpu.VMEM((broad // 128, tall, 128), jnp.float32)],
        compiler_params=PARAMS,
        name="collect_slots",
    )(*parts)


def whole_weights(wholes, ranks):
    qkv, proj, up, down = wholes
    return (qkv.reshape(D, -1), proj.reshape(-1, D), up.reshape(D, -1), down.reshape(-1, D))


def whole_parts(grads, ranks):
    qkv, proj, up, down = grads
    shapes = [whole_shape(entry) for entry in layer_plan(ranks)]
    return [part.reshape(shape) for part, shape in zip((qkv, proj, up, down), shapes)]


GROUP_HEADS = HEADS // 4
GROUP_WIDTH = HEADS * HD // 4


def dot_nt(left, right):
    return lax.dot_general(left, right, (((1,), (1,)), ((), ())), preferred_element_type=jnp.float32)


def dot_tn(left, right):
    return lax.dot_general(left, right, (((0,), (0,)), ((), ())), preferred_element_type=jnp.float32)


def head_parts(packed_ref, head):
    return [
        packed_ref[:, index * GROUP_WIDTH + head * HD : index * GROUP_WIDTH + (head + 1) * HD]
        for index in range(3)
    ]


def head_probs(queries, key_rows):
    scores = dot_nt(queries, key_rows) * HD ** (-0.5)
    powers = jnp.exp(scores - jnp.max(scores, axis=-1, keepdims=True))
    return powers / jnp.sum(powers, axis=-1, keepdims=True)


def pad_columns(values, own):
    rows = values.shape[0]
    gap = jnp.zeros((rows, PROJ_ROWS - own), values.dtype)
    parts = []
    for start in range(0, values.shape[1], own):
        parts += [values[:, start : start + own], gap]
    return jnp.concatenate(parts, axis=1)


def attend_kernel(own, packed_ref, out_ref):
    heads = [head_parts(packed_ref, head) for head in range(GROUP_HEADS)]
    probs = [head_probs(queries, key_rows) for queries, key_rows, unused in heads]
    mixed = [
        product(prob.astype(jnp.bfloat16), parts[2]).astype(out_ref.dtype)
        for prob, parts in zip(probs, heads)
    ]
    out_ref[...] = pad_columns(jnp.concatenate(mixed, axis=1), own)


def attend_back_kernel(packed_ref, grad_ref, spread_ref, out_ref):
    heads = [head_parts(packed_ref, head) for head in range(GROUP_HEADS)]
    every = range(GROUP_HEADS)
    grads = grad_ref[...]
    grad_mixed = [dot_nt(grads, spread_ref[head]).astype(jnp.bfloat16) for head in every]
    probs = [head_probs(queries, key_rows) for queries, key_rows, unused in heads]
    grad_probs = [dot_nt(grad_mixed[head], heads[head][2]) for head in every]
    grad_values = [dot_tn(probs[head].astype(jnp.bfloat16), grad_mixed[head]) for head in every]
    grad_scores = []
    for prob, grad_prob in zip(probs, grad_probs):
        score = prob * (grad_prob - jnp.sum(grad_prob * prob, axis=-1, keepdims=True))
        grad_scores.append((score * HD ** (-0.5)).astype(jnp.bfloat16))
    grad_queries = [product(grad_scores[head], heads[head][1]) for head in every]
    grad_keys = [dot_tn(grad_scores[head], heads[head][0]) for head in every]
    for index, parts in enumerate((grad_queries, grad_keys, grad_values)):
        for head, part in enumerate(parts):
            start = index * GROUP_WIDTH + head * HD
            out_ref[:, start : start + HD] = part.astype(out_ref.dtype)
    rows, width = out_ref.shape
    out_ref[:, 3 * GROUP_WIDTH :] = jnp.zeros((rows, width - 3 * GROUP_WIDTH), out_ref.dtype)


def spread_heads(own):
    columns = jnp.arange(GROUP_WIDTH // own * PROJ_ROWS)
    source = columns // PROJ_ROWS * own + columns % PROJ_ROWS
    source = jnp.where(columns % PROJ_ROWS < own, source, -1)
    hot = jnp.arange(GROUP_WIDTH)[:, None] == source[None, :]
    return hot.astype(jnp.bfloat16).reshape(GROUP_HEADS, HD, -1)


def attend_call(kernel, images, inputs, constants, out_width, name):
    rows = inputs[0].shape[0] // images

    def block(width):
        return pl.BlockSpec((rows, width), lambda image, group: (image, group))

    return pl.pallas_call(
        kernel,
        grid=(images, 4),
        out_shape=jax.ShapeDtypeStruct((images * rows, 4 * out_width), jnp.bfloat16),
        in_specs=[block(one.shape[1] // 4) for one in inputs]
        + [pl.BlockSpec(one.shape, lambda image, group: (0, 0, 0)) for one in constants],
        out_specs=block(out_width),
        compiler_params=PARAMS,
        name=name,
    )(*inputs, *constants)


def attend(packed, own, images):
    kernel = functools.partial(attend_kernel, own)
    return attend_call(kernel, images, [packed], [], GROUP_WIDTH // own * PROJ_ROWS, "attend")


def attend_back(packed, grads, own, images):
    constants = [spread_heads(own)]
    return attend_call(
        attend_back_kernel, images, [packed, grads], constants, QKV_WIDTH, "attend_back"
    )


def own_forward(state, weights, modulate, own):
    qkv_weight, proj_weight, up_weight, down_weight = weights
    images, rows, columns = state.shape
    shift_one, scale_one, gate_one, shift_two, scale_two, gate_two = [
        modulate[:, index, None, :] for index in range(6)
    ]
    normed_one, spread_one = normalize(state)
    full_one = (normed_one * (1.0 + scale_one) + shift_one).astype(jnp.bfloat16)
    flat_one = full_one.reshape(-1, columns)
    packed = product(flat_one, qkv_weight).astype(jnp.bfloat16)
    attended = attend(packed, own, images)
    branch_one = product(attended, proj_weight).reshape(state.shape)
    middle = state + gate_one * branch_one
    normed_two, spread_two = normalize(middle)
    full_two = (normed_two * (1.0 + scale_two) + shift_two).astype(jnp.bfloat16)
    flat_two = full_two.reshape(-1, columns)
    hidden_pre = product(flat_two, up_weight)
    activated = jax.nn.gelu(hidden_pre, approximate=True).astype(jnp.bfloat16)
    branch_two = product(activated, down_weight).reshape(state.shape)
    result = middle + gate_two * branch_two
    saved = (
        normed_one,
        spread_one,
        flat_one,
        packed,
        attended,
        branch_one,
        normed_two,
        spread_two,
        flat_two,
        hidden_pre,
        activated,
        branch_two,
    )
    return (result, saved)


def own_backward(grad_out, saved, weights, modulate, own):
    (
        normed_one,
        spread_one,
        flat_one,
        packed,
        attended,
        branch_one,
        normed_two,
        spread_two,
        flat_two,
        hidden_pre,
        activated,
        branch_two,
    ) = saved
    qkv_weight, proj_weight, up_weight, down_weight = weights
    images, rows, columns = grad_out.shape
    shift_one, scale_one, gate_one, shift_two, scale_two, gate_two = [
        modulate[:, index, None, :] for index in range(6)
    ]
    grad_gate_two = jnp.sum(grad_out * branch_two, axis=1)
    back_two = (gate_two * grad_out).astype(jnp.bfloat16).reshape(-1, columns)
    grad_down = product(activated.T, back_two).astype(jnp.bfloat16)
    grad_act = product(back_two, down_weight.T)
    unused, gelu_back = jax.vjp(lambda pre: jax.nn.gelu(pre, approximate=True), hidden_pre)
    grad_pre = gelu_back(grad_act)[0].astype(jnp.bfloat16)
    grad_up = product(flat_two.T, grad_pre).astype(jnp.bfloat16)
    grad_hidden_two = product(grad_pre, up_weight.T)
    grad_hidden_two = grad_hidden_two.reshape(grad_out.shape)
    grad_shift_two = jnp.sum(grad_hidden_two, axis=1)
    grad_scale_two = jnp.sum(grad_hidden_two * normed_two, axis=1)
    grad_middle = grad_out + normalize_back(
        grad_hidden_two * (1.0 + scale_two), normed_two, spread_two
    )
    grad_gate_one = jnp.sum(grad_middle * branch_one, axis=1)
    back_one = (gate_one * grad_middle).astype(jnp.bfloat16).reshape(-1, columns)
    grad_proj = product(attended.T, back_one).astype(jnp.bfloat16)
    grad_attended = product(back_one, proj_weight.T).astype(jnp.bfloat16)
    grad_packed = attend_back(packed, grad_attended, own, images)
    grad_qkv = product(flat_one.T, grad_packed).astype(jnp.bfloat16)
    grad_hidden_one = product(grad_packed, qkv_weight.T)
    grad_hidden_one = grad_hidden_one.reshape(grad_out.shape)
    grad_shift_one = jnp.sum(grad_hidden_one, axis=1)
    grad_scale_one = jnp.sum(grad_hidden_one * normed_one, axis=1)
    grad_state = grad_middle + normalize_back(
        grad_hidden_one * (1.0 + scale_one), normed_one, spread_one
    )
    grad_mod = jnp.concatenate(
        [
            grad_shift_one,
            grad_scale_one,
            grad_gate_one,
            grad_shift_two,
            grad_scale_two,
            grad_gate_two,
        ],
        axis=1,
    )
    return (grad_state, grad_mod, (grad_qkv, grad_proj, grad_up, grad_down))


def contract(left, right, left_axis, right_axis):
    return lax.dot_general(
        left,
        right,
        (((left_axis,), (right_axis,)), ((), ())),
        preferred_element_type=jnp.float32,
    )


def contract_wide(left, right, left_axis, right_axis):
    return lax.dot_general(
        left.astype(jnp.float32),
        right.astype(jnp.float32),
        (((left_axis,), (right_axis,)), ((), ())),
        precision=highest,
        preferred_element_type=jnp.float32,
    )


def silu_back(values, grads):
    unused, pull = jax.vjp(jax.nn.silu, values)
    return pull(grads)[0]


def local(
    big_copy,
    big_master,
    big_first,
    big_second,
    ada_copy,
    ada_master,
    ada_first,
    ada_second,
    rest_copy,
    rest_master,
    rest_first,
    rest_second,
    owner_tiles,
    kept_patches,
    kept_pos,
    timestep,
    label,
    owner,
    target,
    step,
):
    groups = lax.axis_size("mp")
    ranks = lax.axis_size("dp")
    world = groups * ranks
    my_rank = lax.axis_index("dp")
    micro = kept_patches.shape[0]
    own_columns = D // world
    columns = D

    owned = big_copy.shape[1]
    all_dest, unused_slot = tile_place(owner_tiles, ranks)
    all_hot = all_dest.reshape(ranks, owned, 1) == jnp.arange(ranks)
    rounds = (jnp.max(jnp.sum(all_hot.astype(jnp.int32), axis=1)) + CHUNK_ROWS - 1) // CHUNK_ROWS
    own_tiles = lax.dynamic_slice(owner_tiles, (my_rank * owned,), (owned,))
    dest, slot = tile_place(own_tiles, ranks)
    rank, counts = rank_within(dest, ranks)
    rest_own = rest_copy.reshape(own_columns, REST_ROWS)
    edges = [0, PD, PD + FREQ, PD + FREQ + D, PD + FREQ + D + CLASSES, REST_ROWS]
    win_t, one_t, two_t, table_t, tail_t = [
        rest_own[:, edges[i] : edges[i + 1]] for i in range(5)
    ]
    ends_size = own_columns * (2 * PD + 1)
    one_size = own_columns * FREQ
    whole_numbers = jnp.concatenate([timestep[:, 0], label[:, 0]])
    told = jnp.concatenate(
        [
            jnp.concatenate([win_t, tail_t], axis=1).reshape(-1),
            one_t.reshape(-1),
            (whole_numbers // 32).astype(jnp.bfloat16),
            (whole_numbers % 32).astype(jnp.bfloat16),
        ]
    )
    told = pad_to(told, 0, -(-told.shape[0] // 2048) * 2048).reshape(-1, 128)
    brought = []

    def carry_first(buf, new_tags):
        arrays = [
            [told],
            [target.reshape(-1, 128)],
            [new_tags.reshape(ranks, -1, 128)],
            [buf.reshape(ranks, -1, 128)],
        ]
        kinds = ("push", "share", "swap", "swap")
        got = travel([(kind, (None,), 0) for kind in kinds], arrays, 6, "exchange_inputs")
        brought.extend(got)
        return got[3][0].reshape(buf.shape), got[2][0].reshape(new_tags.shape)

    slots, tags = tiles_to_slots(big_copy[0], dest, slot, rank, counts, rounds, carry_first)
    told = brought[0][0].reshape(world, -1)
    goals = brought[1][0].reshape(ranks, micro, SEQ, PD)
    facts = told[:, ends_size + one_size :][:, : 4 * micro].astype(jnp.int32)
    facts = facts[:, : 2 * micro] * 32 + facts[:, 2 * micro :]
    facts = facts.reshape(ranks, groups, 2 * micro).transpose(1, 0, 2).reshape(world, -1)
    stamps = facts[:, :micro].reshape(-1)
    tags_all = facts[:, micro:].reshape(-1)
    ends = told[:, :ends_size].reshape(columns, -1)
    embed_weight = ends[:, :PD].T
    mask_token = ends[:, PD].astype(jnp.float32)
    head_weight = ends[:, PD + 1 :]
    count_all = micro * world
    features = jax.vmap(time_features)(stamps).astype(jnp.bfloat16)
    pre_time = contract(features, one_t, 1, 1)
    one_whole = told[:, ends_size : ends_size + one_size].reshape(columns, FREQ)
    hidden_all = jax.nn.silu(contract(features, one_whole, 1, 1)).astype(jnp.bfloat16)
    picks = (tags_all[:, None] == jnp.arange(CLASSES, dtype=jnp.int32)[None, :]).astype(
        jnp.bfloat16
    )
    cond_own = contract(hidden_all, two_t, 1, 1) + contract(picks, table_t, 1, 1)
    signal_own = jax.nn.silu(cond_own).astype(jnp.bfloat16)
    ada_own = ada_copy.reshape(own_columns, 14 * columns)
    mod_rows = micro * 14
    mod_entry = (True, 32, columns)
    mods = product(signal_own, ada_own).reshape(world, mod_rows, columns)
    mods = pad_to(mods, 1, mod_entry[1]).reshape(whole_shape(mod_entry))
    plan = layer_plan(ranks) * 2
    wholes, mods = travel(
        (("gather", plan, 16), ("sum", (mod_entry,), 16)),
        [spread_slots(slots, ranks), [mods]],
        1,
        "gather_weights",
    )
    weights = [whole_weights(wholes[:4], ranks), whole_weights(wholes[4:], ranks)]
    own = GROUP_WIDTH // ranks
    mods = mods[0][:mod_rows].reshape(micro, 14, columns)
    mod_enc = mods[:, :6]
    mod_dec = mods[:, 6:12]
    final_shift = mods[:, 12:13]
    final_scale = mods[:, 13:]

    goal = jnp.stack([goals[owner[b, 0], b] for b in range(micro)])
    positions = position_table(columns)
    images = ranks * groups
    inv_count = 1.0 / (PD * micro * images * KEEP)
    place = kept_pos[:, 0]
    patches = kept_patches[:, 0].astype(jnp.bfloat16)
    hits = (
        jnp.arange(SEQ, dtype=jnp.int32)[None, :, None] == place[:, None, :]
    ).astype(jnp.float32)
    hits_low = hits.astype(jnp.bfloat16)
    kept = jnp.sum(hits, axis=2)[:, :, None]
    embedded = product(patches.reshape(-1, PD), embed_weight).reshape(micro, KEEP, columns)
    embedded = embedded + jnp.take(positions, place, axis=0)
    enc_out, enc_saved = own_forward(embedded, weights[0], mod_enc, own)
    sent = enc_out.astype(jnp.bfloat16)
    dec_in = (
        jnp.einsum("bpr,brd->bpd", hits_low, sent, preferred_element_type=jnp.float32)
        + (1.0 - kept) * mask_token[None, None, :]
        + positions[None]
    )
    dec_out, dec_saved = own_forward(dec_in, weights[1], mod_dec, own)
    normed_final, spread_final = normalize(dec_out)
    head_in = (normed_final * (1.0 + final_scale) + final_shift).astype(jnp.bfloat16)
    flat_head = head_in.reshape(-1, columns)
    output = product(flat_head, head_weight).reshape(micro, SEQ, PD)
    error = output - goal
    weight = kept + MASKED_WEIGHT * (1.0 - kept)
    loss_sum = jnp.sum(weight * error * error) * inv_count

    grad_output = (2.0 * inv_count * weight * error).astype(jnp.bfloat16).reshape(-1, PD)
    grad_head = contract(grad_output, flat_head, 0, 0)
    grad_head_in = product(grad_output, head_weight.T).reshape(dec_out.shape)
    grad_final = jnp.concatenate(
        [jnp.sum(grad_head_in, axis=1), jnp.sum(grad_head_in * normed_final, axis=1)], axis=1
    )
    grad_dec_out = normalize_back(grad_head_in * (1.0 + final_scale), normed_final, spread_final)
    grad_dec_in, grad_mod_dec, dec_grads = own_backward(
        grad_dec_out, dec_saved, weights[1], mod_dec, own
    )
    grad_mask = jnp.sum((1.0 - kept) * grad_dec_in, axis=(0, 1))[None, :]
    grad_sent = jnp.einsum(
        "bpr,bpd->brd",
        hits_low,
        grad_dec_in.astype(jnp.bfloat16),
        preferred_element_type=jnp.float32,
    )
    grad_embedded, grad_mod_enc, enc_grads = own_backward(
        grad_sent, enc_saved, weights[0], mod_enc, own
    )
    grad_embed = contract_wide(
        patches.reshape(-1, PD), grad_embedded.reshape(-1, columns), 0, 0
    )

    vectors = jnp.concatenate([grad_mod_enc, grad_mod_dec, grad_final], axis=1)
    vectors = vectors.astype(jnp.bfloat16).reshape(mod_rows, columns)
    vectors = pad_to(vectors, 0, mod_entry[1])
    sums, vectors = travel(
        (("sum", plan, 16), ("gather", (mod_entry,), 16)),
        [whole_parts(enc_grads, ranks) + whole_parts(dec_grads, ranks), [vectors]],
        2,
        "sum_gradients",
    )
    sums, big_squares = collect_slots(sums, owned + 16, ranks)
    vectors = vectors[0]
    back = gather_rows(sums, tags, jnp.bfloat16)
    vectors = vectors.reshape(world, mod_entry[1], columns)[:, :mod_rows].reshape(count_all, -1)
    owned_ada = contract(signal_own, vectors, 0, 0).reshape(-1)
    grad_signal = contract(vectors, ada_own, 1, 1)
    grad_cond = silu_back(cond_own, grad_signal)
    grad_two_t = contract_wide(grad_cond, hidden_all, 0, 0)
    grad_table_t = contract_wide(grad_cond, picks, 0, 0)
    shared = jnp.concatenate(
        [contract_wide(grad_cond, two_t, 1, 0), grad_embed, grad_mask, grad_head], axis=0
    )
    shared_rows = shared.shape[0]
    shared = shared.reshape(shared_rows, ranks, groups, own_columns).transpose(2, 1, 0, 3)
    shared = pad_to(shared.reshape(world, -1), 1, 4096)
    shared_entry = (True, 32, 128)
    shared, back = travel(
        (("sum", (shared_entry,), 32), ("swap", (None,), 0)),
        [[shared.reshape(whole_shape(shared_entry))], [back.reshape(ranks, -1, 128)]],
        5,
        "sum_shared",
    )
    shared = shared[0]
    shared = shared.reshape(-1)[: shared_rows * own_columns].reshape(shared_rows, own_columns)
    grad_pre = silu_back(pre_time, shared[:count_all])
    grad_one_t = contract_wide(grad_pre, features, 0, 0)
    ends_t = shared[count_all:].T
    owned_rest = jnp.concatenate(
        [ends_t[:, :PD], grad_one_t, grad_two_t, grad_table_t, ends_t[:, PD:]], axis=1
    ).reshape(-1)

    squares = jnp.sum(big_squares) + jnp.sum(owned_ada * owned_ada) + jnp.sum(owned_rest * owned_rest)
    totals = jnp.broadcast_to(pad_to(jnp.stack([loss_sum, squares]), 0, 128), (8, 128))
    totals = jnp.sum(push_all(totals, world, 8, "push_totals")[:, 0, :2], axis=0)
    back = back[0].reshape(-1, 128)
    owned_big = slots_to_tiles(sums, back, dest, slot, rank, counts, rounds)
    grad_norm = jnp.sqrt(totals[1])
    clip = jnp.minimum(1.0, MAX_NORM / (grad_norm + 1e-06))
    count = step[0].astype(jnp.float32)
    big_out = adam_update(
        owned_big.reshape(big_master.shape), big_master, big_first, big_second, clip, count
    )
    ada_out = adam_update(owned_ada, ada_master, ada_first, ada_second, clip, count)
    rest_out = adam_update(owned_rest, rest_master, rest_first, rest_second, clip, count)
    return (
        totals[:1],
        grad_norm.reshape(1),
        big_out[0],
        big_out[1],
        big_out[2],
        big_out[3],
        ada_out[0],
        ada_out[1],
        ada_out[2],
        ada_out[3],
        rest_out[0],
        rest_out[1],
        rest_out[2],
        rest_out[3],
    )


def whole_columns(mesh):
    ranks, groups = mesh.shape["dp"], mesh.shape["mp"]
    return groups == 4 and D % (ranks * groups) == 0 and ranks == 8


def solution(mesh):
    body = local if whole_columns(mesh) else local_general
    in_specs = (
        P("mp", "dp", None),
        P("mp", "dp", None),
        P("mp", "dp", None),
        P("mp", "dp", None),
        P(("dp", "mp")),
        P(("dp", "mp")),
        P(("dp", "mp")),
        P(("dp", "mp")),
        P(("dp", "mp")),
        P(("dp", "mp")),
        P(("dp", "mp")),
        P(("dp", "mp")),
        P(),
        P(None, ("dp", "mp"), None, None),
        P(None, ("dp", "mp"), None),
        P(None, ("dp", "mp")),
        P(None, ("dp", "mp")),
        P(None, ("dp", "mp")),
        P(None, ("dp", "mp"), None, None),
        P(),
    )
    out_specs = (
        P(),
        P(),
        P("mp", "dp", None),
        P("mp", "dp", None),
        P("mp", "dp", None),
        P("mp", "dp", None),
        P(("dp", "mp")),
        P(("dp", "mp")),
        P(("dp", "mp")),
        P(("dp", "mp")),
        P(("dp", "mp")),
        P(("dp", "mp")),
        P(("dp", "mp")),
        P(("dp", "mp")),
    )
    return jax.shard_map(body, mesh=mesh, in_specs=in_specs, out_specs=out_specs, check_vma=False)
```

```python
import functools
import math

import jax
import jax.numpy as jnp
import numpy as np
from jax import lax
from jax.experimental import pallas as pl
from jax.experimental.pallas import tpu as pltpu
from jax.sharding import PartitionSpec as P

D = 1152
HEADS = 16
HD = 72
FF = 4608
PD = 16
FREQ = 256
CLASSES = 1001
GRID = 16
SEQ = 256
KEEP = 128


EPS_NORM = 1e-06
MAX_NORM = 0.01
RATE = 0.02
DECAY = 0.1
BETA_ONE = 0.9
BETA_TWO = 0.999
ADAM_EPS = 1e-08
MASKED_WEIGHT = 0.1
highest = lax.Precision.HIGHEST


def partner_2(value, axis, stride):
    mask = 2**stride
    pairs = [(source, source ^ mask) for source in range(lax.axis_size(axis))]
    return lax.ppermute(value, axis, pairs)


def product(left, right):
    return jnp.dot(left, right, preferred_element_type=jnp.float32)


def normalize(values):
    center = values - jnp.mean(values, axis=-1, keepdims=True)
    spread = lax.rsqrt(jnp.mean(center * center, axis=-1, keepdims=True) + EPS_NORM)
    return (center * spread, spread)


def normalize_back(grad_normed, normed, spread):
    adjusted = grad_normed - jnp.mean(grad_normed, axis=-1, keepdims=True)
    adjusted = adjusted - normed * jnp.mean(grad_normed * normed, axis=-1, keepdims=True)
    return spread * adjusted


def position_table(columns):
    quarter = columns // 4
    omegas = 1.0 / 10000.0 ** (jnp.arange(quarter, dtype=jnp.float32) / quarter)
    places = jnp.arange(GRID * GRID, dtype=jnp.int32)

    def half_table(coords):
        angles = coords.astype(jnp.float32)[:, None] * omegas[None, :]
        return jnp.concatenate([jnp.sin(angles), jnp.cos(angles)], axis=1)

    return jnp.concatenate([half_table(places % GRID), half_table(places // GRID)], axis=1)


def position_constant(columns):
    quarter = columns // 4
    omegas = np.float32(1.0) / np.float32(10000.0) ** (np.arange(quarter, dtype=np.float32) / np.float32(quarter))
    places = np.arange(GRID * GRID)

    def half_table(coords):
        angles = (coords.astype(np.float32)[:, None] * omegas[None, :]).astype(np.float64)
        return np.concatenate([np.sin(angles), np.cos(angles)], axis=1).astype(np.float32)

    return np.concatenate([half_table(places % GRID), half_table(places // GRID)], axis=1)


def time_features(stamp):
    halves = FREQ // 2
    frequency = jnp.exp(-math.log(10000.0) * jnp.arange(halves, dtype=jnp.float32) / halves)
    angles = stamp.astype(jnp.float32) * frequency
    return jnp.concatenate([jnp.cos(angles), jnp.sin(angles)])


def row_gather(values):
    return lax.all_gather(values, "mp", axis=0, tiled=True)


def row_sum(values):
    return lax.psum_scatter(values, "mp", scatter_dimension=0, tiled=True)


def route_bit(route, bit):
    return jnp.bitwise_and(jnp.right_shift(route, bit), 1) == 1


def route_ids(values, route, levels):
    for bit in range(levels):
        partner = partner_2(values, "dp", bit)
        values = jnp.where(route_bit(route, bit), partner, values)
    return values


def route_rows(values, route, levels):
    for bit in range(levels):
        partner = partner_2(values, "dp", bit)
        values = jnp.where(route_bit(route, bit), partner, values)
    return values


def route_back(values, route, levels):
    for bit in range(levels):
        partner = partner_2(values, "dp", bit)
        values = jnp.where(route_bit(route, bit), partner, values)
    return values


def unpack_big(flat, columns, groups):
    head_width = HEADS * HD // groups
    hidden_width = FF // groups
    shapes = [
        (columns, 3 * head_width),
        (head_width, columns),
        (columns, hidden_width),
        (hidden_width, columns),
    ]
    levels = []
    offset = 0
    for level_index in range(2):
        pieces = []
        for dims in shapes:
            length = dims[0] * dims[1]
            pieces.append(flat[offset : offset + length].reshape(dims))
            offset += length
        levels.append(tuple(pieces))
    return levels


def unpack_rest(flat, columns):
    matrix = flat.reshape(columns, -1).T
    counts = [PD, FREQ, columns, CLASSES, 1, PD]
    pieces = []
    offset = 0
    for count in counts:
        pieces.append(matrix[offset : offset + count])
        offset += count
    return (pieces[0], pieces[1], pieces[2], pieces[3], pieces[4][0], pieces[5].T)


def split_heads(packed, groups, rows):
    third = packed.shape[1] // 3
    return [
        packed[:, index * third : (index + 1) * third].reshape(groups, rows, third // HD, HD)
        for index in range(3)
    ]


def attention_probs(queries, key_rows):
    scores = jnp.einsum("gqhe,gkhe->ghqk", queries, key_rows, preferred_element_type=jnp.float32)
    return jax.nn.softmax(scores * HD ** (-0.5), axis=-1)


def block_forward(state, weights, modulate):
    qkv_weight, proj_weight, up_weight, down_weight = weights
    shift_one, scale_one, gate_one, shift_two, scale_two, gate_two = jnp.split(modulate, 6)
    rows = state.shape[0]
    normed_one, spread_one = normalize(state)
    full_one = row_gather((normed_one * (1.0 + scale_one) + shift_one).astype(jnp.bfloat16))
    groups = full_one.shape[0] // rows
    packed = product(full_one, qkv_weight).astype(jnp.bfloat16)
    queries, key_rows, value_rows = split_heads(packed, groups, rows)
    probs = attention_probs(queries, key_rows)
    mixed = jnp.einsum(
        "ghqk,gkhe->gqhe",
        probs.astype(jnp.bfloat16),
        value_rows,
        preferred_element_type=jnp.float32,
    )
    attended = mixed.astype(jnp.bfloat16).reshape(groups * rows, -1)
    branch_one = row_sum(product(attended, proj_weight))
    middle = state + gate_one * branch_one
    normed_two, spread_two = normalize(middle)
    full_two = row_gather((normed_two * (1.0 + scale_two) + shift_two).astype(jnp.bfloat16))
    hidden_pre = product(full_two, up_weight)
    activated = jax.nn.gelu(hidden_pre, approximate=True).astype(jnp.bfloat16)
    branch_two = row_sum(product(activated, down_weight))
    result = middle + gate_two * branch_two
    saved = (
        normed_one,
        spread_one,
        full_one,
        packed,
        attended,
        branch_one,
        normed_two,
        spread_two,
        full_two,
        hidden_pre,
        activated,
        branch_two,
    )
    return (result, saved)


def block_backward(grad_out, saved, weights, modulate):
    (
        normed_one,
        spread_one,
        full_one,
        packed,
        attended,
        branch_one,
        normed_two,
        spread_two,
        full_two,
        hidden_pre,
        activated,
        branch_two,
    ) = saved
    qkv_weight, proj_weight, up_weight, down_weight = weights
    shift_one, scale_one, gate_one, shift_two, scale_two, gate_two = jnp.split(modulate, 6)
    rows = grad_out.shape[0]
    groups = full_one.shape[0] // rows
    grad_gate_two = jnp.sum(grad_out * branch_two, axis=0)
    back_two = row_gather((gate_two * grad_out).astype(jnp.bfloat16))
    grad_down = product(activated.T, back_two)
    grad_act = product(back_two, down_weight.T)
    unused, gelu_back = jax.vjp(lambda pre: jax.nn.gelu(pre, approximate=True), hidden_pre)
    grad_pre = gelu_back(grad_act)[0].astype(jnp.bfloat16)
    grad_up = product(full_two.T, grad_pre)
    grad_hidden_two = row_sum(product(grad_pre, up_weight.T))
    grad_shift_two = jnp.sum(grad_hidden_two, axis=0)
    grad_scale_two = jnp.sum(grad_hidden_two * normed_two, axis=0)
    grad_middle = grad_out + normalize_back(
        grad_hidden_two * (1.0 + scale_two), normed_two, spread_two
    )
    grad_gate_one = jnp.sum(grad_middle * branch_one, axis=0)
    back_one = row_gather((gate_one * grad_middle).astype(jnp.bfloat16))
    grad_proj = product(attended.T, back_one)
    grad_attended = product(back_one, proj_weight.T).astype(jnp.bfloat16)
    queries, key_rows, value_rows = split_heads(packed, groups, rows)
    probs = attention_probs(queries, key_rows)
    grad_mixed = grad_attended.reshape(queries.shape)
    grad_probs = jnp.einsum(
        "gqhe,gkhe->ghqk", grad_mixed, value_rows, preferred_element_type=jnp.float32
    )
    grad_values = jnp.einsum(
        "ghqk,gqhe->gkhe",
        probs.astype(jnp.bfloat16),
        grad_mixed,
        preferred_element_type=jnp.float32,
    )
    grad_scores = (
        probs * (grad_probs - jnp.sum(grad_probs * probs, axis=-1, keepdims=True)) * HD ** (-0.5)
    )
    grad_scores = grad_scores.astype(jnp.bfloat16)
    grad_queries = jnp.einsum(
        "ghqk,gkhe->gqhe", grad_scores, key_rows, preferred_element_type=jnp.float32
    )
    grad_keys = jnp.einsum(
        "ghqk,gqhe->gkhe", grad_scores, queries, preferred_element_type=jnp.float32
    )
    grad_packed = jnp.concatenate(
        [
            grad_part.reshape(groups * rows, -1)
            for grad_part in (grad_queries, grad_keys, grad_values)
        ],
        axis=1,
    ).astype(jnp.bfloat16)
    grad_qkv = product(full_one.T, grad_packed)
    grad_hidden_one = row_sum(product(grad_packed, qkv_weight.T))
    grad_shift_one = jnp.sum(grad_hidden_one, axis=0)
    grad_scale_one = jnp.sum(grad_hidden_one * normed_one, axis=0)
    grad_state = grad_middle + normalize_back(
        grad_hidden_one * (1.0 + scale_one), normed_one, spread_one
    )
    grad_mod = jnp.concatenate(
        [
            grad_shift_one,
            grad_scale_one,
            grad_gate_one,
            grad_shift_two,
            grad_scale_two,
            grad_gate_two,
        ]
    )
    return (grad_state, grad_mod, (grad_qkv, grad_proj, grad_up, grad_down))


def condition(stamp, tag, time_one, time_two, table):
    features = time_features(stamp).astype(jnp.bfloat16)[None, :]
    pre_time = product(features, time_one)
    hidden_time = jax.nn.silu(pre_time).astype(jnp.bfloat16)
    cond_value = product(hidden_time, time_two)[0] + table[tag].astype(jnp.float32)
    signal = jax.nn.silu(cond_value).astype(jnp.bfloat16)
    return (signal, (features, pre_time, hidden_time, cond_value))


def condition_back(grad_signal, saved, time_two, tag, table_rows):
    features, pre_time, hidden_time, cond_value = saved
    unused, silu_back = jax.vjp(jax.nn.silu, cond_value)
    grad_cond = silu_back(grad_signal)[0]
    grad_time_two = hidden_time.astype(jnp.float32).T * grad_cond[None, :]
    grad_hidden = jnp.dot(time_two.astype(jnp.float32), grad_cond, precision=highest)
    unused_pre, pre_back = jax.vjp(jax.nn.silu, pre_time)
    grad_pre = pre_back(grad_hidden[None, :])[0]
    grad_time_one = features.astype(jnp.float32).T * grad_pre
    grad_table = (jnp.arange(table_rows, dtype=jnp.int32)[:, None] == tag) * grad_cond[None, :]
    return (grad_time_one, grad_time_two, grad_table)


def adam_update(grad, master, first, second, clip, count):
    scaled = grad * clip
    first = BETA_ONE * first + (1.0 - BETA_ONE) * scaled
    second = BETA_TWO * second + (1.0 - BETA_TWO) * scaled * scaled
    fix_one = 1.0 - BETA_ONE**count
    fix_two = 1.0 - BETA_TWO**count
    master = master - RATE * (
        first / fix_one / (jnp.sqrt(second / fix_two) + ADAM_EPS) + DECAY * master
    )
    return (master, first, second, master.astype(jnp.bfloat16))


def local_general(
    big_copy,
    big_master,
    big_first,
    big_second,
    ada_copy,
    ada_master,
    ada_first,
    ada_second,
    rest_copy,
    rest_master,
    rest_first,
    rest_second,
    owner_tiles,
    kept_patches,
    kept_pos,
    timestep,
    label,
    owner,
    target,
    step,
):
    groups = lax.axis_size("mp")
    ranks = lax.axis_size("dp")
    levels_dp = ranks.bit_length() - 1
    my_rank = lax.axis_index("dp")
    tiles = owner_tiles.shape[0]
    columns = D
    gathered = lax.all_gather(big_copy, "dp", axis=1, tiled=True)[0]
    inverse = jnp.zeros((tiles,), jnp.int32).at[owner_tiles].set(jnp.arange(tiles, dtype=jnp.int32))
    big_flat = jnp.take(gathered, inverse, axis=0).reshape(-1)
    ada_flat, rest_flat = (
        lax.all_gather(ada_copy, ("dp", "mp"), axis=0, tiled=True),
        lax.all_gather(rest_copy, ("dp", "mp"), axis=0, tiled=True),
    )
    levels = unpack_big(big_flat, columns, groups)
    ada_matrix = ada_flat.reshape(columns, 14 * columns)
    embed_weight, time_one, time_two, table, mask_token, head_weight = unpack_rest(
        rest_flat, columns
    )
    positions = position_table(columns)
    images = ranks * groups
    inv_count = 1.0 / (PD * kept_patches.shape[0] * images * KEEP)
    zeros_six = jnp.zeros((6 * columns,), jnp.bfloat16)
    zeros_eight = jnp.zeros((8 * columns,), jnp.bfloat16)

    def micro_step(carry, inputs):
        grads_big, grads_rest, loss_sum = carry
        patches, place, stamp, tag, dest, goal = inputs
        route = jnp.bitwise_xor(dest, my_rank)
        signal_enc, saved_enc = condition(stamp, tag, time_one, time_two, table)
        mod_enc = product(signal_enc[None, :], ada_matrix[:, : 6 * columns])[0]
        embedded = product(patches.astype(jnp.bfloat16), embed_weight) + jnp.take(
            positions, place, axis=0
        )
        enc_out, enc_saved = block_forward(embedded, levels[0], mod_enc)
        sent = enc_out.astype(jnp.bfloat16)
        meta = jnp.concatenate([place, stamp[None], tag[None]])
        got_meta = route_ids(meta, route, levels_dp)
        arrived = route_rows(sent, route, levels_dp)
        keep_rows = place.shape[0]
        dec_place = got_meta[:keep_rows]
        dec_tag = got_meta[keep_rows + 1]
        signal_dec, saved_dec = condition(got_meta[keep_rows], dec_tag, time_one, time_two, table)
        mod_dec = product(signal_dec[None, :], ada_matrix[:, 6 * columns :])[0]
        hits = jnp.arange(SEQ, dtype=jnp.int32)[:, None] == dec_place[None, :]
        kept = jnp.sum(hits.astype(jnp.float32), axis=1, keepdims=True)
        dec_in = (
            product(hits.astype(jnp.bfloat16), arrived)
            + (1.0 - kept) * mask_token.astype(jnp.float32)[None, :]
            + positions
        )
        dec_out, dec_saved = block_forward(dec_in, levels[1], mod_dec[: 6 * columns])
        final_shift = mod_dec[6 * columns : 7 * columns]
        final_scale = mod_dec[7 * columns :]
        normed_final, spread_final = normalize(dec_out)
        head_in = (normed_final * (1.0 + final_scale) + final_shift).astype(jnp.bfloat16)
        output = product(head_in, head_weight)
        error = output - goal
        weight = kept + MASKED_WEIGHT * (1.0 - kept)
        loss_part = jnp.sum(weight * error * error) * inv_count
        grad_output = (2.0 * inv_count * weight * error).astype(jnp.bfloat16)
        grad_head = product(head_in.T, grad_output)
        grad_head_in = product(grad_output, head_weight.T)
        grad_final = jnp.concatenate(
            [jnp.sum(grad_head_in, axis=0), jnp.sum(grad_head_in * normed_final, axis=0)]
        )
        grad_dec_out = normalize_back(
            grad_head_in * (1.0 + final_scale), normed_final, spread_final
        )
        grad_dec_in, grad_mod_dec, dec_grads = block_backward(
            grad_dec_out, dec_saved, levels[1], mod_dec[: 6 * columns]
        )
        grad_mask = jnp.sum((1.0 - kept) * grad_dec_in, axis=0)
        grad_arrived = jnp.take(grad_dec_in, dec_place, axis=0).astype(jnp.bfloat16)
        grad_sent = route_back(grad_arrived, route, levels_dp)
        grad_embedded, grad_mod_enc, enc_grads = block_backward(
            grad_sent.astype(jnp.float32), enc_saved, levels[0], mod_enc
        )
        grad_embed = jnp.dot(
            patches.astype(jnp.bfloat16).astype(jnp.float32).T, grad_embedded, precision=highest
        )
        vector_enc = grad_mod_enc.astype(jnp.bfloat16)
        vector_dec = jnp.concatenate([grad_mod_dec, grad_final]).astype(jnp.bfloat16)
        grad_signal_enc = product(ada_matrix[:, : 6 * columns], vector_enc)
        grad_signal_dec = product(ada_matrix[:, 6 * columns :], vector_dec)
        time_enc = condition_back(grad_signal_enc, saved_enc, time_two, tag, table.shape[0])
        time_dec = condition_back(grad_signal_dec, saved_dec, time_two, dec_tag, table.shape[0])
        rest_terms = [
            grad_embed,
            time_enc[0] + time_dec[0],
            time_enc[1] + time_dec[1],
            time_enc[2] + time_dec[2],
            grad_mask[None, :],
            grad_head.T,
        ]
        grads_rest = grads_rest + jnp.concatenate(rest_terms, axis=0)
        big_terms = [
            term.reshape(-1) for level_grads in (enc_grads, dec_grads) for term in level_grads
        ]
        grads_big = grads_big + jnp.concatenate(big_terms)
        signal_pair = jnp.stack([signal_enc, signal_dec])
        vector_pair = jnp.stack(
            [jnp.concatenate([vector_enc, zeros_eight]), jnp.concatenate([zeros_six, vector_dec])]
        )
        return ((grads_big, grads_rest, loss_sum + loss_part), (signal_pair, vector_pair))

    inputs = (
        kept_patches[:, 0],
        kept_pos[:, 0],
        timestep[:, 0],
        label[:, 0],
        owner[:, 0],
        target[:, 0],
    )
    start_carry = (
        jnp.zeros(big_flat.shape, jnp.float32),
        jnp.zeros((rest_flat.shape[0] // columns, columns), jnp.float32),
        jnp.zeros((), jnp.float32),
    )
    finals, factors = lax.scan(micro_step, start_carry, inputs)
    grads_big, grads_matrix, loss_sum = finals
    grads_rest = grads_matrix.T.reshape(-1)
    signal_rows = factors[0].reshape(-1, columns)
    vector_rows = factors[1].reshape(-1, 14 * columns)
    tile_part = jnp.take(grads_big.reshape(tiles, 128), owner_tiles, axis=0)
    owned_big = lax.psum_scatter(tile_part, "dp", scatter_dimension=0, tiled=True)
    local_ada = product(signal_rows.T, vector_rows).reshape(-1)
    owned_ada, owned_rest = (
        lax.psum_scatter(local_ada, ("dp", "mp"), scatter_dimension=0, tiled=True),
        lax.psum_scatter(grads_rest, ("dp", "mp"), scatter_dimension=0, tiled=True),
    )
    squares = (
        jnp.sum(owned_big * owned_big)
        + jnp.sum(owned_ada * owned_ada)
        + jnp.sum(owned_rest * owned_rest)
    )
    loss_total, square_total = lax.psum((loss_sum, squares), ("dp", "mp"))
    grad_norm = jnp.sqrt(square_total)
    clip = jnp.minimum(1.0, MAX_NORM / (grad_norm + 1e-06))
    count = step[0].astype(jnp.float32)
    big_out = adam_update(
        owned_big.reshape(big_master.shape), big_master, big_first, big_second, clip, count
    )
    ada_out = adam_update(owned_ada, ada_master, ada_first, ada_second, clip, count)
    rest_out = adam_update(owned_rest, rest_master, rest_first, rest_second, clip, count)
    return (
        loss_total.reshape(1),
        grad_norm.reshape(1),
        big_out[0],
        big_out[1],
        big_out[2],
        big_out[3],
        ada_out[0],
        ada_out[1],
        ada_out[2],
        ada_out[3],
        rest_out[0],
        rest_out[1],
        rest_out[2],
        rest_out[3],
    )


CHUNK_ROWS = 1152
REST_ROWS = 2 * PD + FREQ + D + CLASSES + 1


def tile_place(tiles, ranks):
    counts = [count // ranks for count in matrix_tiles()]
    layer_tiles = sum(matrix_tiles())
    level = tiles // layer_tiles
    inside = tiles % layer_tiles
    dest = jnp.zeros_like(tiles)
    slot = jnp.zeros_like(tiles)
    start = 0
    base = 0
    for count, total in zip(counts, matrix_tiles()):
        local_tile = inside - start
        here = (local_tile >= 0) & (local_tile < total)
        dest = jnp.where(here, local_tile // count, dest)
        slot = jnp.where(here, base + level * count + local_tile % count, slot)
        start += total
        base += 2 * count
    return dest, slot


def matrix_tiles():
    groups = 4
    head_width = HEADS * HD // groups
    hidden_width = FF // groups
    sizes = [D * 3 * head_width, head_width * D, D * hidden_width, hidden_width * D]
    return [size // 128 for size in sizes]


def rank_within(dest, ranks):
    n = dest.shape[0]
    inner = 96
    outer = n // inner
    hot = (dest.reshape(outer, inner)[None] == jnp.arange(ranks)[:, None, None]).astype(jnp.bfloat16)
    upto = (jnp.arange(inner)[:, None] < jnp.arange(inner)[None, :]).astype(jnp.bfloat16)
    before = jnp.einsum("roi,ij->roj", hot, upto, preferred_element_type=jnp.float32)
    totals = jnp.sum(hot.astype(jnp.float32), axis=2)
    over = (jnp.arange(outer)[:, None] < jnp.arange(outer)[None, :]).astype(jnp.float32)
    prior = jnp.dot(totals, over, precision=highest)
    rank = jnp.sum(hot.astype(jnp.float32) * (before + prior[:, :, None]), axis=0)
    return rank.astype(jnp.int32).reshape(n), jnp.sum(totals, axis=1).astype(jnp.int32)


def widen(source, dest, rows):
    step = 128 if rows % 128 == 0 else 16
    whole = rows // step

    def body(i, unused):
        at = pl.ds(pl.multiple_of(i * step, step), step)
        dest[at, :] = source[at, :].astype(dest.dtype)
        return unused

    lax.fori_loop(0, whole, body, 0)


def pack_kernel(n, pos_ref, x_ref, buf_ref, wide, sorted_rows):
    widen(x_ref, wide, n)

    def move(i, unused):
        places = [pos_ref[i * 16 + j] for j in range(16)]
        rows = [wide[pl.ds(i * 16 + j, 1), :] for j in range(16)]
        for place, row in zip(places, rows):
            sorted_rows[pl.ds(place, 1), :] = row
        return unused

    lax.fori_loop(0, n // 16, move, 0)
    widen(sorted_rows, buf_ref, buf_ref.shape[0])


def scatter_kernel(total, tag_ref, buf_ref, out_ref, wide, slots):
    widen(buf_ref, wide, total)

    def move(i, unused):
        tags = [tag_ref[i * 16 + j] for j in range(16)]
        rows = [wide[pl.ds(i * 16 + j, 1), :] for j in range(16)]
        for tag, row in zip(tags, rows):
            slots[pl.ds(tag, 1), :] = row
        return unused

    lax.fori_loop(0, total // 16, move, 0)
    widen(slots, out_ref, out_ref.shape[0])


def gather_kernel(total, index_ref, x_ref, out_ref, wide_out):
    def move(i, unused):
        index = [index_ref[i * 16 + j] for j in range(16)]
        rows = [x_ref[pl.ds(place, 1), :] for place in index]
        for j in range(16):
            wide_out[pl.ds(i * 16 + j, 1), :] = rows[j]
        return unused

    lax.fori_loop(0, total // 16, move, 0)
    widen(wide_out, out_ref, total)


SMEM = pl.BlockSpec(memory_space=pltpu.SMEM)
VMEM = pl.BlockSpec(memory_space=pltpu.VMEM)
PARAMS = pltpu.CompilerParams(vmem_limit_bytes=48 * 1024 * 1024)


def pack_rows(rows, pos, total):
    n = rows.shape[0]
    return pl.pallas_call(
        functools.partial(pack_kernel, n),
        out_shape=jax.ShapeDtypeStruct((total, 128), jnp.bfloat16),
        in_specs=[SMEM, VMEM],
        out_specs=VMEM,
        scratch_shapes=[
            pltpu.VMEM((n, 128), jnp.float32),
            pltpu.VMEM((total + 16, 128), jnp.float32),
        ],
        compiler_params=PARAMS,
        name="pack_rows",
    )(pos, rows)


def pack_tags(pos, slot, fill, capacity):
    n = pos.shape[0]
    total = fill.shape[0] * capacity
    lines = total // 128
    here = (pos // 128)[:, None] == jnp.arange(lines)[None, :]
    high = jnp.where(here, (slot // 128)[:, None], 0)
    low = jnp.where(here, (slot % 128)[:, None], 0)
    lanes = ((pos % 128)[:, None] == jnp.arange(128)[None, :]).astype(jnp.bfloat16)
    parts = jnp.concatenate([high, low], axis=1).astype(jnp.bfloat16)
    found = contract(parts, lanes, 0, 0).astype(jnp.int32)
    tags = (found[:lines] * 128 + found[lines:]).reshape(fill.shape[0], capacity)
    return jnp.where(jnp.arange(capacity)[None, :] < fill[:, None], tags, n).reshape(-1)


def scatter_rows(rows, tags, n):
    total = rows.shape[0]
    return pl.pallas_call(
        functools.partial(scatter_kernel, total),
        out_shape=jax.ShapeDtypeStruct((n + 16, 128), jnp.bfloat16),
        in_specs=[SMEM, VMEM],
        out_specs=VMEM,
        scratch_shapes=[
            pltpu.VMEM((total, 128), jnp.float32),
            pltpu.VMEM((n + 16, 128), jnp.float32),
        ],
        compiler_params=PARAMS,
        name="scatter_rows",
    )(tags, rows)


def gather_rows(rows, index, dtype):
    total = index.shape[0]
    return pl.pallas_call(
        functools.partial(gather_kernel, total),
        out_shape=jax.ShapeDtypeStruct((total, 128), dtype),
        in_specs=[SMEM, VMEM],
        out_specs=VMEM,
        scratch_shapes=[pltpu.VMEM((total, 128), jnp.float32)],
        compiler_params=PARAMS,
        name="gather_rows",
    )(index, rows)


MESH = pl.DeviceIdType.MESH
LAG = 2
SLOTS = 4
GATHER_SLOTS = 12


def coordinates():
    rank = lax.axis_index("dp")
    group = lax.axis_index("mp")
    return lax.div(rank, 2), lax.rem(rank, 2), lax.div(group, 2), lax.rem(group, 2)


def device_at(z, x, y, core):
    return (z * 2 + x, y * 2 + core)


def neighbours():
    z, x, y, core = coordinates()
    along_x = device_at(z, 1 - x, y, core)
    along_y = device_at(z, x, 1 - y, core)
    first = tuple(jnp.where(core == 0, b, a) for a, b in zip(along_x, along_y))
    second = tuple(jnp.where(core == 0, a, b) for a, b in zip(along_x, along_y))
    others = [device_at(lax.rem(z + step, 4), x, y, core) for step in (1, 2, 3)]
    return device_at(z, x, y, 1 - core), first, second, others


def greet(peers):
    barrier = pltpu.get_barrier_semaphore()
    for peer in peers:
        pl.semaphore_signal(barrier, inc=1, device_id=peer, device_id_type=MESH)
    pl.semaphore_wait(barrier, len(peers))


def block_of(ref, entry, group, at, side=None):
    stacked, rows, width = entry
    sides = slice(None) if side is None else side
    if stacked:
        return ref.at[group, :, sides, at, :]
    return ref.at[:, sides, at, pl.ds(pl.multiple_of(group * width, 128), width)]


def slice_of(ref, entry, group, z, x, at):
    stacked, rows, width = entry
    if stacked:
        return ref.at[group, z, x, at, :]
    return ref.at[z, x, at, pl.ds(pl.multiple_of(group * width, 128), width)]


def chunk_ranges(plan, chunk):
    ranges = []
    start = 0
    for stacked, rows, width in plan:
        ranges.append((start, start + rows // chunk))
        start += rows // chunk
    return ranges, start


def in_range(unit, low, high):
    return (unit >= low) & (unit < high)


def remote(source, target, send, receive, peer):
    return pltpu.make_async_remote_copy(
        src_ref=source,
        dst_ref=target,
        send_sem=send,
        recv_sem=receive,
        device_id=peer,
        device_id_type=MESH,
    )


def gather_job(plan, chunk, lag, slices, wholes, scratch):
    count = len(plan)
    held, other_held, own_sem, out_sem, z_send, z_recv, a_send, a_recv, b_send, b_recv, c_send, c_recv = scratch
    z, x, y, core = coordinates()
    other, first, second, others = neighbours()
    mine_first = jnp.where(core == 0, y, x)
    mine_second = jnp.where(core == 0, x, y)
    ranges, total = chunk_ranges(plan, chunk)

    def copies(stage, k, unit):
        entry = plan[k]
        slot = lax.rem(unit, GATHER_SLOTS)
        at = pl.ds(pl.multiple_of((unit - ranges[k][0]) * chunk, chunk), chunk)
        cols = pl.ds(0, entry[2])
        own = held.at[slot, mine_first, mine_second, z, :, cols]
        if stage == 0:
            source = slices[k].at[at, :]
            return [pltpu.make_async_copy(source, own, own_sem.at[slot])] + [
                remote(source, own, z_send.at[i, slot], z_recv.at[i, slot], others[i])
                for i in range(3)
            ]
        if stage == 1:
            part = held.at[slot, mine_first, mine_second, :, :, cols]
            return [remote(part, part, a_send.at[slot], a_recv.at[slot], second)]
        if stage == 2:
            part = held.at[slot, mine_first, :, :, :, cols]
            return [remote(part, part, b_send.at[slot], b_recv.at[slot], first)]
        if stage == 3:
            source = held.at[slot, :, :, :, :, cols]
            target = other_held.at[slot, :, :, :, :, cols]
            return [remote(source, target, c_send.at[slot], c_recv.at[slot], other)]
        made = []
        from_other = stage == 5
        ref, owner = (other_held, 1 - core) if from_other else (held, core)
        for i in range(2):
            for j in range(2):
                side = jnp.where(owner == 0, j, i)
                group = 2 * jnp.where(owner == 0, i, j) + owner
                made.append(
                    pltpu.make_async_copy(
                        ref.at[slot, i, j, :, :, cols],
                        block_of(wholes[k], entry, group, at, side),
                        out_sem.at[int(from_other), 2 * i + j, slot],
                    )
                )
        return made

    def go(unit, waits, starts):
        for k in range(count):

            @pl.when(in_range(unit, *ranges[k]))
            def _(k=k):
                for stage in waits:
                    for copy in copies(stage, k, unit):
                        copy.wait()
                for stage in starts:
                    for copy in copies(stage, k, unit):
                        copy.start()

    def step(t):
        go(t - 1 - 4 * lag, (4, 5), ())
        go(t - 4 * lag, (3,), (5,))
        go(t - 3 * lag, (2,), (3, 4))
        go(t - 2 * lag, (1,), (2,))
        go(t - lag, (0,), (1,))
        go(t, (), (0,))

    return step, total + 1 + 4 * lag


def whole_shape(entry):
    stacked, rows, width = entry
    return (4, 4, 2, rows, width) if stacked else (4, 2, rows, 4 * width)


def gather_scratch(plan, chunk, kind):
    dma = pltpu.SemaphoreType.DMA
    held = pltpu.VMEM((GATHER_SLOTS, 2, 2, 4, chunk, max(entry[2] for entry in plan)), kind)
    each = dma((GATHER_SLOTS,))
    three = dma((3, GATHER_SLOTS))
    return [held, held, each, dma((2, 4, GATHER_SLOTS)), three, three] + [each] * 6


def sum_job(plan, chunk, lag, parts, outs, scratch):
    count = len(plan)
    own, from_core, from_first, from_second, from_z, half, quarter, eighth = scratch[:8]
    own_sem, core_send, core_recv, a_send, a_recv, b_send, b_recv, z_send, z_recv = scratch[8:]
    z, x, y, core = coordinates()
    other, first, second, others = neighbours()
    mine_first = jnp.where(core == 0, y, x)
    mine_second = jnp.where(core == 0, x, y)
    ranges, total = chunk_ranges(plan, chunk)

    def copies(stage, width, unit, k=None):
        slot = lax.rem(unit, SLOTS)
        pair = lax.rem(unit, 2)
        cols = pl.ds(0, width)
        if stage == 0:
            made = []
            for j in range(2):
                mine = own.at[pair, j, :, :, :, cols]
                theirs = from_core.at[pair, j, :, :, :, cols]
                if k is None:
                    made.append(pltpu.make_async_copy(mine, mine, own_sem.at[j, pair]))
                    made.append(remote(mine, theirs, core_send.at[j, pair], core_recv.at[j, pair], other))
                else:
                    at = pl.ds(pl.multiple_of((unit - ranges[k][0]) * chunk, chunk), chunk)
                    kept = block_of(parts[k], plan[k], 2 * j + core, at)
                    sent = block_of(parts[k], plan[k], 2 * j + 1 - core, at)
                    made.append(pltpu.make_async_copy(kept, mine, own_sem.at[j, pair]))
                    made.append(remote(sent, theirs, core_send.at[j, pair], core_recv.at[j, pair], other))
            return made
        if stage == 1:
            source = half.at[slot, 1 - mine_first, :, :, :, cols]
            target = from_first.at[slot, :, :, :, cols]
            return [remote(source, target, a_send.at[slot], a_recv.at[slot], first)]
        if stage == 2:
            source = quarter.at[slot, 1 - mine_second, :, :, cols]
            target = from_second.at[slot, :, :, cols]
            return [remote(source, target, b_send.at[slot], b_recv.at[slot], second)]
        made = []
        for i in range(3):
            source = eighth.at[slot, lax.rem(z + i + 1, 4), :, cols]
            target = from_z.at[slot, i, :, cols]
            made.append(remote(source, target, z_send.at[i, slot], z_recv.at[i, slot], others[i]))
        return made

    def wide(ref, index, cols):
        return ref[(*index, slice(None), cols)].astype(jnp.float32)

    def add(stage, width, unit):
        slot = lax.rem(unit, SLOTS)
        pair = lax.rem(unit, 2)
        cols = slice(0, width)
        if stage == 0:
            for i in range(2):
                for j in range(2):
                    lead = jnp.where(core == 0, i, j)
                    last = jnp.where(core == 0, j, i)
                    for k in range(4):
                        value = wide(own, (pair, i, k, j), cols) + wide(from_core, (pair, i, k, j), cols)
                        half[slot, lead, last, k, :, cols] = value.astype(half.dtype)
        elif stage == 1:
            for j in range(2):
                for k in range(4):
                    value = wide(half, (slot, mine_first, j, k), cols) + wide(
                        from_first, (slot, j, k), cols
                    )
                    quarter[slot, j, k, :, cols] = value.astype(quarter.dtype)
        else:
            for k in range(4):
                value = wide(quarter, (slot, mine_second, k), cols) + wide(
                    from_second, (slot, k), cols
                )
                eighth[slot, k, :, cols] = value.astype(eighth.dtype)

    widths = sorted({entry[2] for entry in plan})

    def go(unit, stage):
        for width in widths:
            inside = functools.reduce(
                jnp.logical_or,
                [in_range(unit, *ranges[k]) for k in range(count) if plan[k][2] == width],
            )

            @pl.when(inside)
            def _(width=width):
                for copy in copies(stage, width, unit):
                    copy.wait()
                add(stage, width, unit)
                for copy in copies(stage + 1, width, unit):
                    copy.start()

    def finish(unit):
        for k in range(count):

            @pl.when(in_range(unit, *ranges[k]))
            def _(k=k):
                width = plan[k][2]
                slot = lax.rem(unit, SLOTS)
                cols = slice(0, width)
                for copy in copies(3, width, unit):
                    copy.wait()
                at = pl.ds(pl.multiple_of((unit - ranges[k][0]) * chunk, chunk), chunk)
                value = wide(eighth, (slot, z), cols)
                for i in range(3):
                    value = value + wide(from_z, (slot, i), cols)
                outs[k][at, :] = value

    def begin(unit):
        for k in range(count):

            @pl.when(in_range(unit, *ranges[k]))
            def _(k=k):
                for copy in copies(0, plan[k][2], unit, k):
                    copy.start()

    def step(t):
        finish(t - 1 - 3 * lag)
        go(t - 1 - 2 * lag, 2)
        go(t - 1 - lag, 1)
        go(t - 1, 0)
        begin(t)

    return step, total + 1 + 3 * lag


def sum_scratch(plan, chunk, kind):
    dma = pltpu.SemaphoreType.DMA
    width = max(entry[2] for entry in plan)
    buffers = [
        (2, 2, 4, 2, chunk, width),
        (2, 2, 4, 2, chunk, width),
        (SLOTS, 2, 4, chunk, width),
        (SLOTS, 4, chunk, width),
        (SLOTS, 3, chunk, width),
        (SLOTS, 2, 2, 4, chunk, width),
        (SLOTS, 2, 4, chunk, width),
        (SLOTS, 4, chunk, width),
    ]
    return (
        [pltpu.VMEM(shape, kind) for shape in buffers]
        + [dma((2, 2))] * 3
        + [dma((SLOTS,))] * 4
        + [dma((3, SLOTS))] * 2
    )


def direct_job(kind, sources, targets, scratch):
    source, target = sources[0], targets[0]
    own_sem, send_sem, recv_sem = scratch
    ranks, groups = lax.axis_size("dp"), lax.axis_size("mp")
    rank, group = lax.axis_index("dp"), lax.axis_index("mp")
    me, count = (rank * groups + group, ranks * groups) if kind == "push" else (rank, ranks)

    def part(index):
        return source.at[index] if kind == "swap" else source

    own = pltpu.make_async_copy(part(me), target.at[me], own_sem)

    def copy(i):
        to = lax.rem(me + i, count)
        peer = (lax.div(to, groups), lax.rem(to, groups)) if kind == "push" else (to, group)
        return remote(part(to), target.at[me], send_sem.at[i], recv_sem.at[i], peer)

    def start(i, unused):
        copy(i).start()
        return unused

    def finish(i, unused):
        copy(i).wait()
        return unused

    def begin():
        own.start()
        lax.fori_loop(1, count, start, 0)

    def end():
        own.wait()
        lax.fori_loop(1, count, finish, 0)

    return begin, end


def travel_kernel(jobs, scratch_counts, *refs):
    refs = list(refs)

    def take(number):
        taken = refs[:number]
        del refs[:number]
        return taken

    sources = [take(len(job[1])) for job in jobs]
    targets = [take(len(job[1])) for job in jobs]
    scratch = [take(number) for number in scratch_counts]
    steps = []
    direct = []
    for (kind, plan, chunk, lag), source, target, mine in zip(jobs, sources, targets, scratch):
        if kind == "gather":
            steps.append(gather_job(plan, chunk, lag, source, target, mine))
        elif kind == "sum":
            steps.append(sum_job(plan, chunk, lag, source, target, mine))
        else:
            direct.append(direct_job(kind, source, target, mine))
    if direct:
        greet_all()
    else:
        other, first, second, others = neighbours()
        greet([other, first, second] + others)
    for begin, unused_end in direct:
        begin()

    def step(t, unused):
        for one, unused_count in steps:
            one(t)
        return unused

    if steps:
        lax.fori_loop(0, max(count for unused_step, count in steps), step, 0)
    for unused_begin, end in direct:
        end()


def greet_all():
    groups = lax.axis_size("mp")
    world = lax.axis_size("dp") * groups
    me = lax.axis_index("dp") * groups + lax.axis_index("mp")
    barrier = pltpu.get_barrier_semaphore()

    def hail(i, unused):
        to = lax.rem(me + i, world)
        peer = (lax.div(to, groups), lax.rem(to, groups))
        pl.semaphore_signal(barrier, inc=1, device_id=peer, device_id_type=MESH)
        return unused

    lax.fori_loop(1, world, hail, 0)
    pl.semaphore_wait(barrier, world - 1)


def travel(jobs, arrays, number, name):
    ANY = pl.BlockSpec(memory_space=pl.ANY)
    dma = pltpu.SemaphoreType.DMA
    ranks, groups = lax.axis_size("dp"), lax.axis_size("mp")
    scratch = []
    shapes = []
    specs = []
    for (kind, plan, chunk, unused_lag), mine in zip(jobs, arrays):
        dtype = mine[0].dtype
        if kind == "gather":
            scratch.append(gather_scratch(plan, chunk, dtype))
            shapes += [jax.ShapeDtypeStruct(whole_shape(entry), dtype) for entry in plan]
            specs += [ANY] * len(plan)
        elif kind == "sum":
            scratch.append(sum_scratch(plan, chunk, dtype))
            shapes += [jax.ShapeDtypeStruct(entry[1:], jnp.float32) for entry in plan]
            specs += [VMEM] * len(plan)
        else:
            count = ranks * groups if kind == "push" else ranks
            scratch.append([dma, dma((count,)), dma((count,))])
            shape = mine[0].shape if kind == "swap" else (count,) + mine[0].shape
            shapes.append(jax.ShapeDtypeStruct(shape, dtype))
            specs.append(ANY)
    flat = [array for mine in arrays for array in mine]
    outs = pl.pallas_call(
        functools.partial(travel_kernel, jobs, [len(mine) for mine in scratch]),
        out_shape=shapes,
        in_specs=[
            VMEM if job[0] == "gather" else ANY for job, mine in zip(jobs, arrays) for unused in mine
        ],
        out_specs=specs,
        scratch_shapes=[one for mine in scratch for one in mine],
        compiler_params=pltpu.CompilerParams(
            collective_id=number, has_side_effects=True, vmem_limit_bytes=48 * 1024 * 1024
        ),
        name=name,
    )(*flat)
    results = []
    for unused_kind, plan, unused_chunk, unused_lag in jobs:
        results.append(outs[: len(plan)])
        outs = outs[len(plan) :]
    return results


def push_kernel(world, x_ref, out_ref, send_sem, recv_sem):
    groups = lax.axis_size("mp")
    me = lax.axis_index("dp") * groups + lax.axis_index("mp")

    def peer(i):
        to = lax.rem(me + i, world)
        return (lax.div(to, groups), lax.rem(to, groups))

    barrier = pltpu.get_barrier_semaphore()

    def hail(i, unused):
        pl.semaphore_signal(barrier, inc=1, device_id=peer(i), device_id_type=MESH)
        return unused

    lax.fori_loop(1, world, hail, 0)
    out_ref[me] = x_ref[...]
    pl.semaphore_wait(barrier, world - 1)

    def copy(i):
        return remote(x_ref, out_ref.at[me], send_sem.at[i], recv_sem.at[i], peer(i))

    def start(i, unused):
        copy(i).start()
        return unused

    def finish(i, unused):
        copy(i).wait()
        return unused

    lax.fori_loop(1, world, start, 0)
    lax.fori_loop(1, world, finish, 0)


def push_all(value, world, number, name):
    dma = pltpu.SemaphoreType.DMA
    return pl.pallas_call(
        functools.partial(push_kernel, world),
        out_shape=jax.ShapeDtypeStruct((world,) + value.shape, value.dtype),
        in_specs=[VMEM],
        out_specs=VMEM,
        scratch_shapes=[dma((world,)), dma((world,))],
        compiler_params=pltpu.CompilerParams(collective_id=number, has_side_effects=True),
        name=name,
    )(value)


def swap_ranks(buf, ranks):
    rest = buf.shape[1:]
    split = buf.reshape((ranks, buf.shape[0] // ranks) + rest)
    return lax.all_to_all(split, "dp", 0, 0).reshape(buf.shape)


def round_positions(dest, rank, counts, capacity, turn):
    ranks = counts.shape[0]
    low = turn * capacity
    inside = (rank >= low) & (rank < low + capacity)
    pos = jnp.where(inside, dest * capacity + rank - low, ranks * capacity)
    fill = jnp.clip(counts - low, 0, capacity)
    return pos, fill, inside


def tiles_to_slots(rows, dest, slot, rank, counts, rounds, carry_first):
    n = rows.shape[0]
    ranks = counts.shape[0]
    total = ranks * CHUNK_ROWS

    def packed(turn):
        pos, fill, unused = round_positions(dest, rank, counts, CHUNK_ROWS, turn)
        return pack_rows(rows, pos, total), pack_tags(pos, slot, fill, CHUNK_ROWS)

    got, tags = carry_first(*packed(0))
    first = scatter_rows(got, tags, n)

    def more(carry):
        turn, slots = carry
        more_rows, more_tags = [swap_ranks(part, ranks) for part in packed(turn)]
        added = scatter_rows(more_rows, more_tags, n)
        fresh = jnp.zeros((n + 16,), jnp.bool_).at[more_tags].set(True)
        return turn + 1, jnp.where(fresh[:, None], added, slots)

    unused, slots = lax.while_loop(lambda carry: carry[0] < rounds, more, (1, first))
    return slots, tags


def slots_to_tiles(slots, first, dest, slot, rank, counts, rounds):
    ranks = counts.shape[0]
    total = ranks * CHUNK_ROWS

    def landed(got, turn):
        pos, unused, inside = round_positions(dest, rank, counts, CHUNK_ROWS, turn)
        return gather_rows(got, jnp.minimum(pos, total - 1), jnp.float32), inside

    def more(carry):
        turn, rows = carry
        pos, fill, unused = round_positions(dest, rank, counts, CHUNK_ROWS, turn)
        turn_tags = swap_ranks(pack_tags(pos, slot, fill, CHUNK_ROWS), ranks)
        got = swap_ranks(gather_rows(slots, turn_tags, jnp.bfloat16), ranks)
        added, inside = landed(got.astype(jnp.float32), turn)
        return turn + 1, jnp.where(inside[:, None], added, rows)

    start = (1, landed(first.astype(jnp.float32), 0)[0])
    unused, rows = lax.while_loop(lambda carry: carry[0] < rounds, more, start)
    return rows


QKV_WIDTH = 896
PROJ_ROWS = 48


def layer_plan(ranks):
    return (
        (False, D // ranks, QKV_WIDTH),
        (True, PROJ_ROWS, D),
        (False, D // ranks, FF // 4),
        (True, FF // 4 // ranks, D),
    )


def pad_to(values, axis, size):
    widths = [(0, 0)] * values.ndim
    widths[axis] = (0, size - values.shape[axis])
    return jnp.pad(values, widths)


def slice_places(ranks):
    widths = [3 * HEADS * HD // 4, D, FF // 4, D]
    places = []
    base = 0
    for total, width in zip(matrix_tiles(), widths):
        count = total // ranks
        places.append((count * 128 // width, width, (base, base + count)))
        base += 2 * count
    return places


def row_group(width):
    rows = 128 // math.gcd(width, 128)
    return rows, rows * width // 128


def lane_pieces(start, size, source_width):
    pieces = []
    done = 0
    while done < size:
        row, column = divmod(start + done, source_width)
        block, lane = divmod(column, 128)
        length = min(128 - lane, source_width - column, size - done)
        pieces.append((row, block, lane, done, length))
        done += length
    return pieces


def join_pieces(pieces, load, rows):
    lanes = lax.broadcasted_iota(jnp.int32, (rows, 128), 1)
    value = None
    for row, block, lane, here, length in pieces:
        part = load(row, block)
        if lane != here:
            part = pltpu.roll(part, (here - lane) % 128, 1)
        if value is None:
            inside = lanes < here + length
            value = part if here + length == 128 else jnp.where(inside, part, 0.0)
        else:
            value = jnp.where((lanes >= here) & (lanes < here + length), part, value)
    return value


def spread_kernel(ranks, low_ref, *refs):
    outs, wide, slots_ref = refs[:8], refs[8], refs[9]
    widen(low_ref, slots_ref, low_ref.shape[0])
    for index, (rows, width, bases) in enumerate(slice_places(ranks)):
        group, tiles = row_group(width)
        count = rows // group
        blocks = -(-width // 128)
        for level in range(2):
            out = outs[level * 4 + index]
            for row in range(group):
                for block in range(blocks):
                    start = row * width + block * 128
                    pieces = lane_pieces(start, min(128, width - block * 128), 128)

                    def load(tile, unused, base=bases[level]):
                        return slots_ref[pl.ds(base + tile, count, stride=tiles), :]

                    value = join_pieces(pieces, load, count)
                    at = pl.ds(row, count, stride=group) if group > 1 else pl.ds(0, count)
                    wide[block, at, :] = value
            padded = out.shape[0]
            for block in range(blocks):
                if padded > rows:
                    wide[block, rows:padded, :] = jnp.zeros((padded - rows, 128), jnp.float32)
                out[:, block * 128 : (block + 1) * 128] = wide[block, :padded, :].astype(out.dtype)


def collect_kernel(ranks, *refs):
    parts, slots_ref, square_ref, wide = refs[:8], refs[8], refs[9], refs[10]
    square_ref[...] = jnp.zeros_like(square_ref)
    end = slots_ref.shape[0]
    total = 0
    for index, (rows, width, bases) in enumerate(slice_places(ranks)):
        group, tiles = row_group(width)
        count = rows // group
        total += 2 * count * tiles
        for level in range(2):
            part = parts[level * 4 + index]
            for block in range(-(-width // 128)):
                wide[block, :rows, :] = part[:rows, block * 128 : (block + 1) * 128]
            for tile in range(tiles):
                pieces = lane_pieces(tile * 128, 128, width)

                def load(row, block):
                    at = pl.ds(row, count, stride=group) if group > 1 else pl.ds(0, count)
                    return wide[block, at, :]

                value = join_pieces(pieces, load, count)
                slots_ref[pl.ds(bases[level] + tile, count, stride=tiles), :] = value
                square_ref[:1, :] += jnp.sum(value * value, axis=0, keepdims=True)
    slots_ref[total:end, :] = jnp.zeros((end - total, 128), jnp.float32)


def spread_slots(slots, ranks):
    plan = layer_plan(ranks) * 2
    tall = max(entry[1] for entry in plan)
    broad = max(entry[2] for entry in plan)
    return pl.pallas_call(
        functools.partial(spread_kernel, ranks),
        out_shape=[jax.ShapeDtypeStruct(entry[1:], jnp.bfloat16) for entry in plan],
        in_specs=[VMEM],
        out_specs=[VMEM] * len(plan),
        scratch_shapes=[
            pltpu.VMEM((broad // 128, tall, 128), jnp.float32),
            pltpu.VMEM(slots.shape, jnp.float32),
        ],
        compiler_params=PARAMS,
        name="spread_slots",
    )(slots)


def collect_slots(parts, rows, ranks):
    tall = max(part.shape[0] for part in parts)
    broad = max(part.shape[1] for part in parts)
    return pl.pallas_call(
        functools.partial(collect_kernel, ranks),
        out_shape=(
            jax.ShapeDtypeStruct((rows, 128), jnp.float32),
            jax.ShapeDtypeStruct((8, 128), jnp.float32),
        ),
        in_specs=[VMEM] * len(parts),
        out_specs=(VMEM, VMEM),
        scratch_shapes=[pltpu.VMEM((broad // 128, tall, 128), jnp.float32)],
        compiler_params=PARAMS,
        name="collect_slots",
    )(*parts)


def whole_weights(wholes, ranks):
    qkv, proj, up, down = wholes
    return (qkv.reshape(D, -1), proj.reshape(-1, D), up.reshape(D, -1), down.reshape(-1, D))


def whole_parts(grads, ranks):
    qkv, proj, up, down = grads
    shapes = [whole_shape(entry) for entry in layer_plan(ranks)]
    return [part.reshape(shape) for part, shape in zip((qkv, proj, up, down), shapes)]


GROUP_HEADS = HEADS // 4
GROUP_WIDTH = HEADS * HD // 4


def dot_nt(left, right):
    return lax.dot_general(left, right, (((1,), (1,)), ((), ())), preferred_element_type=jnp.float32)


def dot_tn(left, right):
    return lax.dot_general(left, right, (((0,), (0,)), ((), ())), preferred_element_type=jnp.float32)


def head_parts(packed_ref, head):
    return [
        packed_ref[:, index * GROUP_WIDTH + head * HD : index * GROUP_WIDTH + (head + 1) * HD]
        for index in range(3)
    ]


def head_probs(queries, key_rows):
    scores = dot_nt(queries, key_rows) * HD ** (-0.5)
    powers = jnp.exp(scores - jnp.max(scores, axis=-1, keepdims=True))
    return powers / jnp.sum(powers, axis=-1, keepdims=True)


def pad_columns(values, own):
    rows = values.shape[0]
    gap = jnp.zeros((rows, PROJ_ROWS - own), values.dtype)
    parts = []
    for start in range(0, values.shape[1], own):
        parts += [values[:, start : start + own], gap]
    return jnp.concatenate(parts, axis=1)


def attend_kernel(own, packed_ref, out_ref):
    heads = [head_parts(packed_ref, head) for head in range(GROUP_HEADS)]
    probs = [head_probs(queries, key_rows) for queries, key_rows, unused in heads]
    mixed = [
        product(prob.astype(jnp.bfloat16), parts[2]).astype(out_ref.dtype)
        for prob, parts in zip(probs, heads)
    ]
    out_ref[...] = pad_columns(jnp.concatenate(mixed, axis=1), own)


def attend_back_kernel(packed_ref, grad_ref, spread_ref, out_ref):
    heads = [head_parts(packed_ref, head) for head in range(GROUP_HEADS)]
    every = range(GROUP_HEADS)
    grads = grad_ref[...]
    grad_mixed = [dot_nt(grads, spread_ref[head]).astype(jnp.bfloat16) for head in every]
    probs = [head_probs(queries, key_rows) for queries, key_rows, unused in heads]
    grad_probs = [dot_nt(grad_mixed[head], heads[head][2]) for head in every]
    grad_values = [dot_tn(probs[head].astype(jnp.bfloat16), grad_mixed[head]) for head in every]
    grad_scores = []
    for prob, grad_prob in zip(probs, grad_probs):
        score = prob * (grad_prob - jnp.sum(grad_prob * prob, axis=-1, keepdims=True))
        grad_scores.append((score * HD ** (-0.5)).astype(jnp.bfloat16))
    grad_queries = [product(grad_scores[head], heads[head][1]) for head in every]
    grad_keys = [dot_tn(grad_scores[head], heads[head][0]) for head in every]
    for index, parts in enumerate((grad_queries, grad_keys, grad_values)):
        for head, part in enumerate(parts):
            start = index * GROUP_WIDTH + head * HD
            out_ref[:, start : start + HD] = part.astype(out_ref.dtype)
    rows, width = out_ref.shape
    out_ref[:, 3 * GROUP_WIDTH :] = jnp.zeros((rows, width - 3 * GROUP_WIDTH), out_ref.dtype)


def spread_heads(own):
    columns = jnp.arange(GROUP_WIDTH // own * PROJ_ROWS)
    source = columns // PROJ_ROWS * own + columns % PROJ_ROWS
    source = jnp.where(columns % PROJ_ROWS < own, source, -1)
    hot = jnp.arange(GROUP_WIDTH)[:, None] == source[None, :]
    return hot.astype(jnp.bfloat16).reshape(GROUP_HEADS, HD, -1)


def attend_call(kernel, images, inputs, constants, out_width, name):
    rows = inputs[0].shape[0] // images

    def block(width):
        return pl.BlockSpec((rows, width), lambda image, group: (image, group))

    return pl.pallas_call(
        kernel,
        grid=(images, 4),
        out_shape=jax.ShapeDtypeStruct((images * rows, 4 * out_width), jnp.bfloat16),
        in_specs=[block(one.shape[1] // 4) for one in inputs]
        + [pl.BlockSpec(one.shape, lambda image, group: (0, 0, 0)) for one in constants],
        out_specs=block(out_width),
        compiler_params=PARAMS,
        name=name,
    )(*inputs, *constants)


def attend(packed, own, images):
    kernel = functools.partial(attend_kernel, own)
    return attend_call(kernel, images, [packed], [], GROUP_WIDTH // own * PROJ_ROWS, "attend")


def attend_back(packed, grads, own, images):
    constants = [spread_heads(own)]
    return attend_call(
        attend_back_kernel, images, [packed, grads], constants, QKV_WIDTH, "attend_back"
    )


def gelu_and_slope(values):
    factor = math.sqrt(2.0 / math.pi)
    square = values * values
    bend = jnp.tanh(factor * values * (1.0 + 0.044715 * square))
    half = 0.5 * (1.0 + bend)
    slope = half + 0.5 * values * (1.0 - bend * bend) * factor * (1.0 + 3.0 * 0.044715 * square)
    return values * half, slope


def own_forward(state, weights, modulate, own):
    qkv_weight, proj_weight, up_weight, down_weight = weights
    images, rows, columns = state.shape
    shift_one, scale_one, gate_one, shift_two, scale_two, gate_two = [
        modulate[index] for index in range(6)
    ]
    normed_one, spread_one = normalize(state)
    full_one = (normed_one * (1.0 + scale_one) + shift_one).astype(jnp.bfloat16)
    flat_one = full_one.reshape(-1, columns)
    packed = product(flat_one, qkv_weight).astype(jnp.bfloat16)
    attended = attend(packed, own, images)
    branch_one = product(attended, proj_weight).reshape(state.shape)
    middle = state + gate_one * branch_one
    normed_two, spread_two = normalize(middle)
    full_two = (normed_two * (1.0 + scale_two) + shift_two).astype(jnp.bfloat16)
    flat_two = full_two.reshape(-1, columns)
    activated, slope = gelu_and_slope(product(flat_two, up_weight))
    activated = activated.astype(jnp.bfloat16)
    branch_two = product(activated, down_weight).reshape(state.shape)
    result = middle + gate_two * branch_two
    saved = (
        normed_one,
        spread_one,
        flat_one,
        packed,
        attended,
        branch_one,
        normed_two,
        spread_two,
        flat_two,
        slope,
        activated,
        branch_two,
    )
    return (result, saved)


def own_backward(grad_out, saved, weights, modulate, own):
    (
        normed_one,
        spread_one,
        flat_one,
        packed,
        attended,
        branch_one,
        normed_two,
        spread_two,
        flat_two,
        slope,
        activated,
        branch_two,
    ) = saved
    qkv_weight, proj_weight, up_weight, down_weight = weights
    images, rows, columns = grad_out.shape
    shift_one, scale_one, gate_one, shift_two, scale_two, gate_two = [
        modulate[index] for index in range(6)
    ]
    grad_gate_two = jnp.sum(grad_out * branch_two, axis=1)
    back_two = (gate_two * grad_out).astype(jnp.bfloat16).reshape(-1, columns)
    grad_down = product(activated.T, back_two).astype(jnp.bfloat16)
    grad_pre = (product(back_two, down_weight.T) * slope).astype(jnp.bfloat16)
    grad_up = product(flat_two.T, grad_pre).astype(jnp.bfloat16)
    grad_hidden_two = product(grad_pre, up_weight.T)
    grad_hidden_two = grad_hidden_two.reshape(grad_out.shape)
    grad_shift_two = jnp.sum(grad_hidden_two, axis=1)
    grad_scale_two = jnp.sum(grad_hidden_two * normed_two, axis=1)
    grad_middle = grad_out + normalize_back(
        grad_hidden_two * (1.0 + scale_two), normed_two, spread_two
    )
    grad_gate_one = jnp.sum(grad_middle * branch_one, axis=1)
    back_one = (gate_one * grad_middle).astype(jnp.bfloat16).reshape(-1, columns)
    grad_proj = product(attended.T, back_one).astype(jnp.bfloat16)
    grad_attended = product(back_one, proj_weight.T).astype(jnp.bfloat16)
    grad_packed = attend_back(packed, grad_attended, own, images)
    grad_qkv = product(flat_one.T, grad_packed).astype(jnp.bfloat16)
    grad_hidden_one = product(grad_packed, qkv_weight.T)
    grad_hidden_one = grad_hidden_one.reshape(grad_out.shape)
    grad_shift_one = jnp.sum(grad_hidden_one, axis=1)
    grad_scale_one = jnp.sum(grad_hidden_one * normed_one, axis=1)
    grad_state = grad_middle + normalize_back(
        grad_hidden_one * (1.0 + scale_one), normed_one, spread_one
    )
    grad_mod = jnp.concatenate(
        [
            grad_shift_one,
            grad_scale_one,
            grad_gate_one,
            grad_shift_two,
            grad_scale_two,
            grad_gate_two,
        ],
        axis=1,
    )
    return (grad_state, grad_mod, (grad_qkv, grad_proj, grad_up, grad_down))


def contract(left, right, left_axis, right_axis):
    return lax.dot_general(
        left,
        right,
        (((left_axis,), (right_axis,)), ((), ())),
        preferred_element_type=jnp.float32,
    )


def contract_wide(left, right, left_axis, right_axis):
    return lax.dot_general(
        left.astype(jnp.float32),
        right.astype(jnp.float32),
        (((left_axis,), (right_axis,)), ((), ())),
        precision=highest,
        preferred_element_type=jnp.float32,
    )


def silu_back(values, grads):
    unused, pull = jax.vjp(jax.nn.silu, values)
    return pull(grads)[0]


def local(
    big_copy,
    big_master,
    big_first,
    big_second,
    ada_copy,
    ada_master,
    ada_first,
    ada_second,
    rest_copy,
    rest_master,
    rest_first,
    rest_second,
    owner_tiles,
    kept_patches,
    kept_pos,
    timestep,
    label,
    owner,
    target,
    step,
):
    groups = lax.axis_size("mp")
    ranks = lax.axis_size("dp")
    world = groups * ranks
    my_rank = lax.axis_index("dp")
    micro = kept_patches.shape[0]
    own_columns = D // world
    columns = D

    owned = big_copy.shape[1]
    all_dest, unused_slot = tile_place(owner_tiles, ranks)
    all_hot = all_dest.reshape(ranks, owned, 1) == jnp.arange(ranks)
    rounds = (jnp.max(jnp.sum(all_hot.astype(jnp.int32), axis=1)) + CHUNK_ROWS - 1) // CHUNK_ROWS
    own_tiles = lax.dynamic_slice(owner_tiles, (my_rank * owned,), (owned,))
    dest, slot = tile_place(own_tiles, ranks)
    rank, counts = rank_within(dest, ranks)
    rest_own = rest_copy.reshape(own_columns, REST_ROWS)
    edges = [0, PD, PD + FREQ, PD + FREQ + D, PD + FREQ + D + CLASSES, REST_ROWS]
    win_t, one_t, two_t, table_t, tail_t = [
        rest_own[:, edges[i] : edges[i + 1]] for i in range(5)
    ]
    ends_size = own_columns * (2 * PD + 1)
    one_size = own_columns * FREQ
    whole_numbers = jnp.concatenate([timestep[:, 0], label[:, 0]])
    told = jnp.concatenate(
        [
            jnp.concatenate([win_t, tail_t], axis=1).reshape(-1),
            one_t.reshape(-1),
            (whole_numbers // 32).astype(jnp.bfloat16),
            (whole_numbers % 32).astype(jnp.bfloat16),
        ]
    )
    told = pad_to(told, 0, -(-told.shape[0] // 2048) * 2048).reshape(-1, 128)
    brought = []

    def carry_first(buf, new_tags):
        arrays = [
            [told],
            [target.reshape(-1, 128)],
            [new_tags.reshape(ranks, -1, 128)],
            [buf.reshape(ranks, -1, 128)],
        ]
        kinds = ("push", "share", "swap", "swap")
        got = travel([(kind, (None,), 0, 0) for kind in kinds], arrays, 6, "exchange_inputs")
        brought.extend(got)
        return got[3][0].reshape(buf.shape), got[2][0].reshape(new_tags.shape)

    slots, tags = tiles_to_slots(big_copy[0], dest, slot, rank, counts, rounds, carry_first)
    told = brought[0][0].reshape(world, -1)
    goals = brought[1][0].reshape(ranks, micro, -1, 128)
    facts = told[:, ends_size + one_size :][:, : 4 * micro].astype(jnp.int32)
    facts = facts[:, : 2 * micro] * 32 + facts[:, 2 * micro :]
    facts = facts.reshape(ranks, groups, 2 * micro).transpose(1, 0, 2).reshape(world, -1)
    stamps = facts[:, :micro].reshape(-1)
    tags_all = facts[:, micro:].reshape(-1)
    ends = told[:, :ends_size].reshape(columns, -1)
    embed_weight = ends[:, :PD].T
    mask_token = ends[:, PD].astype(jnp.float32)
    head_weight = ends[:, PD + 1 :]
    count_all = micro * world
    features = jax.vmap(time_features)(stamps).astype(jnp.bfloat16)
    pre_time = contract(features, one_t, 1, 1)
    one_whole = told[:, ends_size : ends_size + one_size].reshape(columns, FREQ)
    hidden_all = jax.nn.silu(contract(features, one_whole, 1, 1)).astype(jnp.bfloat16)
    picks = (tags_all[:, None] == jnp.arange(CLASSES, dtype=jnp.int32)[None, :]).astype(
        jnp.bfloat16
    )
    cond_own = contract(hidden_all, two_t, 1, 1) + contract(picks, table_t, 1, 1)
    signal_own = jax.nn.silu(cond_own).astype(jnp.bfloat16)
    ada_own = ada_copy.reshape(own_columns, 14 * columns)
    mod_rows = micro * 14
    mod_entry = (True, 32, columns)
    mods = product(signal_own, ada_own).reshape(world, mod_rows, columns)
    mods = pad_to(mods, 1, mod_entry[1]).reshape(whole_shape(mod_entry))
    plan = (layer_plan(ranks) * 2)[:-1]
    spread = spread_slots(slots, ranks)
    wholes, mods = travel(
        (("gather", plan, 16, LAG), ("sum", (mod_entry,), 16, 6)),
        [spread[:-1], [mods]],
        1,
        "gather_weights",
    )
    last, wholes = lax.optimization_barrier((spread[-1], wholes))
    last = lax.all_gather(last, ("mp", "dp"), axis=0, tiled=True)
    weights = [whole_weights(wholes[:4], ranks), whole_weights((*wholes[4:], last), ranks)]
    own = GROUP_WIDTH // ranks
    mods = mods[0][:mod_rows].reshape(micro, 14, columns).transpose(1, 0, 2)[:, :, None, :]
    mod_enc = mods[:6]
    mod_dec = mods[6:12]
    final_shift = mods[12]
    final_scale = mods[13]

    goal = jnp.stack([goals[owner[b, 0], b] for b in range(micro)]).reshape(micro, SEQ, PD)
    positions = jnp.asarray(position_constant(columns))
    images = ranks * groups
    inv_count = 1.0 / (PD * micro * images * KEEP)
    place = kept_pos[:, 0]
    patches = kept_patches[:, 0].astype(jnp.bfloat16)
    hits = (
        jnp.arange(SEQ, dtype=jnp.int32)[None, :, None] == place[:, None, :]
    ).astype(jnp.float32)
    hits_low = hits.astype(jnp.bfloat16)
    kept = jnp.sum(hits, axis=2)[:, :, None]
    embedded = product(patches.reshape(-1, PD), embed_weight).reshape(micro, KEEP, columns)
    embedded = embedded + jnp.take(positions, place, axis=0)
    enc_out, enc_saved = own_forward(embedded, weights[0], mod_enc, own)
    sent = enc_out.astype(jnp.bfloat16)
    dec_in = (
        jnp.einsum("bpr,brd->bpd", hits_low, sent, preferred_element_type=jnp.float32)
        + (1.0 - kept) * mask_token[None, None, :]
        + positions[None]
    )
    dec_out, dec_saved = own_forward(dec_in, weights[1], mod_dec, own)
    normed_final, spread_final = normalize(dec_out)
    head_in = (normed_final * (1.0 + final_scale) + final_shift).astype(jnp.bfloat16)
    flat_head = head_in.reshape(-1, columns)
    output = product(flat_head, head_weight).reshape(micro, SEQ, PD)
    error = output - goal
    weight = kept + MASKED_WEIGHT * (1.0 - kept)
    loss_sum = jnp.sum(weight * error * error) * inv_count

    grad_output = (2.0 * inv_count * weight * error).astype(jnp.bfloat16).reshape(-1, PD)
    grad_head = contract(grad_output, flat_head, 0, 0)
    grad_head_in = product(grad_output, head_weight.T).reshape(dec_out.shape)
    grad_final = jnp.concatenate(
        [jnp.sum(grad_head_in, axis=1), jnp.sum(grad_head_in * normed_final, axis=1)], axis=1
    )
    grad_dec_out = normalize_back(grad_head_in * (1.0 + final_scale), normed_final, spread_final)
    grad_dec_in, grad_mod_dec, dec_grads = own_backward(
        grad_dec_out, dec_saved, weights[1], mod_dec, own
    )
    last_sum = lax.psum_scatter(dec_grads[3], ("mp", "dp"), scatter_dimension=0, tiled=True)
    grad_mask = jnp.sum((1.0 - kept) * grad_dec_in, axis=(0, 1))[None, :]
    grad_sent = jnp.einsum(
        "bpr,bpd->brd",
        hits_low,
        grad_dec_in.astype(jnp.bfloat16),
        preferred_element_type=jnp.float32,
    )
    grad_embedded, grad_mod_enc, enc_grads = own_backward(
        grad_sent, enc_saved, weights[0], mod_enc, own
    )
    grad_embed = contract_wide(
        patches.reshape(-1, PD), grad_embedded.reshape(-1, columns), 0, 0
    )

    vectors = jnp.concatenate([grad_mod_enc, grad_mod_dec, grad_final], axis=1)
    vectors = vectors.astype(jnp.bfloat16).reshape(mod_rows, columns)
    vectors = pad_to(vectors, 0, mod_entry[1])
    sums, vectors = travel(
        (("sum", plan, 16, LAG), ("gather", (mod_entry,), 16, 6)),
        [whole_parts(enc_grads, ranks) + whole_parts(dec_grads, ranks)[:-1], [vectors]],
        2,
        "sum_gradients",
    )
    sums = list(sums) + [last_sum.astype(jnp.float32)]
    sums, big_squares = collect_slots(sums, owned + 16, ranks)
    vectors = vectors[0]
    back = gather_rows(sums, tags, jnp.bfloat16)
    vectors = vectors.reshape(world, mod_entry[1], columns)[:, :mod_rows].reshape(count_all, -1)
    owned_ada = contract(signal_own, vectors, 0, 0).reshape(-1)
    grad_signal = contract(vectors, ada_own, 1, 1)
    grad_cond = silu_back(cond_own, grad_signal)
    grad_two_t = contract_wide(grad_cond, hidden_all, 0, 0)
    grad_table_t = contract_wide(grad_cond, picks, 0, 0)
    shared = jnp.concatenate(
        [contract_wide(grad_cond, two_t, 1, 0), grad_embed, grad_mask, grad_head], axis=0
    )
    shared_rows = shared.shape[0]
    shared = shared.reshape(shared_rows, ranks, groups, own_columns).transpose(2, 1, 0, 3)
    shared = pad_to(shared.reshape(world, -1), 1, 4096)
    shared_entry = (True, 32, 128)
    shared, back = travel(
        (("sum", (shared_entry,), 32, LAG), ("swap", (None,), 0, 0)),
        [[shared.reshape(whole_shape(shared_entry))], [back.reshape(ranks, -1, 128)]],
        5,
        "sum_shared",
    )
    shared = shared[0]
    shared = shared.reshape(-1)[: shared_rows * own_columns].reshape(shared_rows, own_columns)
    grad_pre = silu_back(pre_time, shared[:count_all])
    grad_one_t = contract_wide(grad_pre, features, 0, 0)
    ends_t = shared[count_all:].T
    owned_rest = jnp.concatenate(
        [ends_t[:, :PD], grad_one_t, grad_two_t, grad_table_t, ends_t[:, PD:]], axis=1
    ).reshape(-1)

    squares = jnp.sum(big_squares) + jnp.sum(owned_ada * owned_ada) + jnp.sum(owned_rest * owned_rest)
    totals = jnp.broadcast_to(pad_to(jnp.stack([loss_sum, squares]), 0, 128), (8, 128))
    totals = jnp.sum(push_all(totals, world, 8, "push_totals")[:, 0, :2], axis=0)
    back = back[0].reshape(-1, 128)
    owned_big = slots_to_tiles(sums, back, dest, slot, rank, counts, rounds)
    grad_norm = jnp.sqrt(totals[1])
    clip = jnp.minimum(1.0, MAX_NORM / (grad_norm + 1e-06))
    count = step[0].astype(jnp.float32)
    big_out = adam_update(
        owned_big.reshape(big_master.shape), big_master, big_first, big_second, clip, count
    )
    ada_out = adam_update(owned_ada, ada_master, ada_first, ada_second, clip, count)
    rest_out = adam_update(owned_rest, rest_master, rest_first, rest_second, clip, count)
    return (
        totals[:1],
        grad_norm.reshape(1),
        big_out[0],
        big_out[1],
        big_out[2],
        big_out[3],
        ada_out[0],
        ada_out[1],
        ada_out[2],
        ada_out[3],
        rest_out[0],
        rest_out[1],
        rest_out[2],
        rest_out[3],
    )


def whole_columns(mesh):
    ranks, groups = mesh.shape["dp"], mesh.shape["mp"]
    return groups == 4 and D % (ranks * groups) == 0 and ranks == 8


def solution(mesh):
    body = local if whole_columns(mesh) else local_general
    in_specs = (
        P("mp", "dp", None),
        P("mp", "dp", None),
        P("mp", "dp", None),
        P("mp", "dp", None),
        P(("dp", "mp")),
        P(("dp", "mp")),
        P(("dp", "mp")),
        P(("dp", "mp")),
        P(("dp", "mp")),
        P(("dp", "mp")),
        P(("dp", "mp")),
        P(("dp", "mp")),
        P(),
        P(None, ("dp", "mp"), None, None),
        P(None, ("dp", "mp"), None),
        P(None, ("dp", "mp")),
        P(None, ("dp", "mp")),
        P(None, ("dp", "mp")),
        P(None, ("dp", "mp"), None, None),
        P(),
    )
    out_specs = (
        P(),
        P(),
        P("mp", "dp", None),
        P("mp", "dp", None),
        P("mp", "dp", None),
        P("mp", "dp", None),
        P(("dp", "mp")),
        P(("dp", "mp")),
        P(("dp", "mp")),
        P(("dp", "mp")),
        P(("dp", "mp")),
        P(("dp", "mp")),
        P(("dp", "mp")),
        P(("dp", "mp")),
    )
    return jax.shard_map(body, mesh=mesh, in_specs=in_specs, out_specs=out_specs, check_vma=False)
```

```python
import functools
import math

import jax
import jax.numpy as jnp
import numpy as np
from jax import lax
from jax.experimental import pallas as pl
from jax.experimental.pallas import tpu as pltpu
from jax.sharding import PartitionSpec as P

D = 1152
HEADS = 16
HD = 72
FF = 4608
PD = 16
FREQ = 256
CLASSES = 1001
GRID = 16
SEQ = 256
KEEP = 128


EPS_NORM = 1e-06
MAX_NORM = 0.01
RATE = 0.02
DECAY = 0.1
BETA_ONE = 0.9
BETA_TWO = 0.999
ADAM_EPS = 1e-08
MASKED_WEIGHT = 0.1
highest = lax.Precision.HIGHEST


def partner_2(value, axis, stride):
    mask = 2**stride
    pairs = [(source, source ^ mask) for source in range(lax.axis_size(axis))]
    return lax.ppermute(value, axis, pairs)


def product(left, right):
    return jnp.dot(left, right, preferred_element_type=jnp.float32)


def normalize(values):
    center = values - jnp.mean(values, axis=-1, keepdims=True)
    spread = lax.rsqrt(jnp.mean(center * center, axis=-1, keepdims=True) + EPS_NORM)
    return (center * spread, spread)


def normalize_back(grad_normed, normed, spread):
    adjusted = grad_normed - jnp.mean(grad_normed, axis=-1, keepdims=True)
    adjusted = adjusted - normed * jnp.mean(grad_normed * normed, axis=-1, keepdims=True)
    return spread * adjusted


def position_table(columns):
    quarter = columns // 4
    omegas = 1.0 / 10000.0 ** (jnp.arange(quarter, dtype=jnp.float32) / quarter)
    places = jnp.arange(GRID * GRID, dtype=jnp.int32)

    def half_table(coords):
        angles = coords.astype(jnp.float32)[:, None] * omegas[None, :]
        return jnp.concatenate([jnp.sin(angles), jnp.cos(angles)], axis=1)

    return jnp.concatenate([half_table(places % GRID), half_table(places // GRID)], axis=1)


def position_constant(columns):
    quarter = columns // 4
    omegas = np.float32(1.0) / np.float32(10000.0) ** (np.arange(quarter, dtype=np.float32) / np.float32(quarter))
    places = np.arange(GRID * GRID)

    def half_table(coords):
        angles = (coords.astype(np.float32)[:, None] * omegas[None, :]).astype(np.float64)
        return np.concatenate([np.sin(angles), np.cos(angles)], axis=1).astype(np.float32)

    return np.concatenate([half_table(places % GRID), half_table(places // GRID)], axis=1)


def time_features(stamp):
    halves = FREQ // 2
    frequency = jnp.exp(-math.log(10000.0) * jnp.arange(halves, dtype=jnp.float32) / halves)
    angles = stamp.astype(jnp.float32) * frequency
    return jnp.concatenate([jnp.cos(angles), jnp.sin(angles)])


def row_gather(values):
    return lax.all_gather(values, "mp", axis=0, tiled=True)


def row_sum(values):
    return lax.psum_scatter(values, "mp", scatter_dimension=0, tiled=True)


def route_bit(route, bit):
    return jnp.bitwise_and(jnp.right_shift(route, bit), 1) == 1


def route_ids(values, route, levels):
    for bit in range(levels):
        partner = partner_2(values, "dp", bit)
        values = jnp.where(route_bit(route, bit), partner, values)
    return values


def route_rows(values, route, levels):
    for bit in range(levels):
        partner = partner_2(values, "dp", bit)
        values = jnp.where(route_bit(route, bit), partner, values)
    return values


def route_back(values, route, levels):
    for bit in range(levels):
        partner = partner_2(values, "dp", bit)
        values = jnp.where(route_bit(route, bit), partner, values)
    return values


def unpack_big(flat, columns, groups):
    head_width = HEADS * HD // groups
    hidden_width = FF // groups
    shapes = [
        (columns, 3 * head_width),
        (head_width, columns),
        (columns, hidden_width),
        (hidden_width, columns),
    ]
    levels = []
    offset = 0
    for level_index in range(2):
        pieces = []
        for dims in shapes:
            length = dims[0] * dims[1]
            pieces.append(flat[offset : offset + length].reshape(dims))
            offset += length
        levels.append(tuple(pieces))
    return levels


def unpack_rest(flat, columns):
    matrix = flat.reshape(columns, -1).T
    counts = [PD, FREQ, columns, CLASSES, 1, PD]
    pieces = []
    offset = 0
    for count in counts:
        pieces.append(matrix[offset : offset + count])
        offset += count
    return (pieces[0], pieces[1], pieces[2], pieces[3], pieces[4][0], pieces[5].T)


def split_heads(packed, groups, rows):
    third = packed.shape[1] // 3
    return [
        packed[:, index * third : (index + 1) * third].reshape(groups, rows, third // HD, HD)
        for index in range(3)
    ]


def attention_probs(queries, key_rows):
    scores = jnp.einsum("gqhe,gkhe->ghqk", queries, key_rows, preferred_element_type=jnp.float32)
    return jax.nn.softmax(scores * HD ** (-0.5), axis=-1)


def block_forward(state, weights, modulate):
    qkv_weight, proj_weight, up_weight, down_weight = weights
    shift_one, scale_one, gate_one, shift_two, scale_two, gate_two = jnp.split(modulate, 6)
    rows = state.shape[0]
    normed_one, spread_one = normalize(state)
    full_one = row_gather((normed_one * (1.0 + scale_one) + shift_one).astype(jnp.bfloat16))
    groups = full_one.shape[0] // rows
    packed = product(full_one, qkv_weight).astype(jnp.bfloat16)
    queries, key_rows, value_rows = split_heads(packed, groups, rows)
    probs = attention_probs(queries, key_rows)
    mixed = jnp.einsum(
        "ghqk,gkhe->gqhe",
        probs.astype(jnp.bfloat16),
        value_rows,
        preferred_element_type=jnp.float32,
    )
    attended = mixed.astype(jnp.bfloat16).reshape(groups * rows, -1)
    branch_one = row_sum(product(attended, proj_weight))
    middle = state + gate_one * branch_one
    normed_two, spread_two = normalize(middle)
    full_two = row_gather((normed_two * (1.0 + scale_two) + shift_two).astype(jnp.bfloat16))
    hidden_pre = product(full_two, up_weight)
    activated = jax.nn.gelu(hidden_pre, approximate=True).astype(jnp.bfloat16)
    branch_two = row_sum(product(activated, down_weight))
    result = middle + gate_two * branch_two
    saved = (
        normed_one,
        spread_one,
        full_one,
        packed,
        attended,
        branch_one,
        normed_two,
        spread_two,
        full_two,
        hidden_pre,
        activated,
        branch_two,
    )
    return (result, saved)


def block_backward(grad_out, saved, weights, modulate):
    (
        normed_one,
        spread_one,
        full_one,
        packed,
        attended,
        branch_one,
        normed_two,
        spread_two,
        full_two,
        hidden_pre,
        activated,
        branch_two,
    ) = saved
    qkv_weight, proj_weight, up_weight, down_weight = weights
    shift_one, scale_one, gate_one, shift_two, scale_two, gate_two = jnp.split(modulate, 6)
    rows = grad_out.shape[0]
    groups = full_one.shape[0] // rows
    grad_gate_two = jnp.sum(grad_out * branch_two, axis=0)
    back_two = row_gather((gate_two * grad_out).astype(jnp.bfloat16))
    grad_down = product(activated.T, back_two)
    grad_act = product(back_two, down_weight.T)
    unused, gelu_back = jax.vjp(lambda pre: jax.nn.gelu(pre, approximate=True), hidden_pre)
    grad_pre = gelu_back(grad_act)[0].astype(jnp.bfloat16)
    grad_up = product(full_two.T, grad_pre)
    grad_hidden_two = row_sum(product(grad_pre, up_weight.T))
    grad_shift_two = jnp.sum(grad_hidden_two, axis=0)
    grad_scale_two = jnp.sum(grad_hidden_two * normed_two, axis=0)
    grad_middle = grad_out + normalize_back(
        grad_hidden_two * (1.0 + scale_two), normed_two, spread_two
    )
    grad_gate_one = jnp.sum(grad_middle * branch_one, axis=0)
    back_one = row_gather((gate_one * grad_middle).astype(jnp.bfloat16))
    grad_proj = product(attended.T, back_one)
    grad_attended = product(back_one, proj_weight.T).astype(jnp.bfloat16)
    queries, key_rows, value_rows = split_heads(packed, groups, rows)
    probs = attention_probs(queries, key_rows)
    grad_mixed = grad_attended.reshape(queries.shape)
    grad_probs = jnp.einsum(
        "gqhe,gkhe->ghqk", grad_mixed, value_rows, preferred_element_type=jnp.float32
    )
    grad_values = jnp.einsum(
        "ghqk,gqhe->gkhe",
        probs.astype(jnp.bfloat16),
        grad_mixed,
        preferred_element_type=jnp.float32,
    )
    grad_scores = (
        probs * (grad_probs - jnp.sum(grad_probs * probs, axis=-1, keepdims=True)) * HD ** (-0.5)
    )
    grad_scores = grad_scores.astype(jnp.bfloat16)
    grad_queries = jnp.einsum(
        "ghqk,gkhe->gqhe", grad_scores, key_rows, preferred_element_type=jnp.float32
    )
    grad_keys = jnp.einsum(
        "ghqk,gqhe->gkhe", grad_scores, queries, preferred_element_type=jnp.float32
    )
    grad_packed = jnp.concatenate(
        [
            grad_part.reshape(groups * rows, -1)
            for grad_part in (grad_queries, grad_keys, grad_values)
        ],
        axis=1,
    ).astype(jnp.bfloat16)
    grad_qkv = product(full_one.T, grad_packed)
    grad_hidden_one = row_sum(product(grad_packed, qkv_weight.T))
    grad_shift_one = jnp.sum(grad_hidden_one, axis=0)
    grad_scale_one = jnp.sum(grad_hidden_one * normed_one, axis=0)
    grad_state = grad_middle + normalize_back(
        grad_hidden_one * (1.0 + scale_one), normed_one, spread_one
    )
    grad_mod = jnp.concatenate(
        [
            grad_shift_one,
            grad_scale_one,
            grad_gate_one,
            grad_shift_two,
            grad_scale_two,
            grad_gate_two,
        ]
    )
    return (grad_state, grad_mod, (grad_qkv, grad_proj, grad_up, grad_down))


def condition(stamp, tag, time_one, time_two, table):
    features = time_features(stamp).astype(jnp.bfloat16)[None, :]
    pre_time = product(features, time_one)
    hidden_time = jax.nn.silu(pre_time).astype(jnp.bfloat16)
    cond_value = product(hidden_time, time_two)[0] + table[tag].astype(jnp.float32)
    signal = jax.nn.silu(cond_value).astype(jnp.bfloat16)
    return (signal, (features, pre_time, hidden_time, cond_value))


def condition_back(grad_signal, saved, time_two, tag, table_rows):
    features, pre_time, hidden_time, cond_value = saved
    unused, silu_back = jax.vjp(jax.nn.silu, cond_value)
    grad_cond = silu_back(grad_signal)[0]
    grad_time_two = hidden_time.astype(jnp.float32).T * grad_cond[None, :]
    grad_hidden = jnp.dot(time_two.astype(jnp.float32), grad_cond, precision=highest)
    unused_pre, pre_back = jax.vjp(jax.nn.silu, pre_time)
    grad_pre = pre_back(grad_hidden[None, :])[0]
    grad_time_one = features.astype(jnp.float32).T * grad_pre
    grad_table = (jnp.arange(table_rows, dtype=jnp.int32)[:, None] == tag) * grad_cond[None, :]
    return (grad_time_one, grad_time_two, grad_table)


def adam_update(grad, master, first, second, clip, count):
    scaled = grad * clip
    first = BETA_ONE * first + (1.0 - BETA_ONE) * scaled
    second = BETA_TWO * second + (1.0 - BETA_TWO) * scaled * scaled
    fix_one = 1.0 - BETA_ONE**count
    fix_two = 1.0 - BETA_TWO**count
    master = master - RATE * (
        first / fix_one / (jnp.sqrt(second / fix_two) + ADAM_EPS) + DECAY * master
    )
    return (master, first, second, master.astype(jnp.bfloat16))


def local_general(
    big_copy,
    big_master,
    big_first,
    big_second,
    ada_copy,
    ada_master,
    ada_first,
    ada_second,
    rest_copy,
    rest_master,
    rest_first,
    rest_second,
    owner_tiles,
    kept_patches,
    kept_pos,
    timestep,
    label,
    owner,
    target,
    step,
):
    groups = lax.axis_size("mp")
    ranks = lax.axis_size("dp")
    levels_dp = ranks.bit_length() - 1
    my_rank = lax.axis_index("dp")
    tiles = owner_tiles.shape[0]
    columns = D
    gathered = lax.all_gather(big_copy, "dp", axis=1, tiled=True)[0]
    inverse = jnp.zeros((tiles,), jnp.int32).at[owner_tiles].set(jnp.arange(tiles, dtype=jnp.int32))
    big_flat = jnp.take(gathered, inverse, axis=0).reshape(-1)
    ada_flat, rest_flat = (
        lax.all_gather(ada_copy, ("dp", "mp"), axis=0, tiled=True),
        lax.all_gather(rest_copy, ("dp", "mp"), axis=0, tiled=True),
    )
    levels = unpack_big(big_flat, columns, groups)
    ada_matrix = ada_flat.reshape(columns, 14 * columns)
    embed_weight, time_one, time_two, table, mask_token, head_weight = unpack_rest(
        rest_flat, columns
    )
    positions = position_table(columns)
    images = ranks * groups
    inv_count = 1.0 / (PD * kept_patches.shape[0] * images * KEEP)
    zeros_six = jnp.zeros((6 * columns,), jnp.bfloat16)
    zeros_eight = jnp.zeros((8 * columns,), jnp.bfloat16)

    def micro_step(carry, inputs):
        grads_big, grads_rest, loss_sum = carry
        patches, place, stamp, tag, dest, goal = inputs
        route = jnp.bitwise_xor(dest, my_rank)
        signal_enc, saved_enc = condition(stamp, tag, time_one, time_two, table)
        mod_enc = product(signal_enc[None, :], ada_matrix[:, : 6 * columns])[0]
        embedded = product(patches.astype(jnp.bfloat16), embed_weight) + jnp.take(
            positions, place, axis=0
        )
        enc_out, enc_saved = block_forward(embedded, levels[0], mod_enc)
        sent = enc_out.astype(jnp.bfloat16)
        meta = jnp.concatenate([place, stamp[None], tag[None]])
        got_meta = route_ids(meta, route, levels_dp)
        arrived = route_rows(sent, route, levels_dp)
        keep_rows = place.shape[0]
        dec_place = got_meta[:keep_rows]
        dec_tag = got_meta[keep_rows + 1]
        signal_dec, saved_dec = condition(got_meta[keep_rows], dec_tag, time_one, time_two, table)
        mod_dec = product(signal_dec[None, :], ada_matrix[:, 6 * columns :])[0]
        hits = jnp.arange(SEQ, dtype=jnp.int32)[:, None] == dec_place[None, :]
        kept = jnp.sum(hits.astype(jnp.float32), axis=1, keepdims=True)
        dec_in = (
            product(hits.astype(jnp.bfloat16), arrived)
            + (1.0 - kept) * mask_token.astype(jnp.float32)[None, :]
            + positions
        )
        dec_out, dec_saved = block_forward(dec_in, levels[1], mod_dec[: 6 * columns])
        final_shift = mod_dec[6 * columns : 7 * columns]
        final_scale = mod_dec[7 * columns :]
        normed_final, spread_final = normalize(dec_out)
        head_in = (normed_final * (1.0 + final_scale) + final_shift).astype(jnp.bfloat16)
        output = product(head_in, head_weight)
        error = output - goal
        weight = kept + MASKED_WEIGHT * (1.0 - kept)
        loss_part = jnp.sum(weight * error * error) * inv_count
        grad_output = (2.0 * inv_count * weight * error).astype(jnp.bfloat16)
        grad_head = product(head_in.T, grad_output)
        grad_head_in = product(grad_output, head_weight.T)
        grad_final = jnp.concatenate(
            [jnp.sum(grad_head_in, axis=0), jnp.sum(grad_head_in * normed_final, axis=0)]
        )
        grad_dec_out = normalize_back(
            grad_head_in * (1.0 + final_scale), normed_final, spread_final
        )
        grad_dec_in, grad_mod_dec, dec_grads = block_backward(
            grad_dec_out, dec_saved, levels[1], mod_dec[: 6 * columns]
        )
        grad_mask = jnp.sum((1.0 - kept) * grad_dec_in, axis=0)
        grad_arrived = jnp.take(grad_dec_in, dec_place, axis=0).astype(jnp.bfloat16)
        grad_sent = route_back(grad_arrived, route, levels_dp)
        grad_embedded, grad_mod_enc, enc_grads = block_backward(
            grad_sent.astype(jnp.float32), enc_saved, levels[0], mod_enc
        )
        grad_embed = jnp.dot(
            patches.astype(jnp.bfloat16).astype(jnp.float32).T, grad_embedded, precision=highest
        )
        vector_enc = grad_mod_enc.astype(jnp.bfloat16)
        vector_dec = jnp.concatenate([grad_mod_dec, grad_final]).astype(jnp.bfloat16)
        grad_signal_enc = product(ada_matrix[:, : 6 * columns], vector_enc)
        grad_signal_dec = product(ada_matrix[:, 6 * columns :], vector_dec)
        time_enc = condition_back(grad_signal_enc, saved_enc, time_two, tag, table.shape[0])
        time_dec = condition_back(grad_signal_dec, saved_dec, time_two, dec_tag, table.shape[0])
        rest_terms = [
            grad_embed,
            time_enc[0] + time_dec[0],
            time_enc[1] + time_dec[1],
            time_enc[2] + time_dec[2],
            grad_mask[None, :],
            grad_head.T,
        ]
        grads_rest = grads_rest + jnp.concatenate(rest_terms, axis=0)
        big_terms = [
            term.reshape(-1) for level_grads in (enc_grads, dec_grads) for term in level_grads
        ]
        grads_big = grads_big + jnp.concatenate(big_terms)
        signal_pair = jnp.stack([signal_enc, signal_dec])
        vector_pair = jnp.stack(
            [jnp.concatenate([vector_enc, zeros_eight]), jnp.concatenate([zeros_six, vector_dec])]
        )
        return ((grads_big, grads_rest, loss_sum + loss_part), (signal_pair, vector_pair))

    inputs = (
        kept_patches[:, 0],
        kept_pos[:, 0],
        timestep[:, 0],
        label[:, 0],
        owner[:, 0],
        target[:, 0],
    )
    start_carry = (
        jnp.zeros(big_flat.shape, jnp.float32),
        jnp.zeros((rest_flat.shape[0] // columns, columns), jnp.float32),
        jnp.zeros((), jnp.float32),
    )
    finals, factors = lax.scan(micro_step, start_carry, inputs)
    grads_big, grads_matrix, loss_sum = finals
    grads_rest = grads_matrix.T.reshape(-1)
    signal_rows = factors[0].reshape(-1, columns)
    vector_rows = factors[1].reshape(-1, 14 * columns)
    tile_part = jnp.take(grads_big.reshape(tiles, 128), owner_tiles, axis=0)
    owned_big = lax.psum_scatter(tile_part, "dp", scatter_dimension=0, tiled=True)
    local_ada = product(signal_rows.T, vector_rows).reshape(-1)
    owned_ada, owned_rest = (
        lax.psum_scatter(local_ada, ("dp", "mp"), scatter_dimension=0, tiled=True),
        lax.psum_scatter(grads_rest, ("dp", "mp"), scatter_dimension=0, tiled=True),
    )
    squares = (
        jnp.sum(owned_big * owned_big)
        + jnp.sum(owned_ada * owned_ada)
        + jnp.sum(owned_rest * owned_rest)
    )
    loss_total, square_total = lax.psum((loss_sum, squares), ("dp", "mp"))
    grad_norm = jnp.sqrt(square_total)
    clip = jnp.minimum(1.0, MAX_NORM / (grad_norm + 1e-06))
    count = step[0].astype(jnp.float32)
    big_out = adam_update(
        owned_big.reshape(big_master.shape), big_master, big_first, big_second, clip, count
    )
    ada_out = adam_update(owned_ada, ada_master, ada_first, ada_second, clip, count)
    rest_out = adam_update(owned_rest, rest_master, rest_first, rest_second, clip, count)
    return (
        loss_total.reshape(1),
        grad_norm.reshape(1),
        big_out[0],
        big_out[1],
        big_out[2],
        big_out[3],
        ada_out[0],
        ada_out[1],
        ada_out[2],
        ada_out[3],
        rest_out[0],
        rest_out[1],
        rest_out[2],
        rest_out[3],
    )


CHUNK_ROWS = 1152
REST_ROWS = 2 * PD + FREQ + D + CLASSES + 1


def tile_place(tiles, ranks):
    counts = [count // ranks for count in matrix_tiles()]
    layer_tiles = sum(matrix_tiles())
    level = tiles // layer_tiles
    inside = tiles % layer_tiles
    dest = jnp.zeros_like(tiles)
    slot = jnp.zeros_like(tiles)
    start = 0
    base = 0
    for count, total in zip(counts, matrix_tiles()):
        local_tile = inside - start
        here = (local_tile >= 0) & (local_tile < total)
        dest = jnp.where(here, local_tile // count, dest)
        slot = jnp.where(here, base + level * count + local_tile % count, slot)
        start += total
        base += 2 * count
    return dest, slot


def matrix_tiles():
    groups = 4
    head_width = HEADS * HD // groups
    hidden_width = FF // groups
    sizes = [D * 3 * head_width, head_width * D, D * hidden_width, hidden_width * D]
    return [size // 128 for size in sizes]


def rank_within(dest, ranks):
    n = dest.shape[0]
    inner = 96
    outer = n // inner
    hot = (dest.reshape(outer, inner)[None] == jnp.arange(ranks)[:, None, None]).astype(jnp.bfloat16)
    upto = (jnp.arange(inner)[:, None] < jnp.arange(inner)[None, :]).astype(jnp.bfloat16)
    before = jnp.einsum("roi,ij->roj", hot, upto, preferred_element_type=jnp.float32)
    totals = jnp.sum(hot.astype(jnp.float32), axis=2)
    over = (jnp.arange(outer)[:, None] < jnp.arange(outer)[None, :]).astype(jnp.float32)
    prior = jnp.dot(totals, over, precision=highest)
    rank = jnp.sum(hot.astype(jnp.float32) * (before + prior[:, :, None]), axis=0)
    return rank.astype(jnp.int32).reshape(n), jnp.sum(totals, axis=1).astype(jnp.int32)


def widen(source, dest, rows):
    step = 128 if rows % 128 == 0 else 16
    whole = rows // step

    def body(i, unused):
        at = pl.ds(pl.multiple_of(i * step, step), step)
        dest[at, :] = source[at, :].astype(dest.dtype)
        return unused

    lax.fori_loop(0, whole, body, 0)


def pack_kernel(n, pos_ref, x_ref, buf_ref, wide, sorted_rows):
    widen(x_ref, wide, n)

    def move(i, unused):
        places = [pos_ref[i * 16 + j] for j in range(16)]
        rows = [wide[pl.ds(i * 16 + j, 1), :] for j in range(16)]
        for place, row in zip(places, rows):
            sorted_rows[pl.ds(place, 1), :] = row
        return unused

    lax.fori_loop(0, n // 16, move, 0)
    widen(sorted_rows, buf_ref, buf_ref.shape[0])


def scatter_kernel(total, tag_ref, buf_ref, out_ref, wide, slots):
    widen(buf_ref, wide, total)

    def move(i, unused):
        tags = [tag_ref[i * 16 + j] for j in range(16)]
        rows = [wide[pl.ds(i * 16 + j, 1), :] for j in range(16)]
        for tag, row in zip(tags, rows):
            slots[pl.ds(tag, 1), :] = row
        return unused

    lax.fori_loop(0, total // 16, move, 0)
    widen(slots, out_ref, out_ref.shape[0])


def gather_kernel(total, index_ref, x_ref, out_ref, wide_out):
    def move(i, unused):
        index = [index_ref[i * 16 + j] for j in range(16)]
        rows = [x_ref[pl.ds(place, 1), :] for place in index]
        for j in range(16):
            wide_out[pl.ds(i * 16 + j, 1), :] = rows[j]
        return unused

    lax.fori_loop(0, total // 16, move, 0)
    widen(wide_out, out_ref, total)


SMEM = pl.BlockSpec(memory_space=pltpu.SMEM)
VMEM = pl.BlockSpec(memory_space=pltpu.VMEM)
PARAMS = pltpu.CompilerParams(vmem_limit_bytes=48 * 1024 * 1024)


def pack_rows(rows, pos, total):
    n = rows.shape[0]
    return pl.pallas_call(
        functools.partial(pack_kernel, n),
        out_shape=jax.ShapeDtypeStruct((total, 128), jnp.bfloat16),
        in_specs=[SMEM, VMEM],
        out_specs=VMEM,
        scratch_shapes=[
            pltpu.VMEM((n, 128), jnp.float32),
            pltpu.VMEM((total + 16, 128), jnp.float32),
        ],
        compiler_params=PARAMS,
        name="pack_rows",
    )(pos, rows)


def pack_tags(pos, slot, fill, capacity):
    n = pos.shape[0]
    total = fill.shape[0] * capacity
    lines = total // 128
    here = (pos // 128)[:, None] == jnp.arange(lines)[None, :]
    high = jnp.where(here, (slot // 128)[:, None], 0)
    low = jnp.where(here, (slot % 128)[:, None], 0)
    lanes = ((pos % 128)[:, None] == jnp.arange(128)[None, :]).astype(jnp.bfloat16)
    parts = jnp.concatenate([high, low], axis=1).astype(jnp.bfloat16)
    found = contract(parts, lanes, 0, 0).astype(jnp.int32)
    tags = (found[:lines] * 128 + found[lines:]).reshape(fill.shape[0], capacity)
    return jnp.where(jnp.arange(capacity)[None, :] < fill[:, None], tags, n).reshape(-1)


def scatter_rows(rows, tags, n):
    total = rows.shape[0]
    return pl.pallas_call(
        functools.partial(scatter_kernel, total),
        out_shape=jax.ShapeDtypeStruct((n + 16, 128), jnp.bfloat16),
        in_specs=[SMEM, VMEM],
        out_specs=VMEM,
        scratch_shapes=[
            pltpu.VMEM((total, 128), jnp.float32),
            pltpu.VMEM((n + 16, 128), jnp.float32),
        ],
        compiler_params=PARAMS,
        name="scatter_rows",
    )(tags, rows)


def gather_rows(rows, index, dtype):
    total = index.shape[0]
    return pl.pallas_call(
        functools.partial(gather_kernel, total),
        out_shape=jax.ShapeDtypeStruct((total, 128), dtype),
        in_specs=[SMEM, VMEM],
        out_specs=VMEM,
        scratch_shapes=[pltpu.VMEM((total, 128), jnp.float32)],
        compiler_params=PARAMS,
        name="gather_rows",
    )(index, rows)


MESH = pl.DeviceIdType.MESH
LAG = 2
SLOTS = 4
GATHER_SLOTS = 12


def coordinates():
    rank = lax.axis_index("dp")
    group = lax.axis_index("mp")
    return lax.div(rank, 2), lax.rem(rank, 2), lax.div(group, 2), lax.rem(group, 2)


def device_at(z, x, y, core):
    return (z * 2 + x, y * 2 + core)


def neighbours():
    z, x, y, core = coordinates()
    along_x = device_at(z, 1 - x, y, core)
    along_y = device_at(z, x, 1 - y, core)
    first = tuple(jnp.where(core == 0, b, a) for a, b in zip(along_x, along_y))
    second = tuple(jnp.where(core == 0, a, b) for a, b in zip(along_x, along_y))
    others = [device_at(lax.rem(z + step, 4), x, y, core) for step in (1, 2, 3)]
    return device_at(z, x, y, 1 - core), first, second, others


def greet(peers):
    barrier = pltpu.get_barrier_semaphore()
    for peer in peers:
        pl.semaphore_signal(barrier, inc=1, device_id=peer, device_id_type=MESH)
    pl.semaphore_wait(barrier, len(peers))


def block_of(ref, entry, group, at, side=None):
    stacked, rows, width = entry
    sides = slice(None) if side is None else side
    if stacked:
        return ref.at[group, :, sides, at, :]
    return ref.at[:, sides, at, pl.ds(pl.multiple_of(group * width, 128), width)]


def slice_of(ref, entry, group, z, x, at):
    stacked, rows, width = entry
    if stacked:
        return ref.at[group, z, x, at, :]
    return ref.at[z, x, at, pl.ds(pl.multiple_of(group * width, 128), width)]


def chunk_ranges(plan, chunk):
    ranges = []
    start = 0
    for stacked, rows, width in plan:
        ranges.append((start, start + rows // chunk))
        start += rows // chunk
    return ranges, start


def in_range(unit, low, high):
    return (unit >= low) & (unit < high)


def remote(source, target, send, receive, peer):
    return pltpu.make_async_remote_copy(
        src_ref=source,
        dst_ref=target,
        send_sem=send,
        recv_sem=receive,
        device_id=peer,
        device_id_type=MESH,
    )


def gather_job(plan, chunk, lag, slices, wholes, scratch):
    count = len(plan)
    held, other_held, own_sem, out_sem, z_send, z_recv, a_send, a_recv, b_send, b_recv, c_send, c_recv = scratch
    z, x, y, core = coordinates()
    other, first, second, others = neighbours()
    mine_first = jnp.where(core == 0, y, x)
    mine_second = jnp.where(core == 0, x, y)
    ranges, total = chunk_ranges(plan, chunk)

    def copies(stage, k, unit):
        entry = plan[k]
        slot = lax.rem(unit, GATHER_SLOTS)
        at = pl.ds(pl.multiple_of((unit - ranges[k][0]) * chunk, chunk), chunk)
        cols = pl.ds(0, entry[2])
        own = held.at[slot, mine_first, mine_second, z, :, cols]
        if stage == 0:
            source = slices[k].at[at, :]
            return [pltpu.make_async_copy(source, own, own_sem.at[slot])] + [
                remote(source, own, z_send.at[i, slot], z_recv.at[i, slot], others[i])
                for i in range(3)
            ]
        if stage == 1:
            part = held.at[slot, mine_first, mine_second, :, :, cols]
            return [remote(part, part, a_send.at[slot], a_recv.at[slot], second)]
        if stage == 2:
            part = held.at[slot, mine_first, :, :, :, cols]
            return [remote(part, part, b_send.at[slot], b_recv.at[slot], first)]
        if stage == 3:
            source = held.at[slot, :, :, :, :, cols]
            target = other_held.at[slot, :, :, :, :, cols]
            return [remote(source, target, c_send.at[slot], c_recv.at[slot], other)]
        made = []
        from_other = stage == 5
        ref, owner = (other_held, 1 - core) if from_other else (held, core)
        for i in range(2):
            for j in range(2):
                side = jnp.where(owner == 0, j, i)
                group = 2 * jnp.where(owner == 0, i, j) + owner
                made.append(
                    pltpu.make_async_copy(
                        ref.at[slot, i, j, :, :, cols],
                        block_of(wholes[k], entry, group, at, side),
                        out_sem.at[int(from_other), 2 * i + j, slot],
                    )
                )
        return made

    def go(unit, waits, starts):
        for k in range(count):

            @pl.when(in_range(unit, *ranges[k]))
            def _(k=k):
                for stage in waits:
                    for copy in copies(stage, k, unit):
                        copy.wait()
                for stage in starts:
                    for copy in copies(stage, k, unit):
                        copy.start()

    def step(t):
        go(t - 1 - 4 * lag, (4, 5), ())
        go(t - 4 * lag, (3,), (5,))
        go(t - 3 * lag, (2,), (3, 4))
        go(t - 2 * lag, (1,), (2,))
        go(t - lag, (0,), (1,))
        go(t, (), (0,))

    return step, total + 1 + 4 * lag


def whole_shape(entry):
    stacked, rows, width = entry
    return (4, 4, 2, rows, width) if stacked else (4, 2, rows, 4 * width)


def gather_scratch(plan, chunk, kind):
    dma = pltpu.SemaphoreType.DMA
    held = pltpu.VMEM((GATHER_SLOTS, 2, 2, 4, chunk, max(entry[2] for entry in plan)), kind)
    each = dma((GATHER_SLOTS,))
    three = dma((3, GATHER_SLOTS))
    return [held, held, each, dma((2, 4, GATHER_SLOTS)), three, three] + [each] * 6


def sum_job(plan, chunk, lag, parts, outs, scratch):
    count = len(plan)
    own, from_core, from_first, from_second, from_z, half, quarter, eighth = scratch[:8]
    own_sem, core_send, core_recv, a_send, a_recv, b_send, b_recv, z_send, z_recv = scratch[8:]
    z, x, y, core = coordinates()
    other, first, second, others = neighbours()
    mine_first = jnp.where(core == 0, y, x)
    mine_second = jnp.where(core == 0, x, y)
    ranges, total = chunk_ranges(plan, chunk)

    def copies(stage, width, unit, k=None):
        slot = lax.rem(unit, SLOTS)
        pair = lax.rem(unit, 2)
        cols = pl.ds(0, width)
        if stage == 0:
            made = []
            for j in range(2):
                mine = own.at[pair, j, :, :, :, cols]
                theirs = from_core.at[pair, j, :, :, :, cols]
                if k is None:
                    made.append(pltpu.make_async_copy(mine, mine, own_sem.at[j, pair]))
                    made.append(remote(mine, theirs, core_send.at[j, pair], core_recv.at[j, pair], other))
                else:
                    at = pl.ds(pl.multiple_of((unit - ranges[k][0]) * chunk, chunk), chunk)
                    kept = block_of(parts[k], plan[k], 2 * j + core, at)
                    sent = block_of(parts[k], plan[k], 2 * j + 1 - core, at)
                    made.append(pltpu.make_async_copy(kept, mine, own_sem.at[j, pair]))
                    made.append(remote(sent, theirs, core_send.at[j, pair], core_recv.at[j, pair], other))
            return made
        if stage == 1:
            source = half.at[slot, 1 - mine_first, :, :, :, cols]
            target = from_first.at[slot, :, :, :, cols]
            return [remote(source, target, a_send.at[slot], a_recv.at[slot], first)]
        if stage == 2:
            source = quarter.at[slot, 1 - mine_second, :, :, cols]
            target = from_second.at[slot, :, :, cols]
            return [remote(source, target, b_send.at[slot], b_recv.at[slot], second)]
        made = []
        for i in range(3):
            source = eighth.at[slot, lax.rem(z + i + 1, 4), :, cols]
            target = from_z.at[slot, i, :, cols]
            made.append(remote(source, target, z_send.at[i, slot], z_recv.at[i, slot], others[i]))
        return made

    def wide(ref, index, cols):
        return ref[(*index, slice(None), cols)].astype(jnp.float32)

    def add(stage, width, unit):
        slot = lax.rem(unit, SLOTS)
        pair = lax.rem(unit, 2)
        cols = slice(0, width)
        if stage == 0:
            for i in range(2):
                for j in range(2):
                    lead = jnp.where(core == 0, i, j)
                    last = jnp.where(core == 0, j, i)
                    for k in range(4):
                        value = wide(own, (pair, i, k, j), cols) + wide(from_core, (pair, i, k, j), cols)
                        half[slot, lead, last, k, :, cols] = value.astype(half.dtype)
        elif stage == 1:
            for j in range(2):
                for k in range(4):
                    value = wide(half, (slot, mine_first, j, k), cols) + wide(
                        from_first, (slot, j, k), cols
                    )
                    quarter[slot, j, k, :, cols] = value.astype(quarter.dtype)
        else:
            for k in range(4):
                value = wide(quarter, (slot, mine_second, k), cols) + wide(
                    from_second, (slot, k), cols
                )
                eighth[slot, k, :, cols] = value.astype(eighth.dtype)

    widths = sorted({entry[2] for entry in plan})

    def go(unit, stage):
        for width in widths:
            inside = functools.reduce(
                jnp.logical_or,
                [in_range(unit, *ranges[k]) for k in range(count) if plan[k][2] == width],
            )

            @pl.when(inside)
            def _(width=width):
                for copy in copies(stage, width, unit):
                    copy.wait()
                add(stage, width, unit)
                for copy in copies(stage + 1, width, unit):
                    copy.start()

    def finish(unit):
        for k in range(count):

            @pl.when(in_range(unit, *ranges[k]))
            def _(k=k):
                width = plan[k][2]
                slot = lax.rem(unit, SLOTS)
                cols = slice(0, width)
                for copy in copies(3, width, unit):
                    copy.wait()
                at = pl.ds(pl.multiple_of((unit - ranges[k][0]) * chunk, chunk), chunk)
                value = wide(eighth, (slot, z), cols)
                for i in range(3):
                    value = value + wide(from_z, (slot, i), cols)
                outs[k][at, :] = value

    def begin(unit):
        for k in range(count):

            @pl.when(in_range(unit, *ranges[k]))
            def _(k=k):
                for copy in copies(0, plan[k][2], unit, k):
                    copy.start()

    def step(t):
        finish(t - 1 - 3 * lag)
        go(t - 1 - 2 * lag, 2)
        go(t - 1 - lag, 1)
        go(t - 1, 0)
        begin(t)

    return step, total + 1 + 3 * lag


def sum_scratch(plan, chunk, kind):
    dma = pltpu.SemaphoreType.DMA
    width = max(entry[2] for entry in plan)
    buffers = [
        (2, 2, 4, 2, chunk, width),
        (2, 2, 4, 2, chunk, width),
        (SLOTS, 2, 4, chunk, width),
        (SLOTS, 4, chunk, width),
        (SLOTS, 3, chunk, width),
        (SLOTS, 2, 2, 4, chunk, width),
        (SLOTS, 2, 4, chunk, width),
        (SLOTS, 4, chunk, width),
    ]
    return (
        [pltpu.VMEM(shape, kind) for shape in buffers]
        + [dma((2, 2))] * 3
        + [dma((SLOTS,))] * 4
        + [dma((3, SLOTS))] * 2
    )


def direct_job(kind, sources, targets, scratch):
    source, target = sources[0], targets[0]
    own_sem, send_sem, recv_sem = scratch
    ranks, groups = lax.axis_size("dp"), lax.axis_size("mp")
    rank, group = lax.axis_index("dp"), lax.axis_index("mp")
    me, count = (rank * groups + group, ranks * groups) if kind == "push" else (rank, ranks)

    def part(index):
        return source.at[index] if kind == "swap" else source

    own = pltpu.make_async_copy(part(me), target.at[me], own_sem)

    def copy(i):
        to = lax.rem(me + i, count)
        peer = (lax.div(to, groups), lax.rem(to, groups)) if kind == "push" else (to, group)
        return remote(part(to), target.at[me], send_sem.at[i], recv_sem.at[i], peer)

    def start(i, unused):
        copy(i).start()
        return unused

    def finish(i, unused):
        copy(i).wait()
        return unused

    def begin():
        own.start()
        lax.fori_loop(1, count, start, 0)

    def end():
        own.wait()
        lax.fori_loop(1, count, finish, 0)

    return begin, end


def travel_kernel(jobs, scratch_counts, *refs):
    refs = list(refs)

    def take(number):
        taken = refs[:number]
        del refs[:number]
        return taken

    sources = [take(len(job[1])) for job in jobs]
    targets = [take(len(job[1])) for job in jobs]
    scratch = [take(number) for number in scratch_counts]
    steps = []
    direct = []
    for (kind, plan, chunk, lag), source, target, mine in zip(jobs, sources, targets, scratch):
        if kind == "gather":
            steps.append(gather_job(plan, chunk, lag, source, target, mine))
        elif kind == "sum":
            steps.append(sum_job(plan, chunk, lag, source, target, mine))
        else:
            direct.append(direct_job(kind, source, target, mine))
    if direct:
        greet_all()
    else:
        other, first, second, others = neighbours()
        greet([other, first, second] + others)

    def step(t, unused):
        for one, unused_count in steps:
            one(t)
        return unused

    if direct and steps:
        step(0, 0)
    for begin, unused_end in direct:
        begin()
    if steps:
        first_step = 1 if direct else 0
        lax.fori_loop(first_step, max(count for unused_step, count in steps), step, 0)
    for unused_begin, end in direct:
        end()


def greet_all():
    groups = lax.axis_size("mp")
    world = lax.axis_size("dp") * groups
    me = lax.axis_index("dp") * groups + lax.axis_index("mp")
    barrier = pltpu.get_barrier_semaphore()

    def hail(i, unused):
        to = lax.rem(me + i, world)
        peer = (lax.div(to, groups), lax.rem(to, groups))
        pl.semaphore_signal(barrier, inc=1, device_id=peer, device_id_type=MESH)
        return unused

    lax.fori_loop(1, world, hail, 0)
    pl.semaphore_wait(barrier, world - 1)


def travel(jobs, arrays, number, name):
    ANY = pl.BlockSpec(memory_space=pl.ANY)
    dma = pltpu.SemaphoreType.DMA
    ranks, groups = lax.axis_size("dp"), lax.axis_size("mp")
    scratch = []
    shapes = []
    specs = []
    for (kind, plan, chunk, unused_lag), mine in zip(jobs, arrays):
        dtype = mine[0].dtype
        if kind == "gather":
            scratch.append(gather_scratch(plan, chunk, dtype))
            shapes += [jax.ShapeDtypeStruct(whole_shape(entry), dtype) for entry in plan]
            specs += [ANY] * len(plan)
        elif kind == "sum":
            scratch.append(sum_scratch(plan, chunk, dtype))
            shapes += [jax.ShapeDtypeStruct(entry[1:], jnp.float32) for entry in plan]
            specs += [VMEM] * len(plan)
        else:
            count = ranks * groups if kind == "push" else ranks
            scratch.append([dma, dma((count,)), dma((count,))])
            shape = mine[0].shape if kind == "swap" else (count,) + mine[0].shape
            shapes.append(jax.ShapeDtypeStruct(shape, dtype))
            specs.append(ANY)
    flat = [array for mine in arrays for array in mine]
    outs = pl.pallas_call(
        functools.partial(travel_kernel, jobs, [len(mine) for mine in scratch]),
        out_shape=shapes,
        in_specs=[
            VMEM if job[0] == "gather" else ANY for job, mine in zip(jobs, arrays) for unused in mine
        ],
        out_specs=specs,
        scratch_shapes=[one for mine in scratch for one in mine],
        compiler_params=pltpu.CompilerParams(
            collective_id=number, has_side_effects=True, vmem_limit_bytes=48 * 1024 * 1024
        ),
        name=name,
    )(*flat)
    results = []
    for unused_kind, plan, unused_chunk, unused_lag in jobs:
        results.append(outs[: len(plan)])
        outs = outs[len(plan) :]
    return results


def push_kernel(world, x_ref, out_ref, send_sem, recv_sem):
    groups = lax.axis_size("mp")
    me = lax.axis_index("dp") * groups + lax.axis_index("mp")

    def peer(i):
        to = lax.rem(me + i, world)
        return (lax.div(to, groups), lax.rem(to, groups))

    barrier = pltpu.get_barrier_semaphore()

    def hail(i, unused):
        pl.semaphore_signal(barrier, inc=1, device_id=peer(i), device_id_type=MESH)
        return unused

    lax.fori_loop(1, world, hail, 0)
    out_ref[me] = x_ref[...]
    pl.semaphore_wait(barrier, world - 1)

    def copy(i):
        return remote(x_ref, out_ref.at[me], send_sem.at[i], recv_sem.at[i], peer(i))

    def start(i, unused):
        copy(i).start()
        return unused

    def finish(i, unused):
        copy(i).wait()
        return unused

    lax.fori_loop(1, world, start, 0)
    lax.fori_loop(1, world, finish, 0)


def push_all(value, world, number, name):
    dma = pltpu.SemaphoreType.DMA
    return pl.pallas_call(
        functools.partial(push_kernel, world),
        out_shape=jax.ShapeDtypeStruct((world,) + value.shape, value.dtype),
        in_specs=[VMEM],
        out_specs=VMEM,
        scratch_shapes=[dma((world,)), dma((world,))],
        compiler_params=pltpu.CompilerParams(collective_id=number, has_side_effects=True),
        name=name,
    )(value)


def swap_ranks(buf, ranks):
    rest = buf.shape[1:]
    split = buf.reshape((ranks, buf.shape[0] // ranks) + rest)
    return lax.all_to_all(split, "dp", 0, 0).reshape(buf.shape)


def round_positions(dest, rank, counts, capacity, turn):
    ranks = counts.shape[0]
    low = turn * capacity
    inside = (rank >= low) & (rank < low + capacity)
    pos = jnp.where(inside, dest * capacity + rank - low, ranks * capacity)
    fill = jnp.clip(counts - low, 0, capacity)
    return pos, fill, inside


def tiles_to_slots(rows, dest, slot, rank, counts, rounds, carry_first):
    n = rows.shape[0]
    ranks = counts.shape[0]
    total = ranks * CHUNK_ROWS

    def packed(turn):
        pos, fill, unused = round_positions(dest, rank, counts, CHUNK_ROWS, turn)
        return pack_rows(rows, pos, total), pack_tags(pos, slot, fill, CHUNK_ROWS)

    got, tags = carry_first(*packed(0))
    first = scatter_rows(got, tags, n)

    def more(carry):
        turn, slots = carry
        more_rows, more_tags = [swap_ranks(part, ranks) for part in packed(turn)]
        added = scatter_rows(more_rows, more_tags, n)
        fresh = jnp.zeros((n + 16,), jnp.bool_).at[more_tags].set(True)
        return turn + 1, jnp.where(fresh[:, None], added, slots)

    slots = lax.cond(
        rounds > 1,
        lambda start: lax.while_loop(lambda carry: carry[0] < rounds, more, (1, start))[1],
        lambda start: start,
        first,
    )
    return slots, tags


def slots_to_tiles(slots, first, dest, slot, rank, counts, rounds):
    ranks = counts.shape[0]
    total = ranks * CHUNK_ROWS

    def landed(got, turn):
        pos, unused, inside = round_positions(dest, rank, counts, CHUNK_ROWS, turn)
        return gather_rows(got, jnp.minimum(pos, total - 1), jnp.float32), inside

    def more(carry):
        turn, rows = carry
        pos, fill, unused = round_positions(dest, rank, counts, CHUNK_ROWS, turn)
        turn_tags = swap_ranks(pack_tags(pos, slot, fill, CHUNK_ROWS), ranks)
        got = swap_ranks(gather_rows(slots, turn_tags, jnp.bfloat16), ranks)
        added, inside = landed(got.astype(jnp.float32), turn)
        return turn + 1, jnp.where(inside[:, None], added, rows)

    start = (1, landed(first.astype(jnp.float32), 0)[0])
    unused, rows = lax.while_loop(lambda carry: carry[0] < rounds, more, start)
    return rows


QKV_WIDTH = 896
PROJ_ROWS = 48


def layer_plan(ranks):
    return (
        (False, D // ranks, QKV_WIDTH),
        (True, PROJ_ROWS, D),
        (False, D // ranks, FF // 4),
        (True, FF // 4 // ranks, D),
    )


def pad_to(values, axis, size):
    widths = [(0, 0)] * values.ndim
    widths[axis] = (0, size - values.shape[axis])
    return jnp.pad(values, widths)


def slice_places(ranks):
    widths = [3 * HEADS * HD // 4, D, FF // 4, D]
    places = []
    base = 0
    for total, width in zip(matrix_tiles(), widths):
        count = total // ranks
        places.append((count * 128 // width, width, (base, base + count)))
        base += 2 * count
    return places


def row_group(width):
    rows = 128 // math.gcd(width, 128)
    return rows, rows * width // 128


def lane_pieces(start, size, source_width):
    pieces = []
    done = 0
    while done < size:
        row, column = divmod(start + done, source_width)
        block, lane = divmod(column, 128)
        length = min(128 - lane, source_width - column, size - done)
        pieces.append((row, block, lane, done, length))
        done += length
    return pieces


def join_pieces(pieces, load, rows):
    lanes = lax.broadcasted_iota(jnp.int32, (rows, 128), 1)
    value = None
    for row, block, lane, here, length in pieces:
        part = load(row, block)
        if lane != here:
            part = pltpu.roll(part, (here - lane) % 128, 1)
        if value is None:
            inside = lanes < here + length
            value = part if here + length == 128 else jnp.where(inside, part, 0.0)
        else:
            value = jnp.where((lanes >= here) & (lanes < here + length), part, value)
    return value


def spread_kernel(ranks, low_ref, *refs):
    outs, wide, slots_ref = refs[:8], refs[8], refs[9]
    widen(low_ref, slots_ref, low_ref.shape[0])
    for index, (rows, width, bases) in enumerate(slice_places(ranks)):
        group, tiles = row_group(width)
        count = rows // group
        blocks = -(-width // 128)
        for level in range(2):
            out = outs[level * 4 + index]
            for row in range(group):
                for block in range(blocks):
                    start = row * width + block * 128
                    pieces = lane_pieces(start, min(128, width - block * 128), 128)

                    def load(tile, unused, base=bases[level]):
                        return slots_ref[pl.ds(base + tile, count, stride=tiles), :]

                    value = join_pieces(pieces, load, count)
                    at = pl.ds(row, count, stride=group) if group > 1 else pl.ds(0, count)
                    wide[block, at, :] = value
            padded = out.shape[0]
            for block in range(blocks):
                if padded > rows:
                    wide[block, rows:padded, :] = jnp.zeros((padded - rows, 128), jnp.float32)
                out[:, block * 128 : (block + 1) * 128] = wide[block, :padded, :].astype(out.dtype)


def collect_kernel(ranks, *refs):
    parts, slots_ref, square_ref, wide = refs[:8], refs[8], refs[9], refs[10]
    square_ref[...] = jnp.zeros_like(square_ref)
    end = slots_ref.shape[0]
    total = 0
    for index, (rows, width, bases) in enumerate(slice_places(ranks)):
        group, tiles = row_group(width)
        count = rows // group
        total += 2 * count * tiles
        for level in range(2):
            part = parts[level * 4 + index]
            for block in range(-(-width // 128)):
                wide[block, :rows, :] = part[:rows, block * 128 : (block + 1) * 128]
            for tile in range(tiles):
                pieces = lane_pieces(tile * 128, 128, width)

                def load(row, block):
                    at = pl.ds(row, count, stride=group) if group > 1 else pl.ds(0, count)
                    return wide[block, at, :]

                value = join_pieces(pieces, load, count)
                slots_ref[pl.ds(bases[level] + tile, count, stride=tiles), :] = value
                square_ref[:1, :] += jnp.sum(value * value, axis=0, keepdims=True)
    slots_ref[total:end, :] = jnp.zeros((end - total, 128), jnp.float32)


def spread_slots(slots, ranks):
    plan = layer_plan(ranks) * 2
    tall = max(entry[1] for entry in plan)
    broad = max(entry[2] for entry in plan)
    return pl.pallas_call(
        functools.partial(spread_kernel, ranks),
        out_shape=[jax.ShapeDtypeStruct(entry[1:], jnp.bfloat16) for entry in plan],
        in_specs=[VMEM],
        out_specs=[VMEM] * len(plan),
        scratch_shapes=[
            pltpu.VMEM((broad // 128, tall, 128), jnp.float32),
            pltpu.VMEM(slots.shape, jnp.float32),
        ],
        compiler_params=PARAMS,
        name="spread_slots",
    )(slots)


def collect_slots(parts, rows, ranks):
    tall = max(part.shape[0] for part in parts)
    broad = max(part.shape[1] for part in parts)
    return pl.pallas_call(
        functools.partial(collect_kernel, ranks),
        out_shape=(
            jax.ShapeDtypeStruct((rows, 128), jnp.float32),
            jax.ShapeDtypeStruct((8, 128), jnp.float32),
        ),
        in_specs=[VMEM] * len(parts),
        out_specs=(VMEM, VMEM),
        scratch_shapes=[pltpu.VMEM((broad // 128, tall, 128), jnp.float32)],
        compiler_params=PARAMS,
        name="collect_slots",
    )(*parts)


def whole_weights(wholes, ranks):
    qkv, proj, up, down = wholes
    return (qkv.reshape(D, -1), proj.reshape(-1, D), up.reshape(D, -1), down.reshape(-1, D))


def whole_parts(grads, ranks):
    qkv, proj, up, down = grads
    shapes = [whole_shape(entry) for entry in layer_plan(ranks)]
    return [part.reshape(shape) for part, shape in zip((qkv, proj, up, down), shapes)]


GROUP_HEADS = HEADS // 4
GROUP_WIDTH = HEADS * HD // 4


def dot_nt(left, right):
    return lax.dot_general(left, right, (((1,), (1,)), ((), ())), preferred_element_type=jnp.float32)


def dot_tn(left, right):
    return lax.dot_general(left, right, (((0,), (0,)), ((), ())), preferred_element_type=jnp.float32)


def head_parts(packed_ref, head):
    return [
        packed_ref[:, index * GROUP_WIDTH + head * HD : index * GROUP_WIDTH + (head + 1) * HD]
        for index in range(3)
    ]


def head_probs(queries, key_rows):
    scores = dot_nt(queries, key_rows) * HD ** (-0.5)
    powers = jnp.exp(scores - jnp.max(scores, axis=-1, keepdims=True))
    return powers / jnp.sum(powers, axis=-1, keepdims=True)


def pad_columns(values, own):
    rows = values.shape[0]
    gap = jnp.zeros((rows, PROJ_ROWS - own), values.dtype)
    parts = []
    for start in range(0, values.shape[1], own):
        parts += [values[:, start : start + own], gap]
    return jnp.concatenate(parts, axis=1)


def attend_kernel(own, packed_ref, out_ref):
    heads = [head_parts(packed_ref, head) for head in range(GROUP_HEADS)]
    probs = [head_probs(queries, key_rows) for queries, key_rows, unused in heads]
    mixed = [
        product(prob.astype(jnp.bfloat16), parts[2]).astype(out_ref.dtype)
        for prob, parts in zip(probs, heads)
    ]
    out_ref[...] = pad_columns(jnp.concatenate(mixed, axis=1), own)


def attend_back_kernel(packed_ref, grad_ref, spread_ref, out_ref):
    heads = [head_parts(packed_ref, head) for head in range(GROUP_HEADS)]
    every = range(GROUP_HEADS)
    grads = grad_ref[...]
    grad_mixed = [dot_nt(grads, spread_ref[head]).astype(jnp.bfloat16) for head in every]
    probs = [head_probs(queries, key_rows) for queries, key_rows, unused in heads]
    grad_probs = [dot_nt(grad_mixed[head], heads[head][2]) for head in every]
    grad_values = [dot_tn(probs[head].astype(jnp.bfloat16), grad_mixed[head]) for head in every]
    grad_scores = []
    for prob, grad_prob in zip(probs, grad_probs):
        score = prob * (grad_prob - jnp.sum(grad_prob * prob, axis=-1, keepdims=True))
        grad_scores.append((score * HD ** (-0.5)).astype(jnp.bfloat16))
    grad_queries = [product(grad_scores[head], heads[head][1]) for head in every]
    grad_keys = [dot_tn(grad_scores[head], heads[head][0]) for head in every]
    for index, parts in enumerate((grad_queries, grad_keys, grad_values)):
        for head, part in enumerate(parts):
            start = index * GROUP_WIDTH + head * HD
            out_ref[:, start : start + HD] = part.astype(out_ref.dtype)
    rows, width = out_ref.shape
    out_ref[:, 3 * GROUP_WIDTH :] = jnp.zeros((rows, width - 3 * GROUP_WIDTH), out_ref.dtype)


def spread_heads(own):
    columns = jnp.arange(GROUP_WIDTH // own * PROJ_ROWS)
    source = columns // PROJ_ROWS * own + columns % PROJ_ROWS
    source = jnp.where(columns % PROJ_ROWS < own, source, -1)
    hot = jnp.arange(GROUP_WIDTH)[:, None] == source[None, :]
    return hot.astype(jnp.bfloat16).reshape(GROUP_HEADS, HD, -1)


def attend_call(kernel, images, inputs, constants, out_width, name):
    rows = inputs[0].shape[0] // images

    def block(width):
        return pl.BlockSpec((rows, width), lambda image, group: (image, group))

    return pl.pallas_call(
        kernel,
        grid=(images, 4),
        out_shape=jax.ShapeDtypeStruct((images * rows, 4 * out_width), jnp.bfloat16),
        in_specs=[block(one.shape[1] // 4) for one in inputs]
        + [pl.BlockSpec(one.shape, lambda image, group: (0, 0, 0)) for one in constants],
        out_specs=block(out_width),
        compiler_params=PARAMS,
        name=name,
    )(*inputs, *constants)


def attend(packed, own, images):
    kernel = functools.partial(attend_kernel, own)
    return attend_call(kernel, images, [packed], [], GROUP_WIDTH // own * PROJ_ROWS, "attend")


def attend_back(packed, grads, own, images):
    constants = [spread_heads(own)]
    return attend_call(
        attend_back_kernel, images, [packed, grads], constants, QKV_WIDTH, "attend_back"
    )


def gelu_and_slope(values):
    factor = math.sqrt(2.0 / math.pi)
    square = values * values
    bend = jnp.tanh(factor * values * (1.0 + 0.044715 * square))
    half = 0.5 * (1.0 + bend)
    slope = half + 0.5 * values * (1.0 - bend * bend) * factor * (1.0 + 3.0 * 0.044715 * square)
    return values * half, slope


def own_forward(state, weights, modulate, own):
    qkv_weight, proj_weight, up_weight, down_weight = weights
    images, rows, columns = state.shape
    shift_one, scale_one, gate_one, shift_two, scale_two, gate_two = [
        modulate[index] for index in range(6)
    ]
    normed_one, spread_one = normalize(state)
    full_one = (normed_one * (1.0 + scale_one) + shift_one).astype(jnp.bfloat16)
    flat_one = full_one.reshape(-1, columns)
    packed = product(flat_one, qkv_weight).astype(jnp.bfloat16)
    attended = attend(packed, own, images)
    branch_one = product(attended, proj_weight).reshape(state.shape)
    middle = state + gate_one * branch_one
    normed_two, spread_two = normalize(middle)
    full_two = (normed_two * (1.0 + scale_two) + shift_two).astype(jnp.bfloat16)
    flat_two = full_two.reshape(-1, columns)
    activated, slope = gelu_and_slope(product(flat_two, up_weight))
    activated = activated.astype(jnp.bfloat16)
    branch_two = product(activated, down_weight).reshape(state.shape)
    result = middle + gate_two * branch_two
    saved = (
        normed_one,
        spread_one,
        flat_one,
        packed,
        attended,
        branch_one,
        normed_two,
        spread_two,
        flat_two,
        slope,
        activated,
        branch_two,
    )
    return (result, saved)


def own_backward(grad_out, saved, weights, modulate, own):
    (
        normed_one,
        spread_one,
        flat_one,
        packed,
        attended,
        branch_one,
        normed_two,
        spread_two,
        flat_two,
        slope,
        activated,
        branch_two,
    ) = saved
    qkv_weight, proj_weight, up_weight, down_weight = weights
    images, rows, columns = grad_out.shape
    shift_one, scale_one, gate_one, shift_two, scale_two, gate_two = [
        modulate[index] for index in range(6)
    ]
    grad_gate_two = jnp.sum(grad_out * branch_two, axis=1)
    back_two = (gate_two * grad_out).astype(jnp.bfloat16).reshape(-1, columns)
    grad_down = product(activated.T, back_two).astype(jnp.bfloat16)
    grad_pre = (product(back_two, down_weight.T) * slope).astype(jnp.bfloat16)
    grad_up = product(flat_two.T, grad_pre).astype(jnp.bfloat16)
    grad_hidden_two = product(grad_pre, up_weight.T)
    grad_hidden_two = grad_hidden_two.reshape(grad_out.shape)
    grad_shift_two = jnp.sum(grad_hidden_two, axis=1)
    grad_scale_two = jnp.sum(grad_hidden_two * normed_two, axis=1)
    grad_middle = grad_out + normalize_back(
        grad_hidden_two * (1.0 + scale_two), normed_two, spread_two
    )
    grad_gate_one = jnp.sum(grad_middle * branch_one, axis=1)
    back_one = (gate_one * grad_middle).astype(jnp.bfloat16).reshape(-1, columns)
    grad_proj = product(attended.T, back_one).astype(jnp.bfloat16)
    grad_attended = product(back_one, proj_weight.T).astype(jnp.bfloat16)
    grad_packed = attend_back(packed, grad_attended, own, images)
    grad_qkv = product(flat_one.T, grad_packed).astype(jnp.bfloat16)
    grad_hidden_one = product(grad_packed, qkv_weight.T)
    grad_hidden_one = grad_hidden_one.reshape(grad_out.shape)
    grad_shift_one = jnp.sum(grad_hidden_one, axis=1)
    grad_scale_one = jnp.sum(grad_hidden_one * normed_one, axis=1)
    grad_state = grad_middle + normalize_back(
        grad_hidden_one * (1.0 + scale_one), normed_one, spread_one
    )
    grad_mod = jnp.concatenate(
        [
            grad_shift_one,
            grad_scale_one,
            grad_gate_one,
            grad_shift_two,
            grad_scale_two,
            grad_gate_two,
        ],
        axis=1,
    )
    return (grad_state, grad_mod, (grad_qkv, grad_proj, grad_up, grad_down))


def contract(left, right, left_axis, right_axis):
    return lax.dot_general(
        left,
        right,
        (((left_axis,), (right_axis,)), ((), ())),
        preferred_element_type=jnp.float32,
    )


def contract_wide(left, right, left_axis, right_axis):
    return lax.dot_general(
        left.astype(jnp.float32),
        right.astype(jnp.float32),
        (((left_axis,), (right_axis,)), ((), ())),
        precision=highest,
        preferred_element_type=jnp.float32,
    )


def silu_back(values, grads):
    unused, pull = jax.vjp(jax.nn.silu, values)
    return pull(grads)[0]


def local(
    big_copy,
    big_master,
    big_first,
    big_second,
    ada_copy,
    ada_master,
    ada_first,
    ada_second,
    rest_copy,
    rest_master,
    rest_first,
    rest_second,
    owner_tiles,
    kept_patches,
    kept_pos,
    timestep,
    label,
    owner,
    target,
    step,
):
    groups = lax.axis_size("mp")
    ranks = lax.axis_size("dp")
    world = groups * ranks
    my_rank = lax.axis_index("dp")
    micro = kept_patches.shape[0]
    own_columns = D // world
    columns = D

    owned = big_copy.shape[1]
    all_dest, unused_slot = tile_place(owner_tiles, ranks)
    all_hot = all_dest.reshape(ranks, owned, 1) == jnp.arange(ranks)
    rounds = (jnp.max(jnp.sum(all_hot.astype(jnp.int32), axis=1)) + CHUNK_ROWS - 1) // CHUNK_ROWS
    own_tiles = lax.dynamic_slice(owner_tiles, (my_rank * owned,), (owned,))
    dest, slot = tile_place(own_tiles, ranks)
    rank, counts = rank_within(dest, ranks)
    rest_own = rest_copy.reshape(own_columns, REST_ROWS)
    edges = [0, PD, PD + FREQ, PD + FREQ + D, PD + FREQ + D + CLASSES, REST_ROWS]
    win_t, one_t, two_t, table_t, tail_t = [
        rest_own[:, edges[i] : edges[i + 1]] for i in range(5)
    ]
    ends_size = own_columns * (2 * PD + 1)
    one_size = own_columns * FREQ
    whole_numbers = jnp.concatenate([timestep[:, 0], label[:, 0]])
    told = jnp.concatenate(
        [
            jnp.concatenate([win_t, tail_t], axis=1).reshape(-1),
            one_t.reshape(-1),
            (whole_numbers // 32).astype(jnp.bfloat16),
            (whole_numbers % 32).astype(jnp.bfloat16),
        ]
    )
    told = pad_to(told, 0, -(-told.shape[0] // 2048) * 2048).reshape(-1, 128)
    told_entry = (True, told.shape[0], 128)
    brought = []

    def carry_first(buf, new_tags):
        arrays = [
            [told],
            [target.reshape(-1, 128)],
            [new_tags.reshape(ranks, -1, 128)],
            [buf.reshape(ranks, -1, 128)],
        ]
        kinds = ("share", "swap", "swap")
        jobs = [("gather", (told_entry,), told_entry[1], LAG)]
        jobs += [(kind, (None,), 0, 0) for kind in kinds]
        got = travel(jobs, arrays, 6, "exchange_inputs")
        brought.extend(got)
        return got[3][0].reshape(buf.shape), got[2][0].reshape(new_tags.shape)

    slots, tags = tiles_to_slots(big_copy[0], dest, slot, rank, counts, rounds, carry_first)
    told = brought[0][0].reshape(groups, ranks, -1)
    facts = told[:, :, ends_size + one_size : ends_size + one_size + 4 * micro].astype(jnp.int32)
    facts = facts.reshape(world, -1)
    told = told.transpose(1, 0, 2).reshape(world, -1)
    goals = brought[1][0].reshape(ranks, micro, -1, 128)
    facts = facts[:, : 2 * micro] * 32 + facts[:, 2 * micro :]
    stamps = facts[:, :micro].reshape(-1)
    tags_all = facts[:, micro:].reshape(-1)
    ends = told[:, :ends_size].reshape(columns, -1)
    embed_weight = ends[:, :PD].T
    mask_token = ends[:, PD].astype(jnp.float32)
    head_weight = ends[:, PD + 1 :]
    count_all = micro * world
    features = jax.vmap(time_features)(stamps).astype(jnp.bfloat16)
    pre_time = contract(features, one_t, 1, 1)
    one_whole = told[:, ends_size : ends_size + one_size].reshape(columns, FREQ)
    hidden_all = jax.nn.silu(contract(features, one_whole, 1, 1)).astype(jnp.bfloat16)
    picks = (tags_all[:, None] == jnp.arange(CLASSES, dtype=jnp.int32)[None, :]).astype(
        jnp.bfloat16
    )
    cond_own = contract(hidden_all, two_t, 1, 1) + contract(picks, table_t, 1, 1)
    signal_own = jax.nn.silu(cond_own).astype(jnp.bfloat16)
    ada_own = ada_copy.reshape(own_columns, 14 * columns)
    mod_rows = micro * 14
    mod_entry = (True, 32, columns)
    padded = mod_entry[1] // micro
    mods = product(signal_own, pad_to(ada_own, 1, padded * columns)).reshape(-1, padded, columns)
    mods = mods.reshape(whole_shape(mod_entry))
    plan = (layer_plan(ranks) * 2)[:-1]
    spread = spread_slots(slots, ranks)
    wholes, mods = travel(
        (("gather", plan, 16, LAG), ("sum", (mod_entry,), 16, 6)),
        [spread[:-1], [mods]],
        1,
        "gather_weights",
    )
    last, wholes = lax.optimization_barrier((spread[-1], wholes))
    last = lax.all_gather(last, ("mp", "dp"), axis=0, tiled=True)
    weights = [whole_weights(wholes[:4], ranks), whole_weights((*wholes[4:], last), ranks)]
    own = GROUP_WIDTH // ranks
    mods = mods[0].reshape(micro, padded, columns).transpose(1, 0, 2)[:, :, None, :]
    mod_enc = mods[:6]
    mod_dec = mods[6:12]
    final_shift = mods[12]
    final_scale = mods[13]

    goal = jnp.stack([goals[owner[b, 0], b] for b in range(micro)]).reshape(micro, SEQ, PD)
    positions = jnp.asarray(position_constant(columns))
    images = ranks * groups
    inv_count = 1.0 / (PD * micro * images * KEEP)
    place = kept_pos[:, 0]
    patches = kept_patches[:, 0].astype(jnp.bfloat16)
    hits = (
        jnp.arange(SEQ, dtype=jnp.int32)[None, :, None] == place[:, None, :]
    ).astype(jnp.float32)
    hits_low = hits.astype(jnp.bfloat16)
    kept = jnp.sum(hits, axis=2)[:, :, None]
    embedded = product(patches.reshape(-1, PD), embed_weight).reshape(micro, KEEP, columns)
    embedded = embedded + jnp.take(positions, place, axis=0)
    enc_out, enc_saved = own_forward(embedded, weights[0], mod_enc, own)
    sent = enc_out.astype(jnp.bfloat16)
    dec_in = (
        jnp.einsum("bpr,brd->bpd", hits_low, sent, preferred_element_type=jnp.float32)
        + (1.0 - kept) * mask_token[None, None, :]
        + positions[None]
    )
    dec_out, dec_saved = own_forward(dec_in, weights[1], mod_dec, own)
    normed_final, spread_final = normalize(dec_out)
    head_in = (normed_final * (1.0 + final_scale) + final_shift).astype(jnp.bfloat16)
    flat_head = head_in.reshape(-1, columns)
    output = product(flat_head, head_weight).reshape(micro, SEQ, PD)
    error = output - goal
    weight = kept + MASKED_WEIGHT * (1.0 - kept)
    loss_sum = jnp.sum(weight * error * error) * inv_count

    grad_output = (2.0 * inv_count * weight * error).astype(jnp.bfloat16).reshape(-1, PD)
    grad_head = contract(grad_output, flat_head, 0, 0)
    grad_head_in = product(grad_output, head_weight.T).reshape(dec_out.shape)
    grad_final = jnp.concatenate(
        [jnp.sum(grad_head_in, axis=1), jnp.sum(grad_head_in * normed_final, axis=1)], axis=1
    )
    grad_dec_out = normalize_back(grad_head_in * (1.0 + final_scale), normed_final, spread_final)
    grad_dec_in, grad_mod_dec, dec_grads = own_backward(
        grad_dec_out, dec_saved, weights[1], mod_dec, own
    )
    last_sum = lax.psum_scatter(dec_grads[3], ("mp", "dp"), scatter_dimension=0, tiled=True)
    grad_mask = jnp.sum((1.0 - kept) * grad_dec_in, axis=(0, 1))[None, :]
    grad_sent = jnp.einsum(
        "bpr,bpd->brd",
        hits_low,
        grad_dec_in.astype(jnp.bfloat16),
        preferred_element_type=jnp.float32,
    )
    grad_embedded, grad_mod_enc, enc_grads = own_backward(
        grad_sent, enc_saved, weights[0], mod_enc, own
    )
    down_sum = lax.psum_scatter(enc_grads[3], ("mp", "dp"), scatter_dimension=0, tiled=True)
    grad_embed = contract_wide(
        patches.reshape(-1, PD), grad_embedded.reshape(-1, columns), 0, 0
    )

    vectors = jnp.concatenate([grad_mod_enc, grad_mod_dec, grad_final], axis=1)
    vectors = vectors.astype(jnp.bfloat16).reshape(mod_rows, columns)
    vectors = pad_to(vectors, 0, mod_entry[1])
    sums, vectors = travel(
        (("sum", (layer_plan(ranks)[:-1]) * 2, 16, LAG), ("gather", (mod_entry,), 16, 6)),
        [whole_parts(enc_grads, ranks)[:-1] + whole_parts(dec_grads, ranks)[:-1], [vectors]],
        2,
        "sum_gradients",
    )
    sums = [*sums[:3], down_sum.astype(jnp.float32), *sums[3:], last_sum.astype(jnp.float32)]
    sums, big_squares = collect_slots(sums, owned + 16, ranks)
    vectors = vectors[0]
    back = gather_rows(sums, tags, jnp.bfloat16)
    vectors = vectors.reshape(world, mod_entry[1], columns)[:, :mod_rows].reshape(count_all, -1)
    owned_ada = contract(signal_own, vectors, 0, 0).reshape(-1)
    grad_signal = contract(vectors, ada_own, 1, 1)
    grad_cond = silu_back(cond_own, grad_signal)
    grad_two_t = contract_wide(grad_cond, hidden_all, 0, 0)
    grad_table_t = contract_wide(grad_cond, picks, 0, 0)
    shared = jnp.concatenate(
        [contract_wide(grad_cond, two_t, 1, 0), grad_embed, grad_mask, grad_head], axis=0
    )
    shared_rows = shared.shape[0]
    shared = shared.reshape(shared_rows, ranks, groups, own_columns).transpose(2, 1, 0, 3)
    shared = pad_to(shared.reshape(world, -1), 1, 4096)
    shared_entry = (True, 32, 128)
    shared, back = travel(
        (("sum", (shared_entry,), 32, LAG), ("swap", (None,), 0, 0)),
        [[shared.reshape(whole_shape(shared_entry))], [back.reshape(ranks, -1, 128)]],
        5,
        "sum_shared",
    )
    shared = shared[0]
    shared = shared.reshape(-1)[: shared_rows * own_columns].reshape(shared_rows, own_columns)
    grad_pre = silu_back(pre_time, shared[:count_all])
    grad_one_t = contract_wide(grad_pre, features, 0, 0)
    ends_t = shared[count_all:].T
    owned_rest = jnp.concatenate(
        [ends_t[:, :PD], grad_one_t, grad_two_t, grad_table_t, ends_t[:, PD:]], axis=1
    ).reshape(-1)

    squares = jnp.sum(big_squares) + jnp.sum(owned_ada * owned_ada) + jnp.sum(owned_rest * owned_rest)
    totals = jnp.broadcast_to(pad_to(jnp.stack([loss_sum, squares]), 0, 128), (8, 128))
    totals = jnp.sum(push_all(totals, world, 8, "push_totals")[:, 0, :2], axis=0)
    back = back[0].reshape(-1, 128)
    owned_big = slots_to_tiles(sums, back, dest, slot, rank, counts, rounds)
    grad_norm = jnp.sqrt(totals[1])
    clip = jnp.minimum(1.0, MAX_NORM / (grad_norm + 1e-06))
    count = step[0].astype(jnp.float32)
    big_out = adam_update(
        owned_big.reshape(big_master.shape), big_master, big_first, big_second, clip, count
    )
    ada_out = adam_update(owned_ada, ada_master, ada_first, ada_second, clip, count)
    rest_out = adam_update(owned_rest, rest_master, rest_first, rest_second, clip, count)
    return (
        totals[:1],
        grad_norm.reshape(1),
        big_out[0],
        big_out[1],
        big_out[2],
        big_out[3],
        ada_out[0],
        ada_out[1],
        ada_out[2],
        ada_out[3],
        rest_out[0],
        rest_out[1],
        rest_out[2],
        rest_out[3],
    )


def whole_columns(mesh):
    ranks, groups = mesh.shape["dp"], mesh.shape["mp"]
    return groups == 4 and D % (ranks * groups) == 0 and ranks == 8


def solution(mesh):
    body = local if whole_columns(mesh) else local_general
    in_specs = (
        P("mp", "dp", None),
        P("mp", "dp", None),
        P("mp", "dp", None),
        P("mp", "dp", None),
        P(("dp", "mp")),
        P(("dp", "mp")),
        P(("dp", "mp")),
        P(("dp", "mp")),
        P(("dp", "mp")),
        P(("dp", "mp")),
        P(("dp", "mp")),
        P(("dp", "mp")),
        P(),
        P(None, ("dp", "mp"), None, None),
        P(None, ("dp", "mp"), None),
        P(None, ("dp", "mp")),
        P(None, ("dp", "mp")),
        P(None, ("dp", "mp")),
        P(None, ("dp", "mp"), None, None),
        P(),
    )
    out_specs = (
        P(),
        P(),
        P("mp", "dp", None),
        P("mp", "dp", None),
        P("mp", "dp", None),
        P("mp", "dp", None),
        P(("dp", "mp")),
        P(("dp", "mp")),
        P(("dp", "mp")),
        P(("dp", "mp")),
        P(("dp", "mp")),
        P(("dp", "mp")),
        P(("dp", "mp")),
        P(("dp", "mp")),
    )
    return jax.shard_map(body, mesh=mesh, in_specs=in_specs, out_specs=out_specs, check_vma=False)
```

```python
import functools
import math

import jax
import jax.numpy as jnp
import numpy as np
from jax import lax
from jax.experimental import pallas as pl
from jax.experimental.pallas import tpu as pltpu
from jax.sharding import PartitionSpec as P

D = 1152
HEADS = 16
HD = 72
FF = 4608
PD = 16
FREQ = 256
CLASSES = 1001
GRID = 16
SEQ = 256
KEEP = 128


EPS_NORM = 1e-06
MAX_NORM = 0.01
RATE = 0.02
DECAY = 0.1
BETA_ONE = 0.9
BETA_TWO = 0.999
ADAM_EPS = 1e-08
MASKED_WEIGHT = 0.1
highest = lax.Precision.HIGHEST


def partner_2(value, axis, stride):
    mask = 2**stride
    pairs = [(source, source ^ mask) for source in range(lax.axis_size(axis))]
    return lax.ppermute(value, axis, pairs)


def product(left, right):
    return jnp.dot(left, right, preferred_element_type=jnp.float32)


def normalize(values):
    center = values - jnp.mean(values, axis=-1, keepdims=True)
    spread = lax.rsqrt(jnp.mean(center * center, axis=-1, keepdims=True) + EPS_NORM)
    return (center * spread, spread)


def normalize_back(grad_normed, normed, spread):
    adjusted = grad_normed - jnp.mean(grad_normed, axis=-1, keepdims=True)
    adjusted = adjusted - normed * jnp.mean(grad_normed * normed, axis=-1, keepdims=True)
    return spread * adjusted


def position_table(columns):
    quarter = columns // 4
    omegas = 1.0 / 10000.0 ** (jnp.arange(quarter, dtype=jnp.float32) / quarter)
    places = jnp.arange(GRID * GRID, dtype=jnp.int32)

    def half_table(coords):
        angles = coords.astype(jnp.float32)[:, None] * omegas[None, :]
        return jnp.concatenate([jnp.sin(angles), jnp.cos(angles)], axis=1)

    return jnp.concatenate([half_table(places % GRID), half_table(places // GRID)], axis=1)


def position_constant(columns):
    quarter = columns // 4
    omegas = np.float32(1.0) / np.float32(10000.0) ** (np.arange(quarter, dtype=np.float32) / np.float32(quarter))
    places = np.arange(GRID * GRID)

    def half_table(coords):
        angles = (coords.astype(np.float32)[:, None] * omegas[None, :]).astype(np.float64)
        return np.concatenate([np.sin(angles), np.cos(angles)], axis=1).astype(np.float32)

    return np.concatenate([half_table(places % GRID), half_table(places // GRID)], axis=1)


def time_features(stamp):
    halves = FREQ // 2
    frequency = jnp.exp(-math.log(10000.0) * jnp.arange(halves, dtype=jnp.float32) / halves)
    angles = stamp.astype(jnp.float32) * frequency
    return jnp.concatenate([jnp.cos(angles), jnp.sin(angles)])


def row_gather(values):
    return lax.all_gather(values, "mp", axis=0, tiled=True)


def row_sum(values):
    return lax.psum_scatter(values, "mp", scatter_dimension=0, tiled=True)


def route_bit(route, bit):
    return jnp.bitwise_and(jnp.right_shift(route, bit), 1) == 1


def route_ids(values, route, levels):
    for bit in range(levels):
        partner = partner_2(values, "dp", bit)
        values = jnp.where(route_bit(route, bit), partner, values)
    return values


def route_rows(values, route, levels):
    for bit in range(levels):
        partner = partner_2(values, "dp", bit)
        values = jnp.where(route_bit(route, bit), partner, values)
    return values


def route_back(values, route, levels):
    for bit in range(levels):
        partner = partner_2(values, "dp", bit)
        values = jnp.where(route_bit(route, bit), partner, values)
    return values


def unpack_big(flat, columns, groups):
    head_width = HEADS * HD // groups
    hidden_width = FF // groups
    shapes = [
        (columns, 3 * head_width),
        (head_width, columns),
        (columns, hidden_width),
        (hidden_width, columns),
    ]
    levels = []
    offset = 0
    for level_index in range(2):
        pieces = []
        for dims in shapes:
            length = dims[0] * dims[1]
            pieces.append(flat[offset : offset + length].reshape(dims))
            offset += length
        levels.append(tuple(pieces))
    return levels


def unpack_rest(flat, columns):
    matrix = flat.reshape(columns, -1).T
    counts = [PD, FREQ, columns, CLASSES, 1, PD]
    pieces = []
    offset = 0
    for count in counts:
        pieces.append(matrix[offset : offset + count])
        offset += count
    return (pieces[0], pieces[1], pieces[2], pieces[3], pieces[4][0], pieces[5].T)


def split_heads(packed, groups, rows):
    third = packed.shape[1] // 3
    return [
        packed[:, index * third : (index + 1) * third].reshape(groups, rows, third // HD, HD)
        for index in range(3)
    ]


def attention_probs(queries, key_rows):
    scores = jnp.einsum("gqhe,gkhe->ghqk", queries, key_rows, preferred_element_type=jnp.float32)
    return jax.nn.softmax(scores * HD ** (-0.5), axis=-1)


def block_forward(state, weights, modulate):
    qkv_weight, proj_weight, up_weight, down_weight = weights
    shift_one, scale_one, gate_one, shift_two, scale_two, gate_two = jnp.split(modulate, 6)
    rows = state.shape[0]
    normed_one, spread_one = normalize(state)
    full_one = row_gather((normed_one * (1.0 + scale_one) + shift_one).astype(jnp.bfloat16))
    groups = full_one.shape[0] // rows
    packed = product(full_one, qkv_weight).astype(jnp.bfloat16)
    queries, key_rows, value_rows = split_heads(packed, groups, rows)
    probs = attention_probs(queries, key_rows)
    mixed = jnp.einsum(
        "ghqk,gkhe->gqhe",
        probs.astype(jnp.bfloat16),
        value_rows,
        preferred_element_type=jnp.float32,
    )
    attended = mixed.astype(jnp.bfloat16).reshape(groups * rows, -1)
    branch_one = row_sum(product(attended, proj_weight))
    middle = state + gate_one * branch_one
    normed_two, spread_two = normalize(middle)
    full_two = row_gather((normed_two * (1.0 + scale_two) + shift_two).astype(jnp.bfloat16))
    hidden_pre = product(full_two, up_weight)
    activated = jax.nn.gelu(hidden_pre, approximate=True).astype(jnp.bfloat16)
    branch_two = row_sum(product(activated, down_weight))
    result = middle + gate_two * branch_two
    saved = (
        normed_one,
        spread_one,
        full_one,
        packed,
        attended,
        branch_one,
        normed_two,
        spread_two,
        full_two,
        hidden_pre,
        activated,
        branch_two,
    )
    return (result, saved)


def block_backward(grad_out, saved, weights, modulate):
    (
        normed_one,
        spread_one,
        full_one,
        packed,
        attended,
        branch_one,
        normed_two,
        spread_two,
        full_two,
        hidden_pre,
        activated,
        branch_two,
    ) = saved
    qkv_weight, proj_weight, up_weight, down_weight = weights
    shift_one, scale_one, gate_one, shift_two, scale_two, gate_two = jnp.split(modulate, 6)
    rows = grad_out.shape[0]
    groups = full_one.shape[0] // rows
    grad_gate_two = jnp.sum(grad_out * branch_two, axis=0)
    back_two = row_gather((gate_two * grad_out).astype(jnp.bfloat16))
    grad_down = product(activated.T, back_two)
    grad_act = product(back_two, down_weight.T)
    unused, gelu_back = jax.vjp(lambda pre: jax.nn.gelu(pre, approximate=True), hidden_pre)
    grad_pre = gelu_back(grad_act)[0].astype(jnp.bfloat16)
    grad_up = product(full_two.T, grad_pre)
    grad_hidden_two = row_sum(product(grad_pre, up_weight.T))
    grad_shift_two = jnp.sum(grad_hidden_two, axis=0)
    grad_scale_two = jnp.sum(grad_hidden_two * normed_two, axis=0)
    grad_middle = grad_out + normalize_back(
        grad_hidden_two * (1.0 + scale_two), normed_two, spread_two
    )
    grad_gate_one = jnp.sum(grad_middle * branch_one, axis=0)
    back_one = row_gather((gate_one * grad_middle).astype(jnp.bfloat16))
    grad_proj = product(attended.T, back_one)
    grad_attended = product(back_one, proj_weight.T).astype(jnp.bfloat16)
    queries, key_rows, value_rows = split_heads(packed, groups, rows)
    probs = attention_probs(queries, key_rows)
    grad_mixed = grad_attended.reshape(queries.shape)
    grad_probs = jnp.einsum(
        "gqhe,gkhe->ghqk", grad_mixed, value_rows, preferred_element_type=jnp.float32
    )
    grad_values = jnp.einsum(
        "ghqk,gqhe->gkhe",
        probs.astype(jnp.bfloat16),
        grad_mixed,
        preferred_element_type=jnp.float32,
    )
    grad_scores = (
        probs * (grad_probs - jnp.sum(grad_probs * probs, axis=-1, keepdims=True)) * HD ** (-0.5)
    )
    grad_scores = grad_scores.astype(jnp.bfloat16)
    grad_queries = jnp.einsum(
        "ghqk,gkhe->gqhe", grad_scores, key_rows, preferred_element_type=jnp.float32
    )
    grad_keys = jnp.einsum(
        "ghqk,gqhe->gkhe", grad_scores, queries, preferred_element_type=jnp.float32
    )
    grad_packed = jnp.concatenate(
        [
            grad_part.reshape(groups * rows, -1)
            for grad_part in (grad_queries, grad_keys, grad_values)
        ],
        axis=1,
    ).astype(jnp.bfloat16)
    grad_qkv = product(full_one.T, grad_packed)
    grad_hidden_one = row_sum(product(grad_packed, qkv_weight.T))
    grad_shift_one = jnp.sum(grad_hidden_one, axis=0)
    grad_scale_one = jnp.sum(grad_hidden_one * normed_one, axis=0)
    grad_state = grad_middle + normalize_back(
        grad_hidden_one * (1.0 + scale_one), normed_one, spread_one
    )
    grad_mod = jnp.concatenate(
        [
            grad_shift_one,
            grad_scale_one,
            grad_gate_one,
            grad_shift_two,
            grad_scale_two,
            grad_gate_two,
        ]
    )
    return (grad_state, grad_mod, (grad_qkv, grad_proj, grad_up, grad_down))


def condition(stamp, tag, time_one, time_two, table):
    features = time_features(stamp).astype(jnp.bfloat16)[None, :]
    pre_time = product(features, time_one)
    hidden_time = jax.nn.silu(pre_time).astype(jnp.bfloat16)
    cond_value = product(hidden_time, time_two)[0] + table[tag].astype(jnp.float32)
    signal = jax.nn.silu(cond_value).astype(jnp.bfloat16)
    return (signal, (features, pre_time, hidden_time, cond_value))


def condition_back(grad_signal, saved, time_two, tag, table_rows):
    features, pre_time, hidden_time, cond_value = saved
    unused, silu_back = jax.vjp(jax.nn.silu, cond_value)
    grad_cond = silu_back(grad_signal)[0]
    grad_time_two = hidden_time.astype(jnp.float32).T * grad_cond[None, :]
    grad_hidden = jnp.dot(time_two.astype(jnp.float32), grad_cond, precision=highest)
    unused_pre, pre_back = jax.vjp(jax.nn.silu, pre_time)
    grad_pre = pre_back(grad_hidden[None, :])[0]
    grad_time_one = features.astype(jnp.float32).T * grad_pre
    grad_table = (jnp.arange(table_rows, dtype=jnp.int32)[:, None] == tag) * grad_cond[None, :]
    return (grad_time_one, grad_time_two, grad_table)


def adam_update(grad, master, first, second, clip, count):
    scaled = grad * clip
    first = BETA_ONE * first + (1.0 - BETA_ONE) * scaled
    second = BETA_TWO * second + (1.0 - BETA_TWO) * scaled * scaled
    fix_one = 1.0 - BETA_ONE**count
    fix_two = 1.0 - BETA_TWO**count
    master = master - RATE * (
        first / fix_one / (jnp.sqrt(second / fix_two) + ADAM_EPS) + DECAY * master
    )
    return (master, first, second, master.astype(jnp.bfloat16))


def local_general(
    big_copy,
    big_master,
    big_first,
    big_second,
    ada_copy,
    ada_master,
    ada_first,
    ada_second,
    rest_copy,
    rest_master,
    rest_first,
    rest_second,
    owner_tiles,
    kept_patches,
    kept_pos,
    timestep,
    label,
    owner,
    target,
    step,
):
    groups = lax.axis_size("mp")
    ranks = lax.axis_size("dp")
    levels_dp = ranks.bit_length() - 1
    my_rank = lax.axis_index("dp")
    tiles = owner_tiles.shape[0]
    columns = D
    gathered = lax.all_gather(big_copy, "dp", axis=1, tiled=True)[0]
    inverse = jnp.zeros((tiles,), jnp.int32).at[owner_tiles].set(jnp.arange(tiles, dtype=jnp.int32))
    big_flat = jnp.take(gathered, inverse, axis=0).reshape(-1)
    ada_flat, rest_flat = (
        lax.all_gather(ada_copy, ("dp", "mp"), axis=0, tiled=True),
        lax.all_gather(rest_copy, ("dp", "mp"), axis=0, tiled=True),
    )
    levels = unpack_big(big_flat, columns, groups)
    ada_matrix = ada_flat.reshape(columns, 14 * columns)
    embed_weight, time_one, time_two, table, mask_token, head_weight = unpack_rest(
        rest_flat, columns
    )
    positions = position_table(columns)
    images = ranks * groups
    inv_count = 1.0 / (PD * kept_patches.shape[0] * images * KEEP)
    zeros_six = jnp.zeros((6 * columns,), jnp.bfloat16)
    zeros_eight = jnp.zeros((8 * columns,), jnp.bfloat16)

    def micro_step(carry, inputs):
        grads_big, grads_rest, loss_sum = carry
        patches, place, stamp, tag, dest, goal = inputs
        route = jnp.bitwise_xor(dest, my_rank)
        signal_enc, saved_enc = condition(stamp, tag, time_one, time_two, table)
        mod_enc = product(signal_enc[None, :], ada_matrix[:, : 6 * columns])[0]
        embedded = product(patches.astype(jnp.bfloat16), embed_weight) + jnp.take(
            positions, place, axis=0
        )
        enc_out, enc_saved = block_forward(embedded, levels[0], mod_enc)
        sent = enc_out.astype(jnp.bfloat16)
        meta = jnp.concatenate([place, stamp[None], tag[None]])
        got_meta = route_ids(meta, route, levels_dp)
        arrived = route_rows(sent, route, levels_dp)
        keep_rows = place.shape[0]
        dec_place = got_meta[:keep_rows]
        dec_tag = got_meta[keep_rows + 1]
        signal_dec, saved_dec = condition(got_meta[keep_rows], dec_tag, time_one, time_two, table)
        mod_dec = product(signal_dec[None, :], ada_matrix[:, 6 * columns :])[0]
        hits = jnp.arange(SEQ, dtype=jnp.int32)[:, None] == dec_place[None, :]
        kept = jnp.sum(hits.astype(jnp.float32), axis=1, keepdims=True)
        dec_in = (
            product(hits.astype(jnp.bfloat16), arrived)
            + (1.0 - kept) * mask_token.astype(jnp.float32)[None, :]
            + positions
        )
        dec_out, dec_saved = block_forward(dec_in, levels[1], mod_dec[: 6 * columns])
        final_shift = mod_dec[6 * columns : 7 * columns]
        final_scale = mod_dec[7 * columns :]
        normed_final, spread_final = normalize(dec_out)
        head_in = (normed_final * (1.0 + final_scale) + final_shift).astype(jnp.bfloat16)
        output = product(head_in, head_weight)
        error = output - goal
        weight = kept + MASKED_WEIGHT * (1.0 - kept)
        loss_part = jnp.sum(weight * error * error) * inv_count
        grad_output = (2.0 * inv_count * weight * error).astype(jnp.bfloat16)
        grad_head = product(head_in.T, grad_output)
        grad_head_in = product(grad_output, head_weight.T)
        grad_final = jnp.concatenate(
            [jnp.sum(grad_head_in, axis=0), jnp.sum(grad_head_in * normed_final, axis=0)]
        )
        grad_dec_out = normalize_back(
            grad_head_in * (1.0 + final_scale), normed_final, spread_final
        )
        grad_dec_in, grad_mod_dec, dec_grads = block_backward(
            grad_dec_out, dec_saved, levels[1], mod_dec[: 6 * columns]
        )
        grad_mask = jnp.sum((1.0 - kept) * grad_dec_in, axis=0)
        grad_arrived = jnp.take(grad_dec_in, dec_place, axis=0).astype(jnp.bfloat16)
        grad_sent = route_back(grad_arrived, route, levels_dp)
        grad_embedded, grad_mod_enc, enc_grads = block_backward(
            grad_sent.astype(jnp.float32), enc_saved, levels[0], mod_enc
        )
        grad_embed = jnp.dot(
            patches.astype(jnp.bfloat16).astype(jnp.float32).T, grad_embedded, precision=highest
        )
        vector_enc = grad_mod_enc.astype(jnp.bfloat16)
        vector_dec = jnp.concatenate([grad_mod_dec, grad_final]).astype(jnp.bfloat16)
        grad_signal_enc = product(ada_matrix[:, : 6 * columns], vector_enc)
        grad_signal_dec = product(ada_matrix[:, 6 * columns :], vector_dec)
        time_enc = condition_back(grad_signal_enc, saved_enc, time_two, tag, table.shape[0])
        time_dec = condition_back(grad_signal_dec, saved_dec, time_two, dec_tag, table.shape[0])
        rest_terms = [
            grad_embed,
            time_enc[0] + time_dec[0],
            time_enc[1] + time_dec[1],
            time_enc[2] + time_dec[2],
            grad_mask[None, :],
            grad_head.T,
        ]
        grads_rest = grads_rest + jnp.concatenate(rest_terms, axis=0)
        big_terms = [
            term.reshape(-1) for level_grads in (enc_grads, dec_grads) for term in level_grads
        ]
        grads_big = grads_big + jnp.concatenate(big_terms)
        signal_pair = jnp.stack([signal_enc, signal_dec])
        vector_pair = jnp.stack(
            [jnp.concatenate([vector_enc, zeros_eight]), jnp.concatenate([zeros_six, vector_dec])]
        )
        return ((grads_big, grads_rest, loss_sum + loss_part), (signal_pair, vector_pair))

    inputs = (
        kept_patches[:, 0],
        kept_pos[:, 0],
        timestep[:, 0],
        label[:, 0],
        owner[:, 0],
        target[:, 0],
    )
    start_carry = (
        jnp.zeros(big_flat.shape, jnp.float32),
        jnp.zeros((rest_flat.shape[0] // columns, columns), jnp.float32),
        jnp.zeros((), jnp.float32),
    )
    finals, factors = lax.scan(micro_step, start_carry, inputs)
    grads_big, grads_matrix, loss_sum = finals
    grads_rest = grads_matrix.T.reshape(-1)
    signal_rows = factors[0].reshape(-1, columns)
    vector_rows = factors[1].reshape(-1, 14 * columns)
    tile_part = jnp.take(grads_big.reshape(tiles, 128), owner_tiles, axis=0)
    owned_big = lax.psum_scatter(tile_part, "dp", scatter_dimension=0, tiled=True)
    local_ada = product(signal_rows.T, vector_rows).reshape(-1)
    owned_ada, owned_rest = (
        lax.psum_scatter(local_ada, ("dp", "mp"), scatter_dimension=0, tiled=True),
        lax.psum_scatter(grads_rest, ("dp", "mp"), scatter_dimension=0, tiled=True),
    )
    squares = (
        jnp.sum(owned_big * owned_big)
        + jnp.sum(owned_ada * owned_ada)
        + jnp.sum(owned_rest * owned_rest)
    )
    loss_total, square_total = lax.psum((loss_sum, squares), ("dp", "mp"))
    grad_norm = jnp.sqrt(square_total)
    clip = jnp.minimum(1.0, MAX_NORM / (grad_norm + 1e-06))
    count = step[0].astype(jnp.float32)
    big_out = adam_update(
        owned_big.reshape(big_master.shape), big_master, big_first, big_second, clip, count
    )
    ada_out = adam_update(owned_ada, ada_master, ada_first, ada_second, clip, count)
    rest_out = adam_update(owned_rest, rest_master, rest_first, rest_second, clip, count)
    return (
        loss_total.reshape(1),
        grad_norm.reshape(1),
        big_out[0],
        big_out[1],
        big_out[2],
        big_out[3],
        ada_out[0],
        ada_out[1],
        ada_out[2],
        ada_out[3],
        rest_out[0],
        rest_out[1],
        rest_out[2],
        rest_out[3],
    )


CHUNK_ROWS = 1088
TAG_LANES = 64
REST_ROWS = 2 * PD + FREQ + D + CLASSES + 1


def tile_place(tiles, ranks):
    counts = [count // ranks for count in matrix_tiles()]
    layer_tiles = sum(matrix_tiles())
    level = tiles // layer_tiles
    inside = tiles % layer_tiles
    dest = jnp.zeros_like(tiles)
    slot = jnp.zeros_like(tiles)
    start = 0
    base = 0
    for count, total in zip(counts, matrix_tiles()):
        local_tile = inside - start
        here = (local_tile >= 0) & (local_tile < total)
        dest = jnp.where(here, local_tile // count, dest)
        slot = jnp.where(here, base + level * count + local_tile % count, slot)
        start += total
        base += 2 * count
    return dest, slot


def matrix_tiles():
    groups = 4
    head_width = HEADS * HD // groups
    hidden_width = FF // groups
    sizes = [D * 3 * head_width, head_width * D, D * hidden_width, hidden_width * D]
    return [size // 128 for size in sizes]


def rank_within(dest, ranks):
    n = dest.shape[0]
    inner = 96
    outer = n // inner
    hot = (dest.reshape(outer, inner)[None] == jnp.arange(ranks)[:, None, None]).astype(jnp.bfloat16)
    upto = (jnp.arange(inner)[:, None] < jnp.arange(inner)[None, :]).astype(jnp.bfloat16)
    before = jnp.einsum("roi,ij->roj", hot, upto, preferred_element_type=jnp.float32)
    totals = jnp.sum(hot.astype(jnp.float32), axis=2)
    over = (jnp.arange(outer)[:, None] < jnp.arange(outer)[None, :]).astype(jnp.float32)
    prior = jnp.dot(totals, over, precision=highest)
    rank = jnp.sum(hot.astype(jnp.float32) * (before + prior[:, :, None]), axis=0)
    return rank.astype(jnp.int32).reshape(n), jnp.sum(totals, axis=1).astype(jnp.int32)


def widen(source, dest, rows):
    step = 128 if rows % 128 == 0 else 16
    whole = rows // step

    def body(i, unused):
        at = pl.ds(pl.multiple_of(i * step, step), step)
        dest[at, :] = source[at, :].astype(dest.dtype)
        return unused

    lax.fori_loop(0, whole, body, 0)


def pack_kernel(n, pos_ref, x_ref, buf_ref, wide, sorted_rows):
    widen(x_ref, wide, n)

    def move(i, unused):
        places = [pos_ref[i * 16 + j] for j in range(16)]
        rows = [wide[pl.ds(i * 16 + j, 1), :] for j in range(16)]
        for place, row in zip(places, rows):
            sorted_rows[pl.ds(place, 1), :] = row
        return unused

    lax.fori_loop(0, n // 16, move, 0)
    widen(sorted_rows, buf_ref, buf_ref.shape[0])


def scatter_kernel(total, tag_ref, buf_ref, out_ref, wide, slots):
    widen(buf_ref, wide, total)

    def move(i, unused):
        tags = [tag_ref[i * 16 + j] for j in range(16)]
        rows = [wide[pl.ds(i * 16 + j, 1), :] for j in range(16)]
        for tag, row in zip(tags, rows):
            slots[pl.ds(tag, 1), :] = row
        return unused

    lax.fori_loop(0, total // 16, move, 0)
    widen(slots, out_ref, out_ref.shape[0])


def gather_kernel(total, index_ref, x_ref, out_ref, wide_out):
    def move(i, unused):
        index = [index_ref[i * 16 + j] for j in range(16)]
        rows = [x_ref[pl.ds(place, 1), :] for place in index]
        for j in range(16):
            wide_out[pl.ds(i * 16 + j, 1), :] = rows[j]
        return unused

    lax.fori_loop(0, total // 16, move, 0)
    widen(wide_out, out_ref, total)


SMEM = pl.BlockSpec(memory_space=pltpu.SMEM)
VMEM = pl.BlockSpec(memory_space=pltpu.VMEM)
PARAMS = pltpu.CompilerParams(vmem_limit_bytes=48 * 1024 * 1024)


def pack_rows(rows, pos, total):
    n = rows.shape[0]
    return pl.pallas_call(
        functools.partial(pack_kernel, n),
        out_shape=jax.ShapeDtypeStruct((total, 128), jnp.bfloat16),
        in_specs=[SMEM, VMEM],
        out_specs=VMEM,
        scratch_shapes=[
            pltpu.VMEM((n, 128), jnp.float32),
            pltpu.VMEM((total + 16, 128), jnp.float32),
        ],
        compiler_params=PARAMS,
        name="pack_rows",
    )(pos, rows)


def pack_tags(pos, slot, fill, capacity):
    n = pos.shape[0]
    total = fill.shape[0] * capacity
    lines = total // TAG_LANES
    here = (pos // TAG_LANES)[:, None] == jnp.arange(lines)[None, :]
    high = jnp.where(here, (slot // 128)[:, None], 0)
    low = jnp.where(here, (slot % 128)[:, None], 0)
    lanes = ((pos % TAG_LANES)[:, None] == jnp.arange(TAG_LANES)[None, :]).astype(jnp.bfloat16)
    parts = jnp.concatenate([high, low], axis=1).astype(jnp.bfloat16)
    found = contract(parts, lanes, 0, 0).astype(jnp.int32)
    tags = (found[:lines] * 128 + found[lines:]).reshape(fill.shape[0], capacity)
    return jnp.where(jnp.arange(capacity)[None, :] < fill[:, None], tags, n).reshape(-1)


def scatter_rows(rows, tags, n):
    total = rows.shape[0]
    return pl.pallas_call(
        functools.partial(scatter_kernel, total),
        out_shape=jax.ShapeDtypeStruct((n + 16, 128), jnp.bfloat16),
        in_specs=[SMEM, VMEM],
        out_specs=VMEM,
        scratch_shapes=[
            pltpu.VMEM((total, 128), jnp.float32),
            pltpu.VMEM((n + 16, 128), jnp.float32),
        ],
        compiler_params=PARAMS,
        name="scatter_rows",
    )(tags, rows)


def gather_rows(rows, index, dtype):
    total = index.shape[0]
    return pl.pallas_call(
        functools.partial(gather_kernel, total),
        out_shape=jax.ShapeDtypeStruct((total, 128), dtype),
        in_specs=[SMEM, VMEM],
        out_specs=VMEM,
        scratch_shapes=[pltpu.VMEM((total, 128), jnp.float32)],
        compiler_params=PARAMS,
        name="gather_rows",
    )(index, rows)


MESH = pl.DeviceIdType.MESH
LAG = 2
SLOTS = 4
GATHER_SLOTS = 12


def coordinates():
    rank = lax.axis_index("dp")
    group = lax.axis_index("mp")
    return lax.div(rank, 2), lax.rem(rank, 2), lax.div(group, 2), lax.rem(group, 2)


def device_at(z, x, y, core):
    return (z * 2 + x, y * 2 + core)


def neighbours():
    z, x, y, core = coordinates()
    along_x = device_at(z, 1 - x, y, core)
    along_y = device_at(z, x, 1 - y, core)
    first = tuple(jnp.where(core == 0, b, a) for a, b in zip(along_x, along_y))
    second = tuple(jnp.where(core == 0, a, b) for a, b in zip(along_x, along_y))
    others = [device_at(lax.rem(z + step, 4), x, y, core) for step in (1, 2, 3)]
    return device_at(z, x, y, 1 - core), first, second, others


def greet(peers):
    barrier = pltpu.get_barrier_semaphore()
    for peer in peers:
        pl.semaphore_signal(barrier, inc=1, device_id=peer, device_id_type=MESH)
    pl.semaphore_wait(barrier, len(peers))


def block_of(ref, entry, group, at, side=None):
    stacked, rows, width = entry
    sides = slice(None) if side is None else side
    if stacked:
        return ref.at[group, :, sides, at, :]
    return ref.at[:, sides, at, pl.ds(pl.multiple_of(group * width, 128), width)]


def slice_of(ref, entry, group, z, x, at):
    stacked, rows, width = entry
    if stacked:
        return ref.at[group, z, x, at, :]
    return ref.at[z, x, at, pl.ds(pl.multiple_of(group * width, 128), width)]


def chunk_ranges(plan, chunk):
    ranges = []
    start = 0
    for stacked, rows, width in plan:
        ranges.append((start, start + rows // chunk))
        start += rows // chunk
    return ranges, start


def in_range(unit, low, high):
    return (unit >= low) & (unit < high)


def remote(source, target, send, receive, peer):
    return pltpu.make_async_remote_copy(
        src_ref=source,
        dst_ref=target,
        send_sem=send,
        recv_sem=receive,
        device_id=peer,
        device_id_type=MESH,
    )


def gather_job(plan, chunk, lag, slices, wholes, scratch):
    count = len(plan)
    held, other_held, own_sem, out_sem, z_send, z_recv, a_send, a_recv, b_send, b_recv, c_send, c_recv = scratch
    z, x, y, core = coordinates()
    other, first, second, others = neighbours()
    mine_first = jnp.where(core == 0, y, x)
    mine_second = jnp.where(core == 0, x, y)
    ranges, total = chunk_ranges(plan, chunk)

    def copies(stage, k, unit):
        entry = plan[k]
        slot = lax.rem(unit, GATHER_SLOTS)
        at = pl.ds(pl.multiple_of((unit - ranges[k][0]) * chunk, chunk), chunk)
        cols = pl.ds(0, entry[2])
        own = held.at[slot, mine_first, mine_second, z, :, cols]
        if stage == 0:
            source = slices[k].at[at, :]
            return [pltpu.make_async_copy(source, own, own_sem.at[slot])] + [
                remote(source, own, z_send.at[i, slot], z_recv.at[i, slot], others[i])
                for i in range(3)
            ]
        if stage == 1:
            part = held.at[slot, mine_first, mine_second, :, :, cols]
            return [remote(part, part, a_send.at[slot], a_recv.at[slot], second)]
        if stage == 2:
            part = held.at[slot, mine_first, :, :, :, cols]
            return [remote(part, part, b_send.at[slot], b_recv.at[slot], first)]
        if stage == 3:
            source = held.at[slot, :, :, :, :, cols]
            target = other_held.at[slot, :, :, :, :, cols]
            return [remote(source, target, c_send.at[slot], c_recv.at[slot], other)]
        made = []
        from_other = stage == 5
        ref, owner = (other_held, 1 - core) if from_other else (held, core)
        for i in range(2):
            for j in range(2):
                side = jnp.where(owner == 0, j, i)
                group = 2 * jnp.where(owner == 0, i, j) + owner
                made.append(
                    pltpu.make_async_copy(
                        ref.at[slot, i, j, :, :, cols],
                        block_of(wholes[k], entry, group, at, side),
                        out_sem.at[int(from_other), 2 * i + j, slot],
                    )
                )
        return made

    def go(unit, waits, starts):
        for k in range(count):

            @pl.when(in_range(unit, *ranges[k]))
            def _(k=k):
                for stage in waits:
                    for copy in copies(stage, k, unit):
                        copy.wait()
                for stage in starts:
                    for copy in copies(stage, k, unit):
                        copy.start()

    def step(t):
        go(t - 1 - 4 * lag, (4, 5), ())
        go(t - 4 * lag, (3,), (5,))
        go(t - 3 * lag, (2,), (3, 4))
        go(t - 2 * lag, (1,), (2,))
        go(t - lag, (0,), (1,))
        go(t, (), (0,))

    return step, total + 1 + 4 * lag


def whole_shape(entry):
    stacked, rows, width = entry
    return (4, 4, 2, rows, width) if stacked else (4, 2, rows, 4 * width)


def gather_scratch(plan, chunk, kind):
    dma = pltpu.SemaphoreType.DMA
    held = pltpu.VMEM((GATHER_SLOTS, 2, 2, 4, chunk, max(entry[2] for entry in plan)), kind)
    each = dma((GATHER_SLOTS,))
    three = dma((3, GATHER_SLOTS))
    return [held, held, each, dma((2, 4, GATHER_SLOTS)), three, three] + [each] * 6


def sum_job(plan, chunk, lag, parts, outs, scratch):
    count = len(plan)
    own, from_core, from_first, from_second, from_z, half, quarter, eighth = scratch[:8]
    own_sem, core_send, core_recv, a_send, a_recv, b_send, b_recv, z_send, z_recv = scratch[8:]
    z, x, y, core = coordinates()
    other, first, second, others = neighbours()
    mine_first = jnp.where(core == 0, y, x)
    mine_second = jnp.where(core == 0, x, y)
    ranges, total = chunk_ranges(plan, chunk)

    def copies(stage, width, unit, k=None):
        slot = lax.rem(unit, SLOTS)
        pair = lax.rem(unit, 2)
        cols = pl.ds(0, width)
        if stage == 0:
            made = []
            for j in range(2):
                mine = own.at[pair, j, :, :, :, cols]
                theirs = from_core.at[pair, j, :, :, :, cols]
                if k is None:
                    made.append(pltpu.make_async_copy(mine, mine, own_sem.at[j, pair]))
                    made.append(remote(mine, theirs, core_send.at[j, pair], core_recv.at[j, pair], other))
                else:
                    at = pl.ds(pl.multiple_of((unit - ranges[k][0]) * chunk, chunk), chunk)
                    kept = block_of(parts[k], plan[k], 2 * j + core, at)
                    sent = block_of(parts[k], plan[k], 2 * j + 1 - core, at)
                    made.append(pltpu.make_async_copy(kept, mine, own_sem.at[j, pair]))
                    made.append(remote(sent, theirs, core_send.at[j, pair], core_recv.at[j, pair], other))
            return made
        if stage == 1:
            source = half.at[slot, 1 - mine_first, :, :, :, cols]
            target = from_first.at[slot, :, :, :, cols]
            return [remote(source, target, a_send.at[slot], a_recv.at[slot], first)]
        if stage == 2:
            source = quarter.at[slot, 1 - mine_second, :, :, cols]
            target = from_second.at[slot, :, :, cols]
            return [remote(source, target, b_send.at[slot], b_recv.at[slot], second)]
        made = []
        for i in range(3):
            source = eighth.at[slot, lax.rem(z + i + 1, 4), :, cols]
            target = from_z.at[slot, i, :, cols]
            made.append(remote(source, target, z_send.at[i, slot], z_recv.at[i, slot], others[i]))
        return made

    def wide(ref, index, cols):
        return ref[(*index, slice(None), cols)].astype(jnp.float32)

    def add(stage, width, unit):
        slot = lax.rem(unit, SLOTS)
        pair = lax.rem(unit, 2)
        cols = slice(0, width)
        if stage == 0:
            for i in range(2):
                for j in range(2):
                    lead = jnp.where(core == 0, i, j)
                    last = jnp.where(core == 0, j, i)
                    for k in range(4):
                        value = wide(own, (pair, i, k, j), cols) + wide(from_core, (pair, i, k, j), cols)
                        half[slot, lead, last, k, :, cols] = value.astype(half.dtype)
        elif stage == 1:
            for j in range(2):
                for k in range(4):
                    value = wide(half, (slot, mine_first, j, k), cols) + wide(
                        from_first, (slot, j, k), cols
                    )
                    quarter[slot, j, k, :, cols] = value.astype(quarter.dtype)
        else:
            for k in range(4):
                value = wide(quarter, (slot, mine_second, k), cols) + wide(
                    from_second, (slot, k), cols
                )
                eighth[slot, k, :, cols] = value.astype(eighth.dtype)

    widths = sorted({entry[2] for entry in plan})

    def go(unit, stage):
        for width in widths:
            inside = functools.reduce(
                jnp.logical_or,
                [in_range(unit, *ranges[k]) for k in range(count) if plan[k][2] == width],
            )

            @pl.when(inside)
            def _(width=width):
                for copy in copies(stage, width, unit):
                    copy.wait()
                add(stage, width, unit)
                for copy in copies(stage + 1, width, unit):
                    copy.start()

    def finish(unit):
        for k in range(count):

            @pl.when(in_range(unit, *ranges[k]))
            def _(k=k):
                width = plan[k][2]
                slot = lax.rem(unit, SLOTS)
                cols = slice(0, width)
                for copy in copies(3, width, unit):
                    copy.wait()
                at = pl.ds(pl.multiple_of((unit - ranges[k][0]) * chunk, chunk), chunk)
                value = wide(eighth, (slot, z), cols)
                for i in range(3):
                    value = value + wide(from_z, (slot, i), cols)
                outs[k][at, :] = value

    def begin(unit):
        for k in range(count):

            @pl.when(in_range(unit, *ranges[k]))
            def _(k=k):
                for copy in copies(0, plan[k][2], unit, k):
                    copy.start()

    def step(t):
        finish(t - 1 - 3 * lag)
        go(t - 1 - 2 * lag, 2)
        go(t - 1 - lag, 1)
        go(t - 1, 0)
        begin(t)

    return step, total + 1 + 3 * lag


def sum_scratch(plan, chunk, kind):
    dma = pltpu.SemaphoreType.DMA
    width = max(entry[2] for entry in plan)
    buffers = [
        (2, 2, 4, 2, chunk, width),
        (2, 2, 4, 2, chunk, width),
        (SLOTS, 2, 4, chunk, width),
        (SLOTS, 4, chunk, width),
        (SLOTS, 3, chunk, width),
        (SLOTS, 2, 2, 4, chunk, width),
        (SLOTS, 2, 4, chunk, width),
        (SLOTS, 4, chunk, width),
    ]
    return (
        [pltpu.VMEM(shape, kind) for shape in buffers]
        + [dma((2, 2))] * 3
        + [dma((SLOTS,))] * 4
        + [dma((3, SLOTS))] * 2
    )


def direct_job(kind, sources, targets, scratch):
    source, target = sources[0], targets[0]
    own_sem, send_sem, recv_sem = scratch
    ranks, groups = lax.axis_size("dp"), lax.axis_size("mp")
    rank, group = lax.axis_index("dp"), lax.axis_index("mp")
    me, count = (rank * groups + group, ranks * groups) if kind == "push" else (rank, ranks)

    def part(index):
        return source.at[index] if kind == "swap" else source

    own = pltpu.make_async_copy(part(me), target.at[me], own_sem)

    def copy(i):
        to = lax.rem(me + i, count)
        peer = (lax.div(to, groups), lax.rem(to, groups)) if kind == "push" else (to, group)
        return remote(part(to), target.at[me], send_sem.at[i], recv_sem.at[i], peer)

    def start(i, unused):
        copy(i).start()
        return unused

    def finish(i, unused):
        copy(i).wait()
        return unused

    def begin():
        own.start()
        lax.fori_loop(1, count, start, 0)

    def end():
        own.wait()
        lax.fori_loop(1, count, finish, 0)

    return begin, end


def travel_kernel(jobs, scratch_counts, *refs):
    refs = list(refs)

    def take(number):
        taken = refs[:number]
        del refs[:number]
        return taken

    sources = [take(len(job[1])) for job in jobs]
    targets = [take(len(job[1])) for job in jobs]
    scratch = [take(number) for number in scratch_counts]
    steps = []
    direct = []
    for (kind, plan, chunk, lag), source, target, mine in zip(jobs, sources, targets, scratch):
        if kind == "gather":
            steps.append(gather_job(plan, chunk, lag, source, target, mine))
        elif kind == "sum":
            steps.append(sum_job(plan, chunk, lag, source, target, mine))
        else:
            direct.append(direct_job(kind, source, target, mine))
    if direct:
        greet_all()
    else:
        other, first, second, others = neighbours()
        greet([other, first, second] + others)

    def step(t, unused):
        for one, unused_count in steps:
            one(t)
        return unused

    if direct and steps:
        step(0, 0)
    for begin, unused_end in direct:
        begin()
    if steps:
        first_step = 1 if direct else 0
        lax.fori_loop(first_step, max(count for unused_step, count in steps), step, 0)
    for unused_begin, end in direct:
        end()


def greet_all():
    groups = lax.axis_size("mp")
    world = lax.axis_size("dp") * groups
    me = lax.axis_index("dp") * groups + lax.axis_index("mp")
    barrier = pltpu.get_barrier_semaphore()

    def hail(i, unused):
        to = lax.rem(me + i, world)
        peer = (lax.div(to, groups), lax.rem(to, groups))
        pl.semaphore_signal(barrier, inc=1, device_id=peer, device_id_type=MESH)
        return unused

    lax.fori_loop(1, world, hail, 0)
    pl.semaphore_wait(barrier, world - 1)


def travel(jobs, arrays, number, name):
    ANY = pl.BlockSpec(memory_space=pl.ANY)
    dma = pltpu.SemaphoreType.DMA
    ranks, groups = lax.axis_size("dp"), lax.axis_size("mp")
    scratch = []
    shapes = []
    specs = []
    for (kind, plan, chunk, unused_lag), mine in zip(jobs, arrays):
        dtype = mine[0].dtype
        if kind == "gather":
            scratch.append(gather_scratch(plan, chunk, dtype))
            shapes += [jax.ShapeDtypeStruct(whole_shape(entry), dtype) for entry in plan]
            specs += [ANY] * len(plan)
        elif kind == "sum":
            scratch.append(sum_scratch(plan, chunk, dtype))
            shapes += [jax.ShapeDtypeStruct(entry[1:], jnp.float32) for entry in plan]
            specs += [VMEM] * len(plan)
        else:
            count = ranks * groups if kind == "push" else ranks
            scratch.append([dma, dma((count,)), dma((count,))])
            shape = mine[0].shape if kind == "swap" else (count,) + mine[0].shape
            shapes.append(jax.ShapeDtypeStruct(shape, dtype))
            specs.append(ANY)
    flat = [array for mine in arrays for array in mine]
    outs = pl.pallas_call(
        functools.partial(travel_kernel, jobs, [len(mine) for mine in scratch]),
        out_shape=shapes,
        in_specs=[
            VMEM if job[0] == "gather" else ANY for job, mine in zip(jobs, arrays) for unused in mine
        ],
        out_specs=specs,
        scratch_shapes=[one for mine in scratch for one in mine],
        compiler_params=pltpu.CompilerParams(
            collective_id=number, has_side_effects=True, vmem_limit_bytes=48 * 1024 * 1024
        ),
        name=name,
    )(*flat)
    results = []
    for unused_kind, plan, unused_chunk, unused_lag in jobs:
        results.append(outs[: len(plan)])
        outs = outs[len(plan) :]
    return results


def push_kernel(world, x_ref, out_ref, send_sem, recv_sem):
    groups = lax.axis_size("mp")
    me = lax.axis_index("dp") * groups + lax.axis_index("mp")

    def peer(i):
        to = lax.rem(me + i, world)
        return (lax.div(to, groups), lax.rem(to, groups))

    barrier = pltpu.get_barrier_semaphore()

    def hail(i, unused):
        pl.semaphore_signal(barrier, inc=1, device_id=peer(i), device_id_type=MESH)
        return unused

    lax.fori_loop(1, world, hail, 0)
    out_ref[me] = x_ref[...]
    pl.semaphore_wait(barrier, world - 1)

    def copy(i):
        return remote(x_ref, out_ref.at[me], send_sem.at[i], recv_sem.at[i], peer(i))

    def start(i, unused):
        copy(i).start()
        return unused

    def finish(i, unused):
        copy(i).wait()
        return unused

    lax.fori_loop(1, world, start, 0)
    lax.fori_loop(1, world, finish, 0)


def push_all(value, world, number, name):
    dma = pltpu.SemaphoreType.DMA
    return pl.pallas_call(
        functools.partial(push_kernel, world),
        out_shape=jax.ShapeDtypeStruct((world,) + value.shape, value.dtype),
        in_specs=[VMEM],
        out_specs=VMEM,
        scratch_shapes=[dma((world,)), dma((world,))],
        compiler_params=pltpu.CompilerParams(collective_id=number, has_side_effects=True),
        name=name,
    )(value)


def swap_ranks(buf, ranks):
    rest = buf.shape[1:]
    split = buf.reshape((ranks, buf.shape[0] // ranks) + rest)
    return lax.all_to_all(split, "dp", 0, 0).reshape(buf.shape)


def round_positions(dest, rank, counts, capacity, turn):
    ranks = counts.shape[0]
    low = turn * capacity
    inside = (rank >= low) & (rank < low + capacity)
    pos = jnp.where(inside, dest * capacity + rank - low, ranks * capacity)
    fill = jnp.clip(counts - low, 0, capacity)
    return pos, fill, inside


def tiles_to_slots(rows, dest, slot, rank, counts, rounds, carry_first):
    n = rows.shape[0]
    ranks = counts.shape[0]
    total = ranks * CHUNK_ROWS

    def packed(turn):
        pos, fill, unused = round_positions(dest, rank, counts, CHUNK_ROWS, turn)
        return pack_rows(rows, pos, total), pack_tags(pos, slot, fill, CHUNK_ROWS)

    got, tags = carry_first(*packed(0))
    first = scatter_rows(got, tags, n)

    def more(carry):
        turn, slots = carry
        more_rows, more_tags = [swap_ranks(part, ranks) for part in packed(turn)]
        added = scatter_rows(more_rows, more_tags, n)
        fresh = jnp.zeros((n + 16,), jnp.bool_).at[more_tags].set(True)
        return turn + 1, jnp.where(fresh[:, None], added, slots)

    slots = lax.cond(
        rounds > 1,
        lambda start: lax.while_loop(lambda carry: carry[0] < rounds, more, (1, start))[1],
        lambda start: start,
        first,
    )
    return slots, tags


def slots_to_tiles(slots, first, dest, slot, rank, counts, rounds):
    ranks = counts.shape[0]
    total = ranks * CHUNK_ROWS

    def landed(got, turn):
        pos, unused, inside = round_positions(dest, rank, counts, CHUNK_ROWS, turn)
        return gather_rows(got, jnp.minimum(pos, total - 1), jnp.float32), inside

    def more(carry):
        turn, rows = carry
        pos, fill, unused = round_positions(dest, rank, counts, CHUNK_ROWS, turn)
        turn_tags = swap_ranks(pack_tags(pos, slot, fill, CHUNK_ROWS), ranks)
        got = swap_ranks(gather_rows(slots, turn_tags, jnp.bfloat16), ranks)
        added, inside = landed(got.astype(jnp.float32), turn)
        return turn + 1, jnp.where(inside[:, None], added, rows)

    start = (1, landed(first.astype(jnp.float32), 0)[0])
    unused, rows = lax.while_loop(lambda carry: carry[0] < rounds, more, start)
    return rows


QKV_WIDTH = 896
PROJ_ROWS = 48


def layer_plan(ranks):
    return (
        (False, D // ranks, QKV_WIDTH),
        (True, PROJ_ROWS, D),
        (False, D // ranks, FF // 4),
        (True, FF // 4 // ranks, D),
    )


def pad_to(values, axis, size):
    widths = [(0, 0)] * values.ndim
    widths[axis] = (0, size - values.shape[axis])
    return jnp.pad(values, widths)


def slice_places(ranks):
    widths = [3 * HEADS * HD // 4, D, FF // 4, D]
    places = []
    base = 0
    for total, width in zip(matrix_tiles(), widths):
        count = total // ranks
        places.append((count * 128 // width, width, (base, base + count)))
        base += 2 * count
    return places


def row_group(width):
    rows = 128 // math.gcd(width, 128)
    return rows, rows * width // 128


def lane_pieces(start, size, source_width):
    pieces = []
    done = 0
    while done < size:
        row, column = divmod(start + done, source_width)
        block, lane = divmod(column, 128)
        length = min(128 - lane, source_width - column, size - done)
        pieces.append((row, block, lane, done, length))
        done += length
    return pieces


def join_pieces(pieces, load, rows):
    lanes = lax.broadcasted_iota(jnp.int32, (rows, 128), 1)
    value = None
    for row, block, lane, here, length in pieces:
        part = load(row, block)
        if lane != here:
            part = pltpu.roll(part, (here - lane) % 128, 1)
        if value is None:
            inside = lanes < here + length
            value = part if here + length == 128 else jnp.where(inside, part, 0.0)
        else:
            value = jnp.where((lanes >= here) & (lanes < here + length), part, value)
    return value


def spread_kernel(ranks, low_ref, *refs):
    outs, wide, slots_ref = refs[:8], refs[8], refs[9]
    widen(low_ref, slots_ref, low_ref.shape[0])
    for index, (rows, width, bases) in enumerate(slice_places(ranks)):
        group, tiles = row_group(width)
        count = rows // group
        blocks = -(-width // 128)
        for level in range(2):
            out = outs[level * 4 + index]
            for row in range(group):
                for block in range(blocks):
                    start = row * width + block * 128
                    pieces = lane_pieces(start, min(128, width - block * 128), 128)

                    def load(tile, unused, base=bases[level]):
                        return slots_ref[pl.ds(base + tile, count, stride=tiles), :]

                    value = join_pieces(pieces, load, count)
                    at = pl.ds(row, count, stride=group) if group > 1 else pl.ds(0, count)
                    wide[block, at, :] = value
            padded = out.shape[0]
            for block in range(blocks):
                if padded > rows:
                    wide[block, rows:padded, :] = jnp.zeros((padded - rows, 128), jnp.float32)
                out[:, block * 128 : (block + 1) * 128] = wide[block, :padded, :].astype(out.dtype)


def collect_kernel(ranks, *refs):
    parts, slots_ref, square_ref, wide = refs[:8], refs[8], refs[9], refs[10]
    square_ref[...] = jnp.zeros_like(square_ref)
    end = slots_ref.shape[0]
    total = 0
    for index, (rows, width, bases) in enumerate(slice_places(ranks)):
        group, tiles = row_group(width)
        count = rows // group
        total += 2 * count * tiles
        for level in range(2):
            part = parts[level * 4 + index]
            for block in range(-(-width // 128)):
                wide[block, :rows, :] = part[:rows, block * 128 : (block + 1) * 128]
            for tile in range(tiles):
                pieces = lane_pieces(tile * 128, 128, width)

                def load(row, block):
                    at = pl.ds(row, count, stride=group) if group > 1 else pl.ds(0, count)
                    return wide[block, at, :]

                value = join_pieces(pieces, load, count)
                slots_ref[pl.ds(bases[level] + tile, count, stride=tiles), :] = value
                square_ref[:1, :] += jnp.sum(value * value, axis=0, keepdims=True)
    slots_ref[total:end, :] = jnp.zeros((end - total, 128), jnp.float32)


def spread_slots(slots, ranks):
    plan = layer_plan(ranks) * 2
    tall = max(entry[1] for entry in plan)
    broad = max(entry[2] for entry in plan)
    return pl.pallas_call(
        functools.partial(spread_kernel, ranks),
        out_shape=[jax.ShapeDtypeStruct(entry[1:], jnp.bfloat16) for entry in plan],
        in_specs=[VMEM],
        out_specs=[VMEM] * len(plan),
        scratch_shapes=[
            pltpu.VMEM((broad // 128, tall, 128), jnp.float32),
            pltpu.VMEM(slots.shape, jnp.float32),
        ],
        compiler_params=PARAMS,
        name="spread_slots",
    )(slots)


def collect_slots(parts, rows, ranks):
    tall = max(part.shape[0] for part in parts)
    broad = max(part.shape[1] for part in parts)
    return pl.pallas_call(
        functools.partial(collect_kernel, ranks),
        out_shape=(
            jax.ShapeDtypeStruct((rows, 128), jnp.float32),
            jax.ShapeDtypeStruct((8, 128), jnp.float32),
        ),
        in_specs=[VMEM] * len(parts),
        out_specs=(VMEM, VMEM),
        scratch_shapes=[pltpu.VMEM((broad // 128, tall, 128), jnp.float32)],
        compiler_params=PARAMS,
        name="collect_slots",
    )(*parts)


def whole_weights(wholes, ranks):
    qkv, proj, up, down = wholes
    return (qkv.reshape(D, -1), proj.reshape(-1, D), up.reshape(D, -1), down.reshape(-1, D))


def whole_parts(grads, ranks):
    qkv, proj, up, down = grads
    shapes = [whole_shape(entry) for entry in layer_plan(ranks)]
    return [part.reshape(shape) for part, shape in zip((qkv, proj, up, down), shapes)]


GROUP_HEADS = HEADS // 4
GROUP_WIDTH = HEADS * HD // 4


def dot_nt(left, right):
    return lax.dot_general(left, right, (((1,), (1,)), ((), ())), preferred_element_type=jnp.float32)


def dot_tn(left, right):
    return lax.dot_general(left, right, (((0,), (0,)), ((), ())), preferred_element_type=jnp.float32)


def head_parts(packed_ref, head):
    return [
        packed_ref[:, index * GROUP_WIDTH + head * HD : index * GROUP_WIDTH + (head + 1) * HD]
        for index in range(3)
    ]


def head_probs(queries, key_rows):
    scores = dot_nt(queries, key_rows) * HD ** (-0.5)
    powers = jnp.exp(scores - jnp.max(scores, axis=-1, keepdims=True))
    return powers / jnp.sum(powers, axis=-1, keepdims=True)


def pad_columns(values, own):
    rows = values.shape[0]
    gap = jnp.zeros((rows, PROJ_ROWS - own), values.dtype)
    parts = []
    for start in range(0, values.shape[1], own):
        parts += [values[:, start : start + own], gap]
    return jnp.concatenate(parts, axis=1)


def attend_kernel(own, packed_ref, out_ref):
    heads = [head_parts(packed_ref, head) for head in range(GROUP_HEADS)]
    probs = [head_probs(queries, key_rows) for queries, key_rows, unused in heads]
    mixed = [
        product(prob.astype(jnp.bfloat16), parts[2]).astype(out_ref.dtype)
        for prob, parts in zip(probs, heads)
    ]
    out_ref[...] = pad_columns(jnp.concatenate(mixed, axis=1), own)


def attend_back_kernel(packed_ref, grad_ref, spread_ref, out_ref):
    heads = [head_parts(packed_ref, head) for head in range(GROUP_HEADS)]
    every = range(GROUP_HEADS)
    grads = grad_ref[...]
    grad_mixed = [dot_nt(grads, spread_ref[head]).astype(jnp.bfloat16) for head in every]
    probs = [head_probs(queries, key_rows) for queries, key_rows, unused in heads]
    grad_probs = [dot_nt(grad_mixed[head], heads[head][2]) for head in every]
    grad_values = [dot_tn(probs[head].astype(jnp.bfloat16), grad_mixed[head]) for head in every]
    grad_scores = []
    for prob, grad_prob in zip(probs, grad_probs):
        score = prob * (grad_prob - jnp.sum(grad_prob * prob, axis=-1, keepdims=True))
        grad_scores.append((score * HD ** (-0.5)).astype(jnp.bfloat16))
    grad_queries = [product(grad_scores[head], heads[head][1]) for head in every]
    grad_keys = [dot_tn(grad_scores[head], heads[head][0]) for head in every]
    for index, parts in enumerate((grad_queries, grad_keys, grad_values)):
        for head, part in enumerate(parts):
            start = index * GROUP_WIDTH + head * HD
            out_ref[:, start : start + HD] = part.astype(out_ref.dtype)
    rows, width = out_ref.shape
    out_ref[:, 3 * GROUP_WIDTH :] = jnp.zeros((rows, width - 3 * GROUP_WIDTH), out_ref.dtype)


def spread_heads(own):
    columns = jnp.arange(GROUP_WIDTH // own * PROJ_ROWS)
    source = columns // PROJ_ROWS * own + columns % PROJ_ROWS
    source = jnp.where(columns % PROJ_ROWS < own, source, -1)
    hot = jnp.arange(GROUP_WIDTH)[:, None] == source[None, :]
    return hot.astype(jnp.bfloat16).reshape(GROUP_HEADS, HD, -1)


def attend_call(kernel, images, inputs, constants, out_width, name):
    rows = inputs[0].shape[0] // images

    def block(width):
        return pl.BlockSpec((rows, width), lambda image, group: (image, group))

    return pl.pallas_call(
        kernel,
        grid=(images, 4),
        out_shape=jax.ShapeDtypeStruct((images * rows, 4 * out_width), jnp.bfloat16),
        in_specs=[block(one.shape[1] // 4) for one in inputs]
        + [pl.BlockSpec(one.shape, lambda image, group: (0, 0, 0)) for one in constants],
        out_specs=block(out_width),
        compiler_params=PARAMS,
        name=name,
    )(*inputs, *constants)


def attend(packed, own, images):
    kernel = functools.partial(attend_kernel, own)
    return attend_call(kernel, images, [packed], [], GROUP_WIDTH // own * PROJ_ROWS, "attend")


def attend_back(packed, grads, own, images):
    constants = [spread_heads(own)]
    return attend_call(
        attend_back_kernel, images, [packed, grads], constants, QKV_WIDTH, "attend_back"
    )


def gelu_and_slope(values):
    factor = math.sqrt(2.0 / math.pi)
    square = values * values
    bend = jnp.tanh(factor * values * (1.0 + 0.044715 * square))
    half = 0.5 * (1.0 + bend)
    slope = half + 0.5 * values * (1.0 - bend * bend) * factor * (1.0 + 3.0 * 0.044715 * square)
    return values * half, slope


def own_forward(state, weights, modulate, own):
    qkv_weight, proj_weight, up_weight, down_weight = weights
    images, rows, columns = state.shape
    shift_one, scale_one, gate_one, shift_two, scale_two, gate_two = [
        modulate[index] for index in range(6)
    ]
    normed_one, spread_one = normalize(state)
    full_one = (normed_one * (1.0 + scale_one) + shift_one).astype(jnp.bfloat16)
    flat_one = full_one.reshape(-1, columns)
    packed = product(flat_one, qkv_weight).astype(jnp.bfloat16)
    attended = attend(packed, own, images)
    branch_one = product(attended, proj_weight).reshape(state.shape)
    middle = state + gate_one * branch_one
    normed_two, spread_two = normalize(middle)
    full_two = (normed_two * (1.0 + scale_two) + shift_two).astype(jnp.bfloat16)
    flat_two = full_two.reshape(-1, columns)
    activated, slope = gelu_and_slope(product(flat_two, up_weight))
    activated = activated.astype(jnp.bfloat16)
    branch_two = product(activated, down_weight).reshape(state.shape)
    result = middle + gate_two * branch_two
    saved = (
        normed_one,
        spread_one,
        flat_one,
        packed,
        attended,
        branch_one,
        normed_two,
        spread_two,
        flat_two,
        slope,
        activated,
        branch_two,
    )
    return (result, saved)


def own_backward(grad_out, saved, weights, modulate, own):
    (
        normed_one,
        spread_one,
        flat_one,
        packed,
        attended,
        branch_one,
        normed_two,
        spread_two,
        flat_two,
        slope,
        activated,
        branch_two,
    ) = saved
    qkv_weight, proj_weight, up_weight, down_weight = weights
    images, rows, columns = grad_out.shape
    shift_one, scale_one, gate_one, shift_two, scale_two, gate_two = [
        modulate[index] for index in range(6)
    ]
    grad_gate_two = jnp.sum(grad_out * branch_two, axis=1)
    back_two = (gate_two * grad_out).astype(jnp.bfloat16).reshape(-1, columns)
    grad_down = product(activated.T, back_two).astype(jnp.bfloat16)
    grad_pre = (product(back_two, down_weight.T) * slope).astype(jnp.bfloat16)
    grad_up = product(flat_two.T, grad_pre).astype(jnp.bfloat16)
    grad_hidden_two = product(grad_pre, up_weight.T)
    grad_hidden_two = grad_hidden_two.reshape(grad_out.shape)
    grad_shift_two = jnp.sum(grad_hidden_two, axis=1)
    grad_scale_two = jnp.sum(grad_hidden_two * normed_two, axis=1)
    grad_middle = grad_out + normalize_back(
        grad_hidden_two * (1.0 + scale_two), normed_two, spread_two
    )
    grad_gate_one = jnp.sum(grad_middle * branch_one, axis=1)
    back_one = (gate_one * grad_middle).astype(jnp.bfloat16).reshape(-1, columns)
    grad_proj = product(attended.T, back_one).astype(jnp.bfloat16)
    grad_attended = product(back_one, proj_weight.T).astype(jnp.bfloat16)
    grad_packed = attend_back(packed, grad_attended, own, images)
    grad_qkv = product(flat_one.T, grad_packed).astype(jnp.bfloat16)
    grad_hidden_one = product(grad_packed, qkv_weight.T)
    grad_hidden_one = grad_hidden_one.reshape(grad_out.shape)
    grad_shift_one = jnp.sum(grad_hidden_one, axis=1)
    grad_scale_one = jnp.sum(grad_hidden_one * normed_one, axis=1)
    grad_state = grad_middle + normalize_back(
        grad_hidden_one * (1.0 + scale_one), normed_one, spread_one
    )
    grad_mod = jnp.concatenate(
        [
            grad_shift_one,
            grad_scale_one,
            grad_gate_one,
            grad_shift_two,
            grad_scale_two,
            grad_gate_two,
        ],
        axis=1,
    )
    return (grad_state, grad_mod, (grad_qkv, grad_proj, grad_up, grad_down))


def contract(left, right, left_axis, right_axis):
    return lax.dot_general(
        left,
        right,
        (((left_axis,), (right_axis,)), ((), ())),
        preferred_element_type=jnp.float32,
    )


def contract_wide(left, right, left_axis, right_axis):
    return lax.dot_general(
        left.astype(jnp.float32),
        right.astype(jnp.float32),
        (((left_axis,), (right_axis,)), ((), ())),
        precision=highest,
        preferred_element_type=jnp.float32,
    )


def silu_back(values, grads):
    unused, pull = jax.vjp(jax.nn.silu, values)
    return pull(grads)[0]


def local(
    big_copy,
    big_master,
    big_first,
    big_second,
    ada_copy,
    ada_master,
    ada_first,
    ada_second,
    rest_copy,
    rest_master,
    rest_first,
    rest_second,
    owner_tiles,
    kept_patches,
    kept_pos,
    timestep,
    label,
    owner,
    target,
    step,
):
    groups = lax.axis_size("mp")
    ranks = lax.axis_size("dp")
    world = groups * ranks
    my_rank = lax.axis_index("dp")
    micro = kept_patches.shape[0]
    own_columns = D // world
    columns = D

    owned = big_copy.shape[1]
    all_dest, unused_slot = tile_place(owner_tiles, ranks)
    all_hot = all_dest.reshape(ranks, owned, 1) == jnp.arange(ranks)
    rounds = (jnp.max(jnp.sum(all_hot.astype(jnp.int32), axis=1)) + CHUNK_ROWS - 1) // CHUNK_ROWS
    own_tiles = lax.dynamic_slice(owner_tiles, (my_rank * owned,), (owned,))
    dest, slot = tile_place(own_tiles, ranks)
    rank, counts = rank_within(dest, ranks)
    rest_own = rest_copy.reshape(own_columns, REST_ROWS)
    edges = [0, PD, PD + FREQ, PD + FREQ + D, PD + FREQ + D + CLASSES, REST_ROWS]
    win_t, one_t, two_t, table_t, tail_t = [
        rest_own[:, edges[i] : edges[i + 1]] for i in range(5)
    ]
    ends_size = own_columns * (2 * PD + 1)
    one_size = own_columns * FREQ
    whole_numbers = jnp.concatenate([timestep[:, 0], label[:, 0]])
    told = jnp.concatenate(
        [
            jnp.concatenate([win_t, tail_t], axis=1).reshape(-1),
            one_t.reshape(-1),
            (whole_numbers // 32).astype(jnp.bfloat16),
            (whole_numbers % 32).astype(jnp.bfloat16),
        ]
    )
    told = pad_to(told, 0, -(-told.shape[0] // 2048) * 2048).reshape(-1, 128)
    told_entry = (True, told.shape[0], 128)
    brought = []

    def carry_first(buf, new_tags):
        arrays = [
            [told],
            [target.reshape(-1, 128)],
            [new_tags.reshape(ranks, -1, TAG_LANES)],
            [buf.reshape(ranks, -1, 128)],
        ]
        kinds = ("share", "swap", "swap")
        jobs = [("gather", (told_entry,), told_entry[1], LAG)]
        jobs += [(kind, (None,), 0, 0) for kind in kinds]
        got = travel(jobs, arrays, 6, "exchange_inputs")
        brought.extend(got)
        return got[3][0].reshape(buf.shape), got[2][0].reshape(new_tags.shape)

    slots, tags = tiles_to_slots(big_copy[0], dest, slot, rank, counts, rounds, carry_first)
    told = brought[0][0].reshape(groups, ranks, -1)
    facts = told[:, :, ends_size + one_size : ends_size + one_size + 4 * micro].astype(jnp.int32)
    facts = facts.reshape(world, -1)
    told = told.transpose(1, 0, 2).reshape(world, -1)
    goals = brought[1][0].reshape(ranks, micro, -1, 128)
    facts = facts[:, : 2 * micro] * 32 + facts[:, 2 * micro :]
    stamps = facts[:, :micro].reshape(-1)
    tags_all = facts[:, micro:].reshape(-1)
    ends = told[:, :ends_size].reshape(columns, -1)
    embed_weight = ends[:, :PD].T
    mask_token = ends[:, PD].astype(jnp.float32)
    head_weight = ends[:, PD + 1 :]
    count_all = micro * world
    features = jax.vmap(time_features)(stamps).astype(jnp.bfloat16)
    pre_time = contract(features, one_t, 1, 1)
    one_whole = told[:, ends_size : ends_size + one_size].reshape(columns, FREQ)
    hidden_all = jax.nn.silu(contract(features, one_whole, 1, 1)).astype(jnp.bfloat16)
    picks = (tags_all[:, None] == jnp.arange(CLASSES, dtype=jnp.int32)[None, :]).astype(
        jnp.bfloat16
    )
    cond_own = contract(hidden_all, two_t, 1, 1) + contract(picks, table_t, 1, 1)
    signal_own = jax.nn.silu(cond_own).astype(jnp.bfloat16)
    ada_own = ada_copy.reshape(own_columns, 14 * columns)
    mod_rows = micro * 14
    mod_entry = (True, 32, columns)
    padded = mod_entry[1] // micro
    mods = product(signal_own, pad_to(ada_own, 1, padded * columns)).reshape(-1, padded, columns)
    mods = mods.reshape(whole_shape(mod_entry))
    plan = (layer_plan(ranks) * 2)[:-1]
    spread = spread_slots(slots, ranks)
    wholes, mods = travel(
        (("gather", plan, 16, LAG), ("sum", (mod_entry,), 16, 6)),
        [spread[:-1], [mods]],
        1,
        "gather_weights",
    )
    last, wholes = lax.optimization_barrier((spread[-1], wholes))
    last = lax.all_gather(last, ("mp", "dp"), axis=0, tiled=True)
    weights = [whole_weights(wholes[:4], ranks), whole_weights((*wholes[4:], last), ranks)]
    own = GROUP_WIDTH // ranks
    mods = mods[0].reshape(micro, padded, columns).transpose(1, 0, 2)[:, :, None, :]
    mod_enc = mods[:6]
    mod_dec = mods[6:12]
    final_shift = mods[12]
    final_scale = mods[13]

    goal = jnp.stack([goals[owner[b, 0], b] for b in range(micro)]).reshape(micro, SEQ, PD)
    positions = jnp.asarray(position_constant(columns))
    images = ranks * groups
    inv_count = 1.0 / (PD * micro * images * KEEP)
    place = kept_pos[:, 0]
    patches = kept_patches[:, 0].astype(jnp.bfloat16)
    hits = (
        jnp.arange(SEQ, dtype=jnp.int32)[None, :, None] == place[:, None, :]
    ).astype(jnp.float32)
    hits_low = hits.astype(jnp.bfloat16)
    kept = jnp.sum(hits, axis=2)[:, :, None]
    embedded = product(patches.reshape(-1, PD), embed_weight).reshape(micro, KEEP, columns)
    embedded = embedded + jnp.take(positions, place, axis=0)
    enc_out, enc_saved = own_forward(embedded, weights[0], mod_enc, own)
    sent = enc_out.astype(jnp.bfloat16)
    dec_in = (
        jnp.einsum("bpr,brd->bpd", hits_low, sent, preferred_element_type=jnp.float32)
        + (1.0 - kept) * mask_token[None, None, :]
        + positions[None]
    )
    dec_out, dec_saved = own_forward(dec_in, weights[1], mod_dec, own)
    normed_final, spread_final = normalize(dec_out)
    head_in = (normed_final * (1.0 + final_scale) + final_shift).astype(jnp.bfloat16)
    flat_head = head_in.reshape(-1, columns)
    output = product(flat_head, head_weight).reshape(micro, SEQ, PD)
    error = output - goal
    weight = kept + MASKED_WEIGHT * (1.0 - kept)
    loss_sum = jnp.sum(weight * error * error) * inv_count

    grad_output = (2.0 * inv_count * weight * error).astype(jnp.bfloat16).reshape(-1, PD)
    grad_head = contract(grad_output, flat_head, 0, 0)
    grad_head_in = product(grad_output, head_weight.T).reshape(dec_out.shape)
    grad_final = jnp.concatenate(
        [jnp.sum(grad_head_in, axis=1), jnp.sum(grad_head_in * normed_final, axis=1)], axis=1
    )
    grad_dec_out = normalize_back(grad_head_in * (1.0 + final_scale), normed_final, spread_final)
    grad_dec_in, grad_mod_dec, dec_grads = own_backward(
        grad_dec_out, dec_saved, weights[1], mod_dec, own
    )
    last_sum = lax.psum_scatter(dec_grads[3], ("mp", "dp"), scatter_dimension=0, tiled=True)
    grad_mask = jnp.sum((1.0 - kept) * grad_dec_in, axis=(0, 1))[None, :]
    grad_sent = jnp.einsum(
        "bpr,bpd->brd",
        hits_low,
        grad_dec_in.astype(jnp.bfloat16),
        preferred_element_type=jnp.float32,
    )
    grad_embedded, grad_mod_enc, enc_grads = own_backward(
        grad_sent, enc_saved, weights[0], mod_enc, own
    )
    down_sum = lax.psum_scatter(enc_grads[3], ("mp", "dp"), scatter_dimension=0, tiled=True)
    grad_embed = contract_wide(
        patches.reshape(-1, PD), grad_embedded.reshape(-1, columns), 0, 0
    )

    vectors = jnp.concatenate([grad_mod_enc, grad_mod_dec, grad_final], axis=1)
    vectors = vectors.astype(jnp.bfloat16).reshape(mod_rows, columns)
    vectors = pad_to(vectors, 0, mod_entry[1])
    sums, vectors = travel(
        (("sum", (layer_plan(ranks)[:-1]) * 2, 16, LAG), ("gather", (mod_entry,), 16, 6)),
        [whole_parts(enc_grads, ranks)[:-1] + whole_parts(dec_grads, ranks)[:-1], [vectors]],
        2,
        "sum_gradients",
    )
    sums = [*sums[:3], down_sum.astype(jnp.float32), *sums[3:], last_sum.astype(jnp.float32)]
    sums, big_squares = collect_slots(sums, owned + 16, ranks)
    vectors = vectors[0]
    back = gather_rows(sums, tags, jnp.bfloat16)
    vectors = vectors.reshape(world, mod_entry[1], columns)[:, :mod_rows].reshape(count_all, -1)
    owned_ada = contract(signal_own, vectors, 0, 0).reshape(-1)
    grad_signal = contract(vectors, ada_own, 1, 1)
    grad_cond = silu_back(cond_own, grad_signal)
    grad_two_t = contract_wide(grad_cond, hidden_all, 0, 0)
    grad_table_t = contract_wide(grad_cond, picks, 0, 0)
    shared = jnp.concatenate(
        [contract_wide(grad_cond, two_t, 1, 0), grad_embed, grad_mask, grad_head], axis=0
    )
    shared_rows = shared.shape[0]
    shared = shared.reshape(shared_rows, ranks, groups, own_columns).transpose(2, 1, 0, 3)
    shared = pad_to(shared.reshape(world, -1), 1, 4096)
    shared_entry = (True, 32, 128)
    shared, back = travel(
        (("sum", (shared_entry,), 32, LAG), ("swap", (None,), 0, 0)),
        [[shared.reshape(whole_shape(shared_entry))], [back.reshape(ranks, -1, 128)]],
        5,
        "sum_shared",
    )
    shared = shared[0]
    shared = shared.reshape(-1)[: shared_rows * own_columns].reshape(shared_rows, own_columns)
    grad_pre = silu_back(pre_time, shared[:count_all])
    grad_one_t = contract_wide(grad_pre, features, 0, 0)
    ends_t = shared[count_all:].T
    owned_rest = jnp.concatenate(
        [ends_t[:, :PD], grad_one_t, grad_two_t, grad_table_t, ends_t[:, PD:]], axis=1
    ).reshape(-1)

    squares = jnp.sum(big_squares) + jnp.sum(owned_ada * owned_ada) + jnp.sum(owned_rest * owned_rest)
    totals = jnp.broadcast_to(pad_to(jnp.stack([loss_sum, squares]), 0, 128), (8, 128))
    totals = jnp.sum(push_all(totals, world, 8, "push_totals")[:, 0, :2], axis=0)
    back = back[0].reshape(-1, 128)
    owned_big = slots_to_tiles(sums, back, dest, slot, rank, counts, rounds)
    grad_norm = jnp.sqrt(totals[1])
    clip = jnp.minimum(1.0, MAX_NORM / (grad_norm + 1e-06))
    count = step[0].astype(jnp.float32)
    big_out = adam_update(
        owned_big.reshape(big_master.shape), big_master, big_first, big_second, clip, count
    )
    ada_out = adam_update(owned_ada, ada_master, ada_first, ada_second, clip, count)
    rest_out = adam_update(owned_rest, rest_master, rest_first, rest_second, clip, count)
    return (
        totals[:1],
        grad_norm.reshape(1),
        big_out[0],
        big_out[1],
        big_out[2],
        big_out[3],
        ada_out[0],
        ada_out[1],
        ada_out[2],
        ada_out[3],
        rest_out[0],
        rest_out[1],
        rest_out[2],
        rest_out[3],
    )


def whole_columns(mesh):
    ranks, groups = mesh.shape["dp"], mesh.shape["mp"]
    return groups == 4 and D % (ranks * groups) == 0 and ranks == 8


def solution(mesh):
    body = local if whole_columns(mesh) else local_general
    in_specs = (
        P("mp", "dp", None),
        P("mp", "dp", None),
        P("mp", "dp", None),
        P("mp", "dp", None),
        P(("dp", "mp")),
        P(("dp", "mp")),
        P(("dp", "mp")),
        P(("dp", "mp")),
        P(("dp", "mp")),
        P(("dp", "mp")),
        P(("dp", "mp")),
        P(("dp", "mp")),
        P(),
        P(None, ("dp", "mp"), None, None),
        P(None, ("dp", "mp"), None),
        P(None, ("dp", "mp")),
        P(None, ("dp", "mp")),
        P(None, ("dp", "mp")),
        P(None, ("dp", "mp"), None, None),
        P(),
    )
    out_specs = (
        P(),
        P(),
        P("mp", "dp", None),
        P("mp", "dp", None),
        P("mp", "dp", None),
        P("mp", "dp", None),
        P(("dp", "mp")),
        P(("dp", "mp")),
        P(("dp", "mp")),
        P(("dp", "mp")),
        P(("dp", "mp")),
        P(("dp", "mp")),
        P(("dp", "mp")),
        P(("dp", "mp")),
    )
    return jax.shard_map(body, mesh=mesh, in_specs=in_specs, out_specs=out_specs, check_vma=False)
```

```python
import functools
import math

import jax
import jax.numpy as jnp
import numpy as np
from jax import lax
from jax.experimental import pallas as pl
from jax.experimental.pallas import tpu as pltpu
from jax.sharding import PartitionSpec as P

D = 1152
HEADS = 16
HD = 72
FF = 4608
PD = 16
FREQ = 256
CLASSES = 1001
GRID = 16
SEQ = 256
KEEP = 128


EPS_NORM = 1e-06
MAX_NORM = 0.01
RATE = 0.02
DECAY = 0.1
BETA_ONE = 0.9
BETA_TWO = 0.999
ADAM_EPS = 1e-08
MASKED_WEIGHT = 0.1
highest = lax.Precision.HIGHEST


def partner_2(value, axis, stride):
    mask = 2**stride
    pairs = [(source, source ^ mask) for source in range(lax.axis_size(axis))]
    return lax.ppermute(value, axis, pairs)


def product(left, right):
    return jnp.dot(left, right, preferred_element_type=jnp.float32)


def normalize(values):
    center = values - jnp.mean(values, axis=-1, keepdims=True)
    spread = lax.rsqrt(jnp.mean(center * center, axis=-1, keepdims=True) + EPS_NORM)
    return (center * spread, spread)


def normalize_back(grad_normed, normed, spread):
    adjusted = grad_normed - jnp.mean(grad_normed, axis=-1, keepdims=True)
    adjusted = adjusted - normed * jnp.mean(grad_normed * normed, axis=-1, keepdims=True)
    return spread * adjusted


def position_table(columns):
    quarter = columns // 4
    omegas = 1.0 / 10000.0 ** (jnp.arange(quarter, dtype=jnp.float32) / quarter)
    places = jnp.arange(GRID * GRID, dtype=jnp.int32)

    def half_table(coords):
        angles = coords.astype(jnp.float32)[:, None] * omegas[None, :]
        return jnp.concatenate([jnp.sin(angles), jnp.cos(angles)], axis=1)

    return jnp.concatenate([half_table(places % GRID), half_table(places // GRID)], axis=1)


def position_constant(columns):
    quarter = columns // 4
    omegas = np.float32(1.0) / np.float32(10000.0) ** (np.arange(quarter, dtype=np.float32) / np.float32(quarter))
    places = np.arange(GRID * GRID)

    def half_table(coords):
        angles = (coords.astype(np.float32)[:, None] * omegas[None, :]).astype(np.float64)
        return np.concatenate([np.sin(angles), np.cos(angles)], axis=1).astype(np.float32)

    return np.concatenate([half_table(places % GRID), half_table(places // GRID)], axis=1)


def time_features(stamp):
    halves = FREQ // 2
    frequency = jnp.exp(-math.log(10000.0) * jnp.arange(halves, dtype=jnp.float32) / halves)
    angles = stamp.astype(jnp.float32) * frequency
    return jnp.concatenate([jnp.cos(angles), jnp.sin(angles)])


def row_gather(values):
    return lax.all_gather(values, "mp", axis=0, tiled=True)


def row_sum(values):
    return lax.psum_scatter(values, "mp", scatter_dimension=0, tiled=True)


def route_bit(route, bit):
    return jnp.bitwise_and(jnp.right_shift(route, bit), 1) == 1


def route_ids(values, route, levels):
    for bit in range(levels):
        partner = partner_2(values, "dp", bit)
        values = jnp.where(route_bit(route, bit), partner, values)
    return values


def route_rows(values, route, levels):
    for bit in range(levels):
        partner = partner_2(values, "dp", bit)
        values = jnp.where(route_bit(route, bit), partner, values)
    return values


def route_back(values, route, levels):
    for bit in range(levels):
        partner = partner_2(values, "dp", bit)
        values = jnp.where(route_bit(route, bit), partner, values)
    return values


def unpack_big(flat, columns, groups):
    head_width = HEADS * HD // groups
    hidden_width = FF // groups
    shapes = [
        (columns, 3 * head_width),
        (head_width, columns),
        (columns, hidden_width),
        (hidden_width, columns),
    ]
    levels = []
    offset = 0
    for level_index in range(2):
        pieces = []
        for dims in shapes:
            length = dims[0] * dims[1]
            pieces.append(flat[offset : offset + length].reshape(dims))
            offset += length
        levels.append(tuple(pieces))
    return levels


def unpack_rest(flat, columns):
    matrix = flat.reshape(columns, -1).T
    counts = [PD, FREQ, columns, CLASSES, 1, PD]
    pieces = []
    offset = 0
    for count in counts:
        pieces.append(matrix[offset : offset + count])
        offset += count
    return (pieces[0], pieces[1], pieces[2], pieces[3], pieces[4][0], pieces[5].T)


def split_heads(packed, groups, rows):
    third = packed.shape[1] // 3
    return [
        packed[:, index * third : (index + 1) * third].reshape(groups, rows, third // HD, HD)
        for index in range(3)
    ]


def attention_probs(queries, key_rows):
    scores = jnp.einsum("gqhe,gkhe->ghqk", queries, key_rows, preferred_element_type=jnp.float32)
    return jax.nn.softmax(scores * HD ** (-0.5), axis=-1)


def block_forward(state, weights, modulate):
    qkv_weight, proj_weight, up_weight, down_weight = weights
    shift_one, scale_one, gate_one, shift_two, scale_two, gate_two = jnp.split(modulate, 6)
    rows = state.shape[0]
    normed_one, spread_one = normalize(state)
    full_one = row_gather((normed_one * (1.0 + scale_one) + shift_one).astype(jnp.bfloat16))
    groups = full_one.shape[0] // rows
    packed = product(full_one, qkv_weight).astype(jnp.bfloat16)
    queries, key_rows, value_rows = split_heads(packed, groups, rows)
    probs = attention_probs(queries, key_rows)
    mixed = jnp.einsum(
        "ghqk,gkhe->gqhe",
        probs.astype(jnp.bfloat16),
        value_rows,
        preferred_element_type=jnp.float32,
    )
    attended = mixed.astype(jnp.bfloat16).reshape(groups * rows, -1)
    branch_one = row_sum(product(attended, proj_weight))
    middle = state + gate_one * branch_one
    normed_two, spread_two = normalize(middle)
    full_two = row_gather((normed_two * (1.0 + scale_two) + shift_two).astype(jnp.bfloat16))
    hidden_pre = product(full_two, up_weight)
    activated = jax.nn.gelu(hidden_pre, approximate=True).astype(jnp.bfloat16)
    branch_two = row_sum(product(activated, down_weight))
    result = middle + gate_two * branch_two
    saved = (
        normed_one,
        spread_one,
        full_one,
        packed,
        attended,
        branch_one,
        normed_two,
        spread_two,
        full_two,
        hidden_pre,
        activated,
        branch_two,
    )
    return (result, saved)


def block_backward(grad_out, saved, weights, modulate):
    (
        normed_one,
        spread_one,
        full_one,
        packed,
        attended,
        branch_one,
        normed_two,
        spread_two,
        full_two,
        hidden_pre,
        activated,
        branch_two,
    ) = saved
    qkv_weight, proj_weight, up_weight, down_weight = weights
    shift_one, scale_one, gate_one, shift_two, scale_two, gate_two = jnp.split(modulate, 6)
    rows = grad_out.shape[0]
    groups = full_one.shape[0] // rows
    grad_gate_two = jnp.sum(grad_out * branch_two, axis=0)
    back_two = row_gather((gate_two * grad_out).astype(jnp.bfloat16))
    grad_down = product(activated.T, back_two)
    grad_act = product(back_two, down_weight.T)
    unused, gelu_back = jax.vjp(lambda pre: jax.nn.gelu(pre, approximate=True), hidden_pre)
    grad_pre = gelu_back(grad_act)[0].astype(jnp.bfloat16)
    grad_up = product(full_two.T, grad_pre)
    grad_hidden_two = row_sum(product(grad_pre, up_weight.T))
    grad_shift_two = jnp.sum(grad_hidden_two, axis=0)
    grad_scale_two = jnp.sum(grad_hidden_two * normed_two, axis=0)
    grad_middle = grad_out + normalize_back(
        grad_hidden_two * (1.0 + scale_two), normed_two, spread_two
    )
    grad_gate_one = jnp.sum(grad_middle * branch_one, axis=0)
    back_one = row_gather((gate_one * grad_middle).astype(jnp.bfloat16))
    grad_proj = product(attended.T, back_one)
    grad_attended = product(back_one, proj_weight.T).astype(jnp.bfloat16)
    queries, key_rows, value_rows = split_heads(packed, groups, rows)
    probs = attention_probs(queries, key_rows)
    grad_mixed = grad_attended.reshape(queries.shape)
    grad_probs = jnp.einsum(
        "gqhe,gkhe->ghqk", grad_mixed, value_rows, preferred_element_type=jnp.float32
    )
    grad_values = jnp.einsum(
        "ghqk,gqhe->gkhe",
        probs.astype(jnp.bfloat16),
        grad_mixed,
        preferred_element_type=jnp.float32,
    )
    grad_scores = (
        probs * (grad_probs - jnp.sum(grad_probs * probs, axis=-1, keepdims=True)) * HD ** (-0.5)
    )
    grad_scores = grad_scores.astype(jnp.bfloat16)
    grad_queries = jnp.einsum(
        "ghqk,gkhe->gqhe", grad_scores, key_rows, preferred_element_type=jnp.float32
    )
    grad_keys = jnp.einsum(
        "ghqk,gqhe->gkhe", grad_scores, queries, preferred_element_type=jnp.float32
    )
    grad_packed = jnp.concatenate(
        [
            grad_part.reshape(groups * rows, -1)
            for grad_part in (grad_queries, grad_keys, grad_values)
        ],
        axis=1,
    ).astype(jnp.bfloat16)
    grad_qkv = product(full_one.T, grad_packed)
    grad_hidden_one = row_sum(product(grad_packed, qkv_weight.T))
    grad_shift_one = jnp.sum(grad_hidden_one, axis=0)
    grad_scale_one = jnp.sum(grad_hidden_one * normed_one, axis=0)
    grad_state = grad_middle + normalize_back(
        grad_hidden_one * (1.0 + scale_one), normed_one, spread_one
    )
    grad_mod = jnp.concatenate(
        [
            grad_shift_one,
            grad_scale_one,
            grad_gate_one,
            grad_shift_two,
            grad_scale_two,
            grad_gate_two,
        ]
    )
    return (grad_state, grad_mod, (grad_qkv, grad_proj, grad_up, grad_down))


def condition(stamp, tag, time_one, time_two, table):
    features = time_features(stamp).astype(jnp.bfloat16)[None, :]
    pre_time = product(features, time_one)
    hidden_time = jax.nn.silu(pre_time).astype(jnp.bfloat16)
    cond_value = product(hidden_time, time_two)[0] + table[tag].astype(jnp.float32)
    signal = jax.nn.silu(cond_value).astype(jnp.bfloat16)
    return (signal, (features, pre_time, hidden_time, cond_value))


def condition_back(grad_signal, saved, time_two, tag, table_rows):
    features, pre_time, hidden_time, cond_value = saved
    unused, silu_back = jax.vjp(jax.nn.silu, cond_value)
    grad_cond = silu_back(grad_signal)[0]
    grad_time_two = hidden_time.astype(jnp.float32).T * grad_cond[None, :]
    grad_hidden = jnp.dot(time_two.astype(jnp.float32), grad_cond, precision=highest)
    unused_pre, pre_back = jax.vjp(jax.nn.silu, pre_time)
    grad_pre = pre_back(grad_hidden[None, :])[0]
    grad_time_one = features.astype(jnp.float32).T * grad_pre
    grad_table = (jnp.arange(table_rows, dtype=jnp.int32)[:, None] == tag) * grad_cond[None, :]
    return (grad_time_one, grad_time_two, grad_table)


def adam_update(grad, master, first, second, clip, count):
    scaled = grad * clip
    first = BETA_ONE * first + (1.0 - BETA_ONE) * scaled
    second = BETA_TWO * second + (1.0 - BETA_TWO) * scaled * scaled
    fix_one = 1.0 - BETA_ONE**count
    fix_two = 1.0 - BETA_TWO**count
    master = master - RATE * (
        first / fix_one / (jnp.sqrt(second / fix_two) + ADAM_EPS) + DECAY * master
    )
    return (master, first, second, master.astype(jnp.bfloat16))


def local_general(
    big_copy,
    big_master,
    big_first,
    big_second,
    ada_copy,
    ada_master,
    ada_first,
    ada_second,
    rest_copy,
    rest_master,
    rest_first,
    rest_second,
    owner_tiles,
    kept_patches,
    kept_pos,
    timestep,
    label,
    owner,
    target,
    step,
):
    groups = lax.axis_size("mp")
    ranks = lax.axis_size("dp")
    levels_dp = ranks.bit_length() - 1
    my_rank = lax.axis_index("dp")
    tiles = owner_tiles.shape[0]
    columns = D
    gathered = lax.all_gather(big_copy, "dp", axis=1, tiled=True)[0]
    inverse = jnp.zeros((tiles,), jnp.int32).at[owner_tiles].set(jnp.arange(tiles, dtype=jnp.int32))
    big_flat = jnp.take(gathered, inverse, axis=0).reshape(-1)
    ada_flat, rest_flat = (
        lax.all_gather(ada_copy, ("dp", "mp"), axis=0, tiled=True),
        lax.all_gather(rest_copy, ("dp", "mp"), axis=0, tiled=True),
    )
    levels = unpack_big(big_flat, columns, groups)
    ada_matrix = ada_flat.reshape(columns, 14 * columns)
    embed_weight, time_one, time_two, table, mask_token, head_weight = unpack_rest(
        rest_flat, columns
    )
    positions = position_table(columns)
    images = ranks * groups
    inv_count = 1.0 / (PD * kept_patches.shape[0] * images * KEEP)
    zeros_six = jnp.zeros((6 * columns,), jnp.bfloat16)
    zeros_eight = jnp.zeros((8 * columns,), jnp.bfloat16)

    def micro_step(carry, inputs):
        grads_big, grads_rest, loss_sum = carry
        patches, place, stamp, tag, dest, goal = inputs
        route = jnp.bitwise_xor(dest, my_rank)
        signal_enc, saved_enc = condition(stamp, tag, time_one, time_two, table)
        mod_enc = product(signal_enc[None, :], ada_matrix[:, : 6 * columns])[0]
        embedded = product(patches.astype(jnp.bfloat16), embed_weight) + jnp.take(
            positions, place, axis=0
        )
        enc_out, enc_saved = block_forward(embedded, levels[0], mod_enc)
        sent = enc_out.astype(jnp.bfloat16)
        meta = jnp.concatenate([place, stamp[None], tag[None]])
        got_meta = route_ids(meta, route, levels_dp)
        arrived = route_rows(sent, route, levels_dp)
        keep_rows = place.shape[0]
        dec_place = got_meta[:keep_rows]
        dec_tag = got_meta[keep_rows + 1]
        signal_dec, saved_dec = condition(got_meta[keep_rows], dec_tag, time_one, time_two, table)
        mod_dec = product(signal_dec[None, :], ada_matrix[:, 6 * columns :])[0]
        hits = jnp.arange(SEQ, dtype=jnp.int32)[:, None] == dec_place[None, :]
        kept = jnp.sum(hits.astype(jnp.float32), axis=1, keepdims=True)
        dec_in = (
            product(hits.astype(jnp.bfloat16), arrived)
            + (1.0 - kept) * mask_token.astype(jnp.float32)[None, :]
            + positions
        )
        dec_out, dec_saved = block_forward(dec_in, levels[1], mod_dec[: 6 * columns])
        final_shift = mod_dec[6 * columns : 7 * columns]
        final_scale = mod_dec[7 * columns :]
        normed_final, spread_final = normalize(dec_out)
        head_in = (normed_final * (1.0 + final_scale) + final_shift).astype(jnp.bfloat16)
        output = product(head_in, head_weight)
        error = output - goal
        weight = kept + MASKED_WEIGHT * (1.0 - kept)
        loss_part = jnp.sum(weight * error * error) * inv_count
        grad_output = (2.0 * inv_count * weight * error).astype(jnp.bfloat16)
        grad_head = product(head_in.T, grad_output)
        grad_head_in = product(grad_output, head_weight.T)
        grad_final = jnp.concatenate(
            [jnp.sum(grad_head_in, axis=0), jnp.sum(grad_head_in * normed_final, axis=0)]
        )
        grad_dec_out = normalize_back(
            grad_head_in * (1.0 + final_scale), normed_final, spread_final
        )
        grad_dec_in, grad_mod_dec, dec_grads = block_backward(
            grad_dec_out, dec_saved, levels[1], mod_dec[: 6 * columns]
        )
        grad_mask = jnp.sum((1.0 - kept) * grad_dec_in, axis=0)
        grad_arrived = jnp.take(grad_dec_in, dec_place, axis=0).astype(jnp.bfloat16)
        grad_sent = route_back(grad_arrived, route, levels_dp)
        grad_embedded, grad_mod_enc, enc_grads = block_backward(
            grad_sent.astype(jnp.float32), enc_saved, levels[0], mod_enc
        )
        grad_embed = jnp.dot(
            patches.astype(jnp.bfloat16).astype(jnp.float32).T, grad_embedded, precision=highest
        )
        vector_enc = grad_mod_enc.astype(jnp.bfloat16)
        vector_dec = jnp.concatenate([grad_mod_dec, grad_final]).astype(jnp.bfloat16)
        grad_signal_enc = product(ada_matrix[:, : 6 * columns], vector_enc)
        grad_signal_dec = product(ada_matrix[:, 6 * columns :], vector_dec)
        time_enc = condition_back(grad_signal_enc, saved_enc, time_two, tag, table.shape[0])
        time_dec = condition_back(grad_signal_dec, saved_dec, time_two, dec_tag, table.shape[0])
        rest_terms = [
            grad_embed,
            time_enc[0] + time_dec[0],
            time_enc[1] + time_dec[1],
            time_enc[2] + time_dec[2],
            grad_mask[None, :],
            grad_head.T,
        ]
        grads_rest = grads_rest + jnp.concatenate(rest_terms, axis=0)
        big_terms = [
            term.reshape(-1) for level_grads in (enc_grads, dec_grads) for term in level_grads
        ]
        grads_big = grads_big + jnp.concatenate(big_terms)
        signal_pair = jnp.stack([signal_enc, signal_dec])
        vector_pair = jnp.stack(
            [jnp.concatenate([vector_enc, zeros_eight]), jnp.concatenate([zeros_six, vector_dec])]
        )
        return ((grads_big, grads_rest, loss_sum + loss_part), (signal_pair, vector_pair))

    inputs = (
        kept_patches[:, 0],
        kept_pos[:, 0],
        timestep[:, 0],
        label[:, 0],
        owner[:, 0],
        target[:, 0],
    )
    start_carry = (
        jnp.zeros(big_flat.shape, jnp.float32),
        jnp.zeros((rest_flat.shape[0] // columns, columns), jnp.float32),
        jnp.zeros((), jnp.float32),
    )
    finals, factors = lax.scan(micro_step, start_carry, inputs)
    grads_big, grads_matrix, loss_sum = finals
    grads_rest = grads_matrix.T.reshape(-1)
    signal_rows = factors[0].reshape(-1, columns)
    vector_rows = factors[1].reshape(-1, 14 * columns)
    tile_part = jnp.take(grads_big.reshape(tiles, 128), owner_tiles, axis=0)
    owned_big = lax.psum_scatter(tile_part, "dp", scatter_dimension=0, tiled=True)
    local_ada = product(signal_rows.T, vector_rows).reshape(-1)
    owned_ada, owned_rest = (
        lax.psum_scatter(local_ada, ("dp", "mp"), scatter_dimension=0, tiled=True),
        lax.psum_scatter(grads_rest, ("dp", "mp"), scatter_dimension=0, tiled=True),
    )
    squares = (
        jnp.sum(owned_big * owned_big)
        + jnp.sum(owned_ada * owned_ada)
        + jnp.sum(owned_rest * owned_rest)
    )
    loss_total, square_total = lax.psum((loss_sum, squares), ("dp", "mp"))
    grad_norm = jnp.sqrt(square_total)
    clip = jnp.minimum(1.0, MAX_NORM / (grad_norm + 1e-06))
    count = step[0].astype(jnp.float32)
    big_out = adam_update(
        owned_big.reshape(big_master.shape), big_master, big_first, big_second, clip, count
    )
    ada_out = adam_update(owned_ada, ada_master, ada_first, ada_second, clip, count)
    rest_out = adam_update(owned_rest, rest_master, rest_first, rest_second, clip, count)
    return (
        loss_total.reshape(1),
        grad_norm.reshape(1),
        big_out[0],
        big_out[1],
        big_out[2],
        big_out[3],
        ada_out[0],
        ada_out[1],
        ada_out[2],
        ada_out[3],
        rest_out[0],
        rest_out[1],
        rest_out[2],
        rest_out[3],
    )


CHUNK_ROWS = 1088
TAG_LANES = 64
REST_ROWS = 2 * PD + FREQ + D + CLASSES + 1


def tile_place(tiles, ranks):
    counts = [count // ranks for count in matrix_tiles()]
    layer_tiles = sum(matrix_tiles())
    level = tiles // layer_tiles
    inside = tiles % layer_tiles
    dest = jnp.zeros_like(tiles)
    slot = jnp.zeros_like(tiles)
    start = 0
    base = 0
    for count, total in zip(counts, matrix_tiles()):
        local_tile = inside - start
        here = (local_tile >= 0) & (local_tile < total)
        dest = jnp.where(here, local_tile // count, dest)
        slot = jnp.where(here, base + level * count + local_tile % count, slot)
        start += total
        base += 2 * count
    return dest, slot


def matrix_tiles():
    groups = 4
    head_width = HEADS * HD // groups
    hidden_width = FF // groups
    sizes = [D * 3 * head_width, head_width * D, D * hidden_width, hidden_width * D]
    return [size // 128 for size in sizes]


def rank_within(dest, ranks):
    n = dest.shape[0]
    inner = 96
    outer = n // inner
    hot = (dest.reshape(outer, inner)[None] == jnp.arange(ranks)[:, None, None]).astype(jnp.bfloat16)
    upto = (jnp.arange(inner)[:, None] < jnp.arange(inner)[None, :]).astype(jnp.bfloat16)
    before = jnp.einsum("roi,ij->roj", hot, upto, preferred_element_type=jnp.float32)
    totals = jnp.sum(hot.astype(jnp.float32), axis=2)
    over = (jnp.arange(outer)[:, None] < jnp.arange(outer)[None, :]).astype(jnp.float32)
    prior = jnp.dot(totals, over, precision=highest)
    rank = jnp.sum(hot.astype(jnp.float32) * (before + prior[:, :, None]), axis=0)
    return rank.astype(jnp.int32).reshape(n), jnp.sum(totals, axis=1).astype(jnp.int32)


def widen(source, dest, rows):
    step = 128 if rows % 128 == 0 else 16
    whole = rows // step

    def body(i, unused):
        at = pl.ds(pl.multiple_of(i * step, step), step)
        dest[at, :] = source[at, :].astype(dest.dtype)
        return unused

    lax.fori_loop(0, whole, body, 0)


def pack_kernel(n, pos_ref, x_ref, buf_ref, wide, sorted_rows):
    widen(x_ref, wide, n)

    def move(i, unused):
        places = [pos_ref[i * 16 + j] for j in range(16)]
        rows = [wide[pl.ds(i * 16 + j, 1), :] for j in range(16)]
        for place, row in zip(places, rows):
            sorted_rows[pl.ds(place, 1), :] = row
        return unused

    lax.fori_loop(0, n // 16, move, 0)
    widen(sorted_rows, buf_ref, buf_ref.shape[0])


def scatter_kernel(total, tag_ref, buf_ref, out_ref, wide, slots):
    widen(buf_ref, wide, total)

    def move(i, unused):
        tags = [tag_ref[i * 16 + j] for j in range(16)]
        rows = [wide[pl.ds(i * 16 + j, 1), :] for j in range(16)]
        for tag, row in zip(tags, rows):
            slots[pl.ds(tag, 1), :] = row
        return unused

    lax.fori_loop(0, total // 16, move, 0)
    widen(slots, out_ref, out_ref.shape[0])


def gather_kernel(total, index_ref, x_ref, out_ref, wide_out):
    def move(i, unused):
        index = [index_ref[i * 16 + j] for j in range(16)]
        rows = [x_ref[pl.ds(place, 1), :] for place in index]
        for j in range(16):
            wide_out[pl.ds(i * 16 + j, 1), :] = rows[j]
        return unused

    lax.fori_loop(0, total // 16, move, 0)
    widen(wide_out, out_ref, total)


SMEM = pl.BlockSpec(memory_space=pltpu.SMEM)
VMEM = pl.BlockSpec(memory_space=pltpu.VMEM)
PARAMS = pltpu.CompilerParams(vmem_limit_bytes=48 * 1024 * 1024)


def pack_rows(rows, pos, total):
    n = rows.shape[0]
    return pl.pallas_call(
        functools.partial(pack_kernel, n),
        out_shape=jax.ShapeDtypeStruct((total, 128), jnp.bfloat16),
        in_specs=[SMEM, VMEM],
        out_specs=VMEM,
        scratch_shapes=[
            pltpu.VMEM((n, 128), jnp.float32),
            pltpu.VMEM((total + 16, 128), jnp.float32),
        ],
        compiler_params=PARAMS,
        name="pack_rows",
    )(pos, rows)


def pack_tags(pos, slot, fill, capacity):
    n = pos.shape[0]
    total = fill.shape[0] * capacity
    lines = total // TAG_LANES
    here = (pos // TAG_LANES)[:, None] == jnp.arange(lines)[None, :]
    high = jnp.where(here, (slot // 128)[:, None], 0)
    low = jnp.where(here, (slot % 128)[:, None], 0)
    lanes = ((pos % TAG_LANES)[:, None] == jnp.arange(TAG_LANES)[None, :]).astype(jnp.bfloat16)
    parts = jnp.concatenate([high, low], axis=1).astype(jnp.bfloat16)
    found = contract(parts, lanes, 0, 0).astype(jnp.int32)
    tags = (found[:lines] * 128 + found[lines:]).reshape(fill.shape[0], capacity)
    return jnp.where(jnp.arange(capacity)[None, :] < fill[:, None], tags, n).reshape(-1)


def scatter_rows(rows, tags, n):
    total = rows.shape[0]
    return pl.pallas_call(
        functools.partial(scatter_kernel, total),
        out_shape=jax.ShapeDtypeStruct((n + 16, 128), jnp.bfloat16),
        in_specs=[SMEM, VMEM],
        out_specs=VMEM,
        scratch_shapes=[
            pltpu.VMEM((total, 128), jnp.float32),
            pltpu.VMEM((n + 16, 128), jnp.float32),
        ],
        compiler_params=PARAMS,
        name="scatter_rows",
    )(tags, rows)


def gather_rows(rows, index, dtype):
    total = index.shape[0]
    return pl.pallas_call(
        functools.partial(gather_kernel, total),
        out_shape=jax.ShapeDtypeStruct((total, 128), dtype),
        in_specs=[SMEM, VMEM],
        out_specs=VMEM,
        scratch_shapes=[pltpu.VMEM((total, 128), jnp.float32)],
        compiler_params=PARAMS,
        name="gather_rows",
    )(index, rows)


MESH = pl.DeviceIdType.MESH
LAG = 2
SLOTS = 4
GATHER_SLOTS = 12


def coordinates():
    rank = lax.axis_index("dp")
    group = lax.axis_index("mp")
    return lax.div(rank, 2), lax.rem(rank, 2), lax.div(group, 2), lax.rem(group, 2)


def device_at(z, x, y, core):
    return (z * 2 + x, y * 2 + core)


def neighbours():
    z, x, y, core = coordinates()
    along_x = device_at(z, 1 - x, y, core)
    along_y = device_at(z, x, 1 - y, core)
    first = tuple(jnp.where(core == 0, b, a) for a, b in zip(along_x, along_y))
    second = tuple(jnp.where(core == 0, a, b) for a, b in zip(along_x, along_y))
    others = [device_at(lax.rem(z + step, 4), x, y, core) for step in (1, 2, 3)]
    return device_at(z, x, y, 1 - core), first, second, others


def greet(peers):
    barrier = pltpu.get_barrier_semaphore()
    for peer in peers:
        pl.semaphore_signal(barrier, inc=1, device_id=peer, device_id_type=MESH)
    pl.semaphore_wait(barrier, len(peers))


def block_of(ref, entry, group, at, side=None):
    stacked, rows, width = entry
    sides = slice(None) if side is None else side
    if stacked:
        return ref.at[group, :, sides, at, :]
    return ref.at[:, sides, at, pl.ds(pl.multiple_of(group * width, 128), width)]


def slice_of(ref, entry, group, z, x, at):
    stacked, rows, width = entry
    if stacked:
        return ref.at[group, z, x, at, :]
    return ref.at[z, x, at, pl.ds(pl.multiple_of(group * width, 128), width)]


def chunk_ranges(plan, chunk):
    ranges = []
    start = 0
    for stacked, rows, width in plan:
        ranges.append((start, start + rows // chunk))
        start += rows // chunk
    return ranges, start


def in_range(unit, low, high):
    return (unit >= low) & (unit < high)


def remote(source, target, send, receive, peer):
    return pltpu.make_async_remote_copy(
        src_ref=source,
        dst_ref=target,
        send_sem=send,
        recv_sem=receive,
        device_id=peer,
        device_id_type=MESH,
    )


def gather_job(plan, chunk, lag, slices, wholes, scratch):
    count = len(plan)
    held, other_held, own_sem, out_sem, z_send, z_recv, a_send, a_recv, b_send, b_recv, c_send, c_recv = scratch
    z, x, y, core = coordinates()
    other, first, second, others = neighbours()
    mine_first = jnp.where(core == 0, y, x)
    mine_second = jnp.where(core == 0, x, y)
    ranges, total = chunk_ranges(plan, chunk)

    def copies(stage, k, unit):
        entry = plan[k]
        slot = lax.rem(unit, GATHER_SLOTS)
        at = pl.ds(pl.multiple_of((unit - ranges[k][0]) * chunk, chunk), chunk)
        cols = pl.ds(0, entry[2])
        own = held.at[slot, mine_first, mine_second, z, :, cols]
        if stage == 0:
            source = slices[k].at[at, :]
            return [pltpu.make_async_copy(source, own, own_sem.at[slot])] + [
                remote(source, own, z_send.at[i, slot], z_recv.at[i, slot], others[i])
                for i in range(3)
            ]
        if stage == 1:
            part = held.at[slot, mine_first, mine_second, :, :, cols]
            return [remote(part, part, a_send.at[slot], a_recv.at[slot], second)]
        if stage == 2:
            part = held.at[slot, mine_first, :, :, :, cols]
            return [remote(part, part, b_send.at[slot], b_recv.at[slot], first)]
        if stage == 3:
            source = held.at[slot, :, :, :, :, cols]
            target = other_held.at[slot, :, :, :, :, cols]
            return [remote(source, target, c_send.at[slot], c_recv.at[slot], other)]
        made = []
        from_other = stage == 5
        ref, owner = (other_held, 1 - core) if from_other else (held, core)
        for i in range(2):
            for j in range(2):
                side = jnp.where(owner == 0, j, i)
                group = 2 * jnp.where(owner == 0, i, j) + owner
                made.append(
                    pltpu.make_async_copy(
                        ref.at[slot, i, j, :, :, cols],
                        block_of(wholes[k], entry, group, at, side),
                        out_sem.at[int(from_other), 2 * i + j, slot],
                    )
                )
        return made

    def go(unit, waits, starts):
        for k in range(count):

            @pl.when(in_range(unit, *ranges[k]))
            def _(k=k):
                for stage in waits:
                    for copy in copies(stage, k, unit):
                        copy.wait()
                for stage in starts:
                    for copy in copies(stage, k, unit):
                        copy.start()

    def step(t):
        go(t - 1 - 4 * lag, (4, 5), ())
        go(t - 4 * lag, (3,), (5,))
        go(t - 3 * lag, (2,), (3, 4))
        go(t - 2 * lag, (1,), (2,))
        go(t - lag, (0,), (1,))
        go(t, (), (0,))

    return step, total + 1 + 4 * lag


def whole_shape(entry):
    stacked, rows, width = entry
    return (4, 4, 2, rows, width) if stacked else (4, 2, rows, 4 * width)


def gather_scratch(plan, chunk, kind):
    dma = pltpu.SemaphoreType.DMA
    held = pltpu.VMEM((GATHER_SLOTS, 2, 2, 4, chunk, max(entry[2] for entry in plan)), kind)
    each = dma((GATHER_SLOTS,))
    three = dma((3, GATHER_SLOTS))
    return [held, held, each, dma((2, 4, GATHER_SLOTS)), three, three] + [each] * 6


def sum_job(plan, chunk, lag, parts, outs, scratch):
    count = len(plan)
    own, from_core, from_first, from_second, from_z, half, quarter, eighth = scratch[:8]
    own_sem, core_send, core_recv, a_send, a_recv, b_send, b_recv, z_send, z_recv = scratch[8:]
    z, x, y, core = coordinates()
    other, first, second, others = neighbours()
    mine_first = jnp.where(core == 0, y, x)
    mine_second = jnp.where(core == 0, x, y)
    ranges, total = chunk_ranges(plan, chunk)

    def copies(stage, width, unit, k=None):
        slot = lax.rem(unit, SLOTS)
        pair = lax.rem(unit, 2)
        cols = pl.ds(0, width)
        if stage == 0:
            made = []
            for j in range(2):
                mine = own.at[pair, j, :, :, :, cols]
                theirs = from_core.at[pair, j, :, :, :, cols]
                if k is None:
                    made.append(pltpu.make_async_copy(mine, mine, own_sem.at[j, pair]))
                    made.append(remote(mine, theirs, core_send.at[j, pair], core_recv.at[j, pair], other))
                else:
                    at = pl.ds(pl.multiple_of((unit - ranges[k][0]) * chunk, chunk), chunk)
                    kept = block_of(parts[k], plan[k], 2 * j + core, at)
                    sent = block_of(parts[k], plan[k], 2 * j + 1 - core, at)
                    made.append(pltpu.make_async_copy(kept, mine, own_sem.at[j, pair]))
                    made.append(remote(sent, theirs, core_send.at[j, pair], core_recv.at[j, pair], other))
            return made
        if stage == 1:
            source = half.at[slot, 1 - mine_first, :, :, :, cols]
            target = from_first.at[slot, :, :, :, cols]
            return [remote(source, target, a_send.at[slot], a_recv.at[slot], first)]
        if stage == 2:
            source = quarter.at[slot, 1 - mine_second, :, :, cols]
            target = from_second.at[slot, :, :, cols]
            return [remote(source, target, b_send.at[slot], b_recv.at[slot], second)]
        made = []
        for i in range(3):
            source = eighth.at[slot, lax.rem(z + i + 1, 4), :, cols]
            target = from_z.at[slot, i, :, cols]
            made.append(remote(source, target, z_send.at[i, slot], z_recv.at[i, slot], others[i]))
        return made

    def wide(ref, index, cols):
        return ref[(*index, slice(None), cols)].astype(jnp.float32)

    def add(stage, width, unit):
        slot = lax.rem(unit, SLOTS)
        pair = lax.rem(unit, 2)
        cols = slice(0, width)
        if stage == 0:
            for i in range(2):
                for j in range(2):
                    lead = jnp.where(core == 0, i, j)
                    last = jnp.where(core == 0, j, i)
                    for k in range(4):
                        value = wide(own, (pair, i, k, j), cols) + wide(from_core, (pair, i, k, j), cols)
                        half[slot, lead, last, k, :, cols] = value.astype(half.dtype)
        elif stage == 1:
            for j in range(2):
                for k in range(4):
                    value = wide(half, (slot, mine_first, j, k), cols) + wide(
                        from_first, (slot, j, k), cols
                    )
                    quarter[slot, j, k, :, cols] = value.astype(quarter.dtype)
        else:
            for k in range(4):
                value = wide(quarter, (slot, mine_second, k), cols) + wide(
                    from_second, (slot, k), cols
                )
                eighth[slot, k, :, cols] = value.astype(eighth.dtype)

    widths = sorted({entry[2] for entry in plan})

    def go(unit, stage):
        for width in widths:
            inside = functools.reduce(
                jnp.logical_or,
                [in_range(unit, *ranges[k]) for k in range(count) if plan[k][2] == width],
            )

            @pl.when(inside)
            def _(width=width):
                for copy in copies(stage, width, unit):
                    copy.wait()
                add(stage, width, unit)
                for copy in copies(stage + 1, width, unit):
                    copy.start()

    def finish(unit):
        for k in range(count):

            @pl.when(in_range(unit, *ranges[k]))
            def _(k=k):
                width = plan[k][2]
                slot = lax.rem(unit, SLOTS)
                cols = slice(0, width)
                for copy in copies(3, width, unit):
                    copy.wait()
                at = pl.ds(pl.multiple_of((unit - ranges[k][0]) * chunk, chunk), chunk)
                value = wide(eighth, (slot, z), cols)
                for i in range(3):
                    value = value + wide(from_z, (slot, i), cols)
                outs[k][at, :] = value

    def begin(unit):
        for k in range(count):

            @pl.when(in_range(unit, *ranges[k]))
            def _(k=k):
                for copy in copies(0, plan[k][2], unit, k):
                    copy.start()

    def step(t):
        finish(t - 1 - 3 * lag)
        go(t - 1 - 2 * lag, 2)
        go(t - 1 - lag, 1)
        go(t - 1, 0)
        begin(t)

    return step, total + 1 + 3 * lag


def sum_scratch(plan, chunk, kind):
    dma = pltpu.SemaphoreType.DMA
    width = max(entry[2] for entry in plan)
    buffers = [
        (2, 2, 4, 2, chunk, width),
        (2, 2, 4, 2, chunk, width),
        (SLOTS, 2, 4, chunk, width),
        (SLOTS, 4, chunk, width),
        (SLOTS, 3, chunk, width),
        (SLOTS, 2, 2, 4, chunk, width),
        (SLOTS, 2, 4, chunk, width),
        (SLOTS, 4, chunk, width),
    ]
    return (
        [pltpu.VMEM(shape, kind) for shape in buffers]
        + [dma((2, 2))] * 3
        + [dma((SLOTS,))] * 4
        + [dma((3, SLOTS))] * 2
    )


def direct_job(kind, sources, targets, scratch):
    source, target = sources[0], targets[0]
    own_sem, send_sem, recv_sem = scratch
    ranks, groups = lax.axis_size("dp"), lax.axis_size("mp")
    rank, group = lax.axis_index("dp"), lax.axis_index("mp")
    me, count = (rank * groups + group, ranks * groups) if kind == "push" else (rank, ranks)

    def part(index):
        return source.at[index] if kind == "swap" else source

    own = pltpu.make_async_copy(part(me), target.at[me], own_sem)

    def copy(i):
        to = lax.rem(me + i, count)
        peer = (lax.div(to, groups), lax.rem(to, groups)) if kind == "push" else (to, group)
        return remote(part(to), target.at[me], send_sem.at[i], recv_sem.at[i], peer)

    def start(i, unused):
        copy(i).start()
        return unused

    def finish(i, unused):
        copy(i).wait()
        return unused

    def begin():
        own.start()
        lax.fori_loop(1, count, start, 0)

    def end():
        own.wait()
        lax.fori_loop(1, count, finish, 0)

    return begin, end


def travel_kernel(jobs, scratch_counts, *refs):
    refs = list(refs)

    def take(number):
        taken = refs[:number]
        del refs[:number]
        return taken

    sources = [take(len(job[1])) for job in jobs]
    targets = [take(len(job[1])) for job in jobs]
    scratch = [take(number) for number in scratch_counts]
    steps = []
    direct = []
    for (kind, plan, chunk, lag), source, target, mine in zip(jobs, sources, targets, scratch):
        if kind == "gather":
            steps.append(gather_job(plan, chunk, lag, source, target, mine))
        elif kind == "sum":
            steps.append(sum_job(plan, chunk, lag, source, target, mine))
        else:
            direct.append(direct_job(kind, source, target, mine))
    if direct:
        greet_all()
    else:
        other, first, second, others = neighbours()
        greet([other, first, second] + others)

    def step(t, unused):
        for one, unused_count in steps:
            one(t)
        return unused

    if direct and steps:
        step(0, 0)
    for begin, unused_end in direct:
        begin()
    if steps:
        first_step = 1 if direct else 0
        lax.fori_loop(first_step, max(count for unused_step, count in steps), step, 0)
    for unused_begin, end in direct:
        end()


def greet_all():
    groups = lax.axis_size("mp")
    world = lax.axis_size("dp") * groups
    me = lax.axis_index("dp") * groups + lax.axis_index("mp")
    barrier = pltpu.get_barrier_semaphore()

    def hail(i, unused):
        to = lax.rem(me + i, world)
        peer = (lax.div(to, groups), lax.rem(to, groups))
        pl.semaphore_signal(barrier, inc=1, device_id=peer, device_id_type=MESH)
        return unused

    lax.fori_loop(1, world, hail, 0)
    pl.semaphore_wait(barrier, world - 1)


def travel(jobs, arrays, number, name):
    ANY = pl.BlockSpec(memory_space=pl.ANY)
    dma = pltpu.SemaphoreType.DMA
    ranks, groups = lax.axis_size("dp"), lax.axis_size("mp")
    scratch = []
    shapes = []
    specs = []
    for (kind, plan, chunk, unused_lag), mine in zip(jobs, arrays):
        dtype = mine[0].dtype
        if kind == "gather":
            scratch.append(gather_scratch(plan, chunk, dtype))
            shapes += [jax.ShapeDtypeStruct(whole_shape(entry), dtype) for entry in plan]
            specs += [ANY] * len(plan)
        elif kind == "sum":
            scratch.append(sum_scratch(plan, chunk, dtype))
            shapes += [jax.ShapeDtypeStruct(entry[1:], jnp.float32) for entry in plan]
            specs += [VMEM] * len(plan)
        else:
            count = ranks * groups if kind == "push" else ranks
            scratch.append([dma, dma((count,)), dma((count,))])
            shape = mine[0].shape if kind == "swap" else (count,) + mine[0].shape
            shapes.append(jax.ShapeDtypeStruct(shape, dtype))
            specs.append(ANY)
    flat = [array for mine in arrays for array in mine]
    outs = pl.pallas_call(
        functools.partial(travel_kernel, jobs, [len(mine) for mine in scratch]),
        out_shape=shapes,
        in_specs=[
            VMEM if job[0] == "gather" else ANY for job, mine in zip(jobs, arrays) for unused in mine
        ],
        out_specs=specs,
        scratch_shapes=[one for mine in scratch for one in mine],
        compiler_params=pltpu.CompilerParams(
            collective_id=number, has_side_effects=True, vmem_limit_bytes=48 * 1024 * 1024
        ),
        name=name,
    )(*flat)
    results = []
    for unused_kind, plan, unused_chunk, unused_lag in jobs:
        results.append(outs[: len(plan)])
        outs = outs[len(plan) :]
    return results


def push_kernel(world, x_ref, out_ref, send_sem, recv_sem):
    groups = lax.axis_size("mp")
    me = lax.axis_index("dp") * groups + lax.axis_index("mp")

    def peer(i):
        to = lax.rem(me + i, world)
        return (lax.div(to, groups), lax.rem(to, groups))

    barrier = pltpu.get_barrier_semaphore()

    def hail(i, unused):
        pl.semaphore_signal(barrier, inc=1, device_id=peer(i), device_id_type=MESH)
        return unused

    lax.fori_loop(1, world, hail, 0)
    out_ref[me] = x_ref[...]
    pl.semaphore_wait(barrier, world - 1)

    def copy(i):
        return remote(x_ref, out_ref.at[me], send_sem.at[i], recv_sem.at[i], peer(i))

    def start(i, unused):
        copy(i).start()
        return unused

    def finish(i, unused):
        copy(i).wait()
        return unused

    lax.fori_loop(1, world, start, 0)
    lax.fori_loop(1, world, finish, 0)


def push_all(value, world, number, name):
    dma = pltpu.SemaphoreType.DMA
    return pl.pallas_call(
        functools.partial(push_kernel, world),
        out_shape=jax.ShapeDtypeStruct((world,) + value.shape, value.dtype),
        in_specs=[VMEM],
        out_specs=VMEM,
        scratch_shapes=[dma((world,)), dma((world,))],
        compiler_params=pltpu.CompilerParams(collective_id=number, has_side_effects=True),
        name=name,
    )(value)


def swap_ranks(buf, ranks):
    rest = buf.shape[1:]
    split = buf.reshape((ranks, buf.shape[0] // ranks) + rest)
    return lax.all_to_all(split, "dp", 0, 0).reshape(buf.shape)


def round_positions(dest, rank, counts, capacity, turn):
    ranks = counts.shape[0]
    low = turn * capacity
    inside = (rank >= low) & (rank < low + capacity)
    pos = jnp.where(inside, dest * capacity + rank - low, ranks * capacity)
    fill = jnp.clip(counts - low, 0, capacity)
    return pos, fill, inside


def tiles_to_slots(rows, dest, slot, rank, counts, rounds, carry_first):
    n = rows.shape[0]
    ranks = counts.shape[0]
    total = ranks * CHUNK_ROWS

    def packed(turn):
        pos, fill, unused = round_positions(dest, rank, counts, CHUNK_ROWS, turn)
        return pack_rows(rows, pos, total), pack_tags(pos, slot, fill, CHUNK_ROWS)

    got, tags = carry_first(*packed(0))
    first = scatter_rows(got, tags, n)

    def more(carry):
        turn, slots = carry
        more_rows, more_tags = [swap_ranks(part, ranks) for part in packed(turn)]
        added = scatter_rows(more_rows, more_tags, n)
        fresh = jnp.zeros((n + 16,), jnp.bool_).at[more_tags].set(True)
        return turn + 1, jnp.where(fresh[:, None], added, slots)

    slots = lax.cond(
        rounds > 1,
        lambda start: lax.while_loop(lambda carry: carry[0] < rounds, more, (1, start))[1],
        lambda start: start,
        first,
    )
    return slots, tags


def slots_to_tiles(slots, first, dest, slot, rank, counts, rounds):
    ranks = counts.shape[0]
    total = ranks * CHUNK_ROWS

    def landed(got, turn):
        pos, unused, inside = round_positions(dest, rank, counts, CHUNK_ROWS, turn)
        return gather_rows(got, jnp.minimum(pos, total - 1), jnp.float32), inside

    def more(carry):
        turn, rows = carry
        pos, fill, unused = round_positions(dest, rank, counts, CHUNK_ROWS, turn)
        turn_tags = swap_ranks(pack_tags(pos, slot, fill, CHUNK_ROWS), ranks)
        got = swap_ranks(gather_rows(slots, turn_tags, jnp.bfloat16), ranks)
        added, inside = landed(got.astype(jnp.float32), turn)
        return turn + 1, jnp.where(inside[:, None], added, rows)

    start = (1, landed(first.astype(jnp.float32), 0)[0])
    unused, rows = lax.while_loop(lambda carry: carry[0] < rounds, more, start)
    return rows


QKV_WIDTH = 896
PROJ_ROWS = 48


def layer_plan(ranks):
    return (
        (False, D // ranks, QKV_WIDTH),
        (True, PROJ_ROWS, D),
        (False, D // ranks, FF // 4),
        (True, FF // 4 // ranks, D),
    )


def pad_to(values, axis, size):
    widths = [(0, 0)] * values.ndim
    widths[axis] = (0, size - values.shape[axis])
    return jnp.pad(values, widths)


def slice_places(ranks):
    widths = [3 * HEADS * HD // 4, D, FF // 4, D]
    places = []
    base = 0
    for total, width in zip(matrix_tiles(), widths):
        count = total // ranks
        places.append((count * 128 // width, width, (base, base + count)))
        base += 2 * count
    return places


SPARE_ROWS = 24


def row_group(width):
    rows = 128 // math.gcd(width, 128)
    return rows, rows * width // 128


def lane_pieces(start, size, source_width):
    pieces = []
    done = 0
    while done < size:
        row, column = divmod(start + done, source_width)
        block, lane = divmod(column, 128)
        length = min(128 - lane, source_width - column, size - done)
        pieces.append((row, block, lane, done, length))
        done += length
    return pieces


def join_pieces(pieces, load, rows):
    lanes = lax.broadcasted_iota(jnp.int32, (rows, 128), 1)
    value = None
    for row, block, lane, here, length in pieces:
        part = load(row, block)
        if lane != here:
            part = pltpu.roll(part, (here - lane) % 128, 1)
        if value is None:
            inside = lanes < here + length
            value = part if here + length == 128 else jnp.where(inside, part, 0.0)
        else:
            value = jnp.where((lanes >= here) & (lanes < here + length), part, value)
    return value


def spread_kernel(ranks, low_ref, *refs):
    outs, wide, slots_ref = refs[:8], refs[8], refs[9]
    widen(low_ref, slots_ref, low_ref.shape[0])
    for index, (rows, width, bases) in enumerate(slice_places(ranks)):
        group, tiles = row_group(width)
        count = rows // group
        blocks = -(-width // 128)
        for level in range(2):
            out = outs[level * 4 + index]
            for row in range(group):
                for block in range(blocks):
                    start = row * width + block * 128
                    pieces = lane_pieces(start, min(128, width - block * 128), 128)

                    def load(tile, unused, base=bases[level]):
                        return slots_ref[pl.ds(base + tile, count, stride=tiles), :]

                    value = join_pieces(pieces, load, count)
                    at = pl.ds(row, count, stride=group) if group > 1 else pl.ds(0, count)
                    wide[block, at, :] = value
            padded = out.shape[0]
            for block in range(blocks):
                if padded > rows:
                    wide[block, rows:padded, :] = jnp.zeros((padded - rows, 128), jnp.float32)
                out[:, block * 128 : (block + 1) * 128] = wide[block, :padded, :].astype(out.dtype)


def collect_kernel(ranks, *refs):
    parts, slots_ref, square_ref, wide = refs[:8], refs[8], refs[9], refs[10]
    square_ref[...] = jnp.zeros_like(square_ref)
    end = slots_ref.shape[0]
    total = 0
    for index, (rows, width, bases) in enumerate(slice_places(ranks)):
        group, tiles = row_group(width)
        count = rows // group
        total += 2 * count * tiles
        for level in range(2):
            part = parts[level * 4 + index]
            for block in range(-(-width // 128)):
                wide[block, :rows, :] = part[:rows, block * 128 : (block + 1) * 128]
            for tile in range(tiles):
                pieces = lane_pieces(tile * 128, 128, width)

                def load(row, block):
                    at = pl.ds(row, count, stride=group) if group > 1 else pl.ds(0, count)
                    return wide[block, at, :]

                value = join_pieces(pieces, load, count)
                slots_ref[pl.ds(bases[level] + tile, count, stride=tiles), :] = value
                square_ref[:1, :] += jnp.sum(value * value, axis=0, keepdims=True)
    slots_ref[total:end, :] = jnp.zeros((end - total, 128), jnp.float32)


def spread_slots(slots, ranks):
    plan = layer_plan(ranks) * 2
    tall = max(entry[1] for entry in plan)
    broad = max(entry[2] for entry in plan)
    return pl.pallas_call(
        functools.partial(spread_kernel, ranks),
        out_shape=[jax.ShapeDtypeStruct(entry[1:], jnp.bfloat16) for entry in plan],
        in_specs=[VMEM],
        out_specs=[VMEM] * len(plan),
        scratch_shapes=[
            pltpu.VMEM((broad // 128, tall + SPARE_ROWS, 128), jnp.float32),
            pltpu.VMEM(slots.shape, jnp.float32),
        ],
        compiler_params=PARAMS,
        name="spread_slots",
    )(slots)


def collect_slots(parts, rows, ranks):
    tall = max(part.shape[0] for part in parts)
    broad = max(part.shape[1] for part in parts)
    return pl.pallas_call(
        functools.partial(collect_kernel, ranks),
        out_shape=(
            jax.ShapeDtypeStruct((rows, 128), jnp.float32),
            jax.ShapeDtypeStruct((8, 128), jnp.float32),
        ),
        in_specs=[VMEM] * len(parts),
        out_specs=(VMEM, VMEM),
        scratch_shapes=[pltpu.VMEM((broad // 128, tall + SPARE_ROWS, 128), jnp.float32)],
        compiler_params=PARAMS,
        name="collect_slots",
    )(*parts)


def whole_weights(wholes, ranks):
    qkv, proj, up, down = wholes
    return (qkv.reshape(D, -1), proj.reshape(-1, D), up.reshape(D, -1), down.reshape(-1, D))


def whole_parts(grads, ranks):
    qkv, proj, up, down = grads
    shapes = [whole_shape(entry) for entry in layer_plan(ranks)]
    return [part.reshape(shape) for part, shape in zip((qkv, proj, up, down), shapes)]


GROUP_HEADS = HEADS // 4
GROUP_WIDTH = HEADS * HD // 4


def dot_nt(left, right):
    return lax.dot_general(left, right, (((1,), (1,)), ((), ())), preferred_element_type=jnp.float32)


def dot_tn(left, right):
    return lax.dot_general(left, right, (((0,), (0,)), ((), ())), preferred_element_type=jnp.float32)


def head_parts(packed_ref, head):
    return [
        packed_ref[:, index * GROUP_WIDTH + head * HD : index * GROUP_WIDTH + (head + 1) * HD]
        for index in range(3)
    ]


def head_probs(queries, key_rows):
    scores = dot_nt(queries, key_rows) * HD ** (-0.5)
    powers = jnp.exp(scores - jnp.max(scores, axis=-1, keepdims=True))
    return powers / jnp.sum(powers, axis=-1, keepdims=True)


def pad_columns(values, own):
    rows = values.shape[0]
    gap = jnp.zeros((rows, PROJ_ROWS - own), values.dtype)
    parts = []
    for start in range(0, values.shape[1], own):
        parts += [values[:, start : start + own], gap]
    return jnp.concatenate(parts, axis=1)


def attend_kernel(own, packed_ref, out_ref):
    heads = [head_parts(packed_ref, head) for head in range(GROUP_HEADS)]
    probs = [head_probs(queries, key_rows) for queries, key_rows, unused in heads]
    mixed = [
        product(prob.astype(jnp.bfloat16), parts[2]).astype(out_ref.dtype)
        for prob, parts in zip(probs, heads)
    ]
    out_ref[...] = pad_columns(jnp.concatenate(mixed, axis=1), own)


def attend_back_kernel(packed_ref, grad_ref, spread_ref, out_ref):
    heads = [head_parts(packed_ref, head) for head in range(GROUP_HEADS)]
    every = range(GROUP_HEADS)
    grads = grad_ref[...]
    grad_mixed = [dot_nt(grads, spread_ref[head]).astype(jnp.bfloat16) for head in every]
    probs = [head_probs(queries, key_rows) for queries, key_rows, unused in heads]
    grad_probs = [dot_nt(grad_mixed[head], heads[head][2]) for head in every]
    grad_values = [dot_tn(probs[head].astype(jnp.bfloat16), grad_mixed[head]) for head in every]
    grad_scores = []
    for prob, grad_prob in zip(probs, grad_probs):
        score = prob * (grad_prob - jnp.sum(grad_prob * prob, axis=-1, keepdims=True))
        grad_scores.append((score * HD ** (-0.5)).astype(jnp.bfloat16))
    grad_queries = [product(grad_scores[head], heads[head][1]) for head in every]
    grad_keys = [dot_tn(grad_scores[head], heads[head][0]) for head in every]
    for index, parts in enumerate((grad_queries, grad_keys, grad_values)):
        for head, part in enumerate(parts):
            start = index * GROUP_WIDTH + head * HD
            out_ref[:, start : start + HD] = part.astype(out_ref.dtype)
    rows, width = out_ref.shape
    out_ref[:, 3 * GROUP_WIDTH :] = jnp.zeros((rows, width - 3 * GROUP_WIDTH), out_ref.dtype)


def spread_heads(own):
    columns = jnp.arange(GROUP_WIDTH // own * PROJ_ROWS)
    source = columns // PROJ_ROWS * own + columns % PROJ_ROWS
    source = jnp.where(columns % PROJ_ROWS < own, source, -1)
    hot = jnp.arange(GROUP_WIDTH)[:, None] == source[None, :]
    return hot.astype(jnp.bfloat16).reshape(GROUP_HEADS, HD, -1)


def attend_call(kernel, images, inputs, constants, out_width, name):
    rows = inputs[0].shape[0] // images

    def block(width):
        return pl.BlockSpec((rows, width), lambda image, group: (image, group))

    return pl.pallas_call(
        kernel,
        grid=(images, 4),
        out_shape=jax.ShapeDtypeStruct((images * rows, 4 * out_width), jnp.bfloat16),
        in_specs=[block(one.shape[1] // 4) for one in inputs]
        + [pl.BlockSpec(one.shape, lambda image, group: (0, 0, 0)) for one in constants],
        out_specs=block(out_width),
        compiler_params=PARAMS,
        name=name,
    )(*inputs, *constants)


def attend(packed, own, images):
    kernel = functools.partial(attend_kernel, own)
    return attend_call(kernel, images, [packed], [], GROUP_WIDTH // own * PROJ_ROWS, "attend")


def attend_back(packed, grads, own, images):
    constants = [spread_heads(own)]
    return attend_call(
        attend_back_kernel, images, [packed, grads], constants, QKV_WIDTH, "attend_back"
    )


def gelu_and_slope(values):
    factor = math.sqrt(2.0 / math.pi)
    square = values * values
    bend = jnp.tanh(factor * values * (1.0 + 0.044715 * square))
    half = 0.5 * (1.0 + bend)
    slope = half + 0.5 * values * (1.0 - bend * bend) * factor * (1.0 + 3.0 * 0.044715 * square)
    return values * half, slope


def own_forward(state, weights, modulate, own):
    qkv_weight, proj_weight, up_weight, down_weight = weights
    images, rows, columns = state.shape
    shift_one, scale_one, gate_one, shift_two, scale_two, gate_two = [
        modulate[index] for index in range(6)
    ]
    normed_one, spread_one = normalize(state)
    full_one = (normed_one * (1.0 + scale_one) + shift_one).astype(jnp.bfloat16)
    flat_one = full_one.reshape(-1, columns)
    packed = product(flat_one, qkv_weight).astype(jnp.bfloat16)
    attended = attend(packed, own, images)
    branch_one = product(attended, proj_weight).reshape(state.shape)
    middle = state + gate_one * branch_one
    normed_two, spread_two = normalize(middle)
    full_two = (normed_two * (1.0 + scale_two) + shift_two).astype(jnp.bfloat16)
    flat_two = full_two.reshape(-1, columns)
    activated, slope = gelu_and_slope(product(flat_two, up_weight))
    activated = activated.astype(jnp.bfloat16)
    branch_two = product(activated, down_weight).reshape(state.shape)
    result = middle + gate_two * branch_two
    saved = (
        normed_one,
        spread_one,
        flat_one,
        packed,
        attended,
        branch_one,
        normed_two,
        spread_two,
        flat_two,
        slope,
        activated,
        branch_two,
    )
    return (result, saved)


def own_backward(grad_out, saved, weights, modulate, own):
    (
        normed_one,
        spread_one,
        flat_one,
        packed,
        attended,
        branch_one,
        normed_two,
        spread_two,
        flat_two,
        slope,
        activated,
        branch_two,
    ) = saved
    qkv_weight, proj_weight, up_weight, down_weight = weights
    images, rows, columns = grad_out.shape
    shift_one, scale_one, gate_one, shift_two, scale_two, gate_two = [
        modulate[index] for index in range(6)
    ]
    grad_gate_two = jnp.sum(grad_out * branch_two, axis=1)
    back_two = (gate_two * grad_out).astype(jnp.bfloat16).reshape(-1, columns)
    grad_down = product(activated.T, back_two).astype(jnp.bfloat16)
    grad_pre = (product(back_two, down_weight.T) * slope).astype(jnp.bfloat16)
    grad_up = product(flat_two.T, grad_pre).astype(jnp.bfloat16)
    grad_hidden_two = product(grad_pre, up_weight.T)
    grad_hidden_two = grad_hidden_two.reshape(grad_out.shape)
    grad_shift_two = jnp.sum(grad_hidden_two, axis=1)
    grad_scale_two = jnp.sum(grad_hidden_two * normed_two, axis=1)
    grad_middle = grad_out + normalize_back(
        grad_hidden_two * (1.0 + scale_two), normed_two, spread_two
    )
    grad_gate_one = jnp.sum(grad_middle * branch_one, axis=1)
    back_one = (gate_one * grad_middle).astype(jnp.bfloat16).reshape(-1, columns)
    grad_proj = product(attended.T, back_one).astype(jnp.bfloat16)
    grad_attended = product(back_one, proj_weight.T).astype(jnp.bfloat16)
    grad_packed = attend_back(packed, grad_attended, own, images)
    grad_qkv = product(flat_one.T, grad_packed).astype(jnp.bfloat16)
    grad_hidden_one = product(grad_packed, qkv_weight.T)
    grad_hidden_one = grad_hidden_one.reshape(grad_out.shape)
    grad_shift_one = jnp.sum(grad_hidden_one, axis=1)
    grad_scale_one = jnp.sum(grad_hidden_one * normed_one, axis=1)
    grad_state = grad_middle + normalize_back(
        grad_hidden_one * (1.0 + scale_one), normed_one, spread_one
    )
    grad_mod = jnp.concatenate(
        [
            grad_shift_one,
            grad_scale_one,
            grad_gate_one,
            grad_shift_two,
            grad_scale_two,
            grad_gate_two,
        ],
        axis=1,
    )
    return (grad_state, grad_mod, (grad_qkv, grad_proj, grad_up, grad_down))


def contract(left, right, left_axis, right_axis):
    return lax.dot_general(
        left,
        right,
        (((left_axis,), (right_axis,)), ((), ())),
        preferred_element_type=jnp.float32,
    )


def contract_wide(left, right, left_axis, right_axis):
    return lax.dot_general(
        left.astype(jnp.float32),
        right.astype(jnp.float32),
        (((left_axis,), (right_axis,)), ((), ())),
        precision=highest,
        preferred_element_type=jnp.float32,
    )


def silu_back(values, grads):
    unused, pull = jax.vjp(jax.nn.silu, values)
    return pull(grads)[0]


def local(
    big_copy,
    big_master,
    big_first,
    big_second,
    ada_copy,
    ada_master,
    ada_first,
    ada_second,
    rest_copy,
    rest_master,
    rest_first,
    rest_second,
    owner_tiles,
    kept_patches,
    kept_pos,
    timestep,
    label,
    owner,
    target,
    step,
):
    groups = lax.axis_size("mp")
    ranks = lax.axis_size("dp")
    world = groups * ranks
    my_rank = lax.axis_index("dp")
    micro = kept_patches.shape[0]
    own_columns = D // world
    columns = D

    owned = big_copy.shape[1]
    all_dest, unused_slot = tile_place(owner_tiles, ranks)
    all_hot = all_dest.reshape(ranks, owned, 1) == jnp.arange(ranks)
    rounds = (jnp.max(jnp.sum(all_hot.astype(jnp.int32), axis=1)) + CHUNK_ROWS - 1) // CHUNK_ROWS
    own_tiles = lax.dynamic_slice(owner_tiles, (my_rank * owned,), (owned,))
    dest, slot = tile_place(own_tiles, ranks)
    rank, counts = rank_within(dest, ranks)
    rest_own = rest_copy.reshape(own_columns, REST_ROWS)
    edges = [0, PD, PD + FREQ, PD + FREQ + D, PD + FREQ + D + CLASSES, REST_ROWS]
    win_t, one_t, two_t, table_t, tail_t = [
        rest_own[:, edges[i] : edges[i + 1]] for i in range(5)
    ]
    ends_size = own_columns * (2 * PD + 1)
    one_size = own_columns * FREQ
    whole_numbers = jnp.concatenate([timestep[:, 0], label[:, 0]])
    told = jnp.concatenate(
        [
            jnp.concatenate([win_t, tail_t], axis=1).reshape(-1),
            one_t.reshape(-1),
            (whole_numbers // 32).astype(jnp.bfloat16),
            (whole_numbers % 32).astype(jnp.bfloat16),
        ]
    )
    told = pad_to(told, 0, -(-told.shape[0] // 2048) * 2048).reshape(-1, 128)
    told_entry = (True, told.shape[0], 128)
    brought = []

    def carry_first(buf, new_tags):
        arrays = [
            [told],
            [target.reshape(-1, 128)],
            [new_tags.reshape(ranks, -1, TAG_LANES)],
            [buf.reshape(ranks, -1, 128)],
        ]
        kinds = ("share", "swap", "swap")
        jobs = [("gather", (told_entry,), told_entry[1], LAG)]
        jobs += [(kind, (None,), 0, 0) for kind in kinds]
        got = travel(jobs, arrays, 6, "exchange_inputs")
        brought.extend(got)
        return got[3][0].reshape(buf.shape), got[2][0].reshape(new_tags.shape)

    slots, tags = tiles_to_slots(big_copy[0], dest, slot, rank, counts, rounds, carry_first)
    told = brought[0][0].reshape(groups, ranks, -1)
    facts = told[:, :, ends_size + one_size : ends_size + one_size + 4 * micro].astype(jnp.int32)
    facts = facts.reshape(world, -1)
    told = told.transpose(1, 0, 2).reshape(world, -1)
    goals = brought[1][0].reshape(ranks, micro, -1, 128)
    facts = facts[:, : 2 * micro] * 32 + facts[:, 2 * micro :]
    stamps = facts[:, :micro].reshape(-1)
    tags_all = facts[:, micro:].reshape(-1)
    ends = told[:, :ends_size].reshape(columns, -1)
    embed_weight = ends[:, :PD].T
    mask_token = ends[:, PD].astype(jnp.float32)
    head_weight = ends[:, PD + 1 :]
    count_all = micro * world
    features = jax.vmap(time_features)(stamps).astype(jnp.bfloat16)
    pre_time = contract(features, one_t, 1, 1)
    one_whole = told[:, ends_size : ends_size + one_size].reshape(columns, FREQ)
    hidden_all = jax.nn.silu(contract(features, one_whole, 1, 1)).astype(jnp.bfloat16)
    picks = (tags_all[:, None] == jnp.arange(CLASSES, dtype=jnp.int32)[None, :]).astype(
        jnp.bfloat16
    )
    cond_own = contract(hidden_all, two_t, 1, 1) + contract(picks, table_t, 1, 1)
    signal_own = jax.nn.silu(cond_own).astype(jnp.bfloat16)
    ada_own = ada_copy.reshape(own_columns, 14 * columns)
    mod_rows = micro * 14
    mod_entry = (True, 32, columns)
    padded = mod_entry[1] // micro
    mods = product(signal_own, pad_to(ada_own, 1, padded * columns)).reshape(-1, padded, columns)
    mods = mods.reshape(whole_shape(mod_entry))
    plan = (layer_plan(ranks) * 2)[:-1]
    spread = spread_slots(slots, ranks)
    wholes, mods = travel(
        (("gather", plan, 16, LAG), ("sum", (mod_entry,), 16, 6)),
        [spread[:-1], [mods]],
        1,
        "gather_weights",
    )
    last, wholes = lax.optimization_barrier((spread[-1], wholes))
    last = lax.all_gather(last, ("mp", "dp"), axis=0, tiled=True)
    weights = [whole_weights(wholes[:4], ranks), whole_weights((*wholes[4:], last), ranks)]
    own = GROUP_WIDTH // ranks
    mods = mods[0].reshape(micro, padded, columns).transpose(1, 0, 2)[:, :, None, :]
    mod_enc = mods[:6]
    mod_dec = mods[6:12]
    final_shift = mods[12]
    final_scale = mods[13]

    goal = jnp.stack([goals[owner[b, 0], b] for b in range(micro)]).reshape(micro, SEQ, PD)
    positions = jnp.asarray(position_constant(columns))
    images = ranks * groups
    inv_count = 1.0 / (PD * micro * images * KEEP)
    place = kept_pos[:, 0]
    patches = kept_patches[:, 0].astype(jnp.bfloat16)
    hits = (
        jnp.arange(SEQ, dtype=jnp.int32)[None, :, None] == place[:, None, :]
    ).astype(jnp.float32)
    hits_low = hits.astype(jnp.bfloat16)
    kept = jnp.sum(hits, axis=2)[:, :, None]
    embedded = product(patches.reshape(-1, PD), embed_weight).reshape(micro, KEEP, columns)
    embedded = embedded + jnp.take(positions, place, axis=0)
    enc_out, enc_saved = own_forward(embedded, weights[0], mod_enc, own)
    sent = enc_out.astype(jnp.bfloat16)
    dec_in = (
        jnp.einsum("bpr,brd->bpd", hits_low, sent, preferred_element_type=jnp.float32)
        + (1.0 - kept) * mask_token[None, None, :]
        + positions[None]
    )
    dec_out, dec_saved = own_forward(dec_in, weights[1], mod_dec, own)
    normed_final, spread_final = normalize(dec_out)
    head_in = (normed_final * (1.0 + final_scale) + final_shift).astype(jnp.bfloat16)
    flat_head = head_in.reshape(-1, columns)
    output = product(flat_head, head_weight).reshape(micro, SEQ, PD)
    error = output - goal
    weight = kept + MASKED_WEIGHT * (1.0 - kept)
    loss_sum = jnp.sum(weight * error * error) * inv_count

    grad_output = (2.0 * inv_count * weight * error).astype(jnp.bfloat16).reshape(-1, PD)
    grad_head = contract(grad_output, flat_head, 0, 0)
    grad_head_in = product(grad_output, head_weight.T).reshape(dec_out.shape)
    grad_final = jnp.concatenate(
        [jnp.sum(grad_head_in, axis=1), jnp.sum(grad_head_in * normed_final, axis=1)], axis=1
    )
    grad_dec_out = normalize_back(grad_head_in * (1.0 + final_scale), normed_final, spread_final)
    grad_dec_in, grad_mod_dec, dec_grads = own_backward(
        grad_dec_out, dec_saved, weights[1], mod_dec, own
    )
    last_sum = lax.psum_scatter(dec_grads[3], ("mp", "dp"), scatter_dimension=0, tiled=True)
    grad_mask = jnp.sum((1.0 - kept) * grad_dec_in, axis=(0, 1))[None, :]
    grad_sent = jnp.einsum(
        "bpr,bpd->brd",
        hits_low,
        grad_dec_in.astype(jnp.bfloat16),
        preferred_element_type=jnp.float32,
    )
    grad_embedded, grad_mod_enc, enc_grads = own_backward(
        grad_sent, enc_saved, weights[0], mod_enc, own
    )
    down_sum = lax.psum_scatter(enc_grads[3], ("mp", "dp"), scatter_dimension=0, tiled=True)
    grad_embed = contract_wide(
        patches.reshape(-1, PD), grad_embedded.reshape(-1, columns), 0, 0
    )

    vectors = jnp.concatenate([grad_mod_enc, grad_mod_dec, grad_final], axis=1)
    vectors = vectors.astype(jnp.bfloat16).reshape(mod_rows, columns)
    vectors = pad_to(vectors, 0, mod_entry[1])
    sums, vectors = travel(
        (("sum", (layer_plan(ranks)[:-1]) * 2, 16, LAG), ("gather", (mod_entry,), 16, 6)),
        [whole_parts(enc_grads, ranks)[:-1] + whole_parts(dec_grads, ranks)[:-1], [vectors]],
        2,
        "sum_gradients",
    )
    sums = [*sums[:3], down_sum.astype(jnp.float32), *sums[3:], last_sum.astype(jnp.float32)]
    sums, big_squares = collect_slots(sums, owned + 16, ranks)
    vectors = vectors[0]
    back = gather_rows(sums, tags, jnp.bfloat16)
    vectors = vectors.reshape(world, mod_entry[1], columns)[:, :mod_rows].reshape(count_all, -1)
    owned_ada = contract(signal_own, vectors, 0, 0).reshape(-1)
    grad_signal = contract(vectors, ada_own, 1, 1)
    grad_cond = silu_back(cond_own, grad_signal)
    grad_two_t = contract_wide(grad_cond, hidden_all, 0, 0)
    grad_table_t = contract_wide(grad_cond, picks, 0, 0)
    shared = jnp.concatenate(
        [contract_wide(grad_cond, two_t, 1, 0), grad_embed, grad_mask, grad_head], axis=0
    )
    shared_rows = shared.shape[0]
    shared = shared.reshape(shared_rows, ranks, groups, own_columns).transpose(2, 1, 0, 3)
    shared = pad_to(shared.reshape(world, -1), 1, 4096)
    shared_entry = (True, 32, 128)
    shared, back = travel(
        (("sum", (shared_entry,), 32, LAG), ("swap", (None,), 0, 0)),
        [[shared.reshape(whole_shape(shared_entry))], [back.reshape(ranks, -1, 128)]],
        5,
        "sum_shared",
    )
    shared = shared[0]
    shared = shared.reshape(-1)[: shared_rows * own_columns].reshape(shared_rows, own_columns)
    grad_pre = silu_back(pre_time, shared[:count_all])
    grad_one_t = contract_wide(grad_pre, features, 0, 0)
    ends_t = shared[count_all:].T
    owned_rest = jnp.concatenate(
        [ends_t[:, :PD], grad_one_t, grad_two_t, grad_table_t, ends_t[:, PD:]], axis=1
    ).reshape(-1)

    squares = jnp.sum(big_squares) + jnp.sum(owned_ada * owned_ada) + jnp.sum(owned_rest * owned_rest)
    totals = jnp.broadcast_to(pad_to(jnp.stack([loss_sum, squares]), 0, 128), (8, 128))
    totals = jnp.sum(push_all(totals, world, 8, "push_totals")[:, 0, :2], axis=0)
    back = back[0].reshape(-1, 128)
    owned_big = slots_to_tiles(sums, back, dest, slot, rank, counts, rounds)
    grad_norm = jnp.sqrt(totals[1])
    clip = jnp.minimum(1.0, MAX_NORM / (grad_norm + 1e-06))
    count = step[0].astype(jnp.float32)
    big_out = adam_update(
        owned_big.reshape(big_master.shape), big_master, big_first, big_second, clip, count
    )
    ada_out = adam_update(owned_ada, ada_master, ada_first, ada_second, clip, count)
    rest_out = adam_update(owned_rest, rest_master, rest_first, rest_second, clip, count)
    return (
        totals[:1],
        grad_norm.reshape(1),
        big_out[0],
        big_out[1],
        big_out[2],
        big_out[3],
        ada_out[0],
        ada_out[1],
        ada_out[2],
        ada_out[3],
        rest_out[0],
        rest_out[1],
        rest_out[2],
        rest_out[3],
    )


def whole_columns(mesh):
    ranks, groups = mesh.shape["dp"], mesh.shape["mp"]
    return groups == 4 and D % (ranks * groups) == 0 and ranks == 8


def solution(mesh):
    body = local if whole_columns(mesh) else local_general
    in_specs = (
        P("mp", "dp", None),
        P("mp", "dp", None),
        P("mp", "dp", None),
        P("mp", "dp", None),
        P(("dp", "mp")),
        P(("dp", "mp")),
        P(("dp", "mp")),
        P(("dp", "mp")),
        P(("dp", "mp")),
        P(("dp", "mp")),
        P(("dp", "mp")),
        P(("dp", "mp")),
        P(),
        P(None, ("dp", "mp"), None, None),
        P(None, ("dp", "mp"), None),
        P(None, ("dp", "mp")),
        P(None, ("dp", "mp")),
        P(None, ("dp", "mp")),
        P(None, ("dp", "mp"), None, None),
        P(),
    )
    out_specs = (
        P(),
        P(),
        P("mp", "dp", None),
        P("mp", "dp", None),
        P("mp", "dp", None),
        P("mp", "dp", None),
        P(("dp", "mp")),
        P(("dp", "mp")),
        P(("dp", "mp")),
        P(("dp", "mp")),
        P(("dp", "mp")),
        P(("dp", "mp")),
        P(("dp", "mp")),
        P(("dp", "mp")),
    )
    return jax.shard_map(body, mesh=mesh, in_specs=in_specs, out_specs=out_specs, check_vma=False)
```
